32 devices in a mesh: frow: 4 (over y, x), fcol: 8 (over z, core).
Axes of the slice: x: 2, y: 2, z: 4, core: 2. Of those that a mesh axis runs over, the one named last changes fastest.
Arguments:
- vis: float32 [2, 8192], P(None, ('frow', 'fcol')), may hold values from -6 to 6
- station_pairs: int32 [2, 8192], P(None, ('frow', 'fcol')), may hold values from 0 to 511
- visibility_time_slot: int32 [8192], P(('frow', 'fcol')), may hold values from 0 to 15
- station_u_cells: int32 [512], replicated, may hold values from -1024 to 1023
- station_v_cells: int32 [512], replicated, may hold values from -1024 to 1023
- facet_station_gains: float32 [4, 8, 2, 8192], P('frow', 'fcol'), may hold values from -6 to 6
- holder_device_order: int32 [32], replicated, may hold values from 0 to 31, each once
Outputs:
- image: float32 [4096, 4096], P('frow', 'fcol')
The draws below stay inside these ranges and needn't reach their ends.
Inputs may be any that keep to these rules, and one draw needn't show every extreme that they name: `holder_device_order`: a permutation; its first 4 entries name distinct devices.
All inputs are finite; a program needn't handle non-finite values.
Results may differ from the reference program's by a relative error of at most 0.0037.
Values sent between devices are 32-bit elements; how exact they have to be, the bound alone decides.
No kernel may reach another device: no remote copies, remote signals or barrier semaphores. Data moves between devices by JAX's collectives and lax.ppermute only.
A program may use at most 64 MiB of HBM per device.

```python
import math
import jax
import jax.numpy as jnp
from jax import lax

R = 1024
C = 512
M = 64
STATION_COUNT = 512
NT = 16
NBLK = 4
BLOCK_VISIBILITY = 256
IMAGE_ROW_COUNT = 4096
IMAGE_COLUMNS = 4096
N_FROW = 4
N_FCOL = 8
DEVICES = 32


def place_ends(values, rng, low, top_value):
    longest = values.shape.index(max(values.shape))
    spots = []
    for shift in (0, 1):
        where = [jax.random.randint(jax.random.fold_in(rng, axis), (), 0, length) for axis, length in enumerate(values.shape)]
        where[longest] = (where[longest] + shift) % values.shape[longest]
        spots.append(tuple(where))
    return values.at[spots[0]].set(low).at[spots[1]].set(top_value)


def level_of(own_key, dims, cuts, smallest, top_value):
    def one(dim, parts):
        draws = jax.random.uniform(jax.random.fold_in(jax.random.fold_in(own_key, 6), dim), (parts,), jnp.float32, smallest / len(cuts), top_value / len(cuts))
        return jnp.repeat(jnp.exp(draws), dims[dim] // parts).reshape((-1,) + (1,) * (len(dims) - dim - 1))

    loudness = one(*cuts[0])
    for cut in cuts[1:]:
        loudness = loudness * one(*cut)
    return loudness


def noise(own_key, dims, spread, reach, split=(), held_as=jnp.bfloat16):
    drawn = spread * jax.random.normal(own_key, dims, jnp.float32)
    if split:
        drawn = drawn * level_of(own_key, dims, split, -0.22, 0.18)
    return jnp.clip(drawn, -reach, reach).astype(held_as)


def setup_inputs(seed: int = 0) -> dict:
    seeds = jax.random.split(jax.random.key(seed), 8)
    return {
        "vis": noise(seeds[0], (2, DEVICES * BLOCK_VISIBILITY), 1.0, 6.0, ((1, 32),), jnp.float32),
        "station_pairs": place_ends(jax.random.randint(seeds[1], (2, DEVICES * BLOCK_VISIBILITY), 0, STATION_COUNT), jax.random.fold_in(seeds[1], 1), 0, STATION_COUNT - 1).astype(jnp.int32),
        "visibility_time_slot": place_ends(jax.random.randint(seeds[2], (DEVICES * BLOCK_VISIBILITY,), 0, NT), jax.random.fold_in(seeds[2], 1), 0, NT - 1).astype(jnp.int32),
        "station_u_cells": place_ends(jax.random.randint(seeds[3], (STATION_COUNT,), 0 - IMAGE_ROW_COUNT // 4, IMAGE_ROW_COUNT // 4), jax.random.fold_in(seeds[3], 1), 0 - IMAGE_ROW_COUNT // 4, (IMAGE_ROW_COUNT // 4) - 1).astype(jnp.int32),
        "station_v_cells": place_ends(jax.random.randint(seeds[4], (STATION_COUNT,), 0 - IMAGE_COLUMNS // 4, IMAGE_COLUMNS // 4), jax.random.fold_in(seeds[4], 1), 0 - IMAGE_COLUMNS // 4, (IMAGE_COLUMNS // 4) - 1).astype(jnp.int32),
        "facet_station_gains": noise(seeds[5], (N_FROW, N_FCOL, 2, STATION_COUNT * NT), 1.0, 6.0, ((0, 4), (1, 8)), jnp.float32),
        "holder_device_order": jax.random.permutation(seeds[6], DEVICES).astype(jnp.int32),
    }


def taper_line(length):
    index = jnp.arange(length + 2 * M, dtype=jnp.int32).astype(jnp.float32)
    rising = (index + 0.5) / (2.0 * M)
    falling = (length + 2 * M - index - 0.5) / (2.0 * M)
    return jnp.minimum(jnp.minimum(rising, falling), 1.0)

def phase_angles(freq, pixels, modulus):
    cells = jnp.mod(freq, modulus)[None, :] * jnp.mod(pixels, modulus)[:, None] % modulus
    return cells.astype(jnp.float32) * (2.0 * math.pi / modulus)

def block_weights(values, baseline_pairs, slots, g_tab, scale):
    first = baseline_pairs[0] * NT + slots
    second = baseline_pairs[1] * NT + slots
    g1r = g_tab[0][first]
    g1i = g_tab[1][first]
    g2r = g_tab[0][second]
    g2i = g_tab[1][second]
    real_gain = g1r * g2r + g1i * g2i
    imag_gain = g1i * g2r - g1r * g2i
    wreal = scale * (values[0] * real_gain - values[1] * imag_gain)
    wimag = scale * (values[0] * imag_gain + values[1] * real_gain)
    return (wreal, wimag)

def reference(vis, station_pairs, visibility_time_slot, station_u_cells, station_v_cells, facet_station_gains, holder_device_order):
    n_rows = R * N_FROW
    n_cols = C * N_FCOL
    values, baseline_pairs, slots = ([], [], [])
    for step in range(NBLK):
        start_offset = (holder_device_order[step] * BLOCK_VISIBILITY).astype(jnp.int32)
        zero_value = jnp.zeros((), jnp.int32)
        values.append(lax.dynamic_slice(vis, (zero_value, start_offset), (2, BLOCK_VISIBILITY)))
        baseline_pairs.append(lax.dynamic_slice(station_pairs, (zero_value, start_offset), (2, BLOCK_VISIBILITY)))
        slots.append(lax.dynamic_slice(visibility_time_slot, (start_offset,), (BLOCK_VISIBILITY,)))
    values = jnp.concatenate(values, 1)
    baseline_pairs = jnp.concatenate(baseline_pairs, 1)
    slots = jnp.concatenate(slots, 0)
    frequency_u = station_u_cells[baseline_pairs[0]] - station_u_cells[baseline_pairs[1]]
    frequency_v = station_v_cells[baseline_pairs[0]] - station_v_cells[baseline_pairs[1]]
    scale = 0.5 / math.sqrt(NBLK * BLOCK_VISIBILITY)
    row_taper = taper_line(R)
    col_taper = taper_line(C)
    canvas = jnp.zeros((n_rows + 2 * M, n_cols + 2 * M), jnp.float32)

    def one_facet(flat, canvas):
        frow_at = (flat // N_FCOL).astype(jnp.int32)
        fcol_at = (flat % N_FCOL).astype(jnp.int32)
        g_tab = facet_station_gains[frow_at, fcol_at]
        wreal, wimag = block_weights(values, baseline_pairs, slots, g_tab, scale)
        rows = frow_at * R - M + jnp.arange(R + 2 * M, dtype=jnp.int32)
        cols = fcol_at * C - M + jnp.arange(C + 2 * M, dtype=jnp.int32)
        theta = phase_angles(frequency_u, rows, n_rows)
        phi = phase_angles(frequency_v, cols, n_cols).T
        row_table = jnp.concatenate([jnp.cos(theta), jnp.sin(theta)], 1).astype(jnp.bfloat16)
        top = wreal[:, None] * jnp.cos(phi) - wimag[:, None] * jnp.sin(phi)
        bottom = -(wimag[:, None] * jnp.cos(phi) + wreal[:, None] * jnp.sin(phi))
        col_table = jnp.concatenate([top, bottom], 0).astype(jnp.bfloat16)
        facet = jnp.dot(row_table.astype(jnp.float32), col_table.astype(jnp.float32), precision=lax.Precision.HIGHEST)
        tapered = facet * row_taper[:, None] * col_taper[None, :]
        corner = (frow_at * R, fcol_at * C)
        current = lax.dynamic_slice(canvas, corner, (R + 2 * M, C + 2 * M))
        return lax.dynamic_update_slice(canvas, current + tapered, corner)
    canvas = lax.fori_loop(0, N_FROW * N_FCOL, one_facet, canvas)
    return canvas[M:M + n_rows, M:M + n_cols]
```

```python
import math

import jax
import jax.numpy as jnp
from jax import lax
from jax.sharding import PartitionSpec as P

R = 1024
C = 512
M = 64
NT = 16
NBLK = 4


def extended_2(x, sides, width):
    for axis, dim in sides:
        size, length = (lax.axis_size(axis), x.shape[dim])
        up = [(i, (i + 1) % size) for i in range(size - 1)]
        down = [(j, i) for i, j in up]
        last = lax.slice_in_dim(x, length - width, length, axis=dim)
        leading = lax.slice_in_dim(x, 0, width, axis=dim)
        before = lax.ppermute(last, axis, up)
        after = lax.ppermute(leading, axis, down)
        x = jnp.concatenate([before, x, after], axis=dim)
    return x


def taper_line(length):
    index = jnp.arange(length + 2 * M, dtype=jnp.int32).astype(jnp.float32)
    rising = (index + 0.5) / (2.0 * M)
    falling = (length + 2 * M - index - 0.5) / (2.0 * M)
    return jnp.minimum(jnp.minimum(rising, falling), 1.0)


def phase_angles(freq, pixels, modulus):
    cells = jnp.mod(freq, modulus)[None, :] * jnp.mod(pixels, modulus)[:, None] % modulus
    return cells.astype(jnp.float32) * (2.0 * math.pi / modulus)


def block_weights(values, label_names, g_tab, scale):
    first = label_names[0] * NT + label_names[2]
    second = label_names[1] * NT + label_names[2]
    g1r = g_tab[0][first]
    g1i = g_tab[1][first]
    g2r = g_tab[0][second]
    g2i = g_tab[1][second]
    real_gain = g1r * g2r + g1i * g2i
    imag_gain = g1i * g2r - g1r * g2i
    wreal = scale * (values[0] * real_gain - values[1] * imag_gain)
    wimag = scale * (values[0] * imag_gain + values[1] * real_gain)
    return (wreal, wimag)


def fold_columns(field):
    edges = jnp.concatenate([field[:, :M], field[:, -M:]], 1)
    extended = extended_2(edges, (("fcol", 1),), M)
    inner = field[:, M:-M]
    return jnp.concatenate(
        [inner[:, :M] + extended[:, :M], inner[:, M:-M], inner[:, -M:] + extended[:, -M:]], 1
    )


def fold_rows(field):
    edges = jnp.concatenate([field[:M], field[-M:]], 0)
    extended = extended_2(edges, (("frow", 0),), M)
    inner = field[M:-M]
    return jnp.concatenate([inner[:M] + extended[:M], inner[M:-M], inner[-M:] + extended[-M:]], 0)


def shards(
    vis,
    station_pairs,
    visibility_time_slot,
    station_u_cells,
    station_v_cells,
    facet_station_gains,
    holder_device_order,
):
    count_rows = lax.axis_size("frow")
    count_cols = lax.axis_size("fcol")
    n_rows = R * count_rows
    n_cols = C * count_cols
    frow_at = lax.axis_index("frow")
    fcol_at = lax.axis_index("fcol")
    g_tab = facet_station_gains[0, 0]
    label_names = jnp.concatenate([station_pairs, visibility_time_slot[None, :]], 0)
    block_size = vis.shape[1]
    scale = 0.5 / math.sqrt(NBLK * block_size)
    rows = frow_at * R - M + jnp.arange(R + 2 * M, dtype=jnp.int32)
    cols = fcol_at * C - M + jnp.arange(C + 2 * M, dtype=jnp.int32)
    stacked = jnp.concatenate([vis, label_names.astype(jnp.float32)], 0)
    everyone = lax.all_gather(stacked, ("frow", "fcol"))
    gathered = [
        lax.dynamic_index_in_dim(everyone, holder_device_order[step], 0, keepdims=False)
        for step in range(NBLK)
    ]
    total = jnp.zeros((R + 2 * M, C + 2 * M), jnp.float32)
    for step in range(NBLK):
        values = gathered[step][:2]
        tag_names = gathered[step][2:].astype(jnp.int32)
        wreal, wimag = block_weights(values, tag_names, g_tab, scale)
        frequency_u = station_u_cells[tag_names[0]] - station_u_cells[tag_names[1]]
        frequency_v = station_v_cells[tag_names[0]] - station_v_cells[tag_names[1]]
        theta = phase_angles(frequency_u, rows, n_rows)
        phi = phase_angles(frequency_v, cols, n_cols).T
        row_table = jnp.concatenate([jnp.cos(theta), jnp.sin(theta)], 1).astype(jnp.bfloat16)
        top = wreal[:, None] * jnp.cos(phi) - wimag[:, None] * jnp.sin(phi)
        bottom = -(wimag[:, None] * jnp.cos(phi) + wreal[:, None] * jnp.sin(phi))
        col_table = jnp.concatenate([top, bottom], 0).astype(jnp.bfloat16)
        total = total + jnp.dot(row_table, col_table, preferred_element_type=jnp.float32)
    tapered = total * taper_line(R)[:, None] * taper_line(C)[None, :]
    image = fold_rows(fold_columns(tapered))
    return image


def solution(mesh):
    return jax.shard_map(
        shards,
        mesh=mesh,
        in_specs=(
            P(None, ("frow", "fcol")),
            P(None, ("frow", "fcol")),
            P(("frow", "fcol")),
            P(),
            P(),
            P("frow", "fcol", None, None),
            P(),
        ),
        out_specs=P("frow", "fcol"),
        check_vma=False,
    )
```

```python
import math

import jax
import jax.numpy as jnp
from jax import lax
from jax.sharding import PartitionSpec as P

R = 1024
C = 512
M = 64
NT = 16
NBLK = 4


def extended_2(x, sides, width):
    for axis, dim in sides:
        size, length = (lax.axis_size(axis), x.shape[dim])
        up = [(i, (i + 1) % size) for i in range(size - 1)]
        down = [(j, i) for i, j in up]
        last = lax.slice_in_dim(x, length - width, length, axis=dim)
        leading = lax.slice_in_dim(x, 0, width, axis=dim)
        before = lax.ppermute(last, axis, up)
        after = lax.ppermute(leading, axis, down)
        x = jnp.concatenate([before, x, after], axis=dim)
    return x


def taper_line(length):
    index = jnp.arange(length + 2 * M, dtype=jnp.int32).astype(jnp.float32)
    rising = (index + 0.5) / (2.0 * M)
    falling = (length + 2 * M - index - 0.5) / (2.0 * M)
    return jnp.minimum(jnp.minimum(rising, falling), 1.0)


def phase_angles(freq, pixels, modulus):
    cells = jnp.mod(freq, modulus)[None, :] * jnp.mod(pixels, modulus)[:, None] % modulus
    return cells.astype(jnp.float32) * (2.0 * math.pi / modulus)


def block_weights(values, label_names, g_tab, scale):
    first = label_names[0] * NT + label_names[2]
    second = label_names[1] * NT + label_names[2]
    g1r = g_tab[0][first]
    g1i = g_tab[1][first]
    g2r = g_tab[0][second]
    g2i = g_tab[1][second]
    real_gain = g1r * g2r + g1i * g2i
    imag_gain = g1i * g2r - g1r * g2i
    wreal = scale * (values[0] * real_gain - values[1] * imag_gain)
    wimag = scale * (values[0] * imag_gain + values[1] * real_gain)
    return (wreal, wimag)


def fold_columns(field):
    edges = jnp.concatenate([field[:, :M], field[:, -M:]], 1)
    extended = extended_2(edges, (("fcol", 1),), M)
    inner = field[:, M:-M]
    return jnp.concatenate(
        [inner[:, :M] + extended[:, :M], inner[:, M:-M], inner[:, -M:] + extended[:, -M:]], 1
    )


def fold_rows(field):
    edges = jnp.concatenate([field[:M], field[-M:]], 0)
    extended = extended_2(edges, (("frow", 0),), M)
    inner = field[M:-M]
    return jnp.concatenate([inner[:M] + extended[:M], inner[M:-M], inner[-M:] + extended[-M:]], 0)


def shards(
    vis,
    station_pairs,
    visibility_time_slot,
    station_u_cells,
    station_v_cells,
    facet_station_gains,
    holder_device_order,
):
    count_rows = lax.axis_size("frow")
    count_cols = lax.axis_size("fcol")
    n_rows = R * count_rows
    n_cols = C * count_cols
    frow_at = lax.axis_index("frow")
    fcol_at = lax.axis_index("fcol")
    g_tab = facet_station_gains[0, 0]
    label_names = jnp.concatenate([station_pairs, visibility_time_slot[None, :]], 0)
    block_size = vis.shape[1]
    scale = 0.5 / math.sqrt(NBLK * block_size)
    rows = frow_at * R - M + jnp.arange(R + 2 * M, dtype=jnp.int32)
    cols = fcol_at * C - M + jnp.arange(C + 2 * M, dtype=jnp.int32)
    stacked = jnp.concatenate([vis, label_names.astype(jnp.float32)], 0)
    copies = jnp.broadcast_to(stacked[None], (count_rows * count_cols,) + stacked.shape)
    everyone = lax.all_to_all(copies, ("frow", "fcol"), 0, 0)
    gathered = [
        lax.dynamic_index_in_dim(everyone, holder_device_order[step], 0, keepdims=False)
        for step in range(NBLK)
    ]
    total = jnp.zeros((R + 2 * M, C + 2 * M), jnp.float32)
    for step in range(NBLK):
        values = gathered[step][:2]
        tag_names = gathered[step][2:].astype(jnp.int32)
        wreal, wimag = block_weights(values, tag_names, g_tab, scale)
        frequency_u = station_u_cells[tag_names[0]] - station_u_cells[tag_names[1]]
        frequency_v = station_v_cells[tag_names[0]] - station_v_cells[tag_names[1]]
        theta = phase_angles(frequency_u, rows, n_rows)
        phi = phase_angles(frequency_v, cols, n_cols).T
        row_table = jnp.concatenate([jnp.cos(theta), jnp.sin(theta)], 1).astype(jnp.bfloat16)
        top = wreal[:, None] * jnp.cos(phi) - wimag[:, None] * jnp.sin(phi)
        bottom = -(wimag[:, None] * jnp.cos(phi) + wreal[:, None] * jnp.sin(phi))
        col_table = jnp.concatenate([top, bottom], 0).astype(jnp.bfloat16)
        total = total + jnp.dot(row_table, col_table, preferred_element_type=jnp.float32)
    tapered = total * taper_line(R)[:, None] * taper_line(C)[None, :]
    image = fold_rows(fold_columns(tapered))
    return image


def solution(mesh):
    return jax.shard_map(
        shards,
        mesh=mesh,
        in_specs=(
            P(None, ("frow", "fcol")),
            P(None, ("frow", "fcol")),
            P(("frow", "fcol")),
            P(),
            P(),
            P("frow", "fcol", None, None),
            P(),
        ),
        out_specs=P("frow", "fcol"),
        check_vma=False,
    )
```

```python
import functools
import math

import jax
import jax.numpy as jnp
from jax import lax
from jax.experimental import pallas as pl
from jax.experimental.pallas import tpu as pltpu
from jax.sharding import PartitionSpec as P

R = 1024
C = 512
M = 64
NT = 16
NBLK = 4
LANES = 128
SUB = 8
OWN = 0
LEFT, RIGHT, UP, DOWN, UL, UR, DL, DR = range(1, 9)
F32 = jnp.float32
BF16 = jnp.bfloat16


def wrap(m, modulus):
    if modulus & (modulus - 1) == 0:
        return m & (modulus - 1)
    return jnp.remainder(m, modulus)


def turn(m, modulus):
    m = wrap(m, modulus)
    quarter = modulus // 4
    q = (m + modulus // 8) // quarter if quarter & (quarter - 1) else (
        (m + modulus // 8) >> (quarter.bit_length() - 1))
    x = (m - q * quarter).astype(F32) * (2.0 * math.pi / modulus)
    x2 = x * x
    s = x + x * x2 * (-1 / 6 + x2 * (1 / 120 + x2 * (-1 / 5040 + x2 * (1 / 362880))))
    c = 1.0 + x2 * (-0.5 + x2 * (1 / 24 + x2 * (-1 / 720 + x2 * (1 / 40320))))
    odd = (q & 1) == 1
    cos = jnp.where(odd, s, c)
    sin = jnp.where(odd, c, s)
    cos = jnp.where(((q + 1) & 2) != 0, -cos, cos)
    sin = jnp.where((q & 2) != 0, -sin, sin)
    return cos, sin


def times(a, b):
    return a[0] * b[0] - a[1] * b[1], a[0] * b[1] + a[1] * b[0]


def pack_kernel(g_ref, vis_ref, pair_ref, slot_ref, out_ref):
    depth = g_ref.shape[0]
    tail = jnp.concatenate(
        [vis_ref[...], pair_ref[...].astype(F32), slot_ref[...].astype(F32)], 0)
    for copy in range(out_ref.shape[0]):
        out_ref[copy, :depth, :] = g_ref[...]
        out_ref[copy, depth:depth + tail.shape[0], :] = tail


def image_kernel(n_frow, n_fcol, order_ref, mid_ref, left_ref, right_ref, block_ref,
                 u_ref, v_ref, out_ref,
                 s_ref, w_ref, uv_ref, dr_ref, ac_ref, as_ref, tc_ref, ts_ref,
                 uc_ref, us_ref, cc_ref, cs_ref, m1_ref, m2_ref, g1_ref, g2_ref):
    frow_at = lax.axis_index("frow")
    fcol_at = lax.axis_index("fcol")
    half_r, half_c = R // 2, C // 2
    mod_r, mod_c = 2 * R * n_frow, 2 * C * n_fcol
    k_tiles = s_ref.shape[1]
    per_block = k_tiles // NBLK
    shape = (SUB, LANES)

    for b in range(NBLK):
        owner = order_ref[b]
        for q in range(5):
            s_ref[q, b * per_block:(b + 1) * per_block, :] = block_ref[
                owner % n_fcol, owner // n_fcol, q * per_block:(q + 1) * per_block, :]
    a1 = s_ref[2].astype(jnp.int32)
    a2 = s_ref[3].astype(jnp.int32)
    slot = s_ref[4].astype(jnp.int32)

    def pick(row, lane):
        return jnp.take_along_axis(
            jnp.broadcast_to(row, shape), lane, axis=1, mode="promise_in_bounds")

    def cells(table):
        got = [jnp.zeros(shape, jnp.int32)] * 2
        for h in range(table.shape[0]):
            row = table[h:h + 1, :]
            got = [jnp.where((a >> 7) == h, pick(row, a & 127), g)
                   for a, g in zip((a1, a2), got)]
        return got[0] - got[1]

    u = cells(u_ref)
    v = cells(v_ref)
    uv_ref[0] = u
    uv_ref[1] = v

    i1 = a1 * NT + slot
    i2 = a2 * NT + slot
    h1, l1, h2, l2 = i1 >> 7, i1 & 127, i2 >> 7, i2 & 127
    above = jnp.maximum(frow_at - 1, 0)
    below = jnp.minimum(frow_at + 1, n_frow - 1)
    places = [None] * 9
    for row, names in ((frow_at, (LEFT, OWN, RIGHT)), (above, (UL, UP, UR)), (below, (DL, DOWN, DR))):
        for ref, name in zip((left_ref, mid_ref, right_ref), names):
            places[name] = (ref, row)
    steps = 512 * NT // LANES

    def gather(h, acc):
        m1, m2 = h1 == h, h2 == h
        new = []
        for f in range(9):
            ref, row = places[f]
            for comp in range(2):
                line = ref[row, pl.ds(2 * h + comp, 1), :]
                at = 4 * f + 2 * comp
                new.append(jnp.where(m1, pick(line, l1), acc[at]))
                new.append(jnp.where(m2, pick(line, l2), acc[at + 1]))
        return tuple(new)

    acc = lax.fori_loop(0, steps, gather, tuple([jnp.zeros(shape, F32)] * 36), unroll=2)

    centre = times(turn(u * (frow_at * (2 * R) + (R - 1)), mod_r),
                   turn(v * (fcol_at * (2 * C) + (C - 1)), mod_c))
    scale = 0.5 / math.sqrt(NBLK * per_block * LANES)
    value = times((s_ref[0] * scale, s_ref[1] * scale), centre)
    has_up = (frow_at > 0).astype(F32)
    has_down = (frow_at < n_frow - 1).astype(F32)
    for f in range(9):
        g1r, g2r, g1i, g2i = acc[4 * f:4 * f + 4]
        w = times(value, (g1r * g2r + g1i * g2i, g1i * g2r - g1r * g2i))
        keep = {UP: has_up, UL: has_up, UR: has_up,
                DOWN: has_down, DL: has_down, DR: has_down}.get(f)
        for comp in range(2):
            w_ref[2 * f + comp] = w[comp] if keep is None else w[comp] * keep

    iota = lax.broadcasted_iota(jnp.int32, shape, 0)

    def tapers(group, half):
        index = (iota + SUB * group).astype(F32)
        return ((half + M - 0.5 - index) * (1.0 / (2 * M)),
                (index - (half - M - 0.5)) * (1.0 / (2 * M)))

    zero = jnp.zeros((M, LANES), BF16)

    def tables(s, carry):
        lane = pl.ds(pl.multiple_of(s * LANES, LANES), LANES)

        def weight(f):
            return tuple(jnp.broadcast_to(w_ref[2 * f + comp, pl.ds(s, 1), :], shape)
                         for comp in range(2))

        def phases(which, modulus, half):
            freq = jnp.broadcast_to(uv_ref[which, pl.ds(s, 1), :], shape)
            fine = turn(freq * (2 * iota + 1), modulus)
            middle = turn(freq * (16 * iota), modulus)
            coarse = turn(freq * (128 * iota), modulus)
            for a in range(half // 64):
                top = tuple(jnp.broadcast_to(x[a:a + 1], shape) for x in coarse)
                both = times(middle, top)
                for comp in range(2):
                    dr_ref[which, comp, 8 * a:8 * a + 8, :] = both[comp]
            for g in range(half // SUB):
                step = tuple(jnp.broadcast_to(dr_ref[which, comp, g:g + 1, :], shape)
                             for comp in range(2))
                yield times(fine, step)

        pairs = {}

        def put(ref, first, group, x):
            key = (id(ref), first)
            if group % 2 == 0:
                pairs[key] = x
            else:
                start = first + SUB * (group - 1)
                ref[start:start + 16, lane] = jnp.concatenate([pairs.pop(key), x], 0).astype(BF16)

        edge = (half_r - M) // SUB
        rows_w = [weight(f) for f in (UP, DOWN, UL, UR, DL, DR)]
        signs = (-1, 1, -1, -1, 1, 1)
        for g, (cos, sin) in enumerate(phases(0, mod_r, half_r)):
            if g < edge:
                put(ac_ref, 0, g, cos)
                put(as_ref, 0, g, sin)
            else:
                mine, other = tapers(g, half_r)
                put(ac_ref, 0, g, cos * mine)
                put(as_ref, 0, g, sin * mine)
                cos, sin = cos * other, sin * other
                for n, ((wr, wi), sd) in enumerate(zip(rows_w, signs)):
                    put(uc_ref, n * M, g - edge, wr * cos - (sd * wi) * sin)
                    put(us_ref, n * M, g - edge, -(sd * wr) * sin - wi * cos)
        edge = (half_c - M) // SUB
        (wr, wi), (lr, li), (rr, ri) = weight(OWN), weight(LEFT), weight(RIGHT)
        for g, (cos, sin) in enumerate(phases(1, mod_c, half_c)):
            put(cc_ref, 0, g, cos)
            put(cs_ref, 0, g, sin)
            if g < edge:
                own = (cos, sin)
            else:
                mine, other = tapers(g, half_c)
                own = (cos * mine, sin * mine)
                cos, sin = cos * other, sin * other
                at = 2 * half_c + M
                put(tc_ref, at, g - edge, lr * cos + li * sin)
                put(ts_ref, at, g - edge, lr * sin - li * cos)
                put(tc_ref, at + 2 * M, g - edge, rr * cos - ri * sin)
                put(ts_ref, at + 2 * M, g - edge, -(rr * sin + ri * cos))
            put(tc_ref, 0, g, wr * own[0])
            put(tc_ref, half_c, g, -wi * own[1])
            put(ts_ref, 0, g, -wi * own[0])
            put(ts_ref, half_c, g, -wr * own[1])
        for ref in (tc_ref, ts_ref):
            ref[2 * half_c:2 * half_c + M, lane] = zero
            ref[2 * half_c + 2 * M:2 * half_c + 3 * M, lane] = zero
        return carry

    lax.fori_loop(0, k_tiles, tables, 0)

    def dot(a, b):
        return lax.dot_general(a[...], b[...], (((1,), (1,)), ((), ())), preferred_element_type=F32)

    m1_ref[...] = dot(ac_ref, tc_ref)
    m2_ref[...] = dot(as_ref, ts_ref)
    g1_ref[...] = dot(uc_ref, cc_ref)
    g2_ref[...] = dot(us_ref, cs_ref)

    lane_at = lax.broadcasted_iota(jnp.int32, shape, 1)
    back_lane = (LANES - 1) - lane_at
    back_row = (SUB - 1) - iota
    n_lane = half_c // LANES
    edge_c = half_c - M
    edge_r = half_r - M
    col_own, col_other = [], []
    for t in range(n_lane):
        index = (lane_at + t * LANES).astype(F32)
        col_own.append(jnp.minimum((half_c + M - 0.5 - index) * (1.0 / (2 * M)), 1.0))
        col_other.append(jnp.maximum((index - (half_c - M - 0.5)) * (1.0 / (2 * M)), 0.0))

    def flip(x, index, axis):
        return jnp.take_along_axis(x, index, axis=axis, mode="promise_in_bounds")

    def finish(g, edged):
        rows = pl.ds(pl.multiple_of(g * SUB, SUB), SUB)
        for t in range(n_lane):
            def part(ref, which):
                return ref[rows, which * half_c + t * LANES:which * half_c + (t + 1) * LANES]
            p, s_, r, q = part(m1_ref, 0), part(m1_ref, 1), part(m2_ref, 0), part(m2_ref, 1)
            even, odd = p + q, p - q
            plus, minus = r + s_, r - s_
            quad = {(1, 1): even + plus, (-1, -1): even - plus,
                    (1, -1): odd + minus, (-1, 1): odd - minus}
            if (t + 1) * LANES > edge_c:
                base = 2 * half_c
                off = t * LANES - (half_c - LANES)
                for se, start in ((-1, base), (1, base + LANES)):
                    lc = m1_ref[rows, start + off:start + off + LANES]
                    ls = m2_ref[rows, start + off:start + off + LANES]
                    quad[1, se] += lc + ls
                    quad[-1, se] += lc - ls
            if edged:
                def edge(n):
                    at = pl.ds(pl.multiple_of(n * M + g * SUB - edge_r, SUB), SUB)
                    x = g1_ref[at, t * LANES:(t + 1) * LANES]
                    y = g2_ref[at, t * LANES:(t + 1) * LANES]
                    return {1: x + y, -1: x - y}
                for n, sd in ((0, -1), (1, 1)):
                    e = edge(n)
                    for se in (-1, 1):
                        quad[sd, se] += e[se] * col_own[t]
                if (t + 1) * LANES > edge_c:
                    for n, (sd, se) in ((2, (-1, -1)), (3, (-1, 1)), (4, (1, -1)), (5, (1, 1))):
                        quad[sd, se] += edge(n)[se] * col_other[t]
            for (sd, se), x in quad.items():
                if sd < 0:
                    x = flip(x, back_row, 0)
                    at = pl.ds(pl.multiple_of(half_r - SUB - g * SUB, SUB), SUB)
                else:
                    at = pl.ds(pl.multiple_of(half_r + g * SUB, SUB), SUB)
                if se < 0:
                    x = flip(x, back_lane, 1)
                    start = half_c - (t + 1) * LANES
                else:
                    start = half_c + t * LANES
                out_ref[at, start:start + LANES] = x

    def inner(g, carry):
        finish(g, False)
        return carry

    def outer(g, carry):
        finish(g, True)
        return carry

    lax.fori_loop(0, edge_r // SUB, inner, 0, unroll=2)
    lax.fori_loop(edge_r // SUB, half_r // SUB, outer, 0)


def shards(vis, station_pairs, visibility_time_slot, station_u_cells, station_v_cells,
           facet_station_gains, holder_device_order):
    n_frow = lax.axis_size("frow")
    n_fcol = lax.axis_size("fcol")
    block = vis.shape[1]
    per_block = block // LANES
    k_tiles = NBLK * per_block
    k = k_tiles * LANES

    def lines(x):
        return x.reshape(-1, LANES)

    gains = facet_station_gains[0, 0]
    depth = gains.size // LANES
    g_lines = gains.reshape(2, -1, LANES).transpose(1, 0, 2).reshape(depth, LANES)
    tail = 16 * -(-5 * per_block // 16)
    packed = pl.pallas_call(
        pack_kernel,
        out_shape=jax.ShapeDtypeStruct((n_frow, depth + tail, LANES), F32),
        name="pack",
    )(g_lines, lines(vis), lines(station_pairs), lines(visibility_time_slot))
    mine = lax.all_to_all(packed, "frow", 0, 0)
    blocks = jnp.broadcast_to(mine[None, :, depth:], (n_fcol, n_frow, tail, LANES))
    blocks = lax.all_to_all(blocks, "fcol", 0, 0)
    up = [(i, i + 1) for i in range(n_fcol - 1)]
    left = lax.ppermute(mine, "fcol", up)
    right = lax.ppermute(mine, "fcol", [(j, i) for i, j in up])
    vmem = pl.BlockSpec(memory_space=pltpu.VMEM)
    half_r, half_c = R // 2, C // 2
    wide = 2 * half_c + 4 * M
    return pl.pallas_call(
        functools.partial(image_kernel, n_frow, n_fcol),
        out_shape=jax.ShapeDtypeStruct((R, C), F32),
        in_specs=[pl.BlockSpec(memory_space=pltpu.SMEM)] + [vmem] * 6,
        out_specs=vmem,
        scratch_shapes=[
            pltpu.VMEM((5, k_tiles, LANES), F32),
            pltpu.VMEM((18, k_tiles, LANES), F32),
            pltpu.VMEM((2, k_tiles, LANES), jnp.int32),
            pltpu.VMEM((2, 2, half_r // SUB, LANES), F32),
            pltpu.VMEM((half_r, k), BF16),
            pltpu.VMEM((half_r, k), BF16),
            pltpu.VMEM((wide, k), BF16),
            pltpu.VMEM((wide, k), BF16),
            pltpu.VMEM((6 * M, k), BF16),
            pltpu.VMEM((6 * M, k), BF16),
            pltpu.VMEM((half_c, k), BF16),
            pltpu.VMEM((half_c, k), BF16),
            pltpu.VMEM((half_r, wide), F32),
            pltpu.VMEM((half_r, wide), F32),
            pltpu.VMEM((6 * M, half_c), F32),
            pltpu.VMEM((6 * M, half_c), F32),
        ],
        compiler_params=pltpu.CompilerParams(vmem_limit_bytes=40 * 1024 * 1024),
        name="image",
    )(holder_device_order, mine, left, right, blocks,
      lines(station_u_cells), lines(station_v_cells))


def solution(mesh):
    return jax.shard_map(
        shards,
        mesh=mesh,
        in_specs=(
            P(None, ("frow", "fcol")),
            P(None, ("frow", "fcol")),
            P(("frow", "fcol")),
            P(),
            P(),
            P("frow", "fcol", None, None),
            P(),
        ),
        out_specs=P("frow", "fcol"),
        check_vma=False,
    )
```

```python
import functools
import math

import jax
import jax.numpy as jnp
from jax import lax
from jax.experimental import pallas as pl
from jax.experimental.pallas import tpu as pltpu
from jax.sharding import PartitionSpec as P

R = 1024
C = 512
M = 64
NT = 16
NBLK = 4
LANES = 128
SUB = 8
OWN, LEFT, RIGHT, UP, DOWN, UL, UR, DL, DR = range(9)
F32 = jnp.float32
BF16 = jnp.bfloat16


def wrap(m, modulus):
    if modulus & (modulus - 1) == 0:
        return m & (modulus - 1)
    return jnp.remainder(m, modulus)


def turn(m, modulus):
    m = wrap(m, modulus)
    quarter = modulus // 4
    q = (m + modulus // 8) // quarter if quarter & (quarter - 1) else (
        (m + modulus // 8) >> (quarter.bit_length() - 1))
    x = (m - q * quarter).astype(F32) * (2.0 * math.pi / modulus)
    x2 = x * x
    s = x + x * x2 * (-1 / 6 + x2 * (1 / 120 + x2 * (-1 / 5040 + x2 * (1 / 362880))))
    c = 1.0 + x2 * (-0.5 + x2 * (1 / 24 + x2 * (-1 / 720 + x2 * (1 / 40320))))
    odd = (q & 1) == 1
    cos = jnp.where(odd, s, c)
    sin = jnp.where(odd, c, s)
    cos = jnp.where(((q + 1) & 2) != 0, -cos, cos)
    sin = jnp.where((q & 2) != 0, -sin, sin)
    return cos, sin


def times(a, b):
    return a[0] * b[0] - a[1] * b[1], a[0] * b[1] + a[1] * b[0]


def pack_kernel(vis_ref, pair_ref, slot_ref, out_ref):
    block = vis_ref.shape[1]
    lines = [vis_ref[0:1, :], vis_ref[1:2, :], pair_ref[0:1, :].astype(F32),
             pair_ref[1:2, :].astype(F32), slot_ref[...].astype(F32)]
    for copy in range(out_ref.shape[0]):
        for q, line in enumerate(lines):
            out_ref[copy, :, q * block:(q + 1) * block] = line


def pick(row, lane):
    return jnp.take_along_axis(
        jnp.broadcast_to(row, lane.shape), lane, axis=1, mode="promise_in_bounds")


def taper_rows(group, half):
    index = (lax.broadcasted_iota(jnp.int32, (SUB, LANES), 0) + SUB * group).astype(F32)
    return ((half + M - 0.5 - index) * (1.0 / (2 * M)),
            (index - (half - M - 0.5)) * (1.0 / (2 * M)))


def table_kernel(n_frow, n_fcol, order_ref, block_ref, u_ref, v_ref,
                 s_ref, ac_ref, as_ref, ec_ref, es_ref, fc_ref, fs_ref, cc_ref, cs_ref,
                 q_ref, uv_ref, dr_ref):
    frow_at = lax.axis_index("frow")
    fcol_at = lax.axis_index("fcol")
    half_r, half_c = R // 2, C // 2
    mod_r, mod_c = 2 * R * n_frow, 2 * C * n_fcol
    k_tiles = s_ref.shape[1]
    per_block = k_tiles // NBLK
    block = per_block * LANES
    shape = (SUB, LANES)

    for b in range(NBLK):
        owner = order_ref[b]
        for q in range(5):
            for j in range(per_block):
                q_ref[q, b * per_block + j:b * per_block + j + 1, :] = block_ref[
                    owner, :, q * block + j * LANES:q * block + (j + 1) * LANES]
    a1 = q_ref[2].astype(jnp.int32)
    a2 = q_ref[3].astype(jnp.int32)
    slot = q_ref[4].astype(jnp.int32)

    def cells(table):
        got = [jnp.zeros(shape, jnp.int32)] * 2
        for h in range(table.shape[0]):
            row = table[h:h + 1, :]
            got = [jnp.where((a >> 7) == h, pick(row, a & 127), g)
                   for a, g in zip((a1, a2), got)]
        return got[0] - got[1]

    u = cells(u_ref)
    v = cells(v_ref)
    uv_ref[0] = u
    uv_ref[1] = v
    centre = times(turn(u * (frow_at * (2 * R) + (R - 1)), mod_r),
                   turn(v * (fcol_at * (2 * C) + (C - 1)), mod_c))
    scale = 0.5 / math.sqrt(NBLK * per_block * LANES)
    value = times((q_ref[0] * scale, q_ref[1] * scale), centre)
    s_ref[0] = value[0]
    s_ref[1] = value[1]
    s_ref[2] = (a1 * NT + slot).astype(F32)
    s_ref[3] = (a2 * NT + slot).astype(F32)

    iota = lax.broadcasted_iota(jnp.int32, shape, 0)

    def tables(s, carry):
        lane = pl.ds(pl.multiple_of(s * LANES, LANES), LANES)

        def phases(which, modulus, half):
            freq = jnp.broadcast_to(uv_ref[which, pl.ds(s, 1), :], shape)
            fine = turn(freq * (2 * iota + 1), modulus)
            middle = turn(freq * (16 * iota), modulus)
            coarse = turn(freq * (128 * iota), modulus)
            for a in range(half // 64):
                top = tuple(jnp.broadcast_to(x[a:a + 1], shape) for x in coarse)
                both = times(middle, top)
                for comp in range(2):
                    dr_ref[which, comp, 8 * a:8 * a + 8, :] = both[comp]
            for g in range(half // SUB):
                step = tuple(jnp.broadcast_to(dr_ref[which, comp, g:g + 1, :], shape)
                             for comp in range(2))
                yield times(fine, step)

        pairs = {}

        def put(ref, first, group, x):
            key = (id(ref), first)
            if group % 2 == 0:
                pairs[key] = x
            else:
                start = first + SUB * (group - 1)
                ref[start:start + 16, lane] = jnp.concatenate([pairs.pop(key), x], 0).astype(BF16)

        edge = (half_r - M) // SUB
        for g, (cos, sin) in enumerate(phases(0, mod_r, half_r)):
            if g >= edge:
                mine, other = taper_rows(g, half_r)
                at = slice((g - edge) * SUB, (g - edge + 1) * SUB)
                ec_ref[at, lane] = cos * other
                es_ref[at, lane] = sin * other
                cos, sin = cos * mine, sin * mine
            put(ac_ref, 0, g, cos)
            put(as_ref, 0, g, sin)
        for g, (cos, sin) in enumerate(phases(1, mod_c, half_c)):
            put(cc_ref, 0, g, cos)
            put(cs_ref, 0, g, sin)
            at = slice(g * SUB, (g + 1) * SUB)
            fc_ref[at, lane] = cos
            fs_ref[at, lane] = sin
        return carry

    lax.fori_loop(0, k_tiles, tables, 0)


def weight_kernel(s_ref, mid_ref, a_ref, b_ref, w_ref):
    r_odd = lax.rem(lax.axis_index("frow"), 2) == 1
    c_odd = lax.rem(lax.axis_index("fcol"), 2) == 1
    above = jnp.where(r_odd, 1, 2)
    below = jnp.where(r_odd, 2, 1)
    shape = (SUB, LANES)
    i1 = s_ref[2].astype(jnp.int32)
    i2 = s_ref[3].astype(jnp.int32)
    h1, l1, h2, l2 = i1 >> 7, i1 & 127, i2 >> 7, i2 & 127
    places = [(ref, row) for ref in (mid_ref, a_ref, b_ref) for row in (0, above, below)]

    def gather(h, acc):
        m1, m2 = h1 == h, h2 == h
        new = []
        for f, (ref, row) in enumerate(places):
            for comp in range(2):
                line = ref[row, pl.ds(2 * h + comp, 1), :]
                at = 4 * f + 2 * comp
                new.append(jnp.where(m1, pick(line, l1), acc[at]))
                new.append(jnp.where(m2, pick(line, l2), acc[at + 1]))
        return tuple(new)

    acc = lax.fori_loop(0, mid_ref.shape[1] // 2, gather,
                        tuple([jnp.zeros(shape, F32)] * 36), unroll=2)
    value = (s_ref[0], s_ref[1])
    w = []
    for f in range(9):
        g1r, g2r, g1i, g2i = acc[4 * f:4 * f + 4]
        w.append(times(value, (g1r * g2r + g1i * g2i, g1i * g2r - g1r * g2i)))
    for names, at in (((OWN, LEFT, RIGHT), 0), ((UP, UL, UR), 1), ((DOWN, DL, DR), 2)):
        for comp in range(2):
            x, y = w[3 + at][comp], w[6 + at][comp]
            w_ref[2 * names[0] + comp] = w[at][comp]
            w_ref[2 * names[1] + comp] = jnp.where(c_odd, x, y)
            w_ref[2 * names[2] + comp] = jnp.where(c_odd, y, x)


def image_kernel(w_ref, ac_ref, as_ref, ec_ref, es_ref, fc_ref, fs_ref, cc_ref, cs_ref, out_ref,
                 tc_ref, ts_ref, uc_ref, us_ref, m1_ref, m2_ref, g1_ref, g2_ref):
    half_r, half_c = R // 2, C // 2
    k_tiles = w_ref.shape[1]
    shape = (SUB, LANES)
    iota = lax.broadcasted_iota(jnp.int32, shape, 0)
    zero = jnp.zeros((M, LANES), BF16)

    def tables(s, carry):
        lane = pl.ds(pl.multiple_of(s * LANES, LANES), LANES)

        def weight(f):
            return tuple(jnp.broadcast_to(w_ref[2 * f + comp, pl.ds(s, 1), :], shape)
                         for comp in range(2))

        pairs = {}

        def put(ref, first, group, x):
            key = (id(ref), first)
            if group % 2 == 0:
                pairs[key] = x
            else:
                start = first + SUB * (group - 1)
                ref[start:start + 16, lane] = jnp.concatenate([pairs.pop(key), x], 0).astype(BF16)

        rows_w = [weight(f) for f in (UP, DOWN, UL, UR, DL, DR)]
        signs = (-1, 1, -1, -1, 1, 1)
        for g in range(M // SUB):
            at = slice(g * SUB, (g + 1) * SUB)
            cos, sin = ec_ref[at, lane], es_ref[at, lane]
            for n, ((wr, wi), sd) in enumerate(zip(rows_w, signs)):
                put(uc_ref, n * M, g, wr * cos - (sd * wi) * sin)
                put(us_ref, n * M, g, -(sd * wr) * sin - wi * cos)
        edge = (half_c - M) // SUB
        (wr, wi), (lr, li), (rr, ri) = weight(OWN), weight(LEFT), weight(RIGHT)
        for g in range(half_c // SUB):
            at = slice(g * SUB, (g + 1) * SUB)
            cos, sin = fc_ref[at, lane], fs_ref[at, lane]
            own = (cos, sin)
            if g >= edge:
                mine, other = taper_rows(g, half_c)
                own = (cos * mine, sin * mine)
                cos, sin = cos * other, sin * other
                base = 2 * half_c + M
                put(tc_ref, base, g - edge, lr * cos + li * sin)
                put(ts_ref, base, g - edge, lr * sin - li * cos)
                put(tc_ref, base + 2 * M, g - edge, rr * cos - ri * sin)
                put(ts_ref, base + 2 * M, g - edge, -(rr * sin + ri * cos))
            put(tc_ref, 0, g, wr * own[0])
            put(tc_ref, half_c, g, -wi * own[1])
            put(ts_ref, 0, g, -wi * own[0])
            put(ts_ref, half_c, g, -wr * own[1])
        for ref in (tc_ref, ts_ref):
            ref[2 * half_c:2 * half_c + M, lane] = zero
            ref[2 * half_c + 2 * M:2 * half_c + 3 * M, lane] = zero
        return carry

    lax.fori_loop(0, k_tiles, tables, 0)

    def dot(a, b):
        return lax.dot_general(a[...], b[...], (((1,), (1,)), ((), ())), preferred_element_type=F32)

    m1_ref[...] = dot(ac_ref, tc_ref)
    m2_ref[...] = dot(as_ref, ts_ref)
    g1_ref[...] = dot(uc_ref, cc_ref)
    g2_ref[...] = dot(us_ref, cs_ref)

    lane_at = lax.broadcasted_iota(jnp.int32, shape, 1)
    back_lane = (LANES - 1) - lane_at
    back_row = (SUB - 1) - iota
    n_lane = half_c // LANES
    edge_c = half_c - M
    edge_r = half_r - M
    col_own, col_other = [], []
    for t in range(n_lane):
        index = (lane_at + t * LANES).astype(F32)
        col_own.append(jnp.minimum((half_c + M - 0.5 - index) * (1.0 / (2 * M)), 1.0))
        col_other.append(jnp.maximum((index - (half_c - M - 0.5)) * (1.0 / (2 * M)), 0.0))

    def flip(x, index, axis):
        return jnp.take_along_axis(x, index, axis=axis, mode="promise_in_bounds")

    def finish(g, edged):
        rows = pl.ds(pl.multiple_of(g * SUB, SUB), SUB)
        for t in range(n_lane):
            def part(ref, which):
                return ref[rows, which * half_c + t * LANES:which * half_c + (t + 1) * LANES]
            p, s_, r, q = part(m1_ref, 0), part(m1_ref, 1), part(m2_ref, 0), part(m2_ref, 1)
            even, odd = p + q, p - q
            plus, minus = r + s_, r - s_
            quad = {(1, 1): even + plus, (-1, -1): even - plus,
                    (1, -1): odd + minus, (-1, 1): odd - minus}
            if (t + 1) * LANES > edge_c:
                base = 2 * half_c
                off = t * LANES - (half_c - LANES)
                for se, start in ((-1, base), (1, base + LANES)):
                    lc = m1_ref[rows, start + off:start + off + LANES]
                    ls = m2_ref[rows, start + off:start + off + LANES]
                    quad[1, se] += lc + ls
                    quad[-1, se] += lc - ls
            if edged:
                def edge(n):
                    at = pl.ds(pl.multiple_of(n * M + g * SUB - edge_r, SUB), SUB)
                    x = g1_ref[at, t * LANES:(t + 1) * LANES]
                    y = g2_ref[at, t * LANES:(t + 1) * LANES]
                    return {1: x + y, -1: x - y}
                for n, sd in ((0, -1), (1, 1)):
                    e = edge(n)
                    for se in (-1, 1):
                        quad[sd, se] += e[se] * col_own[t]
                if (t + 1) * LANES > edge_c:
                    for n, (sd, se) in ((2, (-1, -1)), (3, (-1, 1)), (4, (1, -1)), (5, (1, 1))):
                        quad[sd, se] += edge(n)[se] * col_other[t]
            for (sd, se), x in quad.items():
                if sd < 0:
                    x = flip(x, back_row, 0)
                    at = pl.ds(pl.multiple_of(half_r - SUB - g * SUB, SUB), SUB)
                else:
                    at = pl.ds(pl.multiple_of(half_r + g * SUB, SUB), SUB)
                if se < 0:
                    x = flip(x, back_lane, 1)
                    start = half_c - (t + 1) * LANES
                else:
                    start = half_c + t * LANES
                out_ref[at, start:start + LANES] = x

    def inner(g, carry):
        finish(g, False)
        return carry

    def outer(g, carry):
        finish(g, True)
        return carry

    lax.fori_loop(0, edge_r // SUB, inner, 0, unroll=2)
    lax.fori_loop(edge_r // SUB, half_r // SUB, outer, 0)


def swaps(size):
    both = []
    for first in (0, 1):
        pairs = [(i, i + 1) for i in range(first, size - 1, 2)]
        both.append(pairs + [(j, i) for i, j in pairs])
    return both


def shards(vis, station_pairs, visibility_time_slot, station_u_cells, station_v_cells,
           facet_station_gains, holder_device_order):
    n_frow = lax.axis_size("frow")
    n_fcol = lax.axis_size("fcol")
    block = vis.shape[1]
    k_tiles = NBLK * block // LANES
    k = k_tiles * LANES
    half_r, half_c = R // 2, C // 2
    wide = 2 * half_c + 4 * M
    vmem = pl.BlockSpec(memory_space=pltpu.VMEM)
    smem = pl.BlockSpec(memory_space=pltpu.SMEM)

    def lines(x):
        return x.reshape(-1, LANES)

    def shaped(*dims, dtype=F32):
        return jax.ShapeDtypeStruct(dims, dtype)

    def params(mib):
        return pltpu.CompilerParams(vmem_limit_bytes=mib * 1024 * 1024)

    gains = facet_station_gains[0, 0]
    depth = gains.size // LANES
    own = gains.reshape(2, -1, LANES).transpose(1, 0, 2).reshape(depth, LANES)
    row_a, row_b = [lax.ppermute(own, "frow", pairs) for pairs in swaps(n_frow)]
    packed = pl.pallas_call(
        pack_kernel,
        out_shape=shaped(n_frow * n_fcol, 1, 5 * block),
        name="pack",
    )(vis, station_pairs, visibility_time_slot.reshape(1, block))
    blocks = lax.all_to_all(packed, ("frow", "fcol"), 0, 0)
    mid = jnp.stack([own, row_a, row_b])
    col_a, col_b = [lax.ppermute(mid, "fcol", pairs) for pairs in swaps(n_fcol)]
    s, *tables = pl.pallas_call(
        functools.partial(table_kernel, n_frow, n_fcol),
        out_shape=[
            shaped(4, k_tiles, LANES),
            shaped(half_r, k, dtype=BF16), shaped(half_r, k, dtype=BF16),
            shaped(M, k), shaped(M, k),
            shaped(half_c, k), shaped(half_c, k),
            shaped(half_c, k, dtype=BF16), shaped(half_c, k, dtype=BF16),
        ],
        in_specs=[smem] + [vmem] * 3,
        out_specs=[vmem] * 9,
        scratch_shapes=[
            pltpu.VMEM((5, k_tiles, LANES), F32),
            pltpu.VMEM((2, k_tiles, LANES), jnp.int32),
            pltpu.VMEM((2, 2, half_r // SUB, LANES), F32),
        ],
        compiler_params=params(24),
        name="tables",
    )(holder_device_order, blocks, lines(station_u_cells), lines(station_v_cells))
    weights = pl.pallas_call(
        weight_kernel,
        out_shape=shaped(18, k_tiles, LANES),
        in_specs=[vmem] * 4,
        out_specs=vmem,
        compiler_params=params(8),
        name="weights",
    )(s, mid, col_a, col_b)
    return pl.pallas_call(
        image_kernel,
        out_shape=shaped(R, C),
        in_specs=[vmem] * 9,
        out_specs=vmem,
        scratch_shapes=[
            pltpu.VMEM((wide, k), BF16),
            pltpu.VMEM((wide, k), BF16),
            pltpu.VMEM((6 * M, k), BF16),
            pltpu.VMEM((6 * M, k), BF16),
            pltpu.VMEM((half_r, wide), F32),
            pltpu.VMEM((half_r, wide), F32),
            pltpu.VMEM((6 * M, half_c), F32),
            pltpu.VMEM((6 * M, half_c), F32),
        ],
        compiler_params=params(32),
        name="image",
    )(weights, *tables)


def solution(mesh):
    return jax.shard_map(
        shards,
        mesh=mesh,
        in_specs=(
            P(None, ("frow", "fcol")),
            P(None, ("frow", "fcol")),
            P(("frow", "fcol")),
            P(),
            P(),
            P("frow", "fcol", None, None),
            P(),
        ),
        out_specs=P("frow", "fcol"),
        check_vma=False,
    )
```

```python
import functools
import math

import jax
import jax.numpy as jnp
from jax import lax
from jax.experimental import pallas as pl
from jax.experimental.pallas import tpu as pltpu
from jax.sharding import PartitionSpec as P

R = 1024
C = 512
M = 64
NT = 16
NBLK = 4
LANES = 128
SUB = 8
OWN, LEFT, RIGHT, UP, DOWN, UL, UR, DL, DR = range(9)
F32 = jnp.float32
BF16 = jnp.bfloat16


def wrap(m, modulus):
    if modulus & (modulus - 1) == 0:
        return m & (modulus - 1)
    return jnp.remainder(m, modulus)


def turn(m, modulus):
    m = wrap(m, modulus)
    quarter = modulus // 4
    q = (m + modulus // 8) // quarter if quarter & (quarter - 1) else (
        (m + modulus // 8) >> (quarter.bit_length() - 1))
    x = (m - q * quarter).astype(F32) * (2.0 * math.pi / modulus)
    x2 = x * x
    s = x + x * x2 * (-1 / 6 + x2 * (1 / 120 + x2 * (-1 / 5040 + x2 * (1 / 362880))))
    c = 1.0 + x2 * (-0.5 + x2 * (1 / 24 + x2 * (-1 / 720 + x2 * (1 / 40320))))
    odd = (q & 1) == 1
    cos = jnp.where(odd, s, c)
    sin = jnp.where(odd, c, s)
    cos = jnp.where(((q + 1) & 2) != 0, -cos, cos)
    sin = jnp.where((q & 2) != 0, -sin, sin)
    return cos, sin


def times(a, b):
    return a[0] * b[0] - a[1] * b[1], a[0] * b[1] + a[1] * b[0]


def pack_kernel(order_ref, vis_ref, pair_ref, slot_ref, u_ref, v_ref,
                out_ref, u_out, v_out):
    flat = lax.axis_index("frow") * lax.axis_size("fcol") + lax.axis_index("fcol")
    per_block = out_ref.shape[1] // NBLK
    u_out[...] = u_ref[...]
    v_out[...] = v_ref[...]
    lines = [vis_ref[0:1, :], vis_ref[1:2, :], pair_ref[0:1, :].astype(F32),
             pair_ref[1:2, :].astype(F32), slot_ref[...].astype(F32)]
    for b in range(NBLK):
        mine = order_ref[b] == flat
        for q, line in enumerate(lines):
            held = jnp.where(mine, line, 0.0)
            for j in range(per_block):
                at = b * per_block + j
                out_ref[q, at:at + 1, :] = held[:, j * LANES:(j + 1) * LANES]


def pick(row, lane):
    return jnp.take_along_axis(
        jnp.broadcast_to(row, lane.shape), lane, axis=1, mode="promise_in_bounds")


def taper_rows(group, half):
    index = (lax.broadcasted_iota(jnp.int32, (SUB, LANES), 0) + SUB * group).astype(F32)
    return ((half + M - 0.5 - index) * (1.0 / (2 * M)),
            (index - (half - M - 0.5)) * (1.0 / (2 * M)))


def table_kernel(n_frow, n_fcol, q_ref, u_ref, v_ref,
                 s_ref, ac_ref, as_ref, ec_ref, es_ref, fc_ref, fs_ref, cc_ref, cs_ref,
                 uv_ref, dr_ref):
    frow_at = lax.axis_index("frow")
    fcol_at = lax.axis_index("fcol")
    half_r, half_c = R // 2, C // 2
    mod_r, mod_c = 2 * R * n_frow, 2 * C * n_fcol
    k_tiles = s_ref.shape[1]
    per_block = k_tiles // NBLK
    shape = (SUB, LANES)

    a1 = q_ref[2].astype(jnp.int32)
    a2 = q_ref[3].astype(jnp.int32)
    slot = q_ref[4].astype(jnp.int32)

    def cells(table):
        got = [jnp.zeros(shape, jnp.int32)] * 2
        for h in range(table.shape[0]):
            row = table[h:h + 1, :]
            got = [jnp.where((a >> 7) == h, pick(row, a & 127), g)
                   for a, g in zip((a1, a2), got)]
        return got[0] - got[1]

    u = cells(u_ref)
    v = cells(v_ref)
    uv_ref[0] = u
    uv_ref[1] = v
    centre = times(turn(u * (frow_at * (2 * R) + (R - 1)), mod_r),
                   turn(v * (fcol_at * (2 * C) + (C - 1)), mod_c))
    scale = 0.5 / math.sqrt(NBLK * per_block * LANES)
    value = times((q_ref[0] * scale, q_ref[1] * scale), centre)
    s_ref[0] = value[0]
    s_ref[1] = value[1]
    s_ref[2] = (a1 * NT + slot).astype(F32)
    s_ref[3] = (a2 * NT + slot).astype(F32)

    iota = lax.broadcasted_iota(jnp.int32, shape, 0)

    def tables(s, carry):
        lane = pl.ds(pl.multiple_of(s * LANES, LANES), LANES)

        def phases(which, modulus, half):
            freq = jnp.broadcast_to(uv_ref[which, pl.ds(s, 1), :], shape)
            fine = turn(freq * (2 * iota + 1), modulus)
            middle = turn(freq * (16 * iota), modulus)
            coarse = turn(freq * (128 * iota), modulus)
            for a in range(half // 64):
                top = tuple(jnp.broadcast_to(x[a:a + 1], shape) for x in coarse)
                both = times(middle, top)
                for comp in range(2):
                    dr_ref[which, comp, 8 * a:8 * a + 8, :] = both[comp]
            for g in range(half // SUB):
                step = tuple(jnp.broadcast_to(dr_ref[which, comp, g:g + 1, :], shape)
                             for comp in range(2))
                yield times(fine, step)

        pairs = {}

        def put(ref, first, group, x):
            key = (id(ref), first)
            if group % 2 == 0:
                pairs[key] = x
            else:
                start = first + SUB * (group - 1)
                ref[start:start + 16, lane] = jnp.concatenate([pairs.pop(key), x], 0).astype(BF16)

        edge = (half_r - M) // SUB
        for g, (cos, sin) in enumerate(phases(0, mod_r, half_r)):
            if g >= edge:
                mine, other = taper_rows(g, half_r)
                at = slice((g - edge) * SUB, (g - edge + 1) * SUB)
                ec_ref[at, lane] = cos * other
                es_ref[at, lane] = sin * other
                cos, sin = cos * mine, sin * mine
            put(ac_ref, 0, g, cos)
            put(as_ref, 0, g, sin)
        for g, (cos, sin) in enumerate(phases(1, mod_c, half_c)):
            put(cc_ref, 0, g, cos)
            put(cs_ref, 0, g, sin)
            at = slice(g * SUB, (g + 1) * SUB)
            fc_ref[at, lane] = cos
            fs_ref[at, lane] = sin
        return carry

    lax.fori_loop(0, k_tiles, tables, 0)


def weight_kernel(s_ref, mid_ref, a_ref, b_ref, w_ref):
    r_odd = lax.rem(lax.axis_index("frow"), 2) == 1
    c_odd = lax.rem(lax.axis_index("fcol"), 2) == 1
    above = jnp.where(r_odd, 1, 2)
    below = jnp.where(r_odd, 2, 1)
    shape = (SUB, LANES)
    i1 = s_ref[2].astype(jnp.int32)
    i2 = s_ref[3].astype(jnp.int32)
    h1, l1, h2, l2 = i1 >> 7, i1 & 127, i2 >> 7, i2 & 127
    places = [(ref, row) for ref in (mid_ref, a_ref, b_ref) for row in (0, above, below)]

    def gather(h, acc):
        m1, m2 = h1 == h, h2 == h
        new = []
        for f, (ref, row) in enumerate(places):
            for comp in range(2):
                line = ref[row, pl.ds(2 * h + comp, 1), :]
                at = 4 * f + 2 * comp
                new.append(jnp.where(m1, pick(line, l1), acc[at]))
                new.append(jnp.where(m2, pick(line, l2), acc[at + 1]))
        return tuple(new)

    acc = lax.fori_loop(0, mid_ref.shape[1] // 2, gather,
                        tuple([jnp.zeros(shape, F32)] * 36), unroll=2)
    value = (s_ref[0], s_ref[1])
    w = []
    for f in range(9):
        g1r, g2r, g1i, g2i = acc[4 * f:4 * f + 4]
        w.append(times(value, (g1r * g2r + g1i * g2i, g1i * g2r - g1r * g2i)))
    for names, at in (((OWN, LEFT, RIGHT), 0), ((UP, UL, UR), 1), ((DOWN, DL, DR), 2)):
        for comp in range(2):
            x, y = w[3 + at][comp], w[6 + at][comp]
            w_ref[2 * names[0] + comp] = w[at][comp]
            w_ref[2 * names[1] + comp] = jnp.where(c_odd, x, y)
            w_ref[2 * names[2] + comp] = jnp.where(c_odd, y, x)


def image_kernel(w_ref, ac_ref, as_ref, ec_ref, es_ref, fc_ref, fs_ref, cc_ref, cs_ref, out_ref,
                 tc_ref, ts_ref, uc_ref, us_ref, m1_ref, m2_ref, g1_ref, g2_ref):
    half_r, half_c = R // 2, C // 2
    k_tiles = w_ref.shape[1]
    shape = (SUB, LANES)
    iota = lax.broadcasted_iota(jnp.int32, shape, 0)
    zero = jnp.zeros((M, LANES), BF16)

    def tables(s, carry):
        lane = pl.ds(pl.multiple_of(s * LANES, LANES), LANES)

        def weight(f):
            return tuple(jnp.broadcast_to(w_ref[2 * f + comp, pl.ds(s, 1), :], shape)
                         for comp in range(2))

        pairs = {}

        def put(ref, first, group, x):
            key = (id(ref), first)
            if group % 2 == 0:
                pairs[key] = x
            else:
                start = first + SUB * (group - 1)
                ref[start:start + 16, lane] = jnp.concatenate([pairs.pop(key), x], 0).astype(BF16)

        rows_w = [weight(f) for f in (UP, DOWN, UL, UR, DL, DR)]
        signs = (-1, 1, -1, -1, 1, 1)
        for g in range(M // SUB):
            at = slice(g * SUB, (g + 1) * SUB)
            cos, sin = ec_ref[at, lane], es_ref[at, lane]
            for n, ((wr, wi), sd) in enumerate(zip(rows_w, signs)):
                put(uc_ref, n * M, g, wr * cos - (sd * wi) * sin)
                put(us_ref, n * M, g, -(sd * wr) * sin - wi * cos)
        edge = (half_c - M) // SUB
        (wr, wi), (lr, li), (rr, ri) = weight(OWN), weight(LEFT), weight(RIGHT)
        for g in range(half_c // SUB):
            at = slice(g * SUB, (g + 1) * SUB)
            cos, sin = fc_ref[at, lane], fs_ref[at, lane]
            own = (cos, sin)
            if g >= edge:
                mine, other = taper_rows(g, half_c)
                own = (cos * mine, sin * mine)
                cos, sin = cos * other, sin * other
                base = 2 * half_c + M
                put(tc_ref, base, g - edge, lr * cos + li * sin)
                put(ts_ref, base, g - edge, lr * sin - li * cos)
                put(tc_ref, base + 2 * M, g - edge, rr * cos - ri * sin)
                put(ts_ref, base + 2 * M, g - edge, -(rr * sin + ri * cos))
            put(tc_ref, 0, g, wr * own[0])
            put(tc_ref, half_c, g, -wi * own[1])
            put(ts_ref, 0, g, -wi * own[0])
            put(ts_ref, half_c, g, -wr * own[1])
        for ref in (tc_ref, ts_ref):
            ref[2 * half_c:2 * half_c + M, lane] = zero
            ref[2 * half_c + 2 * M:2 * half_c + 3 * M, lane] = zero
        return carry

    lax.fori_loop(0, k_tiles, tables, 0)

    def dot(a, b):
        return lax.dot_general(a[...], b[...], (((1,), (1,)), ((), ())), preferred_element_type=F32)

    m1_ref[...] = dot(ac_ref, tc_ref)
    m2_ref[...] = dot(as_ref, ts_ref)
    g1_ref[...] = dot(uc_ref, cc_ref)
    g2_ref[...] = dot(us_ref, cs_ref)

    lane_at = lax.broadcasted_iota(jnp.int32, shape, 1)
    back_lane = (LANES - 1) - lane_at
    back_row = (SUB - 1) - iota
    n_lane = half_c // LANES
    edge_c = half_c - M
    edge_r = half_r - M
    col_own, col_other = [], []
    for t in range(n_lane):
        index = (lane_at + t * LANES).astype(F32)
        col_own.append(jnp.minimum((half_c + M - 0.5 - index) * (1.0 / (2 * M)), 1.0))
        col_other.append(jnp.maximum((index - (half_c - M - 0.5)) * (1.0 / (2 * M)), 0.0))

    def flip(x, index, axis):
        return jnp.take_along_axis(x, index, axis=axis, mode="promise_in_bounds")

    def finish(g, edged):
        rows = pl.ds(pl.multiple_of(g * SUB, SUB), SUB)
        for t in range(n_lane):
            def part(ref, which):
                return ref[rows, which * half_c + t * LANES:which * half_c + (t + 1) * LANES]
            p, s_, r, q = part(m1_ref, 0), part(m1_ref, 1), part(m2_ref, 0), part(m2_ref, 1)
            even, odd = p + q, p - q
            plus, minus = r + s_, r - s_
            quad = {(1, 1): even + plus, (-1, -1): even - plus,
                    (1, -1): odd + minus, (-1, 1): odd - minus}
            if (t + 1) * LANES > edge_c:
                base = 2 * half_c
                off = t * LANES - (half_c - LANES)
                for se, start in ((-1, base), (1, base + LANES)):
                    lc = m1_ref[rows, start + off:start + off + LANES]
                    ls = m2_ref[rows, start + off:start + off + LANES]
                    quad[1, se] += lc + ls
                    quad[-1, se] += lc - ls
            if edged:
                def edge(n):
                    at = pl.ds(pl.multiple_of(n * M + g * SUB - edge_r, SUB), SUB)
                    x = g1_ref[at, t * LANES:(t + 1) * LANES]
                    y = g2_ref[at, t * LANES:(t + 1) * LANES]
                    return {1: x + y, -1: x - y}
                for n, sd in ((0, -1), (1, 1)):
                    e = edge(n)
                    for se in (-1, 1):
                        quad[sd, se] += e[se] * col_own[t]
                if (t + 1) * LANES > edge_c:
                    for n, (sd, se) in ((2, (-1, -1)), (3, (-1, 1)), (4, (1, -1)), (5, (1, 1))):
                        quad[sd, se] += edge(n)[se] * col_other[t]
            for (sd, se), x in quad.items():
                if sd < 0:
                    x = flip(x, back_row, 0)
                    at = pl.ds(pl.multiple_of(half_r - SUB - g * SUB, SUB), SUB)
                else:
                    at = pl.ds(pl.multiple_of(half_r + g * SUB, SUB), SUB)
                if se < 0:
                    x = flip(x, back_lane, 1)
                    start = half_c - (t + 1) * LANES
                else:
                    start = half_c + t * LANES
                out_ref[at, start:start + LANES] = x

    def inner(g, carry):
        finish(g, False)
        return carry

    def outer(g, carry):
        finish(g, True)
        return carry

    lax.fori_loop(0, edge_r // SUB, inner, 0, unroll=2)
    lax.fori_loop(edge_r // SUB, half_r // SUB, outer, 0)


def swaps(size):
    both = []
    for first in (0, 1):
        pairs = [(i, i + 1) for i in range(first, size - 1, 2)]
        both.append(pairs + [(j, i) for i, j in pairs])
    return both


def total(x, axis):
    size = lax.axis_size(axis)
    if size & (size - 1):
        return lax.psum(x, axis)
    bit = 1
    while bit < size:
        x = x + lax.ppermute(x, axis, [(i, i ^ bit) for i in range(size)])
        bit *= 2
    return x


def shards(vis, station_pairs, visibility_time_slot, station_u_cells, station_v_cells,
           facet_station_gains, holder_device_order):
    n_frow = lax.axis_size("frow")
    n_fcol = lax.axis_size("fcol")
    block = vis.shape[1]
    k_tiles = NBLK * block // LANES
    k = k_tiles * LANES
    half_r, half_c = R // 2, C // 2
    wide = 2 * half_c + 4 * M
    vmem = pl.BlockSpec(memory_space=pltpu.VMEM)
    smem = pl.BlockSpec(memory_space=pltpu.SMEM)

    def lines(x):
        return x.reshape(-1, LANES)

    def shaped(*dims, dtype=F32):
        return jax.ShapeDtypeStruct(dims, dtype)

    def params(mib):
        return pltpu.CompilerParams(vmem_limit_bytes=mib * 1024 * 1024)

    gains = facet_station_gains[0, 0]
    depth = gains.size // LANES
    own = gains.reshape(2, -1, LANES).transpose(1, 0, 2).reshape(depth, LANES)
    row_a, row_b = [lax.ppermute(own, "frow", pairs) for pairs in swaps(n_frow)]
    slots, u_lines, v_lines = pl.pallas_call(
        pack_kernel,
        out_shape=[
            shaped(5, k_tiles, LANES),
            shaped(station_u_cells.size // LANES, LANES, dtype=jnp.int32),
            shaped(station_v_cells.size // LANES, LANES, dtype=jnp.int32),
        ],
        in_specs=[smem] + [vmem] * 5,
        out_specs=[vmem] * 3,
        name="pack",
    )(holder_device_order, vis, station_pairs, visibility_time_slot.reshape(1, block),
      lines(station_u_cells), lines(station_v_cells))
    slots = total(total(slots, "fcol"), "frow")
    mid = jnp.stack([own, row_a, row_b])
    col_a, col_b = [lax.ppermute(mid, "fcol", pairs) for pairs in swaps(n_fcol)]
    s, *tables = pl.pallas_call(
        functools.partial(table_kernel, n_frow, n_fcol),
        out_shape=[
            shaped(4, k_tiles, LANES),
            shaped(half_r, k, dtype=BF16), shaped(half_r, k, dtype=BF16),
            shaped(M, k), shaped(M, k),
            shaped(half_c, k), shaped(half_c, k),
            shaped(half_c, k, dtype=BF16), shaped(half_c, k, dtype=BF16),
        ],
        in_specs=[vmem] * 3,
        out_specs=[vmem] * 9,
        scratch_shapes=[
            pltpu.VMEM((2, k_tiles, LANES), jnp.int32),
            pltpu.VMEM((2, 2, half_r // SUB, LANES), F32),
        ],
        compiler_params=params(24),
        name="tables",
    )(slots, u_lines, v_lines)
    weights = pl.pallas_call(
        weight_kernel,
        out_shape=shaped(18, k_tiles, LANES),
        in_specs=[vmem] * 4,
        out_specs=vmem,
        compiler_params=params(8),
        name="weights",
    )(s, mid, col_a, col_b)
    return pl.pallas_call(
        image_kernel,
        out_shape=shaped(R, C),
        in_specs=[vmem] * 9,
        out_specs=vmem,
        scratch_shapes=[
            pltpu.VMEM((wide, k), BF16),
            pltpu.VMEM((wide, k), BF16),
            pltpu.VMEM((6 * M, k), BF16),
            pltpu.VMEM((6 * M, k), BF16),
            pltpu.VMEM((half_r, wide), F32),
            pltpu.VMEM((half_r, wide), F32),
            pltpu.VMEM((6 * M, half_c), F32),
            pltpu.VMEM((6 * M, half_c), F32),
        ],
        compiler_params=params(32),
        name="image",
    )(weights, *tables)


def solution(mesh):
    return jax.shard_map(
        shards,
        mesh=mesh,
        in_specs=(
            P(None, ("frow", "fcol")),
            P(None, ("frow", "fcol")),
            P(("frow", "fcol")),
            P(),
            P(),
            P("frow", "fcol", None, None),
            P(),
        ),
        out_specs=P("frow", "fcol"),
        check_vma=False,
    )
```

```python
import functools
import math

import jax
import jax.numpy as jnp
from jax import lax
from jax.experimental import pallas as pl
from jax.experimental.pallas import tpu as pltpu
from jax.sharding import PartitionSpec as P

R = 1024
C = 512
M = 64
NT = 16
NBLK = 4
LANES = 128
SUB = 8
OWN, LEFT, RIGHT, UP, DOWN, UL, UR, DL, DR = range(9)
F32 = jnp.float32
BF16 = jnp.bfloat16


def wrap(m, modulus):
    if modulus & (modulus - 1) == 0:
        return m & (modulus - 1)
    return jnp.remainder(m, modulus)


def turn(m, modulus):
    m = wrap(m, modulus)
    quarter = modulus // 4
    q = (m + modulus // 8) // quarter if quarter & (quarter - 1) else (
        (m + modulus // 8) >> (quarter.bit_length() - 1))
    x = (m - q * quarter).astype(F32) * (2.0 * math.pi / modulus)
    x2 = x * x
    s = x + x * x2 * (-1 / 6 + x2 * (1 / 120 + x2 * (-1 / 5040 + x2 * (1 / 362880))))
    c = 1.0 + x2 * (-0.5 + x2 * (1 / 24 + x2 * (-1 / 720 + x2 * (1 / 40320))))
    odd = (q & 1) == 1
    cos = jnp.where(odd, s, c)
    sin = jnp.where(odd, c, s)
    cos = jnp.where(((q + 1) & 2) != 0, -cos, cos)
    sin = jnp.where((q & 2) != 0, -sin, sin)
    return cos, sin


def times(a, b):
    return a[0] * b[0] - a[1] * b[1], a[0] * b[1] + a[1] * b[0]


def pack_kernel(order_ref, vis_ref, pair_ref, slot_ref, u_ref, v_ref,
                out_ref, uv_out, order_out):
    block = vis_ref.shape[1]
    lines = [vis_ref[0:1, :], vis_ref[1:2, :], pair_ref[0:1, :].astype(F32),
             pair_ref[1:2, :].astype(F32), slot_ref[...].astype(F32)]
    for copy in range(out_ref.shape[0]):
        for q, line in enumerate(lines):
            out_ref[copy, :, q * block:(q + 1) * block] = line
    uv_out[0] = u_ref[...]
    uv_out[1] = v_ref[...]
    order_out[...] = order_ref[...]


def pick(row, lane):
    return jnp.take_along_axis(
        jnp.broadcast_to(row, lane.shape), lane, axis=1, mode="promise_in_bounds")


def taper_rows(group, half):
    index = (lax.broadcasted_iota(jnp.int32, (SUB, LANES), 0) + SUB * group).astype(F32)
    return ((half + M - 0.5 - index) * (1.0 / (2 * M)),
            (index - (half - M - 0.5)) * (1.0 / (2 * M)))


def table_kernel(n_frow, n_fcol, order_ref, block_ref, cell_ref,
                 s_ref, ac_ref, as_ref, ec_ref, es_ref, fc_ref, fs_ref, cc_ref, cs_ref,
                 q_ref, uv_ref, dr_ref):
    frow_at = lax.axis_index("frow")
    fcol_at = lax.axis_index("fcol")
    half_r, half_c = R // 2, C // 2
    mod_r, mod_c = 2 * R * n_frow, 2 * C * n_fcol
    k_tiles = s_ref.shape[1]
    per_block = k_tiles // NBLK
    block = per_block * LANES
    shape = (SUB, LANES)

    for b in range(NBLK):
        owner = order_ref[0, b]
        for q in range(5):
            for j in range(per_block):
                q_ref[q, b * per_block + j:b * per_block + j + 1, :] = block_ref[
                    owner, :, q * block + j * LANES:q * block + (j + 1) * LANES]
    a1 = q_ref[2].astype(jnp.int32)
    a2 = q_ref[3].astype(jnp.int32)
    slot = q_ref[4].astype(jnp.int32)

    def cells(table):
        got = [jnp.zeros(shape, jnp.int32)] * 2
        for h in range(table.shape[0]):
            row = table[h:h + 1, :]
            got = [jnp.where((a >> 7) == h, pick(row, a & 127), g)
                   for a, g in zip((a1, a2), got)]
        return got[0] - got[1]

    u = cells(cell_ref[0])
    v = cells(cell_ref[1])
    uv_ref[0] = u
    uv_ref[1] = v
    centre = times(turn(u * (frow_at * (2 * R) + (R - 1)), mod_r),
                   turn(v * (fcol_at * (2 * C) + (C - 1)), mod_c))
    scale = 0.5 / math.sqrt(NBLK * per_block * LANES)
    value = times((q_ref[0] * scale, q_ref[1] * scale), centre)
    s_ref[0] = value[0]
    s_ref[1] = value[1]
    for n, a in enumerate((a1, a2)):
        s_ref[2 + n] = ((a >> 3) + (a & 4) * 16).astype(F32)
        s_ref[4 + n] = ((a & 3) * NT + slot).astype(F32)

    iota = lax.broadcasted_iota(jnp.int32, shape, 0)

    def tables(s, carry):
        lane = pl.ds(pl.multiple_of(s * LANES, LANES), LANES)

        def phases(which, modulus, half):
            freq = jnp.broadcast_to(uv_ref[which, pl.ds(s, 1), :], shape)
            fine = turn(freq * (2 * iota + 1), modulus)
            middle = turn(freq * (16 * iota), modulus)
            coarse = turn(freq * (128 * iota), modulus)
            for a in range(half // 64):
                top = tuple(jnp.broadcast_to(x[a:a + 1], shape) for x in coarse)
                both = times(middle, top)
                for comp in range(2):
                    dr_ref[which, comp, 8 * a:8 * a + 8, :] = both[comp]
            for g in range(half // SUB):
                step = tuple(jnp.broadcast_to(dr_ref[which, comp, g:g + 1, :], shape)
                             for comp in range(2))
                yield times(fine, step)

        pairs = {}

        def put(ref, first, group, x):
            key = (id(ref), first)
            if group % 2 == 0:
                pairs[key] = x
            else:
                start = first + SUB * (group - 1)
                ref[start:start + 16, lane] = jnp.concatenate([pairs.pop(key), x], 0).astype(BF16)

        edge = (half_r - M) // SUB
        for g, (cos, sin) in enumerate(phases(0, mod_r, half_r)):
            if g >= edge:
                mine, other = taper_rows(g, half_r)
                at = slice((g - edge) * SUB, (g - edge + 1) * SUB)
                ec_ref[at, lane] = cos * other
                es_ref[at, lane] = sin * other
                cos, sin = cos * mine, sin * mine
            put(ac_ref, 0, g, cos)
            put(as_ref, 0, g, sin)
        for g, (cos, sin) in enumerate(phases(1, mod_c, half_c)):
            put(cc_ref, 0, g, cos)
            put(cs_ref, 0, g, sin)
            at = slice(g * SUB, (g + 1) * SUB)
            fc_ref[at, lane] = cos
            fs_ref[at, lane] = sin
        return carry

    lax.fori_loop(0, k_tiles, tables, 0)


def weight_kernel(s_ref, mid_ref, a_ref, b_ref, w_ref, hot_ref, mask_ref, gain_ref, z_ref):
    r_odd = lax.rem(lax.axis_index("frow"), 2) == 1
    c_odd = lax.rem(lax.axis_index("fcol"), 2) == 1
    above = jnp.where(r_odd, 1, 2)
    below = jnp.where(r_odd, 2, 1)
    k_tiles = s_ref.shape[1]
    depth = mid_ref.shape[1]
    half = depth // 2
    places = [(ref, row) for ref in (mid_ref, a_ref, b_ref) for row in (0, above, below)]

    line_at = lax.broadcasted_iota(jnp.int32, (depth, LANES), 0).astype(F32)
    place_at = line_at[:half]
    for n in range(2):
        for t in range(k_tiles):
            lane = slice((n * k_tiles + t) * LANES, (n * k_tiles + t + 1) * LANES)
            hot = jnp.where(line_at == s_ref[2 + n, t:t + 1, :], 1.0, 0.0).astype(BF16)
            hot_ref[:depth, lane] = hot
            hot_ref[depth:, lane] = hot
            mask_ref[:, lane] = jnp.where(place_at == s_ref[4 + n, t:t + 1, :], 1.0, 0.0)

    low_lane = lax.broadcasted_iota(jnp.int32, (half, LANES), 1) < LANES // 2
    for f, (ref, row) in enumerate(places):
        re = ref[row, pl.ds(0, half, stride=2), :]
        im = ref[row, pl.ds(1, half, stride=2), :]
        top = jnp.where(low_lane, re, pltpu.roll(im, LANES // 2, 1))
        low = jnp.where(low_lane, pltpu.roll(re, LANES // 2, 1), im)
        both = jnp.concatenate([top, low], 0)
        first = both.astype(BF16)
        rest = (both - first.astype(F32)).astype(BF16)
        gain_ref[:depth, f * LANES:(f + 1) * LANES] = first
        gain_ref[depth:, f * LANES:(f + 1) * LANES] = rest

    for f in range(9):
        z_ref[f] = lax.dot_general(gain_ref[:, f * LANES:(f + 1) * LANES], hot_ref[...],
                                   (((0,), (0,)), ((), ())), preferred_element_type=F32)

    def weights(t, carry):
        def looked_up(f, n):
            lane = pl.ds(pl.multiple_of((n * k_tiles + t) * LANES, LANES), LANES)
            mask = mask_ref[:, lane]
            return [jnp.sum(z_ref[f, comp * half:(comp + 1) * half, lane] * mask, axis=0,
                            keepdims=True) for comp in range(2)]

        value = (s_ref[0, pl.ds(t, 1), :], s_ref[1, pl.ds(t, 1), :])
        w = []
        for f in range(9):
            (g1r, g1i), (g2r, g2i) = looked_up(f, 0), looked_up(f, 1)
            w.append(times(value, (g1r * g2r + g1i * g2i, g1i * g2r - g1r * g2i)))
        for names, at in (((OWN, LEFT, RIGHT), 0), ((UP, UL, UR), 1), ((DOWN, DL, DR), 2)):
            for comp in range(2):
                x, y = w[3 + at][comp], w[6 + at][comp]
                w_ref[2 * names[0] + comp, pl.ds(t, 1), :] = w[at][comp]
                w_ref[2 * names[1] + comp, pl.ds(t, 1), :] = jnp.where(c_odd, x, y)
                w_ref[2 * names[2] + comp, pl.ds(t, 1), :] = jnp.where(c_odd, y, x)
        return carry

    lax.fori_loop(0, k_tiles, weights, 0)


def column_kernel(w_ref, ec_ref, es_ref, fc_ref, fs_ref, tc_ref, ts_ref, uc_ref, us_ref):
    half_r, half_c = R // 2, C // 2
    k_tiles = w_ref.shape[1]
    shape = (SUB, LANES)
    iota = lax.broadcasted_iota(jnp.int32, shape, 0)
    zero = jnp.zeros((M, LANES), BF16)

    def tables(s, carry):
        lane = pl.ds(pl.multiple_of(s * LANES, LANES), LANES)

        def weight(f):
            return tuple(jnp.broadcast_to(w_ref[2 * f + comp, pl.ds(s, 1), :], shape)
                         for comp in range(2))

        pairs = {}

        def put(ref, first, group, x):
            key = (id(ref), first)
            if group % 2 == 0:
                pairs[key] = x
            else:
                start = first + SUB * (group - 1)
                ref[start:start + 16, lane] = jnp.concatenate([pairs.pop(key), x], 0).astype(BF16)

        rows_w = [weight(f) for f in (UP, DOWN, UL, UR, DL, DR)]
        signs = (-1, 1, -1, -1, 1, 1)
        for g in range(M // SUB):
            at = slice(g * SUB, (g + 1) * SUB)
            cos, sin = ec_ref[at, lane], es_ref[at, lane]
            for n, ((wr, wi), sd) in enumerate(zip(rows_w, signs)):
                put(uc_ref, n * M, g, wr * cos - (sd * wi) * sin)
                put(us_ref, n * M, g, -(sd * wr) * sin - wi * cos)
        edge = (half_c - M) // SUB
        (wr, wi), (lr, li), (rr, ri) = weight(OWN), weight(LEFT), weight(RIGHT)
        for g in range(half_c // SUB):
            at = slice(g * SUB, (g + 1) * SUB)
            cos, sin = fc_ref[at, lane], fs_ref[at, lane]
            own = (cos, sin)
            if g >= edge:
                mine, other = taper_rows(g, half_c)
                own = (cos * mine, sin * mine)
                cos, sin = cos * other, sin * other
                base = 2 * half_c + M
                put(tc_ref, base, g - edge, lr * cos + li * sin)
                put(ts_ref, base, g - edge, lr * sin - li * cos)
                put(tc_ref, base + 2 * M, g - edge, rr * cos - ri * sin)
                put(ts_ref, base + 2 * M, g - edge, -(rr * sin + ri * cos))
            put(tc_ref, 0, g, wr * own[0])
            put(tc_ref, half_c, g, -wi * own[1])
            put(ts_ref, 0, g, -wi * own[0])
            put(ts_ref, half_c, g, -wr * own[1])
        for ref in (tc_ref, ts_ref):
            ref[2 * half_c:2 * half_c + M, lane] = zero
            ref[2 * half_c + 2 * M:2 * half_c + 3 * M, lane] = zero
        return carry

    lax.fori_loop(0, k_tiles, tables, 0)


def finish_kernel(m1_ref, m2_ref, g1_ref, g2_ref, out_ref):
    half_r, half_c = R // 2, C // 2
    shape = (SUB, LANES)
    iota = lax.broadcasted_iota(jnp.int32, shape, 0)
    lane_at = lax.broadcasted_iota(jnp.int32, shape, 1)
    back_lane = (LANES - 1) - lane_at
    back_row = (SUB - 1) - iota
    n_lane = half_c // LANES
    edge_c = half_c - M
    edge_r = half_r - M
    col_own, col_other = [], []
    for t in range(n_lane):
        index = (lane_at + t * LANES).astype(F32)
        col_own.append(jnp.minimum((half_c + M - 0.5 - index) * (1.0 / (2 * M)), 1.0))
        col_other.append(jnp.maximum((index - (half_c - M - 0.5)) * (1.0 / (2 * M)), 0.0))

    def flip(x, index, axis):
        return jnp.take_along_axis(x, index, axis=axis, mode="promise_in_bounds")

    def finish(g, edged):
        rows = pl.ds(pl.multiple_of(g * SUB, SUB), SUB)
        for t in range(n_lane):
            def part(ref, which):
                return ref[rows, which * half_c + t * LANES:which * half_c + (t + 1) * LANES]
            p, s_, r, q = part(m1_ref, 0), part(m1_ref, 1), part(m2_ref, 0), part(m2_ref, 1)
            even, odd = p + q, p - q
            plus, minus = r + s_, r - s_
            quad = {(1, 1): even + plus, (-1, -1): even - plus,
                    (1, -1): odd + minus, (-1, 1): odd - minus}
            if (t + 1) * LANES > edge_c:
                base = 2 * half_c
                off = t * LANES - (half_c - LANES)
                for se, start in ((-1, base), (1, base + LANES)):
                    lc = m1_ref[rows, start + off:start + off + LANES]
                    ls = m2_ref[rows, start + off:start + off + LANES]
                    quad[1, se] += lc + ls
                    quad[-1, se] += lc - ls
            if edged:
                def edge(n):
                    at = pl.ds(pl.multiple_of(n * M + g * SUB - edge_r, SUB), SUB)
                    x = g1_ref[at, t * LANES:(t + 1) * LANES]
                    y = g2_ref[at, t * LANES:(t + 1) * LANES]
                    return {1: x + y, -1: x - y}
                for n, sd in ((0, -1), (1, 1)):
                    e = edge(n)
                    for se in (-1, 1):
                        quad[sd, se] += e[se] * col_own[t]
                if (t + 1) * LANES > edge_c:
                    for n, (sd, se) in ((2, (-1, -1)), (3, (-1, 1)), (4, (1, -1)), (5, (1, 1))):
                        quad[sd, se] += edge(n)[se] * col_other[t]
            for (sd, se), x in quad.items():
                if sd < 0:
                    x = flip(x, back_row, 0)
                    at = pl.ds(pl.multiple_of(half_r - SUB - g * SUB, SUB), SUB)
                else:
                    at = pl.ds(pl.multiple_of(half_r + g * SUB, SUB), SUB)
                if se < 0:
                    x = flip(x, back_lane, 1)
                    start = half_c - (t + 1) * LANES
                else:
                    start = half_c + t * LANES
                out_ref[at, start:start + LANES] = x

    def inner(g, carry):
        finish(g, False)
        return carry

    def outer(g, carry):
        finish(g, True)
        return carry

    lax.fori_loop(0, edge_r // SUB, inner, 0, unroll=2)
    lax.fori_loop(edge_r // SUB, half_r // SUB, outer, 0)


def swaps(size):
    both = []
    for first in (0, 1):
        pairs = [(i, i + 1) for i in range(first, size - 1, 2)]
        both.append(pairs + [(j, i) for i, j in pairs])
    return both


def shards(vis, station_pairs, visibility_time_slot, station_u_cells, station_v_cells,
           facet_station_gains, holder_device_order):
    n_frow = lax.axis_size("frow")
    n_fcol = lax.axis_size("fcol")
    block = vis.shape[1]
    k_tiles = NBLK * block // LANES
    k = k_tiles * LANES
    half_r, half_c = R // 2, C // 2
    wide = 2 * half_c + 4 * M
    vmem = pl.BlockSpec(memory_space=pltpu.VMEM)
    smem = pl.BlockSpec(memory_space=pltpu.SMEM)

    def lines(x):
        return x.reshape(-1, LANES)

    def shaped(*dims, dtype=F32):
        return jax.ShapeDtypeStruct(dims, dtype)

    def params(mib):
        return pltpu.CompilerParams(vmem_limit_bytes=mib * 1024 * 1024)

    gains = facet_station_gains[0, 0]
    depth = gains.size // LANES
    own = gains.reshape(2, -1, LANES).transpose(1, 0, 2).reshape(depth, LANES)
    row_a, row_b = [lax.ppermute(own, "frow", pairs) for pairs in swaps(n_frow)]
    packed, cells, order = pl.pallas_call(
        pack_kernel,
        out_shape=[
            shaped(n_frow * n_fcol, 1, 5 * block),
            shaped(2, station_u_cells.size // LANES, LANES, dtype=jnp.int32),
            shaped(1, holder_device_order.size, dtype=jnp.int32),
        ],
        name="pack",
    )(holder_device_order.reshape(1, -1), vis, station_pairs,
      visibility_time_slot.reshape(1, block), lines(station_u_cells), lines(station_v_cells))
    blocks = lax.all_to_all(packed, ("frow", "fcol"), 0, 0)
    mid = jnp.stack([own, row_a, row_b])
    col_a, col_b = [lax.ppermute(mid, "fcol", pairs) for pairs in swaps(n_fcol)]
    s, a_cos, a_sin, e_cos, e_sin, f_cos, f_sin, c_cos, c_sin = pl.pallas_call(
        functools.partial(table_kernel, n_frow, n_fcol),
        out_shape=[
            shaped(6, k_tiles, LANES),
            shaped(half_r, k, dtype=BF16), shaped(half_r, k, dtype=BF16),
            shaped(M, k), shaped(M, k),
            shaped(half_c, k), shaped(half_c, k),
            shaped(half_c, k, dtype=BF16), shaped(half_c, k, dtype=BF16),
        ],
        in_specs=[smem] + [vmem] * 2,
        out_specs=[vmem] * 9,
        scratch_shapes=[
            pltpu.VMEM((5, k_tiles, LANES), F32),
            pltpu.VMEM((2, k_tiles, LANES), jnp.int32),
            pltpu.VMEM((2, 2, half_r // SUB, LANES), F32),
        ],
        compiler_params=params(24),
        name="tables",
    )(order, blocks, cells)
    weights = pl.pallas_call(
        weight_kernel,
        out_shape=shaped(18, k_tiles, LANES),
        in_specs=[vmem] * 4,
        out_specs=vmem,
        scratch_shapes=[
            pltpu.VMEM((2 * depth, 2 * k), BF16),
            pltpu.VMEM((depth // 2, 2 * k), F32),
            pltpu.VMEM((2 * depth, 9 * LANES), BF16),
            pltpu.VMEM((9, LANES, 2 * k), F32),
        ],
        compiler_params=params(24),
        name="weights",
    )(s, mid, col_a, col_b)
    t_cos, t_sin, u_cos, u_sin = pl.pallas_call(
        column_kernel,
        out_shape=[shaped(wide, k, dtype=BF16), shaped(wide, k, dtype=BF16),
                   shaped(6 * M, k, dtype=BF16), shaped(6 * M, k, dtype=BF16)],
        in_specs=[vmem] * 5,
        out_specs=[vmem] * 4,
        compiler_params=params(24),
        name="columns",
    )(weights, e_cos, e_sin, f_cos, f_sin)

    def dot(a, b):
        return lax.dot_general(a, b, (((1,), (1,)), ((), ())), preferred_element_type=F32)

    return pl.pallas_call(
        finish_kernel,
        out_shape=shaped(R, C),
        in_specs=[vmem] * 4,
        out_specs=vmem,
        compiler_params=params(24),
        name="finish",
    )(dot(a_cos, t_cos), dot(a_sin, t_sin), dot(u_cos, c_cos), dot(u_sin, c_sin))


def solution(mesh):
    return jax.shard_map(
        shards,
        mesh=mesh,
        in_specs=(
            P(None, ("frow", "fcol")),
            P(None, ("frow", "fcol")),
            P(("frow", "fcol")),
            P(),
            P(),
            P("frow", "fcol", None, None),
            P(),
        ),
        out_specs=P("frow", "fcol"),
        check_vma=False,
    )
```

```python
import functools
import math

import jax
import jax.numpy as jnp
from jax import lax
from jax.experimental import pallas as pl
from jax.experimental.pallas import tpu as pltpu
from jax.sharding import PartitionSpec as P

R = 1024
C = 512
M = 64
NT = 16
NBLK = 4
LANES = 128
SUB = 8
OWN, LEFT, RIGHT, UP, DOWN, UL, UR, DL, DR = range(9)
F32 = jnp.float32
BF16 = jnp.bfloat16


def wrap(m, modulus):
    if modulus & (modulus - 1) == 0:
        return m & (modulus - 1)
    return jnp.remainder(m, modulus)


def turn(m, modulus):
    m = wrap(m, modulus)
    quarter = modulus // 4
    q = (m + modulus // 8) // quarter if quarter & (quarter - 1) else (
        (m + modulus // 8) >> (quarter.bit_length() - 1))
    x = (m - q * quarter).astype(F32) * (2.0 * math.pi / modulus)
    x2 = x * x
    s = x + x * x2 * (-1 / 6 + x2 * (1 / 120 + x2 * (-1 / 5040 + x2 * (1 / 362880))))
    c = 1.0 + x2 * (-0.5 + x2 * (1 / 24 + x2 * (-1 / 720 + x2 * (1 / 40320))))
    odd = (q & 1) == 1
    cos = jnp.where(odd, s, c)
    sin = jnp.where(odd, c, s)
    cos = jnp.where(((q + 1) & 2) != 0, -cos, cos)
    sin = jnp.where((q & 2) != 0, -sin, sin)
    return cos, sin


def times(a, b):
    return a[0] * b[0] - a[1] * b[1], a[0] * b[1] + a[1] * b[0]


def pack_kernel(vis_ref, pair_ref, slot_ref, out_ref):
    block = vis_ref.shape[1]
    lines = [vis_ref[0:1, :], vis_ref[1:2, :], pair_ref[0:1, :].astype(F32),
             pair_ref[1:2, :].astype(F32), slot_ref[...].astype(F32)]
    for copy in range(out_ref.shape[0]):
        for q, line in enumerate(lines):
            out_ref[copy, :, q * block:(q + 1) * block] = line


def pick(row, lane):
    return jnp.take_along_axis(
        jnp.broadcast_to(row, lane.shape), lane, axis=1, mode="promise_in_bounds")


def taper_rows(group, half):
    index = (lax.broadcasted_iota(jnp.int32, (SUB, LANES), 0) + SUB * group).astype(F32)
    return ((half + M - 0.5 - index) * (1.0 / (2 * M)),
            (index - (half - M - 0.5)) * (1.0 / (2 * M)))


def table_kernel(n_frow, n_fcol, n_lines, order_ref, block_ref, cell_ref,
                 s_ref, ac_ref, as_ref, ec_ref, es_ref, fc_ref, fs_ref, cc_ref, cs_ref,
                 q_ref, uv_ref, dr_ref):
    frow_at = lax.axis_index("frow")
    fcol_at = lax.axis_index("fcol")
    half_r, half_c = R // 2, C // 2
    mod_r, mod_c = 2 * R * n_frow, 2 * C * n_fcol
    k_tiles = s_ref.shape[1]
    per_block = k_tiles // NBLK
    block = per_block * LANES
    shape = (SUB, LANES)

    for b in range(NBLK):
        owner = order_ref[2 * n_lines, b]
        for q in range(5):
            for j in range(per_block):
                q_ref[q, b * per_block + j:b * per_block + j + 1, :] = block_ref[
                    owner, :, q * block + j * LANES:q * block + (j + 1) * LANES]
    a1 = q_ref[2].astype(jnp.int32)
    a2 = q_ref[3].astype(jnp.int32)
    slot = q_ref[4].astype(jnp.int32)

    def cells(table):
        got = [jnp.zeros(shape, jnp.int32)] * 2
        for h in range(table.shape[0]):
            row = table[h:h + 1, :]
            got = [jnp.where((a >> 7) == h, pick(row, a & 127), g)
                   for a, g in zip((a1, a2), got)]
        return got[0] - got[1]

    u = cells(cell_ref[:n_lines, :])
    v = cells(cell_ref[n_lines:2 * n_lines, :])
    uv_ref[0] = u
    uv_ref[1] = v
    centre = times(turn(u * (frow_at * (2 * R) + (R - 1)), mod_r),
                   turn(v * (fcol_at * (2 * C) + (C - 1)), mod_c))
    scale = 0.5 / math.sqrt(NBLK * per_block * LANES)
    value = times((q_ref[0] * scale, q_ref[1] * scale), centre)
    s_ref[0] = value[0]
    s_ref[1] = value[1]
    for n, a in enumerate((a1, a2)):
        s_ref[2 + n] = ((a >> 3) + (a & 4) * 16).astype(F32)
        s_ref[4 + n] = ((a & 3) * NT + slot).astype(F32)

    iota = lax.broadcasted_iota(jnp.int32, shape, 0)

    def tables(s, carry):
        lane = pl.ds(pl.multiple_of(s * LANES, LANES), LANES)

        def phases(which, modulus, half):
            freq = jnp.broadcast_to(uv_ref[which, pl.ds(s, 1), :], shape)
            fine = turn(freq * (2 * iota + 1), modulus)
            middle = turn(freq * (16 * iota), modulus)
            coarse = turn(freq * (128 * iota), modulus)
            for a in range(half // 64):
                top = tuple(jnp.broadcast_to(x[a:a + 1], shape) for x in coarse)
                both = times(middle, top)
                for comp in range(2):
                    dr_ref[which, comp, 8 * a:8 * a + 8, :] = both[comp]
            for g in range(half // SUB):
                step = tuple(jnp.broadcast_to(dr_ref[which, comp, g:g + 1, :], shape)
                             for comp in range(2))
                yield times(fine, step)

        pairs = {}

        def put(ref, first, group, x):
            key = (id(ref), first)
            if group % 2 == 0:
                pairs[key] = x
            else:
                start = first + SUB * (group - 1)
                ref[start:start + 16, lane] = jnp.concatenate([pairs.pop(key), x], 0).astype(BF16)

        edge = (half_r - M) // SUB
        for g, (cos, sin) in enumerate(phases(0, mod_r, half_r)):
            if g >= edge:
                mine, other = taper_rows(g, half_r)
                at = slice((g - edge) * SUB, (g - edge + 1) * SUB)
                ec_ref[at, lane] = cos * other
                es_ref[at, lane] = sin * other
                cos, sin = cos * mine, sin * mine
            put(ac_ref, 0, g, cos)
            put(as_ref, 0, g, sin)
        for g, (cos, sin) in enumerate(phases(1, mod_c, half_c)):
            put(cc_ref, 0, g, cos)
            put(cs_ref, 0, g, sin)
            at = slice(g * SUB, (g + 1) * SUB)
            fc_ref[at, lane] = cos
            fs_ref[at, lane] = sin
        return carry

    lax.fori_loop(0, k_tiles, tables, 0)


def column_kernel(s_ref, mid_ref, a_ref, b_ref, ec_ref, es_ref, fc_ref, fs_ref,
                  tc_ref, ts_ref, uc_ref, us_ref, hot_ref, mask_ref, gain_ref, z_ref):
    r_odd = lax.rem(lax.axis_index("frow"), 2) == 1
    c_odd = lax.rem(lax.axis_index("fcol"), 2) == 1
    above = jnp.where(r_odd, 1, 2)
    below = jnp.where(r_odd, 2, 1)
    k_tiles = s_ref.shape[1]
    depth = mid_ref.shape[1]
    half = depth // 2
    places = [(ref, row) for ref in (mid_ref, a_ref, b_ref) for row in (0, above, below)]

    line_at = lax.broadcasted_iota(jnp.int32, (depth, LANES), 0).astype(F32)
    place_at = line_at[:half]
    for n in range(2):
        for t in range(k_tiles):
            lane = slice((n * k_tiles + t) * LANES, (n * k_tiles + t + 1) * LANES)
            hot = jnp.where(line_at == s_ref[2 + n, t:t + 1, :], 1.0, 0.0).astype(BF16)
            hot_ref[:depth, lane] = hot
            hot_ref[depth:, lane] = hot
            mask_ref[:, lane] = jnp.where(place_at == s_ref[4 + n, t:t + 1, :], 1.0, 0.0)

    low_lane = lax.broadcasted_iota(jnp.int32, (half, LANES), 1) < LANES // 2
    for f, (ref, row) in enumerate(places):
        re = ref[row, pl.ds(0, half, stride=2), :]
        im = ref[row, pl.ds(1, half, stride=2), :]
        top = jnp.where(low_lane, re, pltpu.roll(im, LANES // 2, 1))
        low = jnp.where(low_lane, pltpu.roll(re, LANES // 2, 1), im)
        both = jnp.concatenate([top, low], 0)
        first = both.astype(BF16)
        rest = (both - first.astype(F32)).astype(BF16)
        gain_ref[:depth, f * LANES:(f + 1) * LANES] = first
        gain_ref[depth:, f * LANES:(f + 1) * LANES] = rest

    z_ref[...] = lax.dot_general(gain_ref[...], hot_ref[...], (((0,), (0,)), ((), ())),
                                 preferred_element_type=F32)

    half_c = C // 2
    shape = (SUB, LANES)
    zero = jnp.zeros((M, LANES), BF16)

    def tables(t, carry):
        lane = pl.ds(pl.multiple_of(t * LANES, LANES), LANES)

        def looked_up(f, n):
            at = pl.ds(pl.multiple_of((n * k_tiles + t) * LANES, LANES), LANES)
            mask = mask_ref[:, at]
            return [jnp.sum(z_ref[f * LANES + comp * half:f * LANES + (comp + 1) * half, at] * mask,
                            axis=0, keepdims=True) for comp in range(2)]

        value = (s_ref[0, pl.ds(t, 1), :], s_ref[1, pl.ds(t, 1), :])
        w = []
        for f in range(9):
            (g1r, g1i), (g2r, g2i) = looked_up(f, 0), looked_up(f, 1)
            w.append(times(value, (g1r * g2r + g1i * g2i, g1i * g2r - g1r * g2i)))
        named = {}
        for names, at in (((OWN, LEFT, RIGHT), 0), ((UP, UL, UR), 1), ((DOWN, DL, DR), 2)):
            x, y = w[3 + at], w[6 + at]
            named[names[0]] = w[at]
            named[names[1]] = tuple(jnp.where(c_odd, p, q) for p, q in zip(x, y))
            named[names[2]] = tuple(jnp.where(c_odd, q, p) for p, q in zip(x, y))

        def weight(f):
            return tuple(jnp.broadcast_to(x, shape) for x in named[f])

        pairs = {}

        def put(ref, first, group, x):
            key = (id(ref), first)
            if group % 2 == 0:
                pairs[key] = x
            else:
                start = first + SUB * (group - 1)
                ref[start:start + 16, lane] = jnp.concatenate([pairs.pop(key), x], 0).astype(BF16)

        rows_w = [weight(f) for f in (UP, DOWN, UL, UR, DL, DR)]
        signs = (-1, 1, -1, -1, 1, 1)
        for g in range(M // SUB):
            at = slice(g * SUB, (g + 1) * SUB)
            cos, sin = ec_ref[at, lane], es_ref[at, lane]
            for n, ((wr, wi), sd) in enumerate(zip(rows_w, signs)):
                put(uc_ref, n * M, g, wr * cos - (sd * wi) * sin)
                put(us_ref, n * M, g, -(sd * wr) * sin - wi * cos)
        edge = (half_c - M) // SUB
        (wr, wi), (lr, li), (rr, ri) = weight(OWN), weight(LEFT), weight(RIGHT)
        for g in range(half_c // SUB):
            at = slice(g * SUB, (g + 1) * SUB)
            cos, sin = fc_ref[at, lane], fs_ref[at, lane]
            own = (cos, sin)
            if g >= edge:
                mine, other = taper_rows(g, half_c)
                own = (cos * mine, sin * mine)
                cos, sin = cos * other, sin * other
                base = 2 * half_c + M
                put(tc_ref, base, g - edge, lr * cos + li * sin)
                put(ts_ref, base, g - edge, lr * sin - li * cos)
                put(tc_ref, base + 2 * M, g - edge, rr * cos - ri * sin)
                put(ts_ref, base + 2 * M, g - edge, -(rr * sin + ri * cos))
            put(tc_ref, 0, g, wr * own[0])
            put(tc_ref, half_c, g, -wi * own[1])
            put(ts_ref, 0, g, -wi * own[0])
            put(ts_ref, half_c, g, -wr * own[1])
        for ref in (tc_ref, ts_ref):
            ref[2 * half_c:2 * half_c + M, lane] = zero
            ref[2 * half_c + 2 * M:2 * half_c + 3 * M, lane] = zero
        return carry

    lax.fori_loop(0, k_tiles, tables, 0)


def finish_kernel(m1_ref, m2_ref, g1_ref, g2_ref, image_ref, out_ref, sems):
    half_r, half_c = R // 2, C // 2
    shape = (SUB, LANES)
    iota = lax.broadcasted_iota(jnp.int32, shape, 0)
    lane_at = lax.broadcasted_iota(jnp.int32, shape, 1)
    back_lane = (LANES - 1) - lane_at
    back_row = (SUB - 1) - iota
    n_lane = half_c // LANES
    edge_c = half_c - M
    edge_r = half_r - M
    col_own, col_other = [], []
    for t in range(n_lane):
        index = (lane_at + t * LANES).astype(F32)
        col_own.append(jnp.minimum((half_c + M - 0.5 - index) * (1.0 / (2 * M)), 1.0))
        col_other.append(jnp.maximum((index - (half_c - M - 0.5)) * (1.0 / (2 * M)), 0.0))

    def flip(x, index, axis):
        return jnp.take_along_axis(x, index, axis=axis, mode="promise_in_bounds")

    def finish(g, edged):
        rows = pl.ds(pl.multiple_of(g * SUB, SUB), SUB)
        for t in range(n_lane):
            def part(ref, which):
                return ref[rows, which * half_c + t * LANES:which * half_c + (t + 1) * LANES]
            p, s_, r, q = part(m1_ref, 0), part(m1_ref, 1), part(m2_ref, 0), part(m2_ref, 1)
            even, odd = p + q, p - q
            plus, minus = r + s_, r - s_
            quad = {(1, 1): even + plus, (-1, -1): even - plus,
                    (1, -1): odd + minus, (-1, 1): odd - minus}
            if (t + 1) * LANES > edge_c:
                base = 2 * half_c
                off = t * LANES - (half_c - LANES)
                for se, start in ((-1, base), (1, base + LANES)):
                    lc = m1_ref[rows, start + off:start + off + LANES]
                    ls = m2_ref[rows, start + off:start + off + LANES]
                    quad[1, se] += lc + ls
                    quad[-1, se] += lc - ls
            if edged:
                def edge(n):
                    at = pl.ds(pl.multiple_of(n * M + g * SUB - edge_r, SUB), SUB)
                    x = g1_ref[at, t * LANES:(t + 1) * LANES]
                    y = g2_ref[at, t * LANES:(t + 1) * LANES]
                    return {1: x + y, -1: x - y}
                for n, sd in ((0, -1), (1, 1)):
                    e = edge(n)
                    for se in (-1, 1):
                        quad[sd, se] += e[se] * col_own[t]
                if (t + 1) * LANES > edge_c:
                    for n, (sd, se) in ((2, (-1, -1)), (3, (-1, 1)), (4, (1, -1)), (5, (1, 1))):
                        quad[sd, se] += edge(n)[se] * col_other[t]
            for (sd, se), x in quad.items():
                if sd < 0:
                    x = flip(x, back_row, 0)
                    at = pl.ds(pl.multiple_of(half_r - SUB - g * SUB, SUB), SUB)
                else:
                    at = pl.ds(pl.multiple_of(half_r + g * SUB, SUB), SUB)
                if se < 0:
                    x = flip(x, back_lane, 1)
                    start = half_c - (t + 1) * LANES
                else:
                    start = half_c + t * LANES
                out_ref[at, start:start + LANES] = x

    group = M // SUB
    n_groups = half_r // M

    def send(j, sign):
        start = pl.multiple_of(half_r + j * M if sign > 0 else half_r - M - j * M, M)
        rows = pl.ds(start, M)
        return pltpu.make_async_copy(out_ref.at[rows, :], image_ref.at[rows, :],
                                     sems.at[2 * j + (sign > 0)])

    def run(j, edged):
        for i in range(group):
            finish(j * group + i, edged)
        send(j, 1).start()
        send(j, -1).start()

    def inner(j, carry):
        run(j, False)
        return carry

    lax.fori_loop(0, n_groups - 1, inner, 0)
    run(n_groups - 1, True)
    for j in range(n_groups):
        send(j, 1).wait()
        send(j, -1).wait()


def swaps(size):
    both = []
    for first in (0, 1):
        pairs = [(i, i + 1) for i in range(first, size - 1, 2)]
        both.append(pairs + [(j, i) for i, j in pairs])
    return both


def shards(vis, station_pairs, visibility_time_slot, station_u_cells, station_v_cells,
           facet_station_gains, holder_device_order):
    n_frow = lax.axis_size("frow")
    n_fcol = lax.axis_size("fcol")
    block = vis.shape[1]
    k_tiles = NBLK * block // LANES
    k = k_tiles * LANES
    half_r, half_c = R // 2, C // 2
    wide = 2 * half_c + 4 * M
    vmem = pl.BlockSpec(memory_space=pltpu.VMEM)
    smem = pl.BlockSpec(memory_space=pltpu.SMEM)

    def lines(x):
        return x.reshape(-1, LANES)

    def shaped(*dims, dtype=F32):
        return jax.ShapeDtypeStruct(dims, dtype)

    def params(mib):
        return pltpu.CompilerParams(vmem_limit_bytes=mib * 1024 * 1024)

    gains = facet_station_gains[0, 0]
    depth = gains.size // LANES
    own = gains.reshape(2, -1, LANES).transpose(1, 0, 2).reshape(depth, LANES)
    packed = pl.pallas_call(
        pack_kernel,
        out_shape=shaped(n_frow * n_fcol, 1, 5 * block),
        name="pack",
    )(vis, station_pairs, visibility_time_slot.reshape(1, block))
    own, packed = lax.optimization_barrier((own, packed))
    row_a, row_b = [lax.ppermute(own, "frow", pairs) for pairs in swaps(n_frow)]
    n_lines = station_u_cells.size // LANES
    labels = jnp.concatenate([
        lines(station_u_cells), lines(station_v_cells),
        lines(jnp.pad(holder_device_order[:NBLK], (0, LANES - NBLK)))], 0)
    blocks = lax.all_to_all(packed, ("frow", "fcol"), 0, 0)
    mid = jnp.stack([own, row_a, row_b])
    col_a, col_b = [lax.ppermute(mid, "fcol", pairs) for pairs in swaps(n_fcol)]
    s, a_cos, a_sin, e_cos, e_sin, f_cos, f_sin, c_cos, c_sin = pl.pallas_call(
        functools.partial(table_kernel, n_frow, n_fcol, n_lines),
        out_shape=[
            shaped(6, k_tiles, LANES),
            shaped(half_r, k, dtype=BF16), shaped(half_r, k, dtype=BF16),
            shaped(M, k), shaped(M, k),
            shaped(half_c, k), shaped(half_c, k),
            shaped(half_c, k, dtype=BF16), shaped(half_c, k, dtype=BF16),
        ],
        in_specs=[smem] + [vmem] * 2,
        out_specs=[vmem] * 9,
        scratch_shapes=[
            pltpu.VMEM((5, k_tiles, LANES), F32),
            pltpu.VMEM((2, k_tiles, LANES), jnp.int32),
            pltpu.VMEM((2, 2, half_r // SUB, LANES), F32),
        ],
        compiler_params=params(24),
        name="tables",
    )(labels, blocks, labels)
    t_cos, t_sin, u_cos, u_sin = pl.pallas_call(
        column_kernel,
        out_shape=[shaped(wide, k, dtype=BF16), shaped(wide, k, dtype=BF16),
                   shaped(6 * M, k, dtype=BF16), shaped(6 * M, k, dtype=BF16)],
        in_specs=[vmem] * 8,
        out_specs=[vmem] * 4,
        scratch_shapes=[
            pltpu.VMEM((2 * depth, 2 * k), BF16),
            pltpu.VMEM((depth // 2, 2 * k), F32),
            pltpu.VMEM((2 * depth, 9 * LANES), BF16),
            pltpu.VMEM((9 * LANES, 2 * k), F32),
        ],
        compiler_params=params(28),
        name="columns",
    )(s, mid, col_a, col_b, e_cos, e_sin, f_cos, f_sin)

    def dot(a, b):
        return lax.dot_general(a, b, (((1,), (1,)), ((), ())), preferred_element_type=F32)

    return pl.pallas_call(
        finish_kernel,
        out_shape=shaped(R, C),
        in_specs=[vmem] * 4,
        out_specs=pl.BlockSpec(memory_space=pl.ANY),
        scratch_shapes=[pltpu.VMEM((R, C), F32), pltpu.SemaphoreType.DMA((half_r // M * 2,))],
        compiler_params=params(24),
        name="finish",
    )(dot(a_cos, t_cos), dot(a_sin, t_sin), dot(u_cos, c_cos), dot(u_sin, c_sin))


def solution(mesh):
    return jax.shard_map(
        shards,
        mesh=mesh,
        in_specs=(
            P(None, ("frow", "fcol")),
            P(None, ("frow", "fcol")),
            P(("frow", "fcol")),
            P(),
            P(),
            P("frow", "fcol", None, None),
            P(),
        ),
        out_specs=P("frow", "fcol"),
        check_vma=False,
    )
```

```python
import functools
import math

import jax
import jax.numpy as jnp
from jax import lax
from jax.experimental import pallas as pl
from jax.experimental.pallas import tpu as pltpu
from jax.sharding import PartitionSpec as P

R = 1024
C = 512
M = 64
NT = 16
NBLK = 4
LANES = 128
SUB = 8
OWN, LEFT, RIGHT, UP, DOWN, UL, UR, DL, DR = range(9)
F32 = jnp.float32
BF16 = jnp.bfloat16


def wrap(m, modulus):
    if modulus & (modulus - 1) == 0:
        return m & (modulus - 1)
    return jnp.remainder(m, modulus)


def turn(m, modulus):
    m = wrap(m, modulus)
    quarter = modulus // 4
    q = (m + modulus // 8) // quarter if quarter & (quarter - 1) else (
        (m + modulus // 8) >> (quarter.bit_length() - 1))
    x = (m - q * quarter).astype(F32) * (2.0 * math.pi / modulus)
    x2 = x * x
    s = x + x * x2 * (-1 / 6 + x2 * (1 / 120 + x2 * (-1 / 5040 + x2 * (1 / 362880))))
    c = 1.0 + x2 * (-0.5 + x2 * (1 / 24 + x2 * (-1 / 720 + x2 * (1 / 40320))))
    odd = (q & 1) == 1
    cos = jnp.where(odd, s, c)
    sin = jnp.where(odd, c, s)
    cos = jnp.where(((q + 1) & 2) != 0, -cos, cos)
    sin = jnp.where((q & 2) != 0, -sin, sin)
    return cos, sin


def times(a, b):
    return a[0] * b[0] - a[1] * b[1], a[0] * b[1] + a[1] * b[0]


def pack_kernel(vis_ref, pair_ref, slot_ref, out_ref):
    block = vis_ref.shape[1]
    lines = [vis_ref[0:1, :], vis_ref[1:2, :], pair_ref[0:1, :].astype(F32),
             pair_ref[1:2, :].astype(F32), slot_ref[...].astype(F32)]
    for copy in range(out_ref.shape[0]):
        for q, line in enumerate(lines):
            out_ref[copy, :, q * block:(q + 1) * block] = line


def pick(row, lane):
    return jnp.take_along_axis(
        jnp.broadcast_to(row, lane.shape), lane, axis=1, mode="promise_in_bounds")


def taper_rows(group, half):
    index = (lax.broadcasted_iota(jnp.int32, (SUB, LANES), 0) + SUB * group).astype(F32)
    return ((half + M - 0.5 - index) * (1.0 / (2 * M)),
            (index - (half - M - 0.5)) * (1.0 / (2 * M)))


def table_kernel(n_frow, n_fcol, n_lines, order_ref, block_ref, cell_ref,
                 s_ref, ac_ref, as_ref, ec_ref, es_ref, fc_ref, fs_ref, cc_ref, cs_ref,
                 q_ref, uv_ref, dr_ref):
    frow_at = lax.axis_index("frow")
    fcol_at = lax.axis_index("fcol")
    half_r, half_c = R // 2, C // 2
    mod_r, mod_c = 2 * R * n_frow, 2 * C * n_fcol
    k_tiles = s_ref.shape[1]
    per_block = k_tiles // NBLK
    block = per_block * LANES
    shape = (SUB, LANES)

    for b in range(NBLK):
        owner = order_ref[2 * n_lines, b]
        for q in range(5):
            for j in range(per_block):
                q_ref[q, b * per_block + j:b * per_block + j + 1, :] = block_ref[
                    owner, :, q * block + j * LANES:q * block + (j + 1) * LANES]
    a1 = q_ref[2].astype(jnp.int32)
    a2 = q_ref[3].astype(jnp.int32)
    slot = q_ref[4].astype(jnp.int32)

    def cells(table):
        got = [jnp.zeros(shape, jnp.int32)] * 2
        for h in range(table.shape[0]):
            row = table[h:h + 1, :]
            got = [jnp.where((a >> 7) == h, pick(row, a & 127), g)
                   for a, g in zip((a1, a2), got)]
        return got[0] - got[1]

    u = cells(cell_ref[:n_lines, :])
    v = cells(cell_ref[n_lines:2 * n_lines, :])
    uv_ref[0] = u
    uv_ref[1] = v
    centre = times(turn(u * (frow_at * (2 * R) + (R - 1)), mod_r),
                   turn(v * (fcol_at * (2 * C) + (C - 1)), mod_c))
    scale = 0.5 / math.sqrt(NBLK * per_block * LANES)
    value = times((q_ref[0] * scale, q_ref[1] * scale), centre)
    s_ref[0] = value[0]
    s_ref[1] = value[1]
    for n, a in enumerate((a1, a2)):
        s_ref[2 + n] = ((a >> 3) + (a & 4) * 16).astype(F32)
        s_ref[4 + n] = ((a & 3) * NT + slot).astype(F32)

    iota = lax.broadcasted_iota(jnp.int32, shape, 0)

    def tables(s, carry):
        lane = pl.ds(pl.multiple_of(s * LANES, LANES), LANES)

        def phases(which, modulus, half):
            freq = jnp.broadcast_to(uv_ref[which, pl.ds(s, 1), :], shape)
            fine = turn(freq * (2 * iota + 1), modulus)
            middle = turn(freq * (16 * iota), modulus)
            coarse = turn(freq * (128 * iota), modulus)
            for a in range(half // 64):
                top = tuple(jnp.broadcast_to(x[a:a + 1], shape) for x in coarse)
                both = times(middle, top)
                for comp in range(2):
                    dr_ref[which, comp, 8 * a:8 * a + 8, :] = both[comp]
            for g in range(half // SUB):
                step = tuple(jnp.broadcast_to(dr_ref[which, comp, g:g + 1, :], shape)
                             for comp in range(2))
                yield times(fine, step)

        pairs = {}

        def put(ref, first, group, x):
            key = (id(ref), first)
            if group % 2 == 0:
                pairs[key] = x
            else:
                start = first + SUB * (group - 1)
                ref[start:start + 16, lane] = jnp.concatenate([pairs.pop(key), x], 0).astype(BF16)

        edge = (half_r - M) // SUB
        for g, (cos, sin) in enumerate(phases(0, mod_r, half_r)):
            if g >= edge:
                mine, other = taper_rows(g, half_r)
                at = slice((g - edge) * SUB, (g - edge + 1) * SUB)
                ec_ref[at, lane] = cos * other
                es_ref[at, lane] = sin * other
                cos, sin = cos * mine, sin * mine
            put(ac_ref, 0, g, cos)
            put(as_ref, 0, g, sin)
        for g, (cos, sin) in enumerate(phases(1, mod_c, half_c)):
            put(cc_ref, 0, g, cos)
            put(cs_ref, 0, g, sin)
            at = slice(g * SUB, (g + 1) * SUB)
            fc_ref[at, lane] = cos
            fs_ref[at, lane] = sin
        return carry

    lax.fori_loop(0, k_tiles, tables, 0)


def column_kernel(n_frow, s_ref, far_ref, a_ref, b_ref, ec_ref, es_ref, fc_ref, fs_ref,
                  tc_ref, ts_ref, uc_ref, us_ref, hot_ref, mask_ref, gain_ref, z_ref, mid_ref, sem):
    copy = pltpu.make_async_copy(far_ref, mid_ref, sem)
    copy.start()
    frow_at = lax.axis_index("frow")
    c_odd = lax.rem(lax.axis_index("fcol"), 2) == 1
    above = jnp.maximum(frow_at - 1, 0)
    below = jnp.minimum(frow_at + 1, n_frow - 1)
    has = (1.0, (frow_at > 0).astype(F32), (frow_at < n_frow - 1).astype(F32))
    k_tiles = s_ref.shape[1]
    depth = mid_ref.shape[1]
    half = depth // 2
    places = [(ref, row) for ref in (mid_ref, a_ref, b_ref) for row in (frow_at, above, below)]

    line_at = lax.broadcasted_iota(jnp.int32, (depth, LANES), 0).astype(F32)
    place_at = line_at[:half]
    for n in range(2):
        for t in range(k_tiles):
            lane = slice((n * k_tiles + t) * LANES, (n * k_tiles + t + 1) * LANES)
            hot = jnp.where(line_at == s_ref[2 + n, t:t + 1, :], 1.0, 0.0).astype(BF16)
            hot_ref[:depth, lane] = hot
            hot_ref[depth:, lane] = hot
            mask_ref[:, lane] = jnp.where(place_at == s_ref[4 + n, t:t + 1, :], 1.0, 0.0)

    copy.wait()
    low_lane = lax.broadcasted_iota(jnp.int32, (half, LANES), 1) < LANES // 2
    for f, (ref, row) in enumerate(places):
        re = ref[row, pl.ds(0, half, stride=2), :]
        im = ref[row, pl.ds(1, half, stride=2), :]
        top = jnp.where(low_lane, re, pltpu.roll(im, LANES // 2, 1))
        low = jnp.where(low_lane, pltpu.roll(re, LANES // 2, 1), im)
        both = jnp.concatenate([top, low], 0).T
        first = both.astype(BF16)
        gain_ref[f * LANES:(f + 1) * LANES, :depth] = first
        gain_ref[f * LANES:(f + 1) * LANES, depth:] = (both - first.astype(F32)).astype(BF16)

    z_ref[...] = lax.dot_general(gain_ref[...], hot_ref[...], (((1,), (0,)), ((), ())),
                                 preferred_element_type=F32)

    half_c = C // 2
    shape = (SUB, LANES)
    zero = jnp.zeros((M, LANES), BF16)

    def tables(t, carry):
        lane = pl.ds(pl.multiple_of(t * LANES, LANES), LANES)

        def looked_up(f, n):
            at = pl.ds(pl.multiple_of((n * k_tiles + t) * LANES, LANES), LANES)
            mask = mask_ref[:, at]
            return [jnp.sum(z_ref[f * LANES + comp * half:f * LANES + (comp + 1) * half, at] * mask,
                            axis=0, keepdims=True) for comp in range(2)]

        value = (s_ref[0, pl.ds(t, 1), :], s_ref[1, pl.ds(t, 1), :])
        w = []
        for f in range(9):
            (g1r, g1i), (g2r, g2i) = looked_up(f, 0), looked_up(f, 1)
            w.append(times(value, (g1r * g2r + g1i * g2i, g1i * g2r - g1r * g2i)))
        named = {}
        for names, at in (((OWN, LEFT, RIGHT), 0), ((UP, UL, UR), 1), ((DOWN, DL, DR), 2)):
            x, y = w[3 + at], w[6 + at]
            named[names[0]] = tuple(p * has[at] for p in w[at])
            named[names[1]] = tuple(jnp.where(c_odd, p, q) * has[at] for p, q in zip(x, y))
            named[names[2]] = tuple(jnp.where(c_odd, q, p) * has[at] for p, q in zip(x, y))

        def weight(f):
            return tuple(jnp.broadcast_to(x, shape) for x in named[f])

        pairs = {}

        def put(ref, first, group, x):
            key = (id(ref), first)
            if group % 2 == 0:
                pairs[key] = x
            else:
                start = first + SUB * (group - 1)
                ref[start:start + 16, lane] = jnp.concatenate([pairs.pop(key), x], 0).astype(BF16)

        rows_w = [weight(f) for f in (UP, DOWN, UL, UR, DL, DR)]
        signs = (-1, 1, -1, -1, 1, 1)
        for g in range(M // SUB):
            at = slice(g * SUB, (g + 1) * SUB)
            cos, sin = ec_ref[at, lane], es_ref[at, lane]
            for n, ((wr, wi), sd) in enumerate(zip(rows_w, signs)):
                put(uc_ref, n * M, g, wr * cos - (sd * wi) * sin)
                put(us_ref, n * M, g, -(sd * wr) * sin - wi * cos)
        edge = (half_c - M) // SUB
        (wr, wi), (lr, li), (rr, ri) = weight(OWN), weight(LEFT), weight(RIGHT)
        for g in range(half_c // SUB):
            at = slice(g * SUB, (g + 1) * SUB)
            cos, sin = fc_ref[at, lane], fs_ref[at, lane]
            own = (cos, sin)
            if g >= edge:
                mine, other = taper_rows(g, half_c)
                own = (cos * mine, sin * mine)
                cos, sin = cos * other, sin * other
                base = 2 * half_c + M
                put(tc_ref, base, g - edge, lr * cos + li * sin)
                put(ts_ref, base, g - edge, lr * sin - li * cos)
                put(tc_ref, base + 2 * M, g - edge, rr * cos - ri * sin)
                put(ts_ref, base + 2 * M, g - edge, -(rr * sin + ri * cos))
            put(tc_ref, 0, g, wr * own[0])
            put(tc_ref, half_c, g, -wi * own[1])
            put(ts_ref, 0, g, -wi * own[0])
            put(ts_ref, half_c, g, -wr * own[1])
        for ref in (tc_ref, ts_ref):
            ref[2 * half_c:2 * half_c + M, lane] = zero
            ref[2 * half_c + 2 * M:2 * half_c + 3 * M, lane] = zero
        return carry

    lax.fori_loop(0, k_tiles, tables, 0)


def finish_kernel(m1_ref, m2_ref, g1_ref, g2_ref, image_ref, out_ref, sems):
    half_r, half_c = R // 2, C // 2
    shape = (SUB, LANES)
    iota = lax.broadcasted_iota(jnp.int32, shape, 0)
    lane_at = lax.broadcasted_iota(jnp.int32, shape, 1)
    back_lane = (LANES - 1) - lane_at
    back_row = (SUB - 1) - iota
    n_lane = half_c // LANES
    edge_c = half_c - M
    edge_r = half_r - M
    col_own, col_other = [], []
    for t in range(n_lane):
        index = (lane_at + t * LANES).astype(F32)
        col_own.append(jnp.minimum((half_c + M - 0.5 - index) * (1.0 / (2 * M)), 1.0))
        col_other.append(jnp.maximum((index - (half_c - M - 0.5)) * (1.0 / (2 * M)), 0.0))

    def flip(x, index, axis):
        return jnp.take_along_axis(x, index, axis=axis, mode="promise_in_bounds")

    def finish(g, edged):
        rows = pl.ds(pl.multiple_of(g * SUB, SUB), SUB)
        for t in range(n_lane):
            def part(ref, which):
                return ref[rows, which * half_c + t * LANES:which * half_c + (t + 1) * LANES]
            p, s_, r, q = part(m1_ref, 0), part(m1_ref, 1), part(m2_ref, 0), part(m2_ref, 1)
            even, odd = p + q, p - q
            plus, minus = r + s_, r - s_
            quad = {(1, 1): even + plus, (-1, -1): even - plus,
                    (1, -1): odd + minus, (-1, 1): odd - minus}
            if (t + 1) * LANES > edge_c:
                base = 2 * half_c
                off = t * LANES - (half_c - LANES)
                for se, start in ((-1, base), (1, base + LANES)):
                    lc = m1_ref[rows, start + off:start + off + LANES]
                    ls = m2_ref[rows, start + off:start + off + LANES]
                    quad[1, se] += lc + ls
                    quad[-1, se] += lc - ls
            if edged:
                def edge(n):
                    at = pl.ds(pl.multiple_of(n * M + g * SUB - edge_r, SUB), SUB)
                    x = g1_ref[at, t * LANES:(t + 1) * LANES]
                    y = g2_ref[at, t * LANES:(t + 1) * LANES]
                    return {1: x + y, -1: x - y}
                for n, sd in ((0, -1), (1, 1)):
                    e = edge(n)
                    for se in (-1, 1):
                        quad[sd, se] += e[se] * col_own[t]
                if (t + 1) * LANES > edge_c:
                    for n, (sd, se) in ((2, (-1, -1)), (3, (-1, 1)), (4, (1, -1)), (5, (1, 1))):
                        quad[sd, se] += edge(n)[se] * col_other[t]
            for (sd, se), x in quad.items():
                if sd < 0:
                    x = flip(x, back_row, 0)
                    at = pl.ds(pl.multiple_of(half_r - SUB - g * SUB, SUB), SUB)
                else:
                    at = pl.ds(pl.multiple_of(half_r + g * SUB, SUB), SUB)
                if se < 0:
                    x = flip(x, back_lane, 1)
                    start = half_c - (t + 1) * LANES
                else:
                    start = half_c + t * LANES
                out_ref[at, start:start + LANES] = x

    group = M // SUB
    n_groups = half_r // M

    def send(j, sign):
        start = pl.multiple_of(half_r + j * M if sign > 0 else half_r - M - j * M, M)
        rows = pl.ds(start, M)
        return pltpu.make_async_copy(out_ref.at[rows, :], image_ref.at[rows, :],
                                     sems.at[2 * j + (sign > 0)])

    def run(j, edged):
        for i in range(group):
            finish(j * group + i, edged)
        send(j, 1).start()
        send(j, -1).start()

    def inner(j, carry):
        run(j, False)
        return carry

    lax.fori_loop(0, n_groups - 1, inner, 0)
    run(n_groups - 1, True)
    for j in range(n_groups):
        send(j, 1).wait()
        send(j, -1).wait()


def swaps(size):
    both = []
    for first in (0, 1):
        pairs = [(i, i + 1) for i in range(first, size - 1, 2)]
        both.append(pairs + [(j, i) for i, j in pairs])
    return both


def shards(vis, station_pairs, visibility_time_slot, station_u_cells, station_v_cells,
           facet_station_gains, holder_device_order):
    n_frow = lax.axis_size("frow")
    n_fcol = lax.axis_size("fcol")
    block = vis.shape[1]
    k_tiles = NBLK * block // LANES
    k = k_tiles * LANES
    half_r, half_c = R // 2, C // 2
    wide = 2 * half_c + 4 * M
    vmem = pl.BlockSpec(memory_space=pltpu.VMEM)
    smem = pl.BlockSpec(memory_space=pltpu.SMEM)
    hbm = pl.BlockSpec(memory_space=pltpu.HBM)

    def lines(x):
        return x.reshape(-1, LANES)

    def shaped(*dims, dtype=F32):
        return jax.ShapeDtypeStruct(dims, dtype)

    def params(mib):
        return pltpu.CompilerParams(vmem_limit_bytes=mib * 1024 * 1024)

    gains = facet_station_gains[0, 0]
    depth = gains.size // LANES
    own = gains.reshape(2, -1, LANES).transpose(1, 0, 2).reshape(depth, LANES)
    mid = lax.all_gather(own, "frow")
    packed = pl.pallas_call(
        pack_kernel,
        out_shape=shaped(n_frow * n_fcol, 1, 5 * block),
        name="pack",
    )(vis, station_pairs, visibility_time_slot.reshape(1, block))
    blocks = lax.all_to_all(packed, ("frow", "fcol"), 0, 0)
    n_lines = station_u_cells.size // LANES
    labels = jnp.concatenate([
        lines(station_u_cells), lines(station_v_cells),
        lines(jnp.pad(holder_device_order[:NBLK], (0, LANES - NBLK)))], 0)
    col_a, col_b = [lax.ppermute(mid, "fcol", pairs) for pairs in swaps(n_fcol)]
    s, a_cos, a_sin, e_cos, e_sin, f_cos, f_sin, c_cos, c_sin = pl.pallas_call(
        functools.partial(table_kernel, n_frow, n_fcol, n_lines),
        out_shape=[
            shaped(6, k_tiles, LANES),
            shaped(half_r, k, dtype=BF16), shaped(half_r, k, dtype=BF16),
            shaped(M, k), shaped(M, k),
            shaped(half_c, k), shaped(half_c, k),
            shaped(half_c, k, dtype=BF16), shaped(half_c, k, dtype=BF16),
        ],
        in_specs=[smem, vmem, vmem],
        out_specs=[vmem] * 9,
        scratch_shapes=[
            pltpu.VMEM((5, k_tiles, LANES), F32),
            pltpu.VMEM((2, k_tiles, LANES), jnp.int32),
            pltpu.VMEM((2, 2, half_r // SUB, LANES), F32),
        ],
        compiler_params=params(24),
        name="tables",
    )(labels, blocks, labels)
    t_cos, t_sin, u_cos, u_sin = pl.pallas_call(
        functools.partial(column_kernel, n_frow),
        out_shape=[shaped(wide, k, dtype=BF16), shaped(wide, k, dtype=BF16),
                   shaped(6 * M, k, dtype=BF16), shaped(6 * M, k, dtype=BF16)],
        in_specs=[vmem, hbm] + [vmem] * 6,
        out_specs=[vmem] * 4,
        scratch_shapes=[
            pltpu.VMEM((2 * depth, 2 * k), BF16),
            pltpu.VMEM((depth // 2, 2 * k), F32),
            pltpu.VMEM((9 * LANES, 2 * depth), BF16),
            pltpu.VMEM((9 * LANES, 2 * k), F32),
            pltpu.VMEM(mid.shape, F32),
            pltpu.SemaphoreType.DMA,
        ],
        compiler_params=params(28),
        name="columns",
    )(s, mid, col_a, col_b, e_cos, e_sin, f_cos, f_sin)

    def dot(a, b):
        return lax.dot_general(a, b, (((1,), (1,)), ((), ())), preferred_element_type=F32)

    return pl.pallas_call(
        finish_kernel,
        out_shape=shaped(R, C),
        in_specs=[vmem] * 4,
        out_specs=pl.BlockSpec(memory_space=pl.ANY),
        scratch_shapes=[pltpu.VMEM((R, C), F32), pltpu.SemaphoreType.DMA((half_r // M * 2,))],
        compiler_params=params(24),
        name="finish",
    )(dot(a_cos, t_cos), dot(a_sin, t_sin), dot(u_cos, c_cos), dot(u_sin, c_sin))


def solution(mesh):
    return jax.shard_map(
        shards,
        mesh=mesh,
        in_specs=(
            P(None, ("frow", "fcol")),
            P(None, ("frow", "fcol")),
            P(("frow", "fcol")),
            P(),
            P(),
            P("frow", "fcol", None, None),
            P(),
        ),
        out_specs=P("frow", "fcol"),
        check_vma=False,
    )
```

```python
import functools
import math

import jax
import jax.numpy as jnp
from jax import lax
from jax.experimental import pallas as pl
from jax.experimental.pallas import tpu as pltpu
from jax.sharding import PartitionSpec as P

R = 1024
C = 512
M = 64
NT = 16
NBLK = 4
LANES = 128
SUB = 8
OWN, LEFT, RIGHT, UP, DOWN, UL, UR, DL, DR = range(9)
F32 = jnp.float32
BF16 = jnp.bfloat16


def wrap(m, modulus):
    if modulus & (modulus - 1) == 0:
        return m & (modulus - 1)
    return jnp.remainder(m, modulus)


def turn(m, modulus):
    m = wrap(m, modulus)
    quarter = modulus // 4
    q = (m + modulus // 8) // quarter if quarter & (quarter - 1) else (
        (m + modulus // 8) >> (quarter.bit_length() - 1))
    x = (m - q * quarter).astype(F32) * (2.0 * math.pi / modulus)
    x2 = x * x
    s = x + x * x2 * (-1 / 6 + x2 * (1 / 120 + x2 * (-1 / 5040 + x2 * (1 / 362880))))
    c = 1.0 + x2 * (-0.5 + x2 * (1 / 24 + x2 * (-1 / 720 + x2 * (1 / 40320))))
    odd = (q & 1) == 1
    cos = jnp.where(odd, s, c)
    sin = jnp.where(odd, c, s)
    cos = jnp.where(((q + 1) & 2) != 0, -cos, cos)
    sin = jnp.where((q & 2) != 0, -sin, sin)
    return cos, sin


def times(a, b):
    return a[0] * b[0] - a[1] * b[1], a[0] * b[1] + a[1] * b[0]


def pack_kernel(vis_ref, pair_ref, slot_ref, out_ref):
    block = vis_ref.shape[1]
    lines = [vis_ref[0:1, :], vis_ref[1:2, :], pair_ref[0:1, :].astype(F32),
             pair_ref[1:2, :].astype(F32), slot_ref[...].astype(F32)]
    for copy in range(out_ref.shape[0]):
        for q, line in enumerate(lines):
            out_ref[copy, :, q * block:(q + 1) * block] = line


def pick(row, lane):
    return jnp.take_along_axis(
        jnp.broadcast_to(row, lane.shape), lane, axis=1, mode="promise_in_bounds")


def taper_rows(group, half, wide=LANES):
    index = (lax.broadcasted_iota(jnp.int32, (SUB, wide), 0) + SUB * group).astype(F32)
    return ((half + M - 0.5 - index) * (1.0 / (2 * M)),
            (index - (half - M - 0.5)) * (1.0 / (2 * M)))


def table_kernel(n_frow, n_fcol, n_lines, order_ref, block_ref, cell_ref,
                 s_ref, ac_ref, as_ref, ec_ref, es_ref, fc_ref, fs_ref, cc_ref, cs_ref,
                 q_ref, uv_ref, dr_ref):
    frow_at = lax.axis_index("frow")
    fcol_at = lax.axis_index("fcol")
    half_r, half_c = R // 2, C // 2
    mod_r, mod_c = 2 * R * n_frow, 2 * C * n_fcol
    k_tiles = s_ref.shape[1]
    per_block = k_tiles // NBLK
    block = per_block * LANES
    shape = (SUB, LANES)

    for b in range(NBLK):
        owner = order_ref[2 * n_lines, b]
        for q in range(5):
            for j in range(per_block):
                q_ref[q, b * per_block + j:b * per_block + j + 1, :] = block_ref[
                    owner, :, q * block + j * LANES:q * block + (j + 1) * LANES]
    a1 = q_ref[2].astype(jnp.int32)
    a2 = q_ref[3].astype(jnp.int32)
    slot = q_ref[4].astype(jnp.int32)

    def cells(table):
        got = [jnp.zeros(shape, jnp.int32)] * 2
        for h in range(table.shape[0]):
            row = table[h:h + 1, :]
            got = [jnp.where((a >> 7) == h, pick(row, a & 127), g)
                   for a, g in zip((a1, a2), got)]
        return got[0] - got[1]

    u = cells(cell_ref[:n_lines, :])
    v = cells(cell_ref[n_lines:2 * n_lines, :])
    uv_ref[0] = u
    uv_ref[1] = v
    centre = times(turn(u * (frow_at * (2 * R) + (R - 1)), mod_r),
                   turn(v * (fcol_at * (2 * C) + (C - 1)), mod_c))
    scale = 0.5 / math.sqrt(NBLK * per_block * LANES)
    value = times((q_ref[0] * scale, q_ref[1] * scale), centre)
    s_ref[0] = value[0]
    s_ref[1] = value[1]
    for n, a in enumerate((a1, a2)):
        s_ref[2 + n] = ((a >> 3) + (a & 4) * 16).astype(F32)
        s_ref[4 + n] = ((a & 3) * NT + slot).astype(F32)

    iota = lax.broadcasted_iota(jnp.int32, shape, 0)

    def tables(s, carry):
        lane = pl.ds(pl.multiple_of(s * LANES, LANES), LANES)

        def phases(which, modulus, half):
            freq = jnp.broadcast_to(uv_ref[which, pl.ds(s, 1), :], shape)
            fine = turn(freq * (2 * iota + 1), modulus)
            middle = turn(freq * (16 * iota), modulus)
            coarse = turn(freq * (128 * iota), modulus)
            for a in range(half // 64):
                top = tuple(jnp.broadcast_to(x[a:a + 1], shape) for x in coarse)
                both = times(middle, top)
                for comp in range(2):
                    dr_ref[which, comp, 8 * a:8 * a + 8, :] = both[comp]
            for g in range(half // SUB):
                step = tuple(jnp.broadcast_to(dr_ref[which, comp, g:g + 1, :], shape)
                             for comp in range(2))
                yield times(fine, step)

        pairs = {}

        def put(ref, first, group, x):
            key = (id(ref), first)
            if group % 2 == 0:
                pairs[key] = x
            else:
                start = first + SUB * (group - 1)
                ref[start:start + 16, lane] = jnp.concatenate([pairs.pop(key), x], 0).astype(BF16)

        edge = (half_r - M) // SUB
        for g, (cos, sin) in enumerate(phases(0, mod_r, half_r)):
            if g >= edge:
                mine, other = taper_rows(g, half_r)
                at = slice((g - edge) * SUB, (g - edge + 1) * SUB)
                ec_ref[at, lane] = cos * other
                es_ref[at, lane] = sin * other
                cos, sin = cos * mine, sin * mine
            put(ac_ref, 0, g, cos)
            put(as_ref, 0, g, sin)
        for g, (cos, sin) in enumerate(phases(1, mod_c, half_c)):
            put(cc_ref, 0, g, cos)
            put(cs_ref, 0, g, sin)
            at = slice(g * SUB, (g + 1) * SUB)
            fc_ref[at, lane] = cos
            fs_ref[at, lane] = sin
        return carry

    lax.fori_loop(0, k_tiles, tables, 0)


def column_kernel(s_ref, *refs):
    gain_refs, refs = refs[:9], refs[9:]
    ec_ref, es_ref, fc_ref, fs_ref, tc_ref, ts_ref, uc_ref, us_ref, gain_ref = refs
    r_odd = lax.rem(lax.axis_index("frow"), 2) == 1
    c_odd = lax.rem(lax.axis_index("fcol"), 2) == 1
    k_tiles = s_ref.shape[1]
    depth = gain_refs[0].shape[0]
    half = depth // 2
    half_c = C // 2

    low_lane = lax.broadcasted_iota(jnp.int32, (half, LANES), 1) < LANES // 2
    for f, ref in enumerate(gain_refs):
        re = ref[pl.ds(0, half, stride=2), :]
        im = ref[pl.ds(1, half, stride=2), :]
        top = jnp.where(low_lane, re, pltpu.roll(im, LANES // 2, 1))
        low = jnp.where(low_lane, pltpu.roll(re, LANES // 2, 1), im)
        both = jnp.concatenate([top, low], 0).T
        first = both.astype(BF16)
        gain_ref[f * LANES:(f + 1) * LANES, :depth] = first
        gain_ref[f * LANES:(f + 1) * LANES, depth:] = (both - first.astype(F32)).astype(BF16)

    step = 2 if k_tiles % 2 == 0 else 1
    wide = step * LANES
    shape = (SUB, wide)
    line_at = lax.broadcasted_iota(jnp.int32, (depth, wide), 0).astype(F32)
    place_at = line_at[:half]
    zero = jnp.zeros((M, wide), BF16)
    for p in range(k_tiles // step):
        lane = slice(p * wide, (p + 1) * wide)

        def line(q):
            return jnp.concatenate([s_ref[q, p * step + i:p * step + i + 1, :]
                                    for i in range(step)], 1)

        gains = []
        for n in range(2):
            hot = jnp.where(line_at == line(2 + n), 1.0, 0.0).astype(BF16)
            z = jnp.dot(gain_ref[...], jnp.concatenate([hot, hot], 0),
                        preferred_element_type=F32)
            mask = jnp.where(place_at == line(4 + n), 1.0, 0.0)
            gains.append([[jnp.sum(z[f * LANES + comp * half:f * LANES + (comp + 1) * half] * mask,
                                   axis=0, keepdims=True) for comp in range(2)]
                          for f in range(9)])
        value = (line(0), line(1))
        w = []
        for f in range(9):
            (g1r, g1i), (g2r, g2i) = gains[0][f], gains[1][f]
            w.append(times(value, (g1r * g2r + g1i * g2i, g1i * g2r - g1r * g2i)))

        def pick_two(odd, x, y):
            return (tuple(jnp.where(odd, i, j) for i, j in zip(x, y)),
                    tuple(jnp.where(odd, j, i) for i, j in zip(x, y)))

        columns = []
        for c in range(3):
            up, down = pick_two(r_odd, w[3 * c + 1], w[3 * c + 2])
            columns.append((w[3 * c], up, down))
        named = {}
        for r, names in enumerate(((OWN, LEFT, RIGHT), (UP, UL, UR), (DOWN, DL, DR))):
            named[names[0]] = columns[0][r]
            named[names[1]], named[names[2]] = pick_two(c_odd, columns[1][r], columns[2][r])

        def weight(f):
            return tuple(jnp.broadcast_to(x, shape) for x in named[f])

        pairs = {}

        def put(ref, first, group, x):
            key = (id(ref), first)
            if group % 2 == 0:
                pairs[key] = x
            else:
                start = first + SUB * (group - 1)
                ref[start:start + 16, lane] = jnp.concatenate([pairs.pop(key), x], 0).astype(BF16)

        edge = (half_c - M) // SUB
        (wr, wi), (lr, li), (rr, ri) = weight(OWN), weight(LEFT), weight(RIGHT)
        for g in range(half_c // SUB):
            at = slice(g * SUB, (g + 1) * SUB)
            cos, sin = fc_ref[at, lane], fs_ref[at, lane]
            own = (cos, sin)
            if g >= edge:
                mine, other = taper_rows(g, half_c, wide)
                own = (cos * mine, sin * mine)
                cos, sin = cos * other, sin * other
                base = 2 * half_c + M
                put(tc_ref, base, g - edge, lr * cos + li * sin)
                put(ts_ref, base, g - edge, lr * sin - li * cos)
                put(tc_ref, base + 2 * M, g - edge, rr * cos - ri * sin)
                put(ts_ref, base + 2 * M, g - edge, -(rr * sin + ri * cos))
            put(tc_ref, 0, g, wr * own[0])
            put(tc_ref, half_c, g, -wi * own[1])
            put(ts_ref, 0, g, -wi * own[0])
            put(ts_ref, half_c, g, -wr * own[1])
        for ref in (tc_ref, ts_ref):
            ref[2 * half_c:2 * half_c + M, lane] = zero
            ref[2 * half_c + 2 * M:2 * half_c + 3 * M, lane] = zero
        rows_w = [weight(f) for f in (UP, DOWN, UL, UR, DL, DR)]
        signs = (-1, 1, -1, -1, 1, 1)
        for g in range(M // SUB):
            at = slice(g * SUB, (g + 1) * SUB)
            cos, sin = ec_ref[at, lane], es_ref[at, lane]
            for n, ((wr, wi), sd) in enumerate(zip(rows_w, signs)):
                put(uc_ref, n * M, g, wr * cos - (sd * wi) * sin)
                put(us_ref, n * M, g, -(sd * wr) * sin - wi * cos)


def finish_kernel(m1_ref, m2_ref, g1_ref, g2_ref, image_ref, out_ref, sems):
    half_r, half_c = R // 2, C // 2
    shape = (SUB, LANES)
    iota = lax.broadcasted_iota(jnp.int32, shape, 0)
    lane_at = lax.broadcasted_iota(jnp.int32, shape, 1)
    back_lane = (LANES - 1) - lane_at
    back_row = (SUB - 1) - iota
    n_lane = half_c // LANES
    edge_c = half_c - M
    edge_r = half_r - M
    col_own, col_other = [], []
    for t in range(n_lane):
        index = (lane_at + t * LANES).astype(F32)
        col_own.append(jnp.minimum((half_c + M - 0.5 - index) * (1.0 / (2 * M)), 1.0))
        col_other.append(jnp.maximum((index - (half_c - M - 0.5)) * (1.0 / (2 * M)), 0.0))

    def flip(x, index, axis):
        return jnp.take_along_axis(x, index, axis=axis, mode="promise_in_bounds")

    def finish(g, edged):
        rows = pl.ds(pl.multiple_of(g * SUB, SUB), SUB)
        for t in range(n_lane):
            def part(ref, which):
                return ref[rows, which * half_c + t * LANES:which * half_c + (t + 1) * LANES]
            p, s_, r, q = part(m1_ref, 0), part(m1_ref, 1), part(m2_ref, 0), part(m2_ref, 1)
            even, odd = p + q, p - q
            plus, minus = r + s_, r - s_
            quad = {(1, 1): even + plus, (-1, -1): even - plus,
                    (1, -1): odd + minus, (-1, 1): odd - minus}
            if (t + 1) * LANES > edge_c:
                base = 2 * half_c
                off = t * LANES - (half_c - LANES)
                for se, start in ((-1, base), (1, base + LANES)):
                    lc = m1_ref[rows, start + off:start + off + LANES]
                    ls = m2_ref[rows, start + off:start + off + LANES]
                    quad[1, se] += lc + ls
                    quad[-1, se] += lc - ls
            if edged:
                def edge(n):
                    at = pl.ds(pl.multiple_of(n * M + g * SUB - edge_r, SUB), SUB)
                    x = g1_ref[at, t * LANES:(t + 1) * LANES]
                    y = g2_ref[at, t * LANES:(t + 1) * LANES]
                    return {1: x + y, -1: x - y}
                for n, sd in ((0, -1), (1, 1)):
                    e = edge(n)
                    for se in (-1, 1):
                        quad[sd, se] += e[se] * col_own[t]
                if (t + 1) * LANES > edge_c:
                    for n, (sd, se) in ((2, (-1, -1)), (3, (-1, 1)), (4, (1, -1)), (5, (1, 1))):
                        quad[sd, se] += edge(n)[se] * col_other[t]
            for (sd, se), x in quad.items():
                if sd < 0:
                    x = flip(x, back_row, 0)
                    at = pl.ds(pl.multiple_of(half_r - SUB - g * SUB, SUB), SUB)
                else:
                    at = pl.ds(pl.multiple_of(half_r + g * SUB, SUB), SUB)
                if se < 0:
                    x = flip(x, back_lane, 1)
                    start = half_c - (t + 1) * LANES
                else:
                    start = half_c + t * LANES
                out_ref[at, start:start + LANES] = x

    group = M // SUB
    n_groups = half_r // M

    def send(j, sign):
        start = pl.multiple_of(half_r + j * M if sign > 0 else half_r - M - j * M, M)
        rows = pl.ds(start, M)
        return pltpu.make_async_copy(out_ref.at[rows, :], image_ref.at[rows, :],
                                     sems.at[2 * j + (sign > 0)])

    def run(j, edged):
        for i in range(group):
            finish(j * group + i, edged)
        send(j, 1).start()
        send(j, -1).start()

    def inner(j, carry):
        run(j, False)
        return carry

    lax.fori_loop(0, n_groups - 1, inner, 0)
    run(n_groups - 1, True)
    for j in range(n_groups):
        send(j, 1).wait()
        send(j, -1).wait()


def swaps(size):
    both = []
    for first in (0, 1):
        pairs = [(i, i + 1) for i in range(first, size - 1, 2)]
        both.append(pairs + [(j, i) for i, j in pairs])
    return both


def shards(vis, station_pairs, visibility_time_slot, station_u_cells, station_v_cells,
           facet_station_gains, holder_device_order):
    n_frow = lax.axis_size("frow")
    n_fcol = lax.axis_size("fcol")
    block = vis.shape[1]
    k_tiles = NBLK * block // LANES
    k = k_tiles * LANES
    half_r, half_c = R // 2, C // 2
    wide = 2 * half_c + 4 * M
    vmem = pl.BlockSpec(memory_space=pltpu.VMEM)
    smem = pl.BlockSpec(memory_space=pltpu.SMEM)

    def lines(x):
        return x.reshape(-1, LANES)

    def shaped(*dims, dtype=F32):
        return jax.ShapeDtypeStruct(dims, dtype)

    def params(mib):
        return pltpu.CompilerParams(vmem_limit_bytes=mib * 1024 * 1024)

    packed = pl.pallas_call(
        pack_kernel,
        out_shape=shaped(n_frow * n_fcol, 1, 5 * block),
        name="pack",
    )(vis, station_pairs, visibility_time_slot.reshape(1, block))
    n_lines = station_u_cells.size // LANES
    station_u_cells, _ = lax.optimization_barrier((station_u_cells, packed))
    labels = jnp.concatenate([
        lines(station_u_cells), lines(station_v_cells),
        lines(jnp.pad(holder_device_order[:NBLK], (0, LANES - NBLK)))], 0)
    blocks = lax.all_to_all(packed, ("frow", "fcol"), 0, 0)
    facet_station_gains, labels = lax.optimization_barrier((facet_station_gains, labels))
    gains = facet_station_gains[0, 0]
    depth = gains.size // LANES
    own = gains.reshape(2, -1, LANES).transpose(1, 0, 2).reshape(depth, LANES)
    around = []
    for cols in [None] + swaps(n_fcol):
        for rows in [None] + swaps(n_frow):
            pairs = [(i * n_fcol + k, j * n_fcol + l)
                     for i, j in rows or [(r, r) for r in range(n_frow)]
                     for k, l in cols or [(c, c) for c in range(n_fcol)]]
            around.append(own if rows is None and cols is None else
                          lax.ppermute(own, ("frow", "fcol"), pairs))
    s, a_cos, a_sin, e_cos, e_sin, f_cos, f_sin, c_cos, c_sin = pl.pallas_call(
        functools.partial(table_kernel, n_frow, n_fcol, n_lines),
        out_shape=[
            shaped(6, k_tiles, LANES),
            shaped(half_r, k, dtype=BF16), shaped(half_r, k, dtype=BF16),
            shaped(M, k), shaped(M, k),
            shaped(half_c, k), shaped(half_c, k),
            shaped(half_c, k, dtype=BF16), shaped(half_c, k, dtype=BF16),
        ],
        in_specs=[smem] + [vmem] * 2,
        out_specs=[vmem] * 9,
        scratch_shapes=[
            pltpu.VMEM((5, k_tiles, LANES), F32),
            pltpu.VMEM((2, k_tiles, LANES), jnp.int32),
            pltpu.VMEM((2, 2, half_r // SUB, LANES), F32),
        ],
        compiler_params=params(24),
        name="tables",
    )(labels, blocks, labels)
    t_cos, t_sin, u_cos, u_sin = pl.pallas_call(
        column_kernel,
        out_shape=[shaped(wide, k, dtype=BF16), shaped(wide, k, dtype=BF16),
                   shaped(6 * M, k, dtype=BF16), shaped(6 * M, k, dtype=BF16)],
        in_specs=[vmem] * 14,
        out_specs=[vmem] * 4,
        scratch_shapes=[pltpu.VMEM((9 * LANES, 2 * depth), BF16)],
        compiler_params=params(28),
        name="columns",
    )(s, *around, e_cos, e_sin, f_cos, f_sin)

    def dot(a, b):
        return lax.dot_general(a, b, (((1,), (1,)), ((), ())), preferred_element_type=F32)

    return pl.pallas_call(
        finish_kernel,
        out_shape=shaped(R, C),
        in_specs=[vmem] * 4,
        out_specs=pl.BlockSpec(memory_space=pl.ANY),
        scratch_shapes=[pltpu.VMEM((R, C), F32), pltpu.SemaphoreType.DMA((half_r // M * 2,))],
        compiler_params=params(24),
        name="finish",
    )(dot(a_cos, t_cos), dot(a_sin, t_sin), dot(u_cos, c_cos), dot(u_sin, c_sin))


def solution(mesh):
    return jax.shard_map(
        shards,
        mesh=mesh,
        in_specs=(
            P(None, ("frow", "fcol")),
            P(None, ("frow", "fcol")),
            P(("frow", "fcol")),
            P(),
            P(),
            P("frow", "fcol", None, None),
            P(),
        ),
        out_specs=P("frow", "fcol"),
        check_vma=False,
    )
```

```python
import functools
import math

import jax
import jax.numpy as jnp
from jax import lax
from jax.experimental import pallas as pl
from jax.experimental.pallas import tpu as pltpu
from jax.sharding import PartitionSpec as P

R = 1024
C = 512
M = 64
NT = 16
NBLK = 4
LANES = 128
SUB = 8
OWN, LEFT, RIGHT, UP, DOWN, UL, UR, DL, DR = range(9)
F32 = jnp.float32
BF16 = jnp.bfloat16


def wrap(m, modulus):
    if modulus & (modulus - 1) == 0:
        return m & (modulus - 1)
    return jnp.remainder(m, modulus)


def turn(m, modulus):
    m = wrap(m, modulus)
    quarter = modulus // 4
    q = (m + modulus // 8) // quarter if quarter & (quarter - 1) else (
        (m + modulus // 8) >> (quarter.bit_length() - 1))
    x = (m - q * quarter).astype(F32) * (2.0 * math.pi / modulus)
    x2 = x * x
    s = x + x * x2 * (-1 / 6 + x2 * (1 / 120 + x2 * (-1 / 5040 + x2 * (1 / 362880))))
    c = 1.0 + x2 * (-0.5 + x2 * (1 / 24 + x2 * (-1 / 720 + x2 * (1 / 40320))))
    odd = (q & 1) == 1
    cos = jnp.where(odd, s, c)
    sin = jnp.where(odd, c, s)
    cos = jnp.where(((q + 1) & 2) != 0, -cos, cos)
    sin = jnp.where((q & 2) != 0, -sin, sin)
    return cos, sin


def times(a, b):
    return a[0] * b[0] - a[1] * b[1], a[0] * b[1] + a[1] * b[0]


def pack_kernel(order_ref, vis_ref, pair_ref, slot_ref, out_ref):
    block = vis_ref.shape[1]
    lines = [vis_ref[0:1, :], vis_ref[1:2, :], pair_ref[0:1, :].astype(F32),
             pair_ref[1:2, :].astype(F32), slot_ref[...].astype(F32)]
    at = lax.broadcasted_iota(jnp.int32, (1, LANES), 1)
    order = jnp.zeros((1, LANES), jnp.int32)
    for b in range(NBLK):
        order = jnp.where(at == b, order_ref[b], order)
    for copy in range(out_ref.shape[0]):
        for q, line in enumerate(lines):
            out_ref[copy, :, q * block:(q + 1) * block] = line
        out_ref[copy, :, 5 * block:] = order.astype(F32)


def pick(row, lane):
    return jnp.take_along_axis(
        jnp.broadcast_to(row, lane.shape), lane, axis=1, mode="promise_in_bounds")


def taper_rows(group, half, wide=LANES):
    index = (lax.broadcasted_iota(jnp.int32, (SUB, wide), 0) + SUB * group).astype(F32)
    return ((half + M - 0.5 - index) * (1.0 / (2 * M)),
            (index - (half - M - 0.5)) * (1.0 / (2 * M)))


def table_kernel(n_frow, n_fcol, first, n_lines, block_ref, cell_ref,
                 s_ref, ac_ref, as_ref, ec_ref, es_ref, fc_ref, fs_ref, cc_ref, cs_ref,
                 q_ref, uv_ref, dr_ref, order_ref, sem):
    frow_at = lax.axis_index("frow")
    fcol_at = lax.axis_index("fcol")
    half_r, half_c = R // 2, C // 2
    mod_r, mod_c = 2 * R * n_frow, 2 * C * n_fcol
    k_tiles = s_ref.shape[1]
    per_block = k_tiles // NBLK
    block = per_block * LANES
    shape = (SUB, LANES)

    copy = pltpu.make_async_copy(block_ref.at[0, :, 5 * block:], order_ref, sem)
    copy.start()
    copy.wait()
    for b in range(NBLK):
        owner = order_ref[0, b].astype(jnp.int32)
        for q in range(5):
            for j in range(per_block):
                q_ref[q, b * per_block + j:b * per_block + j + 1, :] = block_ref[
                    owner, :, q * block + j * LANES:q * block + (j + 1) * LANES]
    a1 = q_ref[2].astype(jnp.int32)
    a2 = q_ref[3].astype(jnp.int32)
    slot = q_ref[4].astype(jnp.int32)

    def cells(table):
        got = [jnp.zeros(shape, F32)] * 2
        for h in range(table.shape[0]):
            row = table[h:h + 1, :]
            got = [jnp.where((a >> 7) == h, pick(row, a & 127), g)
                   for a, g in zip((a1, a2), got)]
        return (got[0] - got[1]).astype(jnp.int32)

    u = cells(cell_ref[first:first + n_lines, :])
    v = cells(cell_ref[first + n_lines:first + 2 * n_lines, :])
    uv_ref[0] = u
    uv_ref[1] = v
    centre = times(turn(u * (frow_at * (2 * R) + (R - 1)), mod_r),
                   turn(v * (fcol_at * (2 * C) + (C - 1)), mod_c))
    scale = 0.5 / math.sqrt(NBLK * per_block * LANES)
    value = times((q_ref[0] * scale, q_ref[1] * scale), centre)
    s_ref[0] = value[0]
    s_ref[1] = value[1]
    for n, a in enumerate((a1, a2)):
        s_ref[2 + n] = ((a >> 3) + (a & 4) * 16).astype(F32)
        s_ref[4 + n] = ((a & 3) * NT + slot).astype(F32)

    iota = lax.broadcasted_iota(jnp.int32, shape, 0)

    def tables(s, carry):
        lane = pl.ds(pl.multiple_of(s * LANES, LANES), LANES)

        def phases(which, modulus, half):
            freq = jnp.broadcast_to(uv_ref[which, pl.ds(s, 1), :], shape)
            fine = turn(freq * (2 * iota + 1), modulus)
            middle = turn(freq * (16 * iota), modulus)
            coarse = turn(freq * (128 * iota), modulus)
            for a in range(half // 64):
                top = tuple(jnp.broadcast_to(x[a:a + 1], shape) for x in coarse)
                both = times(middle, top)
                for comp in range(2):
                    dr_ref[which, comp, 8 * a:8 * a + 8, :] = both[comp]
            for g in range(half // SUB):
                step = tuple(jnp.broadcast_to(dr_ref[which, comp, g:g + 1, :], shape)
                             for comp in range(2))
                yield times(fine, step)

        pairs = {}

        def put(ref, first, group, x):
            key = (id(ref), first)
            if group % 2 == 0:
                pairs[key] = x
            else:
                start = first + SUB * (group - 1)
                ref[start:start + 16, lane] = jnp.concatenate([pairs.pop(key), x], 0).astype(BF16)

        edge = (half_r - M) // SUB
        for g, (cos, sin) in enumerate(phases(0, mod_r, half_r)):
            if g >= edge:
                mine, other = taper_rows(g, half_r)
                at = slice((g - edge) * SUB, (g - edge + 1) * SUB)
                ec_ref[at, lane] = cos * other
                es_ref[at, lane] = sin * other
                cos, sin = cos * mine, sin * mine
            put(ac_ref, 0, g, cos)
            put(as_ref, 0, g, sin)
        for g, (cos, sin) in enumerate(phases(1, mod_c, half_c)):
            put(cc_ref, 0, g, cos)
            put(cs_ref, 0, g, sin)
            at = slice(g * SUB, (g + 1) * SUB)
            fc_ref[at, lane] = cos
            fs_ref[at, lane] = sin
        return carry

    lax.fori_loop(0, k_tiles, tables, 0, unroll=4)


def column_kernel(depth, s_ref, mid_ref, a_ref, b_ref, ec_ref, es_ref, fc_ref, fs_ref,
                  tc_ref, ts_ref, uc_ref, us_ref, gain_ref):
    r_odd = lax.rem(lax.axis_index("frow"), 2) == 1
    c_odd = lax.rem(lax.axis_index("fcol"), 2) == 1
    k_tiles = s_ref.shape[1]
    half = depth // 2
    half_c = C // 2

    low_lane = lax.broadcasted_iota(jnp.int32, (half, LANES), 1) < LANES // 2
    for f in range(9):
        ref, row = (mid_ref, a_ref, b_ref)[f // 3], f % 3 * depth
        re = ref[pl.ds(row, half, stride=2), :]
        im = ref[pl.ds(row + 1, half, stride=2), :]
        top = jnp.where(low_lane, re, pltpu.roll(im, LANES // 2, 1))
        low = jnp.where(low_lane, pltpu.roll(re, LANES // 2, 1), im)
        both = jnp.concatenate([top, low], 0).T
        first = both.astype(BF16)
        gain_ref[f * LANES:(f + 1) * LANES, :depth] = first
        gain_ref[f * LANES:(f + 1) * LANES, depth:] = (both - first.astype(F32)).astype(BF16)

    step = 2 if k_tiles % 2 == 0 else 1
    wide = step * LANES
    shape = (SUB, wide)
    line_at = lax.broadcasted_iota(jnp.int32, (depth, wide), 0).astype(F32)
    place_at = line_at[:half]
    zero = jnp.zeros((M, wide), BF16)
    for p in range(k_tiles // step):
        lane = slice(p * wide, (p + 1) * wide)

        def line(q):
            return jnp.concatenate([s_ref[q, p * step + i:p * step + i + 1, :]
                                    for i in range(step)], 1)

        gains = []
        for n in range(2):
            hot = jnp.where(line_at == line(2 + n), 1.0, 0.0).astype(BF16)
            z = jnp.dot(gain_ref[...], jnp.concatenate([hot, hot], 0),
                        preferred_element_type=F32)
            mask = jnp.where(place_at == line(4 + n), 1.0, 0.0)
            gains.append([[jnp.sum(z[f * LANES + comp * half:f * LANES + (comp + 1) * half] * mask,
                                   axis=0, keepdims=True) for comp in range(2)]
                          for f in range(9)])
        value = (line(0), line(1))
        w = []
        for f in range(9):
            (g1r, g1i), (g2r, g2i) = gains[0][f], gains[1][f]
            w.append(times(value, (g1r * g2r + g1i * g2i, g1i * g2r - g1r * g2i)))

        def pick_two(odd, x, y):
            return (tuple(jnp.where(odd, i, j) for i, j in zip(x, y)),
                    tuple(jnp.where(odd, j, i) for i, j in zip(x, y)))

        columns = []
        for c in range(3):
            up, down = pick_two(r_odd, w[3 * c + 1], w[3 * c + 2])
            columns.append((w[3 * c], up, down))
        named = {}
        for r, names in enumerate(((OWN, LEFT, RIGHT), (UP, UL, UR), (DOWN, DL, DR))):
            named[names[0]] = columns[0][r]
            named[names[1]], named[names[2]] = pick_two(c_odd, columns[1][r], columns[2][r])

        def weight(f):
            return tuple(jnp.broadcast_to(x, shape) for x in named[f])

        pairs = {}

        def put(ref, first, group, x):
            key = (id(ref), first)
            if group % 2 == 0:
                pairs[key] = x
            else:
                start = first + SUB * (group - 1)
                ref[start:start + 16, lane] = jnp.concatenate([pairs.pop(key), x], 0).astype(BF16)

        edge = (half_c - M) // SUB
        (wr, wi), (lr, li), (rr, ri) = weight(OWN), weight(LEFT), weight(RIGHT)
        for g in range(half_c // SUB):
            at = slice(g * SUB, (g + 1) * SUB)
            cos, sin = fc_ref[at, lane], fs_ref[at, lane]
            own = (cos, sin)
            if g >= edge:
                mine, other = taper_rows(g, half_c, wide)
                own = (cos * mine, sin * mine)
                cos, sin = cos * other, sin * other
                base = 2 * half_c + M
                put(tc_ref, base, g - edge, lr * cos + li * sin)
                put(ts_ref, base, g - edge, lr * sin - li * cos)
                put(tc_ref, base + 2 * M, g - edge, rr * cos - ri * sin)
                put(ts_ref, base + 2 * M, g - edge, -(rr * sin + ri * cos))
            put(tc_ref, 0, g, wr * own[0])
            put(tc_ref, half_c, g, -wi * own[1])
            put(ts_ref, 0, g, -wi * own[0])
            put(ts_ref, half_c, g, -wr * own[1])
        for ref in (tc_ref, ts_ref):
            ref[2 * half_c:2 * half_c + M, lane] = zero
            ref[2 * half_c + 2 * M:2 * half_c + 3 * M, lane] = zero
        rows_w = [weight(f) for f in (UP, DOWN, UL, UR, DL, DR)]
        signs = (-1, 1, -1, -1, 1, 1)
        for g in range(M // SUB):
            at = slice(g * SUB, (g + 1) * SUB)
            cos, sin = ec_ref[at, lane], es_ref[at, lane]
            for n, ((wr, wi), sd) in enumerate(zip(rows_w, signs)):
                put(uc_ref, n * M, g, wr * cos - (sd * wi) * sin)
                put(us_ref, n * M, g, -(sd * wr) * sin - wi * cos)


def finish_kernel(m1_ref, m2_ref, g1_ref, g2_ref, image_ref, out_ref, sems):
    half_r, half_c = R // 2, C // 2
    shape = (SUB, LANES)
    iota = lax.broadcasted_iota(jnp.int32, shape, 0)
    lane_at = lax.broadcasted_iota(jnp.int32, shape, 1)
    back_lane = (LANES - 1) - lane_at
    back_row = (SUB - 1) - iota
    n_lane = half_c // LANES
    edge_c = half_c - M
    edge_r = half_r - M
    col_own, col_other = [], []
    for t in range(n_lane):
        index = (lane_at + t * LANES).astype(F32)
        col_own.append(jnp.minimum((half_c + M - 0.5 - index) * (1.0 / (2 * M)), 1.0))
        col_other.append(jnp.maximum((index - (half_c - M - 0.5)) * (1.0 / (2 * M)), 0.0))

    def flip(x, index, axis):
        return jnp.take_along_axis(x, index, axis=axis, mode="promise_in_bounds")

    def finish(g, edged):
        rows = pl.ds(pl.multiple_of(g * SUB, SUB), SUB)
        for t in range(n_lane):
            def part(ref, which):
                return ref[rows, which * half_c + t * LANES:which * half_c + (t + 1) * LANES]
            p, s_, r, q = part(m1_ref, 0), part(m1_ref, 1), part(m2_ref, 0), part(m2_ref, 1)
            even, odd = p + q, p - q
            plus, minus = r + s_, r - s_
            quad = {(1, 1): even + plus, (-1, -1): even - plus,
                    (1, -1): odd + minus, (-1, 1): odd - minus}
            if (t + 1) * LANES > edge_c:
                base = 2 * half_c
                off = t * LANES - (half_c - LANES)
                for se, start in ((-1, base), (1, base + LANES)):
                    lc = m1_ref[rows, start + off:start + off + LANES]
                    ls = m2_ref[rows, start + off:start + off + LANES]
                    quad[1, se] += lc + ls
                    quad[-1, se] += lc - ls
            if edged:
                def edge(n):
                    at = pl.ds(pl.multiple_of(n * M + g * SUB - edge_r, SUB), SUB)
                    x = g1_ref[at, t * LANES:(t + 1) * LANES]
                    y = g2_ref[at, t * LANES:(t + 1) * LANES]
                    return {1: x + y, -1: x - y}
                for n, sd in ((0, -1), (1, 1)):
                    e = edge(n)
                    for se in (-1, 1):
                        quad[sd, se] += e[se] * col_own[t]
                if (t + 1) * LANES > edge_c:
                    for n, (sd, se) in ((2, (-1, -1)), (3, (-1, 1)), (4, (1, -1)), (5, (1, 1))):
                        quad[sd, se] += edge(n)[se] * col_other[t]
            for (sd, se), x in quad.items():
                if sd < 0:
                    x = flip(x, back_row, 0)
                    at = pl.ds(pl.multiple_of(half_r - SUB - g * SUB, SUB), SUB)
                else:
                    at = pl.ds(pl.multiple_of(half_r + g * SUB, SUB), SUB)
                if se < 0:
                    x = flip(x, back_lane, 1)
                    start = half_c - (t + 1) * LANES
                else:
                    start = half_c + t * LANES
                out_ref[at, start:start + LANES] = x

    group = M // SUB
    n_groups = half_r // M

    def send(j, sign):
        start = pl.multiple_of(half_r + j * M if sign > 0 else half_r - M - j * M, M)
        rows = pl.ds(start, M)
        return pltpu.make_async_copy(out_ref.at[rows, :], image_ref.at[rows, :],
                                     sems.at[2 * j + (sign > 0)])

    def run(j, edged):
        for i in range(group):
            finish(j * group + i, edged)
        send(j, 1).start()
        send(j, -1).start()

    def inner(j, carry):
        run(j, False)
        return carry

    lax.fori_loop(0, n_groups - 1, inner, 0)
    run(n_groups - 1, True)
    for j in range(n_groups):
        send(j, 1).wait()
        send(j, -1).wait()


def swaps(size):
    both = []
    for first in (0, 1):
        pairs = [(i, i + 1) for i in range(first, size - 1, 2)]
        both.append(pairs + [(j, i) for i, j in pairs])
    return both


def shards(vis, station_pairs, visibility_time_slot, station_u_cells, station_v_cells,
           facet_station_gains, holder_device_order):
    n_frow = lax.axis_size("frow")
    n_fcol = lax.axis_size("fcol")
    block = vis.shape[1]
    k_tiles = NBLK * block // LANES
    k = k_tiles * LANES
    half_r, half_c = R // 2, C // 2
    wide = 2 * half_c + 4 * M
    vmem = pl.BlockSpec(memory_space=pltpu.VMEM)
    smem = pl.BlockSpec(memory_space=pltpu.SMEM)

    def lines(x):
        return x.reshape(-1, LANES)

    def shaped(*dims, dtype=F32):
        return jax.ShapeDtypeStruct(dims, dtype)

    def params(mib):
        return pltpu.CompilerParams(vmem_limit_bytes=mib * 1024 * 1024)

    packed = pl.pallas_call(
        pack_kernel,
        out_shape=shaped(n_frow * n_fcol, 1, 5 * block + LANES),
        in_specs=[smem] + [vmem] * 3,
        name="pack",
    )(holder_device_order, vis, station_pairs, visibility_time_slot.reshape(1, block))
    facet_station_gains, packed = lax.optimization_barrier((facet_station_gains, packed))
    gains = facet_station_gains[0, 0]
    depth = gains.size // LANES
    own = gains.reshape(2, -1, LANES).transpose(1, 0, 2).reshape(depth, LANES)
    row_a, row_b = [lax.ppermute(own, "frow", pairs) for pairs in swaps(n_frow)]
    blocks = lax.all_to_all(packed, ("frow", "fcol"), 0, 0)
    n_lines = station_u_cells.size // LANES
    mid = jnp.concatenate([own, row_a, row_b, lines(station_u_cells).astype(F32),
                           lines(station_v_cells).astype(F32)], 0)
    col_a, col_b = [lax.ppermute(mid, "fcol", pairs) for pairs in swaps(n_fcol)]
    s, a_cos, a_sin, e_cos, e_sin, f_cos, f_sin, c_cos, c_sin = pl.pallas_call(
        functools.partial(table_kernel, n_frow, n_fcol, 3 * depth, n_lines),
        out_shape=[
            shaped(6, k_tiles, LANES),
            shaped(half_r, k, dtype=BF16), shaped(half_r, k, dtype=BF16),
            shaped(M, k), shaped(M, k),
            shaped(half_c, k), shaped(half_c, k),
            shaped(half_c, k, dtype=BF16), shaped(half_c, k, dtype=BF16),
        ],
        in_specs=[vmem] * 2,
        out_specs=[vmem] * 9,
        scratch_shapes=[
            pltpu.VMEM((5, k_tiles, LANES), F32),
            pltpu.VMEM((2, k_tiles, LANES), jnp.int32),
            pltpu.VMEM((2, 2, half_r // SUB, LANES), F32),
            pltpu.SMEM((1, LANES), F32),
            pltpu.SemaphoreType.DMA,
        ],
        compiler_params=params(24),
        name="tables",
    )(blocks, mid)
    t_cos, t_sin, u_cos, u_sin = pl.pallas_call(
        functools.partial(column_kernel, depth),
        out_shape=[shaped(wide, k, dtype=BF16), shaped(wide, k, dtype=BF16),
                   shaped(6 * M, k, dtype=BF16), shaped(6 * M, k, dtype=BF16)],
        in_specs=[vmem] * 8,
        out_specs=[vmem] * 4,
        scratch_shapes=[pltpu.VMEM((9 * LANES, 2 * depth), BF16)],
        compiler_params=params(28),
        name="columns",
    )(s, mid, col_a, col_b, e_cos, e_sin, f_cos, f_sin)

    def dot(a, b):
        return lax.dot_general(a, b, (((1,), (1,)), ((), ())), preferred_element_type=F32)

    return pl.pallas_call(
        finish_kernel,
        out_shape=shaped(R, C),
        in_specs=[vmem] * 4,
        out_specs=pl.BlockSpec(memory_space=pl.ANY),
        scratch_shapes=[pltpu.VMEM((R, C), F32), pltpu.SemaphoreType.DMA((half_r // M * 2,))],
        compiler_params=params(24),
        name="finish",
    )(dot(a_cos, t_cos), dot(a_sin, t_sin), dot(u_cos, c_cos), dot(u_sin, c_sin))


def solution(mesh):
    return jax.shard_map(
        shards,
        mesh=mesh,
        in_specs=(
            P(None, ("frow", "fcol")),
            P(None, ("frow", "fcol")),
            P(("frow", "fcol")),
            P(),
            P(),
            P("frow", "fcol", None, None),
            P(),
        ),
        out_specs=P("frow", "fcol"),
        check_vma=False,
    )
```

```python
import functools
import math

import jax
import jax.numpy as jnp
from jax import lax
from jax.experimental import pallas as pl
from jax.experimental.pallas import tpu as pltpu
from jax.sharding import PartitionSpec as P

R = 1024
C = 512
M = 64
NT = 16
NBLK = 4
LANES = 128
SUB = 8
OWN, LEFT, RIGHT, UP, DOWN, UL, UR, DL, DR = range(9)
F32 = jnp.float32
BF16 = jnp.bfloat16


def wrap(m, modulus):
    if modulus & (modulus - 1) == 0:
        return m & (modulus - 1)
    return jnp.remainder(m, modulus)


def turn(m, modulus):
    m = wrap(m, modulus)
    quarter = modulus // 4
    q = (m + modulus // 8) // quarter if quarter & (quarter - 1) else (
        (m + modulus // 8) >> (quarter.bit_length() - 1))
    x = (m - q * quarter).astype(F32) * (2.0 * math.pi / modulus)
    x2 = x * x
    s = x + x * x2 * (-1 / 6 + x2 * (1 / 120 + x2 * (-1 / 5040 + x2 * (1 / 362880))))
    c = 1.0 + x2 * (-0.5 + x2 * (1 / 24 + x2 * (-1 / 720 + x2 * (1 / 40320))))
    odd = (q & 1) == 1
    cos = jnp.where(odd, s, c)
    sin = jnp.where(odd, c, s)
    cos = jnp.where(((q + 1) & 2) != 0, -cos, cos)
    sin = jnp.where((q & 2) != 0, -sin, sin)
    return cos, sin


def times(a, b):
    return a[0] * b[0] - a[1] * b[1], a[0] * b[1] + a[1] * b[0]


def pack_kernel(order_ref, vis_ref, pair_ref, slot_ref, u_ref, v_ref, out_ref, label_ref):
    block = vis_ref.shape[1]
    lines = [vis_ref[0:1, :], vis_ref[1:2, :], pair_ref[0:1, :].astype(F32),
             pair_ref[1:2, :].astype(F32), slot_ref[...].astype(F32)]
    for copy in range(out_ref.shape[0]):
        for q, line in enumerate(lines):
            out_ref[copy, :, q * block:(q + 1) * block] = line
    n_lines = u_ref.shape[0]
    at = lax.broadcasted_iota(jnp.int32, (SUB, LANES), 1)
    order = jnp.zeros((SUB, LANES), jnp.int32)
    for b in range(NBLK):
        order = jnp.where(at == b, order_ref[b], order)
    label_ref[:SUB] = order.astype(F32)
    label_ref[SUB:SUB + n_lines] = u_ref[...].astype(F32)
    label_ref[SUB + n_lines:SUB + 2 * n_lines] = v_ref[...].astype(F32)


def pick(row, lane):
    return jnp.take_along_axis(
        jnp.broadcast_to(row, lane.shape), lane, axis=1, mode="promise_in_bounds")


def taper_rows(group, half, wide=LANES):
    index = (lax.broadcasted_iota(jnp.int32, (SUB, wide), 0) + SUB * group).astype(F32)
    return ((half + M - 0.5 - index) * (1.0 / (2 * M)),
            (index - (half - M - 0.5)) * (1.0 / (2 * M)))


def table_kernel(n_frow, n_fcol, first, n_lines, block_ref, cell_ref,
                 s_ref, ac_ref, as_ref, ec_ref, es_ref, fc_ref, fs_ref, cc_ref, cs_ref,
                 q_ref, uv_ref, dr_ref, order_ref, sem):
    frow_at = lax.axis_index("frow")
    fcol_at = lax.axis_index("fcol")
    half_r, half_c = R // 2, C // 2
    mod_r, mod_c = 2 * R * n_frow, 2 * C * n_fcol
    k_tiles = s_ref.shape[1]
    per_block = k_tiles // NBLK
    block = per_block * LANES
    shape = (SUB, LANES)

    copy = pltpu.make_async_copy(cell_ref.at[first:first + SUB, :], order_ref, sem)
    copy.start()
    copy.wait()
    for b in range(NBLK):
        owner = order_ref[0, b].astype(jnp.int32)
        for q in range(5):
            for j in range(per_block):
                q_ref[q, b * per_block + j:b * per_block + j + 1, :] = block_ref[
                    owner, :, q * block + j * LANES:q * block + (j + 1) * LANES]
    a1 = q_ref[2].astype(jnp.int32)
    a2 = q_ref[3].astype(jnp.int32)
    slot = q_ref[4].astype(jnp.int32)

    at = first + SUB

    def cells(table):
        got = [jnp.zeros(shape, F32)] * 2
        for h in range(table.shape[0]):
            row = table[h:h + 1, :]
            got = [jnp.where((a >> 7) == h, pick(row, a & 127), g)
                   for a, g in zip((a1, a2), got)]
        return (got[0] - got[1]).astype(jnp.int32)

    u = cells(cell_ref[at:at + n_lines, :])
    v = cells(cell_ref[at + n_lines:at + 2 * n_lines, :])
    uv_ref[0] = u
    uv_ref[1] = v
    centre = times(turn(u * (frow_at * (2 * R) + (R - 1)), mod_r),
                   turn(v * (fcol_at * (2 * C) + (C - 1)), mod_c))
    scale = 0.5 / math.sqrt(NBLK * per_block * LANES)
    value = times((q_ref[0] * scale, q_ref[1] * scale), centre)
    s_ref[0] = value[0]
    s_ref[1] = value[1]
    for n, a in enumerate((a1, a2)):
        s_ref[2 + n] = ((a >> 3) + (a & 4) * 16).astype(F32)
        s_ref[4 + n] = ((a & 3) * NT + slot).astype(F32)

    iota = lax.broadcasted_iota(jnp.int32, shape, 0)

    def tables(s, carry):
        lane = pl.ds(pl.multiple_of(s * LANES, LANES), LANES)

        def phases(which, modulus, half):
            freq = jnp.broadcast_to(uv_ref[which, pl.ds(s, 1), :], shape)
            fine = turn(freq * (2 * iota + 1), modulus)
            middle = turn(freq * (16 * iota), modulus)
            coarse = turn(freq * (128 * iota), modulus)
            for a in range(half // 64):
                top = tuple(jnp.broadcast_to(x[a:a + 1], shape) for x in coarse)
                both = times(middle, top)
                for comp in range(2):
                    dr_ref[which, comp, 8 * a:8 * a + 8, :] = both[comp]
            for g in range(half // SUB):
                step = tuple(jnp.broadcast_to(dr_ref[which, comp, g:g + 1, :], shape)
                             for comp in range(2))
                yield times(fine, step)

        pairs = {}

        def put(ref, first, group, x):
            key = (id(ref), first)
            if group % 2 == 0:
                pairs[key] = x
            else:
                start = first + SUB * (group - 1)
                ref[start:start + 16, lane] = jnp.concatenate([pairs.pop(key), x], 0).astype(BF16)

        edge = (half_r - M) // SUB
        for g, (cos, sin) in enumerate(phases(0, mod_r, half_r)):
            if g >= edge:
                mine, other = taper_rows(g, half_r)
                at = slice((g - edge) * SUB, (g - edge + 1) * SUB)
                ec_ref[at, lane] = cos * other
                es_ref[at, lane] = sin * other
                cos, sin = cos * mine, sin * mine
            put(ac_ref, 0, g, cos)
            put(as_ref, 0, g, sin)
        for g, (cos, sin) in enumerate(phases(1, mod_c, half_c)):
            put(cc_ref, 0, g, cos)
            put(cs_ref, 0, g, sin)
            at = slice(g * SUB, (g + 1) * SUB)
            fc_ref[at, lane] = cos
            fs_ref[at, lane] = sin
        return carry

    lax.fori_loop(0, k_tiles, tables, 0, unroll=4)


def image_kernel(depth, s_ref, mid_ref, a_ref, b_ref, ac_ref, as_ref, ec_ref, es_ref,
                 fc_ref, fs_ref, cc_ref, cs_ref, image_ref,
                 out_ref, tc_ref, ts_ref, uc_ref, us_ref, gain_ref,
                 m1_ref, m2_ref, g1_ref, g2_ref, sems):
    r_odd = lax.rem(lax.axis_index("frow"), 2) == 1
    c_odd = lax.rem(lax.axis_index("fcol"), 2) == 1
    k_tiles = s_ref.shape[1]
    half = depth // 2
    half_c = C // 2

    low_lane = lax.broadcasted_iota(jnp.int32, (half, LANES), 1) < LANES // 2
    for f in range(9):
        ref, row = (mid_ref, a_ref, b_ref)[f // 3], f % 3 * depth
        re = ref[pl.ds(row, half, stride=2), :]
        im = ref[pl.ds(row + 1, half, stride=2), :]
        top = jnp.where(low_lane, re, pltpu.roll(im, LANES // 2, 1))
        low = jnp.where(low_lane, pltpu.roll(re, LANES // 2, 1), im)
        both = jnp.concatenate([top, low], 0).T
        first = both.astype(BF16)
        gain_ref[f * LANES:(f + 1) * LANES, :depth] = first
        gain_ref[f * LANES:(f + 1) * LANES, depth:] = (both - first.astype(F32)).astype(BF16)

    step = 2 if k_tiles % 2 == 0 else 1
    wide = step * LANES
    shape = (SUB, wide)
    line_at = lax.broadcasted_iota(jnp.int32, (depth, wide), 0).astype(F32)
    place_at = line_at[:half]
    zero = jnp.zeros((M, wide), BF16)
    edge_rows = []
    for p in range(k_tiles // step):
        lane = slice(p * wide, (p + 1) * wide)

        def line(q):
            return jnp.concatenate([s_ref[q, p * step + i:p * step + i + 1, :]
                                    for i in range(step)], 1)

        gains = []
        for n in range(2):
            hot = jnp.where(line_at == line(2 + n), 1.0, 0.0).astype(BF16)
            z = jnp.dot(gain_ref[...], jnp.concatenate([hot, hot], 0),
                        preferred_element_type=F32)
            mask = jnp.where(place_at == line(4 + n), 1.0, 0.0)
            gains.append([[jnp.sum(z[f * LANES + comp * half:f * LANES + (comp + 1) * half] * mask,
                                   axis=0, keepdims=True) for comp in range(2)]
                          for f in range(9)])
        value = (line(0), line(1))
        w = []
        for f in range(9):
            (g1r, g1i), (g2r, g2i) = gains[0][f], gains[1][f]
            w.append(times(value, (g1r * g2r + g1i * g2i, g1i * g2r - g1r * g2i)))

        def pick_two(odd, x, y):
            return (tuple(jnp.where(odd, i, j) for i, j in zip(x, y)),
                    tuple(jnp.where(odd, j, i) for i, j in zip(x, y)))

        columns = []
        for c in range(3):
            up, down = pick_two(r_odd, w[3 * c + 1], w[3 * c + 2])
            columns.append((w[3 * c], up, down))
        named = {}
        for r, names in enumerate(((OWN, LEFT, RIGHT), (UP, UL, UR), (DOWN, DL, DR))):
            named[names[0]] = columns[0][r]
            named[names[1]], named[names[2]] = pick_two(c_odd, columns[1][r], columns[2][r])

        def weight(f):
            return tuple(jnp.broadcast_to(x, shape) for x in named[f])

        pairs = {}

        def put(ref, first, group, x):
            key = (id(ref), first)
            if group % 2 == 0:
                pairs[key] = x
            else:
                start = first + SUB * (group - 1)
                ref[start:start + 16, lane] = jnp.concatenate([pairs.pop(key), x], 0).astype(BF16)

        edge = (half_c - M) // SUB
        (wr, wi), (lr, li), (rr, ri) = weight(OWN), weight(LEFT), weight(RIGHT)
        for g in range(half_c // SUB):
            at = slice(g * SUB, (g + 1) * SUB)
            cos, sin = fc_ref[at, lane], fs_ref[at, lane]
            own = (cos, sin)
            if g >= edge:
                mine, other = taper_rows(g, half_c, wide)
                own = (cos * mine, sin * mine)
                cos, sin = cos * other, sin * other
                base = 2 * half_c + M
                put(tc_ref, base, g - edge, lr * cos + li * sin)
                put(ts_ref, base, g - edge, lr * sin - li * cos)
                put(tc_ref, base + 2 * M, g - edge, rr * cos - ri * sin)
                put(ts_ref, base + 2 * M, g - edge, -(rr * sin + ri * cos))
            put(tc_ref, 0, g, wr * own[0])
            put(tc_ref, half_c, g, -wi * own[1])
            put(ts_ref, 0, g, -wi * own[0])
            put(ts_ref, half_c, g, -wr * own[1])
        for ref in (tc_ref, ts_ref):
            ref[2 * half_c:2 * half_c + M, lane] = zero
            ref[2 * half_c + 2 * M:2 * half_c + 3 * M, lane] = zero
        edge_rows.append([named[f] for f in (UP, DOWN, UL, UR, DL, DR)])

    def dot(a, b):
        return lax.dot_general(a, b, (((1,), (1,)), ((), ())), preferred_element_type=F32)

    half_r = R // 2
    part = half_r // 2

    def own_products(i):
        rows = slice(i * part, (i + 1) * part)
        m1_ref[rows, :] = dot(ac_ref[rows, :], tc_ref[...])
        m2_ref[rows, :] = dot(as_ref[rows, :], ts_ref[...])

    own_products(0)
    signs = (-1, 1, -1, -1, 1, 1)
    for p, rows_w in enumerate(edge_rows):
        lane = slice(p * wide, (p + 1) * wide)
        for n, (w, sd) in enumerate(zip(rows_w, signs)):
            wr, wi = [jnp.broadcast_to(x, shape) for x in w]
            for g in range(0, M // SUB, 2):
                tops, lows = [], []
                for i in range(2):
                    at = slice((g + i) * SUB, (g + i + 1) * SUB)
                    cos, sin = ec_ref[at, lane], es_ref[at, lane]
                    tops.append(wr * cos - (sd * wi) * sin)
                    lows.append(-(sd * wr) * sin - wi * cos)
                at = slice(n * M + g * SUB, n * M + (g + 2) * SUB)
                uc_ref[at, lane] = jnp.concatenate(tops, 0).astype(BF16)
                us_ref[at, lane] = jnp.concatenate(lows, 0).astype(BF16)
    own_products(1)
    g1_ref[...] = dot(uc_ref[...], cc_ref[...])
    g2_ref[...] = dot(us_ref[...], cs_ref[...])

    shape = (SUB, LANES)
    iota = lax.broadcasted_iota(jnp.int32, shape, 0)
    lane_at = lax.broadcasted_iota(jnp.int32, shape, 1)
    back_lane = (LANES - 1) - lane_at
    back_row = (SUB - 1) - iota
    n_lane = half_c // LANES
    edge_c = half_c - M
    edge_r = half_r - M
    col_own, col_other = [], []
    for t in range(n_lane):
        index = (lane_at + t * LANES).astype(F32)
        col_own.append(jnp.minimum((half_c + M - 0.5 - index) * (1.0 / (2 * M)), 1.0))
        col_other.append(jnp.maximum((index - (half_c - M - 0.5)) * (1.0 / (2 * M)), 0.0))

    def flip(x, index, axis):
        return jnp.take_along_axis(x, index, axis=axis, mode="promise_in_bounds")

    def finish(g, edged):
        rows = slice(g * SUB, (g + 1) * SUB)
        for t in range(n_lane):
            def part(ref, which):
                return ref[rows, which * half_c + t * LANES:which * half_c + (t + 1) * LANES]
            p, s_, r, q = part(m1_ref, 0), part(m1_ref, 1), part(m2_ref, 0), part(m2_ref, 1)
            even, odd = p + q, p - q
            plus, minus = r + s_, r - s_
            quad = {(1, 1): even + plus, (-1, -1): even - plus,
                    (1, -1): odd + minus, (-1, 1): odd - minus}
            if (t + 1) * LANES > edge_c:
                base = 2 * half_c
                off = t * LANES - (half_c - LANES)
                for se, start in ((-1, base), (1, base + LANES)):
                    lc = m1_ref[rows, start + off:start + off + LANES]
                    ls = m2_ref[rows, start + off:start + off + LANES]
                    quad[1, se] += lc + ls
                    quad[-1, se] += lc - ls
            if edged:
                def edge(n):
                    at = slice(n * M + g * SUB - edge_r, n * M + (g + 1) * SUB - edge_r)
                    x = g1_ref[at, t * LANES:(t + 1) * LANES]
                    y = g2_ref[at, t * LANES:(t + 1) * LANES]
                    return {1: x + y, -1: x - y}
                for n, sd in ((0, -1), (1, 1)):
                    e = edge(n)
                    for se in (-1, 1):
                        quad[sd, se] += e[se] * col_own[t]
                if (t + 1) * LANES > edge_c:
                    for n, (sd, se) in ((2, (-1, -1)), (3, (-1, 1)), (4, (1, -1)), (5, (1, 1))):
                        quad[sd, se] += edge(n)[se] * col_other[t]
            for (sd, se), x in quad.items():
                if sd < 0:
                    x = flip(x, back_row, 0)
                    at = slice(half_r - SUB - g * SUB, half_r - g * SUB)
                else:
                    at = slice(half_r + g * SUB, half_r + (g + 1) * SUB)
                if se < 0:
                    x = flip(x, back_lane, 1)
                    start = half_c - (t + 1) * LANES
                else:
                    start = half_c + t * LANES
                out_ref[at, start:start + LANES] = x

    group = M // SUB
    n_groups = half_r // M

    def send(j, sign):
        start = half_r + j * M if sign > 0 else half_r - M - j * M
        rows = slice(start, start + M)
        return pltpu.make_async_copy(out_ref.at[rows, :], image_ref.at[rows, :],
                                     sems.at[2 * j + (sign > 0)])

    def run(j, edged):
        for i in range(group):
            finish(j * group + i, edged)
        send(j, 1).start()
        send(j, -1).start()

    for j in range(n_groups):
        run(j, j == n_groups - 1)
    for j in range(n_groups):
        send(j, 1).wait()
        send(j, -1).wait()


def swaps(size):
    both = []
    for first in (0, 1):
        pairs = [(i, i + 1) for i in range(first, size - 1, 2)]
        both.append(pairs + [(j, i) for i, j in pairs])
    return both


def shards(vis, station_pairs, visibility_time_slot, station_u_cells, station_v_cells,
           facet_station_gains, holder_device_order):
    n_frow = lax.axis_size("frow")
    n_fcol = lax.axis_size("fcol")
    block = vis.shape[1]
    k_tiles = NBLK * block // LANES
    k = k_tiles * LANES
    half_r, half_c = R // 2, C // 2
    wide = 2 * half_c + 4 * M
    vmem = pl.BlockSpec(memory_space=pltpu.VMEM)
    smem = pl.BlockSpec(memory_space=pltpu.SMEM)

    def lines(x):
        return x.reshape(-1, LANES)

    def shaped(*dims, dtype=F32):
        return jax.ShapeDtypeStruct(dims, dtype)

    def params(mib):
        return pltpu.CompilerParams(vmem_limit_bytes=mib * 1024 * 1024)

    n_lines = station_u_cells.size // LANES
    packed, labels = pl.pallas_call(
        pack_kernel,
        out_shape=[shaped(n_frow * n_fcol, 1, 5 * block), shaped(SUB + 2 * n_lines, LANES)],
        in_specs=[smem] + [vmem] * 5,
        name="pack",
    )(holder_device_order, vis, station_pairs, visibility_time_slot.reshape(1, block),
      lines(station_u_cells), lines(station_v_cells))
    facet_station_gains, packed = lax.optimization_barrier((facet_station_gains, packed))
    gains = facet_station_gains[0, 0]
    depth = gains.size // LANES
    own = gains.reshape(2, -1, LANES).transpose(1, 0, 2).reshape(depth, LANES)
    row_a, row_b = [lax.ppermute(own, "frow", pairs) for pairs in swaps(n_frow)]
    blocks = lax.all_to_all(packed, ("frow", "fcol"), 0, 0)
    mid = jnp.concatenate([own, row_a, row_b, labels], 0)
    col_a, col_b = [lax.ppermute(mid, "fcol", pairs) for pairs in swaps(n_fcol)]
    s, a_cos, a_sin, e_cos, e_sin, f_cos, f_sin, c_cos, c_sin = pl.pallas_call(
        functools.partial(table_kernel, n_frow, n_fcol, 3 * depth, n_lines),
        out_shape=[
            shaped(6, k_tiles, LANES),
            shaped(half_r, k, dtype=BF16), shaped(half_r, k, dtype=BF16),
            shaped(M, k), shaped(M, k),
            shaped(half_c, k), shaped(half_c, k),
            shaped(half_c, k, dtype=BF16), shaped(half_c, k, dtype=BF16),
        ],
        in_specs=[vmem] * 2,
        out_specs=[vmem] * 9,
        scratch_shapes=[
            pltpu.VMEM((5, k_tiles, LANES), F32),
            pltpu.VMEM((2, k_tiles, LANES), jnp.int32),
            pltpu.VMEM((2, 2, half_r // SUB, LANES), F32),
            pltpu.SMEM((SUB, LANES), F32),
            pltpu.SemaphoreType.DMA,
        ],
        compiler_params=params(24),
        name="tables",
    )(blocks, mid)
    return pl.pallas_call(
        functools.partial(image_kernel, depth),
        out_shape=shaped(R, C),
        in_specs=[vmem] * 12,
        out_specs=pl.BlockSpec(memory_space=pl.ANY),
        scratch_shapes=[
            pltpu.VMEM((R, C), F32),
            pltpu.VMEM((wide, k), BF16),
            pltpu.VMEM((wide, k), BF16),
            pltpu.VMEM((6 * M, k), BF16),
            pltpu.VMEM((6 * M, k), BF16),
            pltpu.VMEM((9 * depth, 2 * depth), BF16),
            pltpu.VMEM((half_r, wide), F32),
            pltpu.VMEM((half_r, wide), F32),
            pltpu.VMEM((6 * M, half_c), F32),
            pltpu.VMEM((6 * M, half_c), F32),
            pltpu.SemaphoreType.DMA((2 * half_r // M,)),
        ],
        compiler_params=params(36),
        name="image",
    )(s, mid, col_a, col_b, a_cos, a_sin, e_cos, e_sin, f_cos, f_sin, c_cos, c_sin)


def solution(mesh):
    return jax.shard_map(
        shards,
        mesh=mesh,
        in_specs=(
            P(None, ("frow", "fcol")),
            P(None, ("frow", "fcol")),
            P(("frow", "fcol")),
            P(),
            P(),
            P("frow", "fcol", None, None),
            P(),
        ),
        out_specs=P("frow", "fcol"),
        check_vma=False,
    )
```

```python
import functools
import math

import jax
import jax.numpy as jnp
from jax import lax
from jax.experimental import pallas as pl
from jax.experimental.pallas import tpu as pltpu
from jax.sharding import PartitionSpec as P

R = 1024
C = 512
M = 64
NT = 16
NBLK = 4
LANES = 128
SUB = 8
OWN, LEFT, RIGHT, UP, DOWN, UL, UR, DL, DR = range(9)
F32 = jnp.float32
BF16 = jnp.bfloat16


def wrap(m, modulus):
    if modulus & (modulus - 1) == 0:
        return m & (modulus - 1)
    return jnp.remainder(m, modulus)


def turn(m, modulus):
    m = wrap(m, modulus)
    quarter = modulus // 4
    q = (m + modulus // 8) // quarter if quarter & (quarter - 1) else (
        (m + modulus // 8) >> (quarter.bit_length() - 1))
    x = (m - q * quarter).astype(F32) * (2.0 * math.pi / modulus)
    x2 = x * x
    s = x + x * x2 * (-1 / 6 + x2 * (1 / 120 + x2 * (-1 / 5040 + x2 * (1 / 362880))))
    c = 1.0 + x2 * (-0.5 + x2 * (1 / 24 + x2 * (-1 / 720 + x2 * (1 / 40320))))
    odd = (q & 1) == 1
    cos = jnp.where(odd, s, c)
    sin = jnp.where(odd, c, s)
    cos = jnp.where(((q + 1) & 2) != 0, -cos, cos)
    sin = jnp.where((q & 2) != 0, -sin, sin)
    return cos, sin


def times(a, b):
    return a[0] * b[0] - a[1] * b[1], a[0] * b[1] + a[1] * b[0]


def pack_kernel(order_ref, vis_ref, pair_ref, slot_ref, u_ref, v_ref, out_ref, label_ref):
    block = vis_ref.shape[1]
    lines = [vis_ref[0:1, :], vis_ref[1:2, :], pair_ref[0:1, :].astype(F32),
             pair_ref[1:2, :].astype(F32), slot_ref[...].astype(F32)]
    for copy in range(out_ref.shape[0]):
        for q, line in enumerate(lines):
            out_ref[copy, :, q * block:(q + 1) * block] = line
    n_lines = u_ref.shape[0]
    at = lax.broadcasted_iota(jnp.int32, (SUB, LANES), 1)
    order = jnp.zeros((SUB, LANES), jnp.int32)
    for b in range(NBLK):
        order = jnp.where(at == b, order_ref[b], order)
    label_ref[:SUB] = order.astype(F32)
    label_ref[SUB:SUB + n_lines] = u_ref[...].astype(F32)
    label_ref[SUB + n_lines:SUB + 2 * n_lines] = v_ref[...].astype(F32)


def pick(row, lane):
    return jnp.take_along_axis(
        jnp.broadcast_to(row, lane.shape), lane, axis=1, mode="promise_in_bounds")


def taper_rows(group, half, wide=LANES):
    index = (lax.broadcasted_iota(jnp.int32, (SUB, wide), 0) + SUB * group).astype(F32)
    return ((half + M - 0.5 - index) * (1.0 / (2 * M)),
            (index - (half - M - 0.5)) * (1.0 / (2 * M)))


def table_kernel(n_frow, n_fcol, first, n_lines, block_ref, cell_ref,
                 s_ref, ac_ref, as_ref, ec_ref, es_ref, fc_ref, fs_ref, cc_ref, cs_ref,
                 q_ref, uv_ref, dr_ref, order_ref, sem):
    frow_at = lax.axis_index("frow")
    fcol_at = lax.axis_index("fcol")
    half_r, half_c = R // 2, C // 2
    mod_r, mod_c = 2 * R * n_frow, 2 * C * n_fcol
    k_tiles = s_ref.shape[1]
    per_block = k_tiles // NBLK
    block = per_block * LANES
    shape = (SUB, LANES)

    copy = pltpu.make_async_copy(cell_ref.at[first:first + SUB, :], order_ref, sem)
    copy.start()
    copy.wait()
    for b in range(NBLK):
        owner = order_ref[0, b].astype(jnp.int32)
        for q in range(5):
            for j in range(per_block):
                q_ref[q, b * per_block + j:b * per_block + j + 1, :] = block_ref[
                    owner, :, q * block + j * LANES:q * block + (j + 1) * LANES]
    a1 = q_ref[2].astype(jnp.int32)
    a2 = q_ref[3].astype(jnp.int32)
    slot = q_ref[4].astype(jnp.int32)

    at = first + SUB

    def cells(table):
        got = [jnp.zeros(shape, F32)] * 2
        for h in range(table.shape[0]):
            row = table[h:h + 1, :]
            got = [jnp.where((a >> 7) == h, pick(row, a & 127), g)
                   for a, g in zip((a1, a2), got)]
        return (got[0] - got[1]).astype(jnp.int32)

    u = cells(cell_ref[at:at + n_lines, :])
    v = cells(cell_ref[at + n_lines:at + 2 * n_lines, :])
    uv_ref[0] = u
    uv_ref[1] = v
    centre = times(turn(u * (frow_at * (2 * R) + (R - 1)), mod_r),
                   turn(v * (fcol_at * (2 * C) + (C - 1)), mod_c))
    scale = 0.5 / math.sqrt(NBLK * per_block * LANES)
    value = times((q_ref[0] * scale, q_ref[1] * scale), centre)
    s_ref[0] = value[0]
    s_ref[1] = value[1]
    for n, a in enumerate((a1, a2)):
        s_ref[2 + n] = ((a >> 3) + (a & 6) * 32).astype(F32)
        s_ref[4 + n] = ((a & 1) * NT + slot).astype(F32)

    iota = lax.broadcasted_iota(jnp.int32, shape, 0)

    def tables(s, carry):
        lane = pl.ds(pl.multiple_of(s * LANES, LANES), LANES)

        def phases(which, modulus, half):
            freq = jnp.broadcast_to(uv_ref[which, pl.ds(s, 1), :], shape)
            fine = turn(freq * (2 * iota + 1), modulus)
            middle = turn(freq * (16 * iota), modulus)
            coarse = turn(freq * (128 * iota), modulus)
            for a in range(half // 64):
                top = tuple(jnp.broadcast_to(x[a:a + 1], shape) for x in coarse)
                both = times(middle, top)
                for comp in range(2):
                    dr_ref[which, comp, 8 * a:8 * a + 8, :] = both[comp]
            for g in range(half // SUB):
                step = tuple(jnp.broadcast_to(dr_ref[which, comp, g:g + 1, :], shape)
                             for comp in range(2))
                yield times(fine, step)

        pairs = {}

        def put(ref, first, group, x):
            key = (id(ref), first)
            if group % 2 == 0:
                pairs[key] = x
            else:
                start = first + SUB * (group - 1)
                ref[start:start + 16, lane] = jnp.concatenate([pairs.pop(key), x], 0).astype(BF16)

        edge = (half_r - M) // SUB
        for g, (cos, sin) in enumerate(phases(0, mod_r, half_r)):
            if g >= edge:
                mine, other = taper_rows(g, half_r)
                at = slice((g - edge) * SUB, (g - edge + 1) * SUB)
                ec_ref[at, lane] = cos * other
                es_ref[at, lane] = sin * other
                cos, sin = cos * mine, sin * mine
            put(ac_ref, 0, g, cos)
            put(as_ref, 0, g, sin)
        for g, (cos, sin) in enumerate(phases(1, mod_c, half_c)):
            put(cc_ref, 0, g, cos)
            put(cs_ref, 0, g, sin)
            at = slice(g * SUB, (g + 1) * SUB)
            fc_ref[at, lane] = cos
            fs_ref[at, lane] = sin
        return carry

    lax.fori_loop(0, k_tiles, tables, 0, unroll=True)


def image_kernel(depth, s_ref, mid_ref, a_ref, b_ref, ac_ref, as_ref, ec_ref, es_ref,
                 fc_ref, fs_ref, cc_ref, cs_ref, image_ref,
                 out_ref, tc_ref, ts_ref, uc_ref, us_ref, gain_ref,
                 m1_ref, m2_ref, g1_ref, g2_ref, sems):
    r_odd = lax.rem(lax.axis_index("frow"), 2) == 1
    c_odd = lax.rem(lax.axis_index("fcol"), 2) == 1
    k_tiles = s_ref.shape[1]
    half = depth // 2
    half_c = C // 2
    places = 2 * NT

    low_lane = lax.broadcasted_iota(jnp.int32, (places, LANES), 1) < LANES // 2
    for f in range(9):
        ref, row = (mid_ref, a_ref, b_ref)[f // 3], f % 3 * depth
        both = jnp.concatenate([ref[pl.ds(row, half, stride=2), :],
                                ref[pl.ds(row + 1, half, stride=2), :]], 0).T
        quarter = [both[i * places:(i + 1) * places] for i in range(4)]
        turned = [pltpu.roll(x, LANES // 2, 1) for x in quarter]
        for t in range(2):
            re = jnp.where(low_lane, quarter[2 * t], turned[2 * t + 1])
            im = jnp.where(low_lane, turned[2 * t], quarter[2 * t + 1])
            for comp, x in enumerate((re, im)):
                at = slice((2 * f + comp) * places, (2 * f + comp + 1) * places)
                high = x.astype(BF16)
                gain_ref[at, t * LANES:(t + 1) * LANES] = high
                gain_ref[at, (t + 2) * LANES:(t + 3) * LANES] = (x - high.astype(F32)).astype(BF16)

    step = 2 if k_tiles % 2 == 0 else 1
    wide = step * LANES
    shape = (SUB, wide)
    line_at = lax.broadcasted_iota(jnp.int32, (2 * depth, wide), 0).astype(F32)
    place_at = line_at[:places]
    zero = jnp.zeros((M, wide), BF16)
    edge_rows = []
    for p in range(k_tiles // step):
        lane = slice(p * wide, (p + 1) * wide)

        def line(q):
            return jnp.concatenate([s_ref[q, p * step + i:p * step + i + 1, :]
                                    for i in range(step)], 1)

        gains = []
        for n in range(2):
            hot = jnp.where(line_at == line(2 + n), 1.0, 0.0).astype(BF16)
            z = jnp.dot(gain_ref[...], jnp.concatenate([hot, hot], 0),
                        preferred_element_type=F32)
            mask = jnp.where(place_at == line(4 + n), 1.0, 0.0)
            gains.append([[jnp.sum(z[(2 * f + comp) * places:(2 * f + comp + 1) * places] * mask,
                                   axis=0, keepdims=True) for comp in range(2)]
                          for f in range(9)])
        value = (line(0), line(1))
        w = []
        for f in range(9):
            (g1r, g1i), (g2r, g2i) = gains[0][f], gains[1][f]
            w.append(times(value, (g1r * g2r + g1i * g2i, g1i * g2r - g1r * g2i)))

        def pick_two(odd, x, y):
            return (tuple(jnp.where(odd, i, j) for i, j in zip(x, y)),
                    tuple(jnp.where(odd, j, i) for i, j in zip(x, y)))

        columns = []
        for c in range(3):
            up, down = pick_two(r_odd, w[3 * c + 1], w[3 * c + 2])
            columns.append((w[3 * c], up, down))
        named = {}
        for r, names in enumerate(((OWN, LEFT, RIGHT), (UP, UL, UR), (DOWN, DL, DR))):
            named[names[0]] = columns[0][r]
            named[names[1]], named[names[2]] = pick_two(c_odd, columns[1][r], columns[2][r])

        def weight(f):
            return tuple(jnp.broadcast_to(x, shape) for x in named[f])

        pairs = {}

        def put(ref, first, group, x):
            key = (id(ref), first)
            if group % 2 == 0:
                pairs[key] = x
            else:
                start = first + SUB * (group - 1)
                ref[start:start + 16, lane] = jnp.concatenate([pairs.pop(key), x], 0).astype(BF16)

        edge = (half_c - M) // SUB
        (wr, wi), (lr, li), (rr, ri) = weight(OWN), weight(LEFT), weight(RIGHT)
        for g in range(half_c // SUB):
            at = slice(g * SUB, (g + 1) * SUB)
            cos, sin = fc_ref[at, lane], fs_ref[at, lane]
            own = (cos, sin)
            if g >= edge:
                mine, other = taper_rows(g, half_c, wide)
                own = (cos * mine, sin * mine)
                cos, sin = cos * other, sin * other
                base = 2 * half_c + M
                put(tc_ref, base, g - edge, lr * cos + li * sin)
                put(ts_ref, base, g - edge, lr * sin - li * cos)
                put(tc_ref, base + 2 * M, g - edge, rr * cos - ri * sin)
                put(ts_ref, base + 2 * M, g - edge, -(rr * sin + ri * cos))
            put(tc_ref, 0, g, wr * own[0])
            put(tc_ref, half_c, g, -wi * own[1])
            put(ts_ref, 0, g, -wi * own[0])
            put(ts_ref, half_c, g, -wr * own[1])
        for ref in (tc_ref, ts_ref):
            ref[2 * half_c:2 * half_c + M, lane] = zero
            ref[2 * half_c + 2 * M:2 * half_c + 3 * M, lane] = zero
        edge_rows.append([named[f] for f in (UP, DOWN, UL, UR, DL, DR)])

    def dot(a, b):
        return lax.dot_general(a, b, (((1,), (1,)), ((), ())), preferred_element_type=F32)

    half_r = R // 2
    part = half_r // 2

    def own_products(i):
        rows = slice(i * part, (i + 1) * part)
        m1_ref[rows, :] = dot(ac_ref[rows, :], tc_ref[...])
        m2_ref[rows, :] = dot(as_ref[rows, :], ts_ref[...])

    own_products(0)
    signs = (-1, 1, -1, -1, 1, 1)
    for p, rows_w in enumerate(edge_rows):
        lane = slice(p * wide, (p + 1) * wide)
        for n, (w, sd) in enumerate(zip(rows_w, signs)):
            wr, wi = [jnp.broadcast_to(x, shape) for x in w]
            for g in range(0, M // SUB, 2):
                tops, lows = [], []
                for i in range(2):
                    at = slice((g + i) * SUB, (g + i + 1) * SUB)
                    cos, sin = ec_ref[at, lane], es_ref[at, lane]
                    tops.append(wr * cos - (sd * wi) * sin)
                    lows.append(-(sd * wr) * sin - wi * cos)
                at = slice(n * M + g * SUB, n * M + (g + 2) * SUB)
                uc_ref[at, lane] = jnp.concatenate(tops, 0).astype(BF16)
                us_ref[at, lane] = jnp.concatenate(lows, 0).astype(BF16)
    g1_ref[...] = dot(uc_ref[...], cc_ref[...])
    g2_ref[...] = dot(us_ref[...], cs_ref[...])

    shape = (SUB, LANES)
    iota = lax.broadcasted_iota(jnp.int32, shape, 0)
    lane_at = lax.broadcasted_iota(jnp.int32, shape, 1)
    back_lane = (LANES - 1) - lane_at
    back_row = (SUB - 1) - iota
    n_lane = half_c // LANES
    edge_c = half_c - M
    edge_r = half_r - M
    col_own, col_other = [], []
    for t in range(n_lane):
        index = (lane_at + t * LANES).astype(F32)
        col_own.append(jnp.minimum((half_c + M - 0.5 - index) * (1.0 / (2 * M)), 1.0))
        col_other.append(jnp.maximum((index - (half_c - M - 0.5)) * (1.0 / (2 * M)), 0.0))

    def flip(x, index, axis):
        return jnp.take_along_axis(x, index, axis=axis, mode="promise_in_bounds")

    def finish(g, edged):
        rows = slice(g * SUB, (g + 1) * SUB)
        for t in range(n_lane):
            def part(ref, which):
                return ref[rows, which * half_c + t * LANES:which * half_c + (t + 1) * LANES]
            p, s_, r, q = part(m1_ref, 0), part(m1_ref, 1), part(m2_ref, 0), part(m2_ref, 1)
            even, odd = p + q, p - q
            plus, minus = r + s_, r - s_
            quad = {(1, 1): even + plus, (-1, -1): even - plus,
                    (1, -1): odd + minus, (-1, 1): odd - minus}
            if (t + 1) * LANES > edge_c:
                base = 2 * half_c
                off = t * LANES - (half_c - LANES)
                for se, start in ((-1, base), (1, base + LANES)):
                    lc = m1_ref[rows, start + off:start + off + LANES]
                    ls = m2_ref[rows, start + off:start + off + LANES]
                    quad[1, se] += lc + ls
                    quad[-1, se] += lc - ls
            if edged:
                def edge(n):
                    at = slice(n * M + g * SUB - edge_r, n * M + (g + 1) * SUB - edge_r)
                    x = g1_ref[at, t * LANES:(t + 1) * LANES]
                    y = g2_ref[at, t * LANES:(t + 1) * LANES]
                    return {1: x + y, -1: x - y}
                for n, sd in ((0, -1), (1, 1)):
                    e = edge(n)
                    for se in (-1, 1):
                        quad[sd, se] += e[se] * col_own[t]
                if (t + 1) * LANES > edge_c:
                    for n, (sd, se) in ((2, (-1, -1)), (3, (-1, 1)), (4, (1, -1)), (5, (1, 1))):
                        quad[sd, se] += edge(n)[se] * col_other[t]
            for (sd, se), x in quad.items():
                if sd < 0:
                    x = flip(x, back_row, 0)
                    at = slice(half_r - SUB - g * SUB, half_r - g * SUB)
                else:
                    at = slice(half_r + g * SUB, half_r + (g + 1) * SUB)
                if se < 0:
                    x = flip(x, back_lane, 1)
                    start = half_c - (t + 1) * LANES
                else:
                    start = half_c + t * LANES
                out_ref[at, start:start + LANES] = x

    group = M // SUB
    n_groups = half_r // M

    def send(j, sign):
        start = half_r + j * M if sign > 0 else half_r - M - j * M
        rows = slice(start, start + M)
        return pltpu.make_async_copy(out_ref.at[rows, :], image_ref.at[rows, :],
                                     sems.at[2 * j + (sign > 0)])

    def run(j, edged):
        for i in range(group):
            finish(j * group + i, edged)
        send(j, 1).start()
        send(j, -1).start()

    own_products(1)
    for j in range(n_groups):
        run(j, j == n_groups - 1)
    for j in range(n_groups):
        send(j, 1).wait()
        send(j, -1).wait()


def swaps(size):
    both = []
    for first in (0, 1):
        pairs = [(i, i + 1) for i in range(first, size - 1, 2)]
        both.append(pairs + [(j, i) for i, j in pairs])
    return both


def shards(vis, station_pairs, visibility_time_slot, station_u_cells, station_v_cells,
           facet_station_gains, holder_device_order):
    n_frow = lax.axis_size("frow")
    n_fcol = lax.axis_size("fcol")
    block = vis.shape[1]
    k_tiles = NBLK * block // LANES
    k = k_tiles * LANES
    half_r, half_c = R // 2, C // 2
    wide = 2 * half_c + 4 * M
    vmem = pl.BlockSpec(memory_space=pltpu.VMEM)
    smem = pl.BlockSpec(memory_space=pltpu.SMEM)

    def lines(x):
        return x.reshape(-1, LANES)

    def shaped(*dims, dtype=F32):
        return jax.ShapeDtypeStruct(dims, dtype)

    def params(mib):
        return pltpu.CompilerParams(vmem_limit_bytes=mib * 1024 * 1024)

    n_lines = station_u_cells.size // LANES
    packed, labels = pl.pallas_call(
        pack_kernel,
        out_shape=[shaped(n_frow * n_fcol, 1, 5 * block), shaped(SUB + 2 * n_lines, LANES)],
        in_specs=[smem] + [vmem] * 5,
        name="pack",
    )(holder_device_order, vis, station_pairs, visibility_time_slot.reshape(1, block),
      lines(station_u_cells), lines(station_v_cells))
    facet_station_gains, packed = lax.optimization_barrier((facet_station_gains, packed))
    gains = facet_station_gains[0, 0]
    depth = gains.size // LANES
    own = gains.reshape(2, -1, LANES).transpose(1, 0, 2).reshape(depth, LANES)
    row_a, row_b = [lax.ppermute(own, "frow", pairs) for pairs in swaps(n_frow)]
    blocks = lax.all_to_all(packed, ("frow", "fcol"), 0, 0)
    mid = jnp.concatenate([own, row_a, row_b, labels], 0)
    col_a, col_b = [lax.ppermute(mid, "fcol", pairs) for pairs in swaps(n_fcol)]
    s, a_cos, a_sin, e_cos, e_sin, f_cos, f_sin, c_cos, c_sin = pl.pallas_call(
        functools.partial(table_kernel, n_frow, n_fcol, 3 * depth, n_lines),
        out_shape=[
            shaped(6, k_tiles, LANES),
            shaped(half_r, k, dtype=BF16), shaped(half_r, k, dtype=BF16),
            shaped(M, k), shaped(M, k),
            shaped(half_c, k), shaped(half_c, k),
            shaped(half_c, k, dtype=BF16), shaped(half_c, k, dtype=BF16),
        ],
        in_specs=[vmem] * 2,
        out_specs=[vmem] * 9,
        scratch_shapes=[
            pltpu.VMEM((5, k_tiles, LANES), F32),
            pltpu.VMEM((2, k_tiles, LANES), jnp.int32),
            pltpu.VMEM((2, 2, half_r // SUB, LANES), F32),
            pltpu.SMEM((SUB, LANES), F32),
            pltpu.SemaphoreType.DMA,
        ],
        compiler_params=params(24),
        name="tables",
    )(blocks, mid)
    return pl.pallas_call(
        functools.partial(image_kernel, depth),
        out_shape=shaped(R, C),
        in_specs=[vmem] * 12,
        out_specs=pl.BlockSpec(memory_space=pl.ANY),
        scratch_shapes=[
            pltpu.VMEM((R, C), F32),
            pltpu.VMEM((wide, k), BF16),
            pltpu.VMEM((wide, k), BF16),
            pltpu.VMEM((6 * M, k), BF16),
            pltpu.VMEM((6 * M, k), BF16),
            pltpu.VMEM((36 * NT, 4 * depth), BF16),
            pltpu.VMEM((half_r, wide), F32),
            pltpu.VMEM((half_r, wide), F32),
            pltpu.VMEM((6 * M, half_c), F32),
            pltpu.VMEM((6 * M, half_c), F32),
            pltpu.SemaphoreType.DMA((2 * half_r // M,)),
        ],
        compiler_params=params(36),
        name="image",
    )(s, mid, col_a, col_b, a_cos, a_sin, e_cos, e_sin, f_cos, f_sin, c_cos, c_sin)


def solution(mesh):
    return jax.shard_map(
        shards,
        mesh=mesh,
        in_specs=(
            P(None, ("frow", "fcol")),
            P(None, ("frow", "fcol")),
            P(("frow", "fcol")),
            P(),
            P(),
            P("frow", "fcol", None, None),
            P(),
        ),
        out_specs=P("frow", "fcol"),
        check_vma=False,
    )
```

```python
import functools
import math

import jax
import jax.numpy as jnp
from jax import lax
from jax.experimental import pallas as pl
from jax.experimental.pallas import tpu as pltpu
from jax.sharding import PartitionSpec as P

R = 1024
C = 512
M = 64
NT = 16
NBLK = 4
LANES = 128
SUB = 8
OWN, LEFT, RIGHT, UP, DOWN, UL, UR, DL, DR = range(9)
F32 = jnp.float32
BF16 = jnp.bfloat16


def wrap(m, modulus):
    if modulus & (modulus - 1) == 0:
        return m & (modulus - 1)
    return jnp.remainder(m, modulus)


def turn(m, modulus):
    m = wrap(m, modulus)
    quarter = modulus // 4
    q = (m + modulus // 8) // quarter if quarter & (quarter - 1) else (
        (m + modulus // 8) >> (quarter.bit_length() - 1))
    x = (m - q * quarter).astype(F32) * (2.0 * math.pi / modulus)
    x2 = x * x
    s = x + x * x2 * (-1 / 6 + x2 * (1 / 120 + x2 * (-1 / 5040 + x2 * (1 / 362880))))
    c = 1.0 + x2 * (-0.5 + x2 * (1 / 24 + x2 * (-1 / 720 + x2 * (1 / 40320))))
    odd = (q & 1) == 1
    cos = jnp.where(odd, s, c)
    sin = jnp.where(odd, c, s)
    cos = jnp.where(((q + 1) & 2) != 0, -cos, cos)
    sin = jnp.where((q & 2) != 0, -sin, sin)
    return cos, sin


def times(a, b):
    return a[0] * b[0] - a[1] * b[1], a[0] * b[1] + a[1] * b[0]


def pack_kernel(order_ref, vis_ref, pair_ref, slot_ref, u_ref, v_ref, out_ref, label_ref):
    block = vis_ref.shape[1]
    lines = [vis_ref[0:1, :], vis_ref[1:2, :], pair_ref[0:1, :].astype(F32),
             pair_ref[1:2, :].astype(F32), slot_ref[...].astype(F32)]
    for copy in range(out_ref.shape[0]):
        for q, line in enumerate(lines):
            out_ref[copy, :, q * block:(q + 1) * block] = line
    n_lines = u_ref.shape[0]
    at = lax.broadcasted_iota(jnp.int32, (SUB, LANES), 1)
    order = jnp.zeros((SUB, LANES), jnp.int32)
    for b in range(NBLK):
        order = jnp.where(at == b, order_ref[b], order)
    label_ref[:SUB] = order.astype(F32)
    label_ref[SUB:SUB + n_lines] = u_ref[...].astype(F32)
    label_ref[SUB + n_lines:SUB + 2 * n_lines] = v_ref[...].astype(F32)


def pick(row, lane):
    return jnp.take_along_axis(
        jnp.broadcast_to(row, lane.shape), lane, axis=1, mode="promise_in_bounds")


def taper_rows(group, half, wide=LANES):
    index = (lax.broadcasted_iota(jnp.int32, (SUB, wide), 0) + SUB * group).astype(F32)
    return ((half + M - 0.5 - index) * (1.0 / (2 * M)),
            (index - (half - M - 0.5)) * (1.0 / (2 * M)))


def table_kernel(n_frow, n_fcol, first, n_lines, block_ref, cell_ref,
                 s_ref, ac_ref, as_ref, ec_ref, es_ref, fc_ref, fs_ref, cc_ref, cs_ref,
                 q_ref, uv_ref, dr_ref, order_ref, sem):
    frow_at = lax.axis_index("frow")
    fcol_at = lax.axis_index("fcol")
    half_r, half_c = R // 2, C // 2
    mod_r, mod_c = 2 * R * n_frow, 2 * C * n_fcol
    k_tiles = s_ref.shape[1]
    per_block = k_tiles // NBLK
    block = per_block * LANES
    shape = (SUB, LANES)

    copy = pltpu.make_async_copy(cell_ref.at[first:first + SUB, :], order_ref, sem)
    copy.start()
    copy.wait()
    for b in range(NBLK):
        owner = order_ref[0, b].astype(jnp.int32)
        for q in range(5):
            for j in range(per_block):
                q_ref[q, b * per_block + j:b * per_block + j + 1, :] = block_ref[
                    owner, :, q * block + j * LANES:q * block + (j + 1) * LANES]
    a1 = q_ref[2].astype(jnp.int32)
    a2 = q_ref[3].astype(jnp.int32)
    slot = q_ref[4].astype(jnp.int32)

    at = first + SUB

    def cells(table):
        got = [jnp.zeros(shape, F32)] * 2
        for h in range(table.shape[0]):
            row = table[h:h + 1, :]
            got = [jnp.where((a >> 7) == h, pick(row, a & 127), g)
                   for a, g in zip((a1, a2), got)]
        return (got[0] - got[1]).astype(jnp.int32)

    u = cells(cell_ref[at:at + n_lines, :])
    v = cells(cell_ref[at + n_lines:at + 2 * n_lines, :])
    uv_ref[0] = u
    uv_ref[1] = v
    centre = times(turn(u * (frow_at * (2 * R) + (R - 1)), mod_r),
                   turn(v * (fcol_at * (2 * C) + (C - 1)), mod_c))
    scale = 0.5 / math.sqrt(NBLK * per_block * LANES)
    value = times((q_ref[0] * scale, q_ref[1] * scale), centre)
    s_ref[0] = value[0]
    s_ref[1] = value[1]
    for n, a in enumerate((a1, a2)):
        s_ref[2 + n] = ((a >> 3) + (a & 6) * 32).astype(F32)
        s_ref[4 + n] = ((a & 1) * NT + slot).astype(F32)

    iota = lax.broadcasted_iota(jnp.int32, shape, 0)

    def tables(s, carry):
        lane = pl.ds(pl.multiple_of(s * LANES, LANES), LANES)

        def phases(which, modulus, half):
            freq = jnp.broadcast_to(uv_ref[which, pl.ds(s, 1), :], shape)
            fine = turn(freq * (2 * iota + 1), modulus)
            middle = turn(freq * (16 * iota), modulus)
            coarse = turn(freq * (128 * iota), modulus)
            for a in range(half // 64):
                top = tuple(jnp.broadcast_to(x[a:a + 1], shape) for x in coarse)
                both = times(middle, top)
                for comp in range(2):
                    dr_ref[which, comp, 8 * a:8 * a + 8, :] = both[comp]
            for g in range(half // SUB):
                step = tuple(jnp.broadcast_to(dr_ref[which, comp, g:g + 1, :], shape)
                             for comp in range(2))
                yield times(fine, step)

        pairs = {}

        def put(ref, first, group, x):
            key = (id(ref), first)
            if group % 2 == 0:
                pairs[key] = x
            else:
                start = first + SUB * (group - 1)
                ref[start:start + 16, lane] = jnp.concatenate([pairs.pop(key), x], 0).astype(BF16)

        edge = (half_r - M) // SUB
        for g, (cos, sin) in enumerate(phases(0, mod_r, half_r)):
            if g >= edge:
                mine, other = taper_rows(g, half_r)
                at = slice((g - edge) * SUB, (g - edge + 1) * SUB)
                ec_ref[at, lane] = cos * other
                es_ref[at, lane] = sin * other
                cos, sin = cos * mine, sin * mine
            put(ac_ref, 0, g, cos)
            put(as_ref, 0, g, sin)
        for g, (cos, sin) in enumerate(phases(1, mod_c, half_c)):
            put(cc_ref, 0, g, cos)
            put(cs_ref, 0, g, sin)
            at = slice(g * SUB, (g + 1) * SUB)
            fc_ref[at, lane] = cos
            fs_ref[at, lane] = sin
        return carry

    lax.fori_loop(0, k_tiles, tables, 0, unroll=True)


def image_kernel(depth, s_ref, mid_ref, a_ref, b_ref, ac_ref, as_ref, ec_ref, es_ref,
                 fc_ref, fs_ref, cc_ref, cs_ref, image_ref,
                 out_ref, tc_ref, ts_ref, uc_ref, us_ref, gain_ref,
                 m1_ref, m2_ref, g1_ref, g2_ref, sems):
    r_odd = lax.rem(lax.axis_index("frow"), 2) == 1
    c_odd = lax.rem(lax.axis_index("fcol"), 2) == 1
    k_tiles = s_ref.shape[1]
    half = depth // 2
    half_c = C // 2
    places = 2 * NT

    low_lane = lax.broadcasted_iota(jnp.int32, (places, LANES), 1) < LANES // 2
    for f in range(9):
        ref, row = (mid_ref, a_ref, b_ref)[f // 3], f % 3 * depth
        both = jnp.concatenate([ref[pl.ds(row, half, stride=2), :],
                                ref[pl.ds(row + 1, half, stride=2), :]], 0).T
        quarter = [both[i * places:(i + 1) * places] for i in range(4)]
        turned = [pltpu.roll(x, LANES // 2, 1) for x in quarter]
        for t in range(2):
            re = jnp.where(low_lane, quarter[2 * t], turned[2 * t + 1])
            im = jnp.where(low_lane, turned[2 * t], quarter[2 * t + 1])
            for comp, x in enumerate((re, im)):
                at = slice((2 * f + comp) * places, (2 * f + comp + 1) * places)
                high = x.astype(BF16)
                gain_ref[at, t * LANES:(t + 1) * LANES] = high
                gain_ref[at, (t + 2) * LANES:(t + 3) * LANES] = (x - high.astype(F32)).astype(BF16)

    step = 2 if k_tiles % 2 == 0 else 1
    wide = step * LANES
    shape = (SUB, wide)
    line_at = lax.broadcasted_iota(jnp.int32, (2 * depth, wide), 0).astype(F32)
    place_at = line_at[:places]
    zero = jnp.zeros((M, wide), BF16)
    edge_rows = []
    for p in range(k_tiles // step):
        lane = slice(p * wide, (p + 1) * wide)

        def line(q):
            return jnp.concatenate([s_ref[q, p * step + i:p * step + i + 1, :]
                                    for i in range(step)], 1)

        gains = []
        for n in range(2):
            hot = jnp.where(line_at == line(2 + n), 1.0, 0.0).astype(BF16)
            z = jnp.dot(gain_ref[...], jnp.concatenate([hot, hot], 0),
                        preferred_element_type=F32)
            mask = jnp.where(place_at == line(4 + n), 1.0, 0.0)
            gains.append([[jnp.sum(z[(2 * f + comp) * places:(2 * f + comp + 1) * places] * mask,
                                   axis=0, keepdims=True) for comp in range(2)]
                          for f in range(9)])
        value = (line(0), line(1))
        w = []
        for f in range(9):
            (g1r, g1i), (g2r, g2i) = gains[0][f], gains[1][f]
            w.append(times(value, (g1r * g2r + g1i * g2i, g1i * g2r - g1r * g2i)))

        def pick_two(odd, x, y):
            return (tuple(jnp.where(odd, i, j) for i, j in zip(x, y)),
                    tuple(jnp.where(odd, j, i) for i, j in zip(x, y)))

        columns = []
        for c in range(3):
            up, down = pick_two(r_odd, w[3 * c + 1], w[3 * c + 2])
            columns.append((w[3 * c], up, down))
        named = {}
        for r, names in enumerate(((OWN, LEFT, RIGHT), (UP, UL, UR), (DOWN, DL, DR))):
            named[names[0]] = columns[0][r]
            named[names[1]], named[names[2]] = pick_two(c_odd, columns[1][r], columns[2][r])

        def weight(f):
            return tuple(jnp.broadcast_to(x, shape) for x in named[f])

        pairs = {}

        def put(ref, first, group, x):
            key = (id(ref), first)
            if group % 2 == 0:
                pairs[key] = x
            else:
                start = first + SUB * (group - 1)
                ref[start:start + 16, lane] = jnp.concatenate([pairs.pop(key), x], 0).astype(BF16)

        edge = (half_c - M) // SUB
        (wr, wi), (lr, li), (rr, ri) = weight(OWN), weight(LEFT), weight(RIGHT)
        for g in range(half_c // SUB):
            at = slice(g * SUB, (g + 1) * SUB)
            cos, sin = fc_ref[at, lane], fs_ref[at, lane]
            own = (cos, sin)
            if g >= edge:
                mine, other = taper_rows(g, half_c, wide)
                own = (cos * mine, sin * mine)
                cos, sin = cos * other, sin * other
                base = 2 * half_c + M
                put(tc_ref, base, g - edge, lr * cos + li * sin)
                put(ts_ref, base, g - edge, lr * sin - li * cos)
                put(tc_ref, base + 2 * M, g - edge, rr * cos - ri * sin)
                put(ts_ref, base + 2 * M, g - edge, -(rr * sin + ri * cos))
            base = g * SUB // LANES * LANES
            put(tc_ref, base, g, wr * own[0])
            put(tc_ref, base + LANES, g, -wi * own[1])
            put(ts_ref, base, g, -wi * own[0])
            put(ts_ref, base + LANES, g, -wr * own[1])
        for ref in (tc_ref, ts_ref):
            ref[2 * half_c:2 * half_c + M, lane] = zero
            ref[2 * half_c + 2 * M:2 * half_c + 3 * M, lane] = zero
        edge_rows.append([named[f] for f in (UP, DOWN, UL, UR, DL, DR)])

    def dot(a, b):
        return lax.dot_general(a, b, (((1,), (1,)), ((), ())), preferred_element_type=F32)

    half_r = R // 2
    n_lane = half_c // LANES

    def own_products(t):
        cols = slice(2 * t * LANES, 2 * (t + 1) * LANES if t < n_lane - 1 else tc_ref.shape[0])
        m1_ref[:, cols] = dot(ac_ref[...], tc_ref[cols, :])
        m2_ref[:, cols] = dot(as_ref[...], ts_ref[cols, :])

    own_products(0)
    signs = (-1, 1, -1, -1, 1, 1)
    for p, rows_w in enumerate(edge_rows):
        lane = slice(p * wide, (p + 1) * wide)
        for n, (w, sd) in enumerate(zip(rows_w, signs)):
            wr, wi = [jnp.broadcast_to(x, shape) for x in w]
            for g in range(0, M // SUB, 2):
                tops, lows = [], []
                for i in range(2):
                    at = slice((g + i) * SUB, (g + i + 1) * SUB)
                    cos, sin = ec_ref[at, lane], es_ref[at, lane]
                    tops.append(wr * cos - (sd * wi) * sin)
                    lows.append(-(sd * wr) * sin - wi * cos)
                at = slice(n * M + g * SUB, n * M + (g + 2) * SUB)
                uc_ref[at, lane] = jnp.concatenate(tops, 0).astype(BF16)
                us_ref[at, lane] = jnp.concatenate(lows, 0).astype(BF16)
    g1_ref[...] = dot(uc_ref[...], cc_ref[...])
    g2_ref[...] = dot(us_ref[...], cs_ref[...])

    shape = (SUB, LANES)
    iota = lax.broadcasted_iota(jnp.int32, shape, 0)
    lane_at = lax.broadcasted_iota(jnp.int32, shape, 1)
    back_lane = (LANES - 1) - lane_at
    back_row = (SUB - 1) - iota
    edge_c = half_c - M
    edge_r = half_r - M
    col_own, col_other = [], []
    for t in range(n_lane):
        index = (lane_at + t * LANES).astype(F32)
        col_own.append(jnp.minimum((half_c + M - 0.5 - index) * (1.0 / (2 * M)), 1.0))
        col_other.append(jnp.maximum((index - (half_c - M - 0.5)) * (1.0 / (2 * M)), 0.0))

    def flip(x, index, axis):
        return jnp.take_along_axis(x, index, axis=axis, mode="promise_in_bounds")

    def finish(g, t, edged):
        rows = slice(g * SUB, (g + 1) * SUB)
        def part(ref, which):
            return ref[rows, (2 * t + which) * LANES:(2 * t + which + 1) * LANES]
        p, s_, r, q = part(m1_ref, 0), part(m1_ref, 1), part(m2_ref, 0), part(m2_ref, 1)
        even, odd = p + q, p - q
        plus, minus = r + s_, r - s_
        quad = {(1, 1): even + plus, (-1, -1): even - plus,
                (1, -1): odd + minus, (-1, 1): odd - minus}
        if (t + 1) * LANES > edge_c:
            base = 2 * half_c
            off = t * LANES - (half_c - LANES)
            for se, start in ((-1, base), (1, base + LANES)):
                lc = m1_ref[rows, start + off:start + off + LANES]
                ls = m2_ref[rows, start + off:start + off + LANES]
                quad[1, se] += lc + ls
                quad[-1, se] += lc - ls
        if edged:
            def edge(n):
                at = slice(n * M + g * SUB - edge_r, n * M + (g + 1) * SUB - edge_r)
                x = g1_ref[at, t * LANES:(t + 1) * LANES]
                y = g2_ref[at, t * LANES:(t + 1) * LANES]
                return {1: x + y, -1: x - y}
            for n, sd in ((0, -1), (1, 1)):
                e = edge(n)
                for se in (-1, 1):
                    quad[sd, se] += e[se] * col_own[t]
            if (t + 1) * LANES > edge_c:
                for n, (sd, se) in ((2, (-1, -1)), (3, (-1, 1)), (4, (1, -1)), (5, (1, 1))):
                    quad[sd, se] += edge(n)[se] * col_other[t]
        for (sd, se), x in quad.items():
            if sd < 0:
                x = flip(x, back_row, 0)
                at = slice(half_r - SUB - g * SUB, half_r - g * SUB)
            else:
                at = slice(half_r + g * SUB, half_r + (g + 1) * SUB)
            if se < 0:
                x = flip(x, back_lane, 1)
                start = half_c - (t + 1) * LANES
            else:
                start = half_c + t * LANES
            out_ref[at, start:start + LANES] = x

    n_groups = half_r // M

    def sends(j, t):
        copies = []
        for row in (half_r + 2 * M * j, half_r - 2 * M * (j + 1)):
            for col in (half_c + t * LANES, half_c - (t + 1) * LANES):
                at = (slice(row, row + 2 * M), slice(col, col + LANES))
                copies.append(pltpu.make_async_copy(
                    out_ref.at[at], image_ref.at[at], sems.at[(j * n_lane + t) * 4 + len(copies)]))
        return copies

    for t in range(1, n_lane):
        own_products(t)
    for t in range(n_lane):
        for j in range(n_groups):
            for g in range(j * M // SUB, (j + 1) * M // SUB):
                finish(g, t, j == n_groups - 1)
            if j % 2:
                for copy in sends(j // 2, t):
                    copy.start()
    for t in range(n_lane):
        for j in range(n_groups // 2):
            for copy in sends(j, t):
                copy.wait()


def swaps(size):
    both = []
    for first in (0, 1):
        pairs = [(i, i + 1) for i in range(first, size - 1, 2)]
        both.append(pairs + [(j, i) for i, j in pairs])
    return both


def shards(vis, station_pairs, visibility_time_slot, station_u_cells, station_v_cells,
           facet_station_gains, holder_device_order):
    n_frow = lax.axis_size("frow")
    n_fcol = lax.axis_size("fcol")
    block = vis.shape[1]
    k_tiles = NBLK * block // LANES
    k = k_tiles * LANES
    half_r, half_c = R // 2, C // 2
    wide = 2 * half_c + 4 * M
    vmem = pl.BlockSpec(memory_space=pltpu.VMEM)
    smem = pl.BlockSpec(memory_space=pltpu.SMEM)

    def lines(x):
        return x.reshape(-1, LANES)

    def shaped(*dims, dtype=F32):
        return jax.ShapeDtypeStruct(dims, dtype)

    def params(mib):
        return pltpu.CompilerParams(vmem_limit_bytes=mib * 1024 * 1024)

    n_lines = station_u_cells.size // LANES
    packed, labels = pl.pallas_call(
        pack_kernel,
        out_shape=[shaped(n_frow * n_fcol, 1, 5 * block), shaped(SUB + 2 * n_lines, LANES)],
        in_specs=[smem] + [vmem] * 5,
        name="pack",
    )(holder_device_order, vis, station_pairs, visibility_time_slot.reshape(1, block),
      lines(station_u_cells), lines(station_v_cells))
    facet_station_gains, packed = lax.optimization_barrier((facet_station_gains, packed))
    gains = facet_station_gains[0, 0]
    depth = gains.size // LANES
    own = gains.reshape(2, -1, LANES).transpose(1, 0, 2).reshape(depth, LANES)
    row_a, row_b = [lax.ppermute(own, "frow", pairs) for pairs in swaps(n_frow)]
    blocks = lax.all_to_all(packed, ("frow", "fcol"), 0, 0)
    mid = jnp.concatenate([own, row_a, row_b, labels], 0)
    col_a, col_b = [lax.ppermute(mid, "fcol", pairs) for pairs in swaps(n_fcol)]
    s, a_cos, a_sin, e_cos, e_sin, f_cos, f_sin, c_cos, c_sin = pl.pallas_call(
        functools.partial(table_kernel, n_frow, n_fcol, 3 * depth, n_lines),
        out_shape=[
            shaped(6, k_tiles, LANES),
            shaped(half_r, k, dtype=BF16), shaped(half_r, k, dtype=BF16),
            shaped(M, k), shaped(M, k),
            shaped(half_c, k), shaped(half_c, k),
            shaped(half_c, k, dtype=BF16), shaped(half_c, k, dtype=BF16),
        ],
        in_specs=[vmem] * 2,
        out_specs=[vmem] * 9,
        scratch_shapes=[
            pltpu.VMEM((5, k_tiles, LANES), F32),
            pltpu.VMEM((2, k_tiles, LANES), jnp.int32),
            pltpu.VMEM((2, 2, half_r // SUB, LANES), F32),
            pltpu.SMEM((SUB, LANES), F32),
            pltpu.SemaphoreType.DMA,
        ],
        compiler_params=params(24),
        name="tables",
    )(blocks, mid)
    return pl.pallas_call(
        functools.partial(image_kernel, depth),
        out_shape=shaped(R, C),
        in_specs=[vmem] * 12,
        out_specs=pl.BlockSpec(memory_space=pl.ANY),
        scratch_shapes=[
            pltpu.VMEM((R, C), F32),
            pltpu.VMEM((wide, k), BF16),
            pltpu.VMEM((wide, k), BF16),
            pltpu.VMEM((6 * M, k), BF16),
            pltpu.VMEM((6 * M, k), BF16),
            pltpu.VMEM((36 * NT, 4 * depth), BF16),
            pltpu.VMEM((half_r, wide), F32),
            pltpu.VMEM((half_r, wide), F32),
            pltpu.VMEM((6 * M, half_c), F32),
            pltpu.VMEM((6 * M, half_c), F32),
            pltpu.SemaphoreType.DMA((2 * half_r // M * (half_c // LANES),)),
        ],
        compiler_params=params(36),
        name="image",
    )(s, mid, col_a, col_b, a_cos, a_sin, e_cos, e_sin, f_cos, f_sin, c_cos, c_sin)


def solution(mesh):
    return jax.shard_map(
        shards,
        mesh=mesh,
        in_specs=(
            P(None, ("frow", "fcol")),
            P(None, ("frow", "fcol")),
            P(("frow", "fcol")),
            P(),
            P(),
            P("frow", "fcol", None, None),
            P(),
        ),
        out_specs=P("frow", "fcol"),
        check_vma=False,
    )
```

```python
import functools
import math

import jax
import jax.numpy as jnp
from jax import lax
from jax.experimental import pallas as pl
from jax.experimental.pallas import tpu as pltpu
from jax.sharding import PartitionSpec as P

R = 1024
C = 512
M = 64
NT = 16
NBLK = 4
LANES = 128
SUB = 8
OWN, LEFT, RIGHT, UP, DOWN, UL, UR, DL, DR = range(9)
F32 = jnp.float32
BF16 = jnp.bfloat16


def wrap(m, modulus):
    if modulus & (modulus - 1) == 0:
        return m & (modulus - 1)
    return jnp.remainder(m, modulus)


def turn(m, modulus):
    m = wrap(m, modulus)
    quarter = modulus // 4
    q = (m + modulus // 8) // quarter if quarter & (quarter - 1) else (
        (m + modulus // 8) >> (quarter.bit_length() - 1))
    x = (m - q * quarter).astype(F32) * (2.0 * math.pi / modulus)
    x2 = x * x
    s = x + x * x2 * (-1 / 6 + x2 * (1 / 120 + x2 * (-1 / 5040 + x2 * (1 / 362880))))
    c = 1.0 + x2 * (-0.5 + x2 * (1 / 24 + x2 * (-1 / 720 + x2 * (1 / 40320))))
    odd = (q & 1) == 1
    cos = jnp.where(odd, s, c)
    sin = jnp.where(odd, c, s)
    cos = jnp.where(((q + 1) & 2) != 0, -cos, cos)
    sin = jnp.where((q & 2) != 0, -sin, sin)
    return cos, sin


def times(a, b):
    return a[0] * b[0] - a[1] * b[1], a[0] * b[1] + a[1] * b[0]


def pack_kernel(order_ref, vis_ref, pair_ref, slot_ref, u_ref, v_ref, out_ref, label_ref):
    block = vis_ref.shape[1]
    lines = [vis_ref[0:1, :], vis_ref[1:2, :], pair_ref[0:1, :].astype(F32),
             pair_ref[1:2, :].astype(F32), slot_ref[...].astype(F32)]
    for copy in range(out_ref.shape[0]):
        for q, line in enumerate(lines):
            out_ref[copy, :, q * block:(q + 1) * block] = line
    n_lines = u_ref.shape[0]
    at = lax.broadcasted_iota(jnp.int32, (SUB, LANES), 1)
    order = jnp.zeros((SUB, LANES), jnp.int32)
    for b in range(NBLK):
        order = jnp.where(at == b, order_ref[b], order)
    label_ref[:SUB] = order.astype(F32)
    label_ref[SUB:SUB + n_lines] = u_ref[...].astype(F32)
    label_ref[SUB + n_lines:SUB + 2 * n_lines] = v_ref[...].astype(F32)


def pick(row, lane):
    return jnp.take_along_axis(
        jnp.broadcast_to(row, lane.shape), lane, axis=1, mode="promise_in_bounds")


def taper_rows(group, half, wide=LANES):
    index = (lax.broadcasted_iota(jnp.int32, (SUB, wide), 0) + SUB * group).astype(F32)
    return ((half + M - 0.5 - index) * (1.0 / (2 * M)),
            (index - (half - M - 0.5)) * (1.0 / (2 * M)))


def table_kernel(n_frow, n_fcol, first, n_lines, block_ref, other_ref, cell_ref,
                 s_ref, ac_ref, as_ref, ec_ref, es_ref, fc_ref, fs_ref, cc_ref, cs_ref,
                 q_ref, uv_ref, dr_ref):
    frow_at = lax.axis_index("frow")
    fcol_at = lax.axis_index("fcol")
    half_r, half_c = R // 2, C // 2
    mod_r, mod_c = 2 * R * n_frow, 2 * C * n_fcol
    k_tiles = s_ref.shape[1]
    per_block = k_tiles // NBLK
    block = per_block * LANES
    shape = (SUB, LANES)

    order = cell_ref[first:first + 1, :]
    place = lax.broadcasted_iota(jnp.int32, (1, LANES), 1)
    owners = [jnp.sum(jnp.where(place == b, order, 0.0)).astype(jnp.int32) for b in range(NBLK)]
    for b, owner in enumerate(owners):
        mine = lax.rem(owner, 2) == lax.rem(fcol_at, 2)
        at = owner // 2
        for q in range(5):
            for j in range(per_block):
                lane = slice(q * block + j * LANES, q * block + (j + 1) * LANES)
                q_ref[q, b * per_block + j:b * per_block + j + 1, :] = jnp.where(
                    mine, block_ref[at, :, lane], other_ref[at, :, lane])
    a1 = q_ref[2].astype(jnp.int32)
    a2 = q_ref[3].astype(jnp.int32)
    slot = q_ref[4].astype(jnp.int32)

    at = first + SUB

    def cells(table):
        got = [jnp.zeros(shape, F32)] * 2
        for h in range(table.shape[0]):
            row = table[h:h + 1, :]
            got = [jnp.where((a >> 7) == h, pick(row, a & 127), g)
                   for a, g in zip((a1, a2), got)]
        return (got[0] - got[1]).astype(jnp.int32)

    u = cells(cell_ref[at:at + n_lines, :])
    v = cells(cell_ref[at + n_lines:at + 2 * n_lines, :])
    uv_ref[0] = u
    uv_ref[1] = v
    centre = times(turn(u * (frow_at * (2 * R) + (R - 1)), mod_r),
                   turn(v * (fcol_at * (2 * C) + (C - 1)), mod_c))
    scale = 0.5 / math.sqrt(NBLK * per_block * LANES)
    value = times((q_ref[0] * scale, q_ref[1] * scale), centre)
    s_ref[0] = value[0]
    s_ref[1] = value[1]
    for n, a in enumerate((a1, a2)):
        s_ref[2 + n] = ((a >> 3) + (a & 6) * 32).astype(F32)
        s_ref[4 + n] = ((a & 1) * NT + slot).astype(F32)

    iota = lax.broadcasted_iota(jnp.int32, shape, 0)

    def tables(s, carry):
        lane = pl.ds(pl.multiple_of(s * LANES, LANES), LANES)

        def phases(which, modulus, half):
            freq = jnp.broadcast_to(uv_ref[which, pl.ds(s, 1), :], shape)
            fine = turn(freq * (2 * iota + 1), modulus)
            middle = turn(freq * (16 * iota), modulus)
            coarse = turn(freq * (128 * iota), modulus)
            for a in range(half // 64):
                top = tuple(jnp.broadcast_to(x[a:a + 1], shape) for x in coarse)
                both = times(middle, top)
                for comp in range(2):
                    dr_ref[which, comp, 8 * a:8 * a + 8, :] = both[comp]
            for g in range(half // SUB):
                step = tuple(jnp.broadcast_to(dr_ref[which, comp, g:g + 1, :], shape)
                             for comp in range(2))
                yield times(fine, step)

        pairs = {}

        def put(ref, first, group, x):
            key = (id(ref), first)
            if group % 2 == 0:
                pairs[key] = x
            else:
                start = first + SUB * (group - 1)
                ref[start:start + 16, lane] = jnp.concatenate([pairs.pop(key), x], 0).astype(BF16)

        edge = (half_r - M) // SUB
        for g, (cos, sin) in enumerate(phases(0, mod_r, half_r)):
            if g >= edge:
                mine, other = taper_rows(g, half_r)
                at = slice((g - edge) * SUB, (g - edge + 1) * SUB)
                ec_ref[at, lane] = cos * other
                es_ref[at, lane] = sin * other
                cos, sin = cos * mine, sin * mine
            put(ac_ref, 0, g, cos)
            put(as_ref, 0, g, sin)
        for g, (cos, sin) in enumerate(phases(1, mod_c, half_c)):
            put(cc_ref, 0, g, cos)
            put(cs_ref, 0, g, sin)
            at = slice(g * SUB, (g + 1) * SUB)
            fc_ref[at, lane] = cos
            fs_ref[at, lane] = sin
        return carry

    lax.fori_loop(0, k_tiles, tables, 0, unroll=True)


def image_kernel(depth, s_ref, mid_ref, a_ref, b_ref, ac_ref, as_ref, ec_ref, es_ref,
                 fc_ref, fs_ref, cc_ref, cs_ref, image_ref,
                 out_ref, tc_ref, ts_ref, uc_ref, us_ref, gain_ref,
                 m1_ref, m2_ref, g1_ref, g2_ref, sems):
    r_odd = lax.rem(lax.axis_index("frow"), 2) == 1
    c_odd = lax.rem(lax.axis_index("fcol"), 2) == 1
    k_tiles = s_ref.shape[1]
    half = depth // 2
    half_c = C // 2
    places = 2 * NT

    low_lane = lax.broadcasted_iota(jnp.int32, (places, LANES), 1) < LANES // 2
    for f in range(9):
        ref, row = (mid_ref, a_ref, b_ref)[f // 3], f % 3 * depth
        both = jnp.concatenate([ref[pl.ds(row, half, stride=2), :],
                                ref[pl.ds(row + 1, half, stride=2), :]], 0).T
        quarter = [both[i * places:(i + 1) * places] for i in range(4)]
        turned = [pltpu.roll(x, LANES // 2, 1) for x in quarter]
        for t in range(2):
            re = jnp.where(low_lane, quarter[2 * t], turned[2 * t + 1])
            im = jnp.where(low_lane, turned[2 * t], quarter[2 * t + 1])
            for comp, x in enumerate((re, im)):
                at = slice((2 * f + comp) * places, (2 * f + comp + 1) * places)
                high = x.astype(BF16)
                gain_ref[at, t * LANES:(t + 1) * LANES] = high
                gain_ref[at, (t + 2) * LANES:(t + 3) * LANES] = (x - high.astype(F32)).astype(BF16)

    step = 2 if k_tiles % 2 == 0 else 1
    wide = step * LANES
    shape = (SUB, wide)
    line_at = lax.broadcasted_iota(jnp.int32, (2 * depth, wide), 0).astype(F32)
    place_at = line_at[:places]
    zero = jnp.zeros((M, wide), BF16)
    edge_rows = []
    half_r = R // 2
    n_lane = half_c // LANES

    def dot(a, b):
        return lax.dot_general(a, b, (((1,), (1,)), ((), ())), preferred_element_type=F32)

    def own_products(t, first):
        cols = slice(2 * t * LANES, 2 * (t + 1) * LANES if t < n_lane - 1 else tc_ref.shape[0])
        k = tc_ref.shape[1]
        ks = slice(0, k // 2) if first else slice(k // 2, k)
        for m_ref, rows, table in ((m1_ref, ac_ref, tc_ref), (m2_ref, as_ref, ts_ref)):
            x = dot(rows[:, ks], table[cols, ks])
            m_ref[:, cols] = x if first else m_ref[:, cols] + x

    steps = k_tiles // step
    for p in range(steps):
        if p == steps // 2:
            for t in range(n_lane):
                own_products(t, True)
        lane = slice(p * wide, (p + 1) * wide)

        def line(q):
            return jnp.concatenate([s_ref[q, p * step + i:p * step + i + 1, :]
                                    for i in range(step)], 1)

        gains = []
        for n in range(2):
            hot = jnp.where(line_at == line(2 + n), 1.0, 0.0).astype(BF16)
            z = jnp.dot(gain_ref[...], jnp.concatenate([hot, hot], 0),
                        preferred_element_type=F32)
            mask = jnp.where(place_at == line(4 + n), 1.0, 0.0)
            gains.append([[jnp.sum(z[(2 * f + comp) * places:(2 * f + comp + 1) * places] * mask,
                                   axis=0, keepdims=True) for comp in range(2)]
                          for f in range(9)])
        value = (line(0), line(1))
        w = []
        for f in range(9):
            (g1r, g1i), (g2r, g2i) = gains[0][f], gains[1][f]
            w.append(times(value, (g1r * g2r + g1i * g2i, g1i * g2r - g1r * g2i)))

        def pick_two(odd, x, y):
            return (tuple(jnp.where(odd, i, j) for i, j in zip(x, y)),
                    tuple(jnp.where(odd, j, i) for i, j in zip(x, y)))

        columns = []
        for c in range(3):
            up, down = pick_two(r_odd, w[3 * c + 1], w[3 * c + 2])
            columns.append((w[3 * c], up, down))
        named = {}
        for r, names in enumerate(((OWN, LEFT, RIGHT), (UP, UL, UR), (DOWN, DL, DR))):
            named[names[0]] = columns[0][r]
            named[names[1]], named[names[2]] = pick_two(c_odd, columns[1][r], columns[2][r])

        def weight(f):
            return tuple(jnp.broadcast_to(x, shape) for x in named[f])

        pairs = {}

        def put(ref, first, group, x):
            key = (id(ref), first)
            if group % 2 == 0:
                pairs[key] = x
            else:
                start = first + SUB * (group - 1)
                ref[start:start + 16, lane] = jnp.concatenate([pairs.pop(key), x], 0).astype(BF16)

        edge = (half_c - M) // SUB
        (wr, wi), (lr, li), (rr, ri) = weight(OWN), weight(LEFT), weight(RIGHT)
        for g in range(half_c // SUB):
            at = slice(g * SUB, (g + 1) * SUB)
            cos, sin = fc_ref[at, lane], fs_ref[at, lane]
            own = (cos, sin)
            if g >= edge:
                mine, other = taper_rows(g, half_c, wide)
                own = (cos * mine, sin * mine)
                cos, sin = cos * other, sin * other
                base = 2 * half_c + M
                put(tc_ref, base, g - edge, lr * cos + li * sin)
                put(ts_ref, base, g - edge, lr * sin - li * cos)
                put(tc_ref, base + 2 * M, g - edge, rr * cos - ri * sin)
                put(ts_ref, base + 2 * M, g - edge, -(rr * sin + ri * cos))
            base = g * SUB // LANES * LANES
            put(tc_ref, base, g, wr * own[0])
            put(tc_ref, base + LANES, g, -wi * own[1])
            put(ts_ref, base, g, -wi * own[0])
            put(ts_ref, base + LANES, g, -wr * own[1])
        for ref in (tc_ref, ts_ref):
            ref[2 * half_c:2 * half_c + M, lane] = zero
            ref[2 * half_c + 2 * M:2 * half_c + 3 * M, lane] = zero
        edge_rows.append([named[f] for f in (UP, DOWN, UL, UR, DL, DR)])

    own_products(0, False)
    signs = (-1, 1, -1, -1, 1, 1)
    for p, rows_w in enumerate(edge_rows):
        lane = slice(p * wide, (p + 1) * wide)
        for n, (w, sd) in enumerate(zip(rows_w, signs)):
            wr, wi = [jnp.broadcast_to(x, shape) for x in w]
            for g in range(0, M // SUB, 2):
                tops, lows = [], []
                for i in range(2):
                    at = slice((g + i) * SUB, (g + i + 1) * SUB)
                    cos, sin = ec_ref[at, lane], es_ref[at, lane]
                    tops.append(wr * cos - (sd * wi) * sin)
                    lows.append(-(sd * wr) * sin - wi * cos)
                at = slice(n * M + g * SUB, n * M + (g + 2) * SUB)
                uc_ref[at, lane] = jnp.concatenate(tops, 0).astype(BF16)
                us_ref[at, lane] = jnp.concatenate(lows, 0).astype(BF16)
    g1_ref[...] = dot(uc_ref[...], cc_ref[...])
    g2_ref[...] = dot(us_ref[...], cs_ref[...])

    shape = (SUB, LANES)
    iota = lax.broadcasted_iota(jnp.int32, shape, 0)
    lane_at = lax.broadcasted_iota(jnp.int32, shape, 1)
    back_lane = (LANES - 1) - lane_at
    back_row = (SUB - 1) - iota
    edge_c = half_c - M
    edge_r = half_r - M
    col_own, col_other = [], []
    for t in range(n_lane):
        index = (lane_at + t * LANES).astype(F32)
        col_own.append(jnp.minimum((half_c + M - 0.5 - index) * (1.0 / (2 * M)), 1.0))
        col_other.append(jnp.maximum((index - (half_c - M - 0.5)) * (1.0 / (2 * M)), 0.0))

    def flip(x, index, axis):
        return jnp.take_along_axis(x, index, axis=axis, mode="promise_in_bounds")

    def finish(g, t, edged):
        rows = slice(g * SUB, (g + 1) * SUB)
        def part(ref, which):
            return ref[rows, (2 * t + which) * LANES:(2 * t + which + 1) * LANES]
        p, s_, r, q = part(m1_ref, 0), part(m1_ref, 1), part(m2_ref, 0), part(m2_ref, 1)
        even, odd = p + q, p - q
        plus, minus = r + s_, r - s_
        quad = {(1, 1): even + plus, (-1, -1): even - plus,
                (1, -1): odd + minus, (-1, 1): odd - minus}
        if (t + 1) * LANES > edge_c:
            base = 2 * half_c
            off = t * LANES - (half_c - LANES)
            for se, start in ((-1, base), (1, base + LANES)):
                lc = m1_ref[rows, start + off:start + off + LANES]
                ls = m2_ref[rows, start + off:start + off + LANES]
                quad[1, se] += lc + ls
                quad[-1, se] += lc - ls
        if edged:
            def edge(n):
                at = slice(n * M + g * SUB - edge_r, n * M + (g + 1) * SUB - edge_r)
                x = g1_ref[at, t * LANES:(t + 1) * LANES]
                y = g2_ref[at, t * LANES:(t + 1) * LANES]
                return {1: x + y, -1: x - y}
            for n, sd in ((0, -1), (1, 1)):
                e = edge(n)
                for se in (-1, 1):
                    quad[sd, se] += e[se] * col_own[t]
            if (t + 1) * LANES > edge_c:
                for n, (sd, se) in ((2, (-1, -1)), (3, (-1, 1)), (4, (1, -1)), (5, (1, 1))):
                    quad[sd, se] += edge(n)[se] * col_other[t]
        for (sd, se), x in quad.items():
            if sd < 0:
                x = flip(x, back_row, 0)
                at = slice(half_r - SUB - g * SUB, half_r - g * SUB)
            else:
                at = slice(half_r + g * SUB, half_r + (g + 1) * SUB)
            if se < 0:
                x = flip(x, back_lane, 1)
                start = half_c - (t + 1) * LANES
            else:
                start = half_c + t * LANES
            out_ref[at, start:start + LANES] = x

    n_groups = half_r // M

    def sends(j, t):
        copies = []
        for row in (half_r + 2 * M * j, half_r - 2 * M * (j + 1)):
            for col in (half_c + t * LANES, half_c - (t + 1) * LANES):
                at = (slice(row, row + 2 * M), slice(col, col + LANES))
                copies.append(pltpu.make_async_copy(
                    out_ref.at[at], image_ref.at[at], sems.at[(j * n_lane + t) * 4 + len(copies)]))
        return copies

    for t in range(1, n_lane):
        own_products(t, False)
    for t in range(n_lane):
        for j in range(n_groups):
            for g in range(j * M // SUB, (j + 1) * M // SUB):
                finish(g, t, j == n_groups - 1)
            if j % 2:
                for copy in sends(j // 2, t):
                    copy.start()
    for t in range(n_lane):
        for j in range(n_groups // 2):
            for copy in sends(j, t):
                copy.wait()


def swaps(size):
    both = []
    for first in (0, 1):
        pairs = [(i, i + 1) for i in range(first, size - 1, 2)]
        both.append(pairs + [(j, i) for i, j in pairs])
    return both


def shards(vis, station_pairs, visibility_time_slot, station_u_cells, station_v_cells,
           facet_station_gains, holder_device_order):
    n_frow = lax.axis_size("frow")
    n_fcol = lax.axis_size("fcol")
    block = vis.shape[1]
    k_tiles = NBLK * block // LANES
    k = k_tiles * LANES
    half_r, half_c = R // 2, C // 2
    wide = 2 * half_c + 4 * M
    vmem = pl.BlockSpec(memory_space=pltpu.VMEM)
    smem = pl.BlockSpec(memory_space=pltpu.SMEM)

    def lines(x):
        return x.reshape(-1, LANES)

    def shaped(*dims, dtype=F32):
        return jax.ShapeDtypeStruct(dims, dtype)

    def params(mib):
        return pltpu.CompilerParams(vmem_limit_bytes=mib * 1024 * 1024)

    n_lines = station_u_cells.size // LANES
    packed, labels = pl.pallas_call(
        pack_kernel,
        out_shape=[shaped(n_frow * n_fcol // 2, 1, 5 * block), shaped(SUB + 2 * n_lines, LANES)],
        in_specs=[smem] + [vmem] * 5,
        name="pack",
    )(holder_device_order, vis, station_pairs, visibility_time_slot.reshape(1, block),
      lines(station_u_cells), lines(station_v_cells))
    facet_station_gains, packed = lax.optimization_barrier((facet_station_gains, packed))
    gains = facet_station_gains[0, 0]
    depth = gains.size // LANES
    own = gains.reshape(2, -1, LANES).transpose(1, 0, 2).reshape(depth, LANES)
    row_a, row_b = [lax.ppermute(own, "frow", pairs) for pairs in swaps(n_frow)]
    same = [list(range(first, n_frow * n_fcol, 2)) for first in range(2)]
    blocks = lax.all_to_all(packed, ("frow", "fcol"), 0, 0, axis_index_groups=same)
    mid = jnp.concatenate([own, row_a, row_b, labels], 0)
    col_a, col_b = [lax.ppermute(mid, "fcol", pairs) for pairs in swaps(n_fcol)]
    others = lax.ppermute(blocks, "fcol", [(i, i ^ 1) for i in range(n_fcol)])
    s, a_cos, a_sin, e_cos, e_sin, f_cos, f_sin, c_cos, c_sin = pl.pallas_call(
        functools.partial(table_kernel, n_frow, n_fcol, 3 * depth, n_lines),
        out_shape=[
            shaped(6, k_tiles, LANES),
            shaped(half_r, k, dtype=BF16), shaped(half_r, k, dtype=BF16),
            shaped(M, k), shaped(M, k),
            shaped(half_c, k), shaped(half_c, k),
            shaped(half_c, k, dtype=BF16), shaped(half_c, k, dtype=BF16),
        ],
        in_specs=[vmem] * 3,
        out_specs=[vmem] * 9,
        scratch_shapes=[
            pltpu.VMEM((5, k_tiles, LANES), F32),
            pltpu.VMEM((2, k_tiles, LANES), jnp.int32),
            pltpu.VMEM((2, 2, half_r // SUB, LANES), F32),
        ],
        compiler_params=params(24),
        name="tables",
    )(blocks, others, mid)
    return pl.pallas_call(
        functools.partial(image_kernel, depth),
        out_shape=shaped(R, C),
        in_specs=[vmem] * 12,
        out_specs=pl.BlockSpec(memory_space=pl.ANY),
        scratch_shapes=[
            pltpu.VMEM((R, C), F32),
            pltpu.VMEM((wide, k), BF16),
            pltpu.VMEM((wide, k), BF16),
            pltpu.VMEM((6 * M, k), BF16),
            pltpu.VMEM((6 * M, k), BF16),
            pltpu.VMEM((36 * NT, 4 * depth), BF16),
            pltpu.VMEM((half_r, wide), F32),
            pltpu.VMEM((half_r, wide), F32),
            pltpu.VMEM((6 * M, half_c), F32),
            pltpu.VMEM((6 * M, half_c), F32),
            pltpu.SemaphoreType.DMA((2 * half_r // M * (half_c // LANES),)),
        ],
        compiler_params=params(36),
        name="image",
    )(s, mid, col_a, col_b, a_cos, a_sin, e_cos, e_sin, f_cos, f_sin, c_cos, c_sin)


def solution(mesh):
    return jax.shard_map(
        shards,
        mesh=mesh,
        in_specs=(
            P(None, ("frow", "fcol")),
            P(None, ("frow", "fcol")),
            P(("frow", "fcol")),
            P(),
            P(),
            P("frow", "fcol", None, None),
            P(),
        ),
        out_specs=P("frow", "fcol"),
        check_vma=False,
    )
```

```python
import functools
import math

import jax
import jax.numpy as jnp
from jax import lax
from jax.experimental import pallas as pl
from jax.experimental.pallas import tpu as pltpu
from jax.sharding import PartitionSpec as P

R = 1024
C = 512
M = 64
NT = 16
NBLK = 4
LANES = 128
SUB = 8
OWN, LEFT, RIGHT, UP, DOWN, UL, UR, DL, DR = range(9)
F32 = jnp.float32
BF16 = jnp.bfloat16


def wrap(m, modulus):
    if modulus & (modulus - 1) == 0:
        return m & (modulus - 1)
    return jnp.remainder(m, modulus)


def turn(m, modulus):
    m = wrap(m, modulus)
    quarter = modulus // 4
    q = (m + modulus // 8) // quarter if quarter & (quarter - 1) else (
        (m + modulus // 8) >> (quarter.bit_length() - 1))
    x = (m - q * quarter).astype(F32) * (2.0 * math.pi / modulus)
    x2 = x * x
    s = x + x * x2 * (-1 / 6 + x2 * (1 / 120 + x2 * (-1 / 5040 + x2 * (1 / 362880))))
    c = 1.0 + x2 * (-0.5 + x2 * (1 / 24 + x2 * (-1 / 720 + x2 * (1 / 40320))))
    odd = (q & 1) == 1
    cos = jnp.where(odd, s, c)
    sin = jnp.where(odd, c, s)
    cos = jnp.where(((q + 1) & 2) != 0, -cos, cos)
    sin = jnp.where((q & 2) != 0, -sin, sin)
    return cos, sin


def times(a, b):
    return a[0] * b[0] - a[1] * b[1], a[0] * b[1] + a[1] * b[0]


def pack_kernel(order_ref, vis_ref, pair_ref, slot_ref, u_ref, v_ref, out_ref, label_ref):
    block = vis_ref.shape[1]
    lines = [vis_ref[0:1, :], vis_ref[1:2, :], pair_ref[0:1, :].astype(F32),
             pair_ref[1:2, :].astype(F32), slot_ref[...].astype(F32)]
    for copy in range(out_ref.shape[0]):
        for q, line in enumerate(lines):
            out_ref[copy, :, q * block:(q + 1) * block] = line
    n_lines = u_ref.shape[0]
    at = lax.broadcasted_iota(jnp.int32, (SUB, LANES), 1)
    order = jnp.zeros((SUB, LANES), jnp.int32)
    for b in range(NBLK):
        order = jnp.where(at == b, order_ref[b], order)
    label_ref[:SUB] = order.astype(F32)
    label_ref[SUB:SUB + n_lines] = u_ref[...].astype(F32)
    label_ref[SUB + n_lines:SUB + 2 * n_lines] = v_ref[...].astype(F32)


def pick(row, lane):
    return jnp.take_along_axis(
        jnp.broadcast_to(row, lane.shape), lane, axis=1, mode="promise_in_bounds")


def taper_rows(group, half, wide=LANES):
    index = (lax.broadcasted_iota(jnp.int32, (SUB, wide), 0) + SUB * group).astype(F32)
    return ((half + M - 0.5 - index) * (1.0 / (2 * M)),
            (index - (half - M - 0.5)) * (1.0 / (2 * M)))


def table_kernel(n_frow, n_fcol, first, n_lines, block_ref, cell_ref,
                 s_ref, ac_ref, as_ref, ec_ref, es_ref, fc_ref, fs_ref, cc_ref, cs_ref,
                 q_ref, uv_ref, dr_ref):
    frow_at = lax.axis_index("frow")
    fcol_at = lax.axis_index("fcol")
    half_r, half_c = R // 2, C // 2
    mod_r, mod_c = 2 * R * n_frow, 2 * C * n_fcol
    k_tiles = s_ref.shape[1]
    per_block = k_tiles // NBLK
    block = per_block * LANES
    shape = (SUB, LANES)

    order = cell_ref[first:first + 1, :]
    place = lax.broadcasted_iota(jnp.int32, (1, LANES), 1)
    owners = [jnp.sum(jnp.where(place == b, order, 0.0)).astype(jnp.int32) for b in range(NBLK)]
    for b, owner in enumerate(owners):
        for q in range(5):
            for j in range(per_block):
                q_ref[q, b * per_block + j:b * per_block + j + 1, :] = block_ref[
                    owner, :, q * block + j * LANES:q * block + (j + 1) * LANES]
    a1 = q_ref[2].astype(jnp.int32)
    a2 = q_ref[3].astype(jnp.int32)
    slot = q_ref[4].astype(jnp.int32)

    at = first + SUB

    def cells(table):
        got = [jnp.zeros(shape, F32)] * 2
        for h in range(table.shape[0]):
            row = table[h:h + 1, :]
            got = [jnp.where((a >> 7) == h, pick(row, a & 127), g)
                   for a, g in zip((a1, a2), got)]
        return (got[0] - got[1]).astype(jnp.int32)

    u = cells(cell_ref[at:at + n_lines, :])
    v = cells(cell_ref[at + n_lines:at + 2 * n_lines, :])
    uv_ref[0] = u
    uv_ref[1] = v
    centre = times(turn(u * (frow_at * (2 * R) + (R - 1)), mod_r),
                   turn(v * (fcol_at * (2 * C) + (C - 1)), mod_c))
    scale = 0.5 / math.sqrt(NBLK * per_block * LANES)
    value = times((q_ref[0] * scale, q_ref[1] * scale), centre)
    s_ref[0] = value[0]
    s_ref[1] = value[1]
    for n, a in enumerate((a1, a2)):
        s_ref[2 + n] = ((a >> 3) + (a & 6) * 32).astype(F32)
        s_ref[4 + n] = ((a & 1) * NT + slot).astype(F32)

    iota = lax.broadcasted_iota(jnp.int32, shape, 0)

    def tables(s, carry):
        lane = pl.ds(pl.multiple_of(s * LANES, LANES), LANES)

        def phases(which, modulus, half):
            freq = jnp.broadcast_to(uv_ref[which, pl.ds(s, 1), :], shape)
            fine = turn(freq * (2 * iota + 1), modulus)
            middle = turn(freq * (16 * iota), modulus)
            coarse = turn(freq * (128 * iota), modulus)
            for a in range(half // 64):
                top = tuple(jnp.broadcast_to(x[a:a + 1], shape) for x in coarse)
                both = times(middle, top)
                for comp in range(2):
                    dr_ref[which, comp, 8 * a:8 * a + 8, :] = both[comp]
            for g in range(half // SUB):
                step = tuple(jnp.broadcast_to(dr_ref[which, comp, g:g + 1, :], shape)
                             for comp in range(2))
                yield times(fine, step)

        pairs = {}

        def put(ref, first, group, x):
            key = (id(ref), first)
            if group % 2 == 0:
                pairs[key] = x
            else:
                start = first + SUB * (group - 1)
                ref[start:start + 16, lane] = jnp.concatenate([pairs.pop(key), x], 0).astype(BF16)

        edge = (half_r - M) // SUB
        for g, (cos, sin) in enumerate(phases(0, mod_r, half_r)):
            if g >= edge:
                mine, other = taper_rows(g, half_r)
                at = slice((g - edge) * SUB, (g - edge + 1) * SUB)
                ec_ref[at, lane] = cos * other
                es_ref[at, lane] = sin * other
                cos, sin = cos * mine, sin * mine
            put(ac_ref, 0, g, cos)
            put(as_ref, 0, g, sin)
        for g, (cos, sin) in enumerate(phases(1, mod_c, half_c)):
            put(cc_ref, 0, g, cos)
            put(cs_ref, 0, g, sin)
            at = slice(g * SUB, (g + 1) * SUB)
            fc_ref[at, lane] = cos
            fs_ref[at, lane] = sin
        return carry

    lax.fori_loop(0, k_tiles, tables, 0, unroll=True)


def image_kernel(depth, s_ref, mid_ref, a_ref, b_ref, ac_ref, as_ref, ec_ref, es_ref,
                 fc_ref, fs_ref, cc_ref, cs_ref, image_ref,
                 out_ref, tc_ref, ts_ref, uc_ref, us_ref, own_ref, gain_ref, w_ref,
                 m1_ref, m2_ref, g1_ref, g2_ref, sems):
    r_odd = lax.rem(lax.axis_index("frow"), 2) == 1
    c_odd = lax.rem(lax.axis_index("fcol"), 2) == 1
    k_tiles = s_ref.shape[1]
    half = depth // 2
    half_c = C // 2
    places = 2 * NT

    low_lane = lax.broadcasted_iota(jnp.int32, (places, LANES), 1) < LANES // 2
    for f in range(9):
        ref, row = (mid_ref, a_ref, b_ref)[f // 3], f % 3 * depth
        both = jnp.concatenate([ref[pl.ds(row, half, stride=2), :],
                                ref[pl.ds(row + 1, half, stride=2), :]], 0).T
        quarter = [both[i * places:(i + 1) * places] for i in range(4)]
        turned = [pltpu.roll(x, LANES // 2, 1) for x in quarter]
        for t in range(2):
            re = jnp.where(low_lane, quarter[2 * t], turned[2 * t + 1])
            im = jnp.where(low_lane, turned[2 * t], quarter[2 * t + 1])
            for comp, x in enumerate((re, im)):
                high = x.astype(BF16)
                if f == 0:
                    at = slice(comp * places, (comp + 1) * places)
                    own_ref[at, t * LANES:(t + 1) * LANES] = high
                    own_ref[at, (t + 2) * LANES:(t + 3) * LANES] = (
                        x - high.astype(F32)).astype(BF16)
                else:
                    at = (2 * (f - 1) + comp) * places
                    gain_ref[at:at + places, t * LANES:(t + 1) * LANES] = high

    r_first, r_second = jnp.where(r_odd, 1, 2), jnp.where(r_odd, 2, 1)
    c_first, c_second = jnp.where(c_odd, 1, 2), jnp.where(c_odd, 2, 1)
    rows = {UP: r_first - 1, DOWN: r_second - 1, LEFT: 3 * c_first - 1, RIGHT: 3 * c_second - 1,
            UL: 3 * c_first + r_first - 1, UR: 3 * c_second + r_first - 1,
            DL: 3 * c_first + r_second - 1, DR: 3 * c_second + r_second - 1}

    step = 2 if k_tiles % 2 == 0 else 1
    wide = step * LANES
    shape = (SUB, wide)
    line_at = lax.broadcasted_iota(jnp.int32, (2 * depth, wide), 0).astype(F32)
    place_at = line_at[:places]
    row_at = lax.broadcasted_iota(jnp.int32, shape, 0)
    zero = jnp.zeros((M, wide), BF16)

    def fold(parts):
        parts = [parts[i] for i in (0, 4, 2, 6, 1, 5, 3, 7)]
        for distance in (1, 2, 4):
            low = (row_at & distance) == 0
            count = len(parts) // 2
            parts = [jnp.where(low, x, y) + pltpu.roll(jnp.where(low, y, x), distance, 0)
                     for x, y in zip(parts[:count], parts[count:])]
        return parts[0]

    def gain_product(first, second):
        (g1r, g1i), (g2r, g2i) = first, second
        return g1r * g2r + g1i * g2i, g1i * g2r - g1r * g2i

    def weight(f, lane):
        return tuple(jnp.broadcast_to(w_ref[comp, pl.ds(rows[f], 1), lane], shape)
                     for comp in range(2))

    for p in range(k_tiles // step):
        lane = slice(p * wide, (p + 1) * wide)

        def line(q):
            return jnp.concatenate([s_ref[q, p * step + i:p * step + i + 1, :]
                                    for i in range(step)], 1)

        owns, nears = [], []
        for n in range(2):
            hot = jnp.where(line_at == line(2 + n), 1.0, 0.0).astype(BF16)
            mask = jnp.where(place_at == line(4 + n), 1.0, 0.0)
            z = jnp.dot(own_ref[...], jnp.concatenate([hot, hot], 0), preferred_element_type=F32)
            owns.append([jnp.sum(z[comp * places:(comp + 1) * places] * mask, axis=0, keepdims=True)
                         for comp in range(2)])
            z = jnp.dot(gain_ref[...], hot, preferred_element_type=F32)

            def part(f, comp):
                at = (2 * f + comp) * places
                x = z[at:at + places] * mask
                return sum(x[i * SUB:(i + 1) * SUB] for i in range(1, places // SUB)) + x[:SUB]

            nears.append([fold([part(f, comp) for f in range(SUB)]) for comp in range(2)])
        value = (line(0), line(1))
        own_w = times(value, gain_product(*owns))
        near_w = times(tuple(jnp.broadcast_to(x, shape) for x in value), gain_product(*nears))
        for comp in range(2):
            w_ref[comp, :, lane] = near_w[comp]

        pairs = {}

        def put(ref, first, group, x):
            key = (id(ref), first)
            if group % 2 == 0:
                pairs[key] = x
            else:
                start = first + SUB * (group - 1)
                ref[start:start + 16, lane] = jnp.concatenate([pairs.pop(key), x], 0).astype(BF16)

        edge = (half_c - M) // SUB
        wr, wi = [jnp.broadcast_to(x, shape) for x in own_w]
        (lr, li), (rr, ri) = weight(LEFT, lane), weight(RIGHT, lane)
        for g in range(half_c // SUB):
            at = slice(g * SUB, (g + 1) * SUB)
            cos, sin = fc_ref[at, lane], fs_ref[at, lane]
            own = (cos, sin)
            if g >= edge:
                mine, other = taper_rows(g, half_c, wide)
                own = (cos * mine, sin * mine)
                cos, sin = cos * other, sin * other
                base = 2 * half_c + M
                put(tc_ref, base, g - edge, lr * cos + li * sin)
                put(ts_ref, base, g - edge, lr * sin - li * cos)
                put(tc_ref, base + 2 * M, g - edge, rr * cos - ri * sin)
                put(ts_ref, base + 2 * M, g - edge, -(rr * sin + ri * cos))
            base = g * SUB // LANES * LANES
            put(tc_ref, base, g, wr * own[0])
            put(tc_ref, base + LANES, g, -wi * own[1])
            put(ts_ref, base, g, -wi * own[0])
            put(ts_ref, base + LANES, g, -wr * own[1])
        for ref in (tc_ref, ts_ref):
            ref[2 * half_c:2 * half_c + M, lane] = zero
            ref[2 * half_c + 2 * M:2 * half_c + 3 * M, lane] = zero

    def dot(a, b):
        return lax.dot_general(a, b, (((1,), (1,)), ((), ())), preferred_element_type=F32)

    half_r = R // 2
    n_lane = half_c // LANES

    def own_products(t):
        cols = slice(2 * t * LANES, 2 * (t + 1) * LANES if t < n_lane - 1 else tc_ref.shape[0])
        m1_ref[:, cols] = dot(ac_ref[...], tc_ref[cols, :])
        m2_ref[:, cols] = dot(as_ref[...], ts_ref[cols, :])

    own_products(0)
    signs = (-1, 1, -1, -1, 1, 1)
    for p in range(k_tiles // step):
        lane = slice(p * wide, (p + 1) * wide)
        for n, (f, sd) in enumerate(zip((UP, DOWN, UL, UR, DL, DR), signs)):
            wr, wi = weight(f, lane)
            for g in range(0, M // SUB, 2):
                tops, lows = [], []
                for i in range(2):
                    at = slice((g + i) * SUB, (g + i + 1) * SUB)
                    cos, sin = ec_ref[at, lane], es_ref[at, lane]
                    tops.append(wr * cos - (sd * wi) * sin)
                    lows.append(-(sd * wr) * sin - wi * cos)
                at = slice(n * M + g * SUB, n * M + (g + 2) * SUB)
                uc_ref[at, lane] = jnp.concatenate(tops, 0).astype(BF16)
                us_ref[at, lane] = jnp.concatenate(lows, 0).astype(BF16)
    g1_ref[...] = dot(uc_ref[...], cc_ref[...])
    g2_ref[...] = dot(us_ref[...], cs_ref[...])

    shape = (SUB, LANES)
    iota = lax.broadcasted_iota(jnp.int32, shape, 0)
    lane_at = lax.broadcasted_iota(jnp.int32, shape, 1)
    back_lane = (LANES - 1) - lane_at
    back_row = (SUB - 1) - iota
    edge_c = half_c - M
    edge_r = half_r - M
    col_own, col_other = [], []
    for t in range(n_lane):
        index = (lane_at + t * LANES).astype(F32)
        col_own.append(jnp.minimum((half_c + M - 0.5 - index) * (1.0 / (2 * M)), 1.0))
        col_other.append(jnp.maximum((index - (half_c - M - 0.5)) * (1.0 / (2 * M)), 0.0))

    def flip(x, index, axis):
        return jnp.take_along_axis(x, index, axis=axis, mode="promise_in_bounds")

    def finish(g, t, edged):
        rows = slice(g * SUB, (g + 1) * SUB)
        def part(ref, which):
            return ref[rows, (2 * t + which) * LANES:(2 * t + which + 1) * LANES]
        p, s_, r, q = part(m1_ref, 0), part(m1_ref, 1), part(m2_ref, 0), part(m2_ref, 1)
        even, odd = p + q, p - q
        plus, minus = r + s_, r - s_
        quad = {(1, 1): even + plus, (-1, -1): even - plus,
                (1, -1): odd + minus, (-1, 1): odd - minus}
        if (t + 1) * LANES > edge_c:
            base = 2 * half_c
            off = t * LANES - (half_c - LANES)
            for se, start in ((-1, base), (1, base + LANES)):
                lc = m1_ref[rows, start + off:start + off + LANES]
                ls = m2_ref[rows, start + off:start + off + LANES]
                quad[1, se] += lc + ls
                quad[-1, se] += lc - ls
        if edged:
            def edge(n):
                at = slice(n * M + g * SUB - edge_r, n * M + (g + 1) * SUB - edge_r)
                x = g1_ref[at, t * LANES:(t + 1) * LANES]
                y = g2_ref[at, t * LANES:(t + 1) * LANES]
                return {1: x + y, -1: x - y}
            for n, sd in ((0, -1), (1, 1)):
                e = edge(n)
                for se in (-1, 1):
                    quad[sd, se] += e[se] * col_own[t]
            if (t + 1) * LANES > edge_c:
                for n, (sd, se) in ((2, (-1, -1)), (3, (-1, 1)), (4, (1, -1)), (5, (1, 1))):
                    quad[sd, se] += edge(n)[se] * col_other[t]
        for (sd, se), x in quad.items():
            if sd < 0:
                x = flip(x, back_row, 0)
                at = slice(half_r - SUB - g * SUB, half_r - g * SUB)
            else:
                at = slice(half_r + g * SUB, half_r + (g + 1) * SUB)
            if se < 0:
                x = flip(x, back_lane, 1)
                start = half_c - (t + 1) * LANES
            else:
                start = half_c + t * LANES
            out_ref[at, start:start + LANES] = x

    n_groups = half_r // M

    def sends(j, t):
        copies = []
        for row in (half_r + 2 * M * j, half_r - 2 * M * (j + 1)):
            for col in (half_c + t * LANES, half_c - (t + 1) * LANES):
                at = (slice(row, row + 2 * M), slice(col, col + LANES))
                copies.append(pltpu.make_async_copy(
                    out_ref.at[at], image_ref.at[at], sems.at[(j * n_lane + t) * 4 + len(copies)]))
        return copies

    for t in range(1, n_lane):
        own_products(t)
    for t in range(n_lane):
        for j in range(n_groups):
            for g in range(j * M // SUB, (j + 1) * M // SUB):
                finish(g, t, j == n_groups - 1)
            if j % 2:
                for copy in sends(j // 2, t):
                    copy.start()
    for t in range(n_lane):
        for j in range(n_groups // 2):
            for copy in sends(j, t):
                copy.wait()


def swaps(size):
    both = []
    for first in (0, 1):
        pairs = [(i, i + 1) for i in range(first, size - 1, 2)]
        both.append(pairs + [(j, i) for i, j in pairs])
    return both


def shards(vis, station_pairs, visibility_time_slot, station_u_cells, station_v_cells,
           facet_station_gains, holder_device_order):
    n_frow = lax.axis_size("frow")
    n_fcol = lax.axis_size("fcol")
    block = vis.shape[1]
    k_tiles = NBLK * block // LANES
    k = k_tiles * LANES
    half_r, half_c = R // 2, C // 2
    wide = 2 * half_c + 4 * M
    vmem = pl.BlockSpec(memory_space=pltpu.VMEM)
    smem = pl.BlockSpec(memory_space=pltpu.SMEM)

    def lines(x):
        return x.reshape(-1, LANES)

    def shaped(*dims, dtype=F32):
        return jax.ShapeDtypeStruct(dims, dtype)

    def params(mib):
        return pltpu.CompilerParams(vmem_limit_bytes=mib * 1024 * 1024)

    n_lines = station_u_cells.size // LANES
    packed, labels = pl.pallas_call(
        pack_kernel,
        out_shape=[shaped(n_frow * n_fcol, 1, 5 * block), shaped(SUB + 2 * n_lines, LANES)],
        in_specs=[smem] + [vmem] * 5,
        name="pack",
    )(holder_device_order, vis, station_pairs, visibility_time_slot.reshape(1, block),
      lines(station_u_cells), lines(station_v_cells))
    facet_station_gains, packed = lax.optimization_barrier((facet_station_gains, packed))
    gains = facet_station_gains[0, 0]
    depth = gains.size // LANES
    own = gains.reshape(2, -1, LANES).transpose(1, 0, 2).reshape(depth, LANES)
    row_a, row_b = [lax.ppermute(own, "frow", pairs) for pairs in swaps(n_frow)]
    blocks = lax.all_to_all(packed, ("frow", "fcol"), 0, 0)
    mid = jnp.concatenate([own, row_a, row_b, labels], 0)
    col_a, col_b = [lax.ppermute(mid, "fcol", pairs) for pairs in swaps(n_fcol)]
    s, a_cos, a_sin, e_cos, e_sin, f_cos, f_sin, c_cos, c_sin = pl.pallas_call(
        functools.partial(table_kernel, n_frow, n_fcol, 3 * depth, n_lines),
        out_shape=[
            shaped(6, k_tiles, LANES),
            shaped(half_r, k, dtype=BF16), shaped(half_r, k, dtype=BF16),
            shaped(M, k), shaped(M, k),
            shaped(half_c, k), shaped(half_c, k),
            shaped(half_c, k, dtype=BF16), shaped(half_c, k, dtype=BF16),
        ],
        in_specs=[vmem] * 2,
        out_specs=[vmem] * 9,
        scratch_shapes=[
            pltpu.VMEM((5, k_tiles, LANES), F32),
            pltpu.VMEM((2, k_tiles, LANES), jnp.int32),
            pltpu.VMEM((2, 2, half_r // SUB, LANES), F32),
        ],
        compiler_params=params(24),
        name="tables",
    )(blocks, mid)
    return pl.pallas_call(
        functools.partial(image_kernel, depth),
        out_shape=shaped(R, C),
        in_specs=[vmem] * 12,
        out_specs=pl.BlockSpec(memory_space=pl.ANY),
        scratch_shapes=[
            pltpu.VMEM((R, C), F32),
            pltpu.VMEM((wide, k), BF16),
            pltpu.VMEM((wide, k), BF16),
            pltpu.VMEM((6 * M, k), BF16),
            pltpu.VMEM((6 * M, k), BF16),
            pltpu.VMEM((4 * NT, 4 * depth), BF16),
            pltpu.VMEM((32 * NT, 2 * depth), BF16),
            pltpu.VMEM((2, SUB, k), F32),
            pltpu.VMEM((half_r, wide), F32),
            pltpu.VMEM((half_r, wide), F32),
            pltpu.VMEM((6 * M, half_c), F32),
            pltpu.VMEM((6 * M, half_c), F32),
            pltpu.SemaphoreType.DMA((2 * half_r // M * (half_c // LANES),)),
        ],
        compiler_params=params(36),
        name="image",
    )(s, mid, col_a, col_b, a_cos, a_sin, e_cos, e_sin, f_cos, f_sin, c_cos, c_sin)


def solution(mesh):
    return jax.shard_map(
        shards,
        mesh=mesh,
        in_specs=(
            P(None, ("frow", "fcol")),
            P(None, ("frow", "fcol")),
            P(("frow", "fcol")),
            P(),
            P(),
            P("frow", "fcol", None, None),
            P(),
        ),
        out_specs=P("frow", "fcol"),
        check_vma=False,
    )
```

```python
import functools
import math

import jax
import jax.numpy as jnp
from jax import lax
from jax.experimental import pallas as pl
from jax.experimental.pallas import tpu as pltpu
from jax.sharding import PartitionSpec as P

R = 1024
C = 512
M = 64
NT = 16
NBLK = 4
LANES = 128
SUB = 8
OWN, LEFT, RIGHT, UP, DOWN, UL, UR, DL, DR = range(9)
F32 = jnp.float32
BF16 = jnp.bfloat16


def wrap(m, modulus):
    if modulus & (modulus - 1) == 0:
        return m & (modulus - 1)
    return jnp.remainder(m, modulus)


def turn(m, modulus):
    m = wrap(m, modulus)
    quarter = modulus // 4
    q = (m + modulus // 8) // quarter if quarter & (quarter - 1) else (
        (m + modulus // 8) >> (quarter.bit_length() - 1))
    x = (m - q * quarter).astype(F32) * (2.0 * math.pi / modulus)
    x2 = x * x
    s = x + x * x2 * (-1 / 6 + x2 * (1 / 120 + x2 * (-1 / 5040 + x2 * (1 / 362880))))
    c = 1.0 + x2 * (-0.5 + x2 * (1 / 24 + x2 * (-1 / 720 + x2 * (1 / 40320))))
    odd = (q & 1) == 1
    cos = jnp.where(odd, s, c)
    sin = jnp.where(odd, c, s)
    cos = jnp.where(((q + 1) & 2) != 0, -cos, cos)
    sin = jnp.where((q & 2) != 0, -sin, sin)
    return cos, sin


def times(a, b):
    return a[0] * b[0] - a[1] * b[1], a[0] * b[1] + a[1] * b[0]


def pack_kernel(order_ref, vis_ref, pair_ref, slot_ref, u_ref, v_ref, out_ref, label_ref):
    block = vis_ref.shape[1]
    lines = [vis_ref[0:1, :], vis_ref[1:2, :], pair_ref[0:1, :].astype(F32),
             pair_ref[1:2, :].astype(F32), slot_ref[...].astype(F32)]
    for copy in range(out_ref.shape[0]):
        for q, line in enumerate(lines):
            out_ref[copy, :, q * block:(q + 1) * block] = line
    n_lines = u_ref.shape[0]
    at = lax.broadcasted_iota(jnp.int32, (SUB, LANES), 1)
    order = jnp.zeros((SUB, LANES), jnp.int32)
    for b in range(NBLK):
        order = jnp.where(at == b, order_ref[b], order)
    label_ref[:SUB] = order.astype(F32)
    label_ref[SUB:SUB + n_lines] = u_ref[...].astype(F32)
    label_ref[SUB + n_lines:SUB + 2 * n_lines] = v_ref[...].astype(F32)


def pick(row, lane):
    return jnp.take_along_axis(
        jnp.broadcast_to(row, lane.shape), lane, axis=1, mode="promise_in_bounds")


def taper_rows(group, half, wide=LANES):
    index = (lax.broadcasted_iota(jnp.int32, (SUB, wide), 0) + SUB * group).astype(F32)
    return ((half + M - 0.5 - index) * (1.0 / (2 * M)),
            (index - (half - M - 0.5)) * (1.0 / (2 * M)))


def table_kernel(n_frow, n_fcol, first, n_lines, block_ref, cell_ref,
                 s_ref, ac_ref, as_ref, ec_ref, es_ref, fc_ref, fs_ref, cc_ref, cs_ref,
                 q_ref, uv_ref, dr_ref):
    frow_at = lax.axis_index("frow")
    fcol_at = lax.axis_index("fcol")
    half_r, half_c = R // 2, C // 2
    mod_r, mod_c = 2 * R * n_frow, 2 * C * n_fcol
    k_tiles = s_ref.shape[1]
    per_block = k_tiles // NBLK
    block = per_block * LANES
    shape = (SUB, LANES)

    order = cell_ref[first:first + 1, :]
    place = lax.broadcasted_iota(jnp.int32, (1, LANES), 1)
    owners = [jnp.sum(jnp.where(place == b, order, 0.0)).astype(jnp.int32) for b in range(NBLK)]
    for b, owner in enumerate(owners):
        for q in range(5):
            for j in range(per_block):
                q_ref[q, b * per_block + j:b * per_block + j + 1, :] = block_ref[
                    owner, :, q * block + j * LANES:q * block + (j + 1) * LANES]
    a1 = q_ref[2].astype(jnp.int32)
    a2 = q_ref[3].astype(jnp.int32)
    slot = q_ref[4].astype(jnp.int32)

    at = first + SUB

    def cells(table):
        got = [jnp.zeros(shape, F32)] * 2
        for h in range(table.shape[0]):
            row = table[h:h + 1, :]
            got = [jnp.where((a >> 7) == h, pick(row, a & 127), g)
                   for a, g in zip((a1, a2), got)]
        return (got[0] - got[1]).astype(jnp.int32)

    u = cells(cell_ref[at:at + n_lines, :])
    v = cells(cell_ref[at + n_lines:at + 2 * n_lines, :])
    uv_ref[0] = u
    uv_ref[1] = v
    centre = times(turn(u * (frow_at * (2 * R) + (R - 1)), mod_r),
                   turn(v * (fcol_at * (2 * C) + (C - 1)), mod_c))
    scale = 0.5 / math.sqrt(NBLK * per_block * LANES)
    value = times((q_ref[0] * scale, q_ref[1] * scale), centre)
    s_ref[0] = value[0]
    s_ref[1] = value[1]
    for n, a in enumerate((a1, a2)):
        s_ref[2 + n] = ((a >> 3) + (a & 6) * 32).astype(F32)
        s_ref[4 + n] = ((a & 1) * NT + slot).astype(F32)

    iota = lax.broadcasted_iota(jnp.int32, shape, 0)

    def tables(s, carry):
        lane = pl.ds(pl.multiple_of(s * LANES, LANES), LANES)

        def phases(which, modulus, half):
            freq = jnp.broadcast_to(uv_ref[which, pl.ds(s, 1), :], shape)
            fine = turn(freq * (2 * iota + 1), modulus)
            middle = turn(freq * (16 * iota), modulus)
            coarse = turn(freq * (128 * iota), modulus)
            for a in range(half // 64):
                top = tuple(jnp.broadcast_to(x[a:a + 1], shape) for x in coarse)
                both = times(middle, top)
                for comp in range(2):
                    dr_ref[which, comp, 8 * a:8 * a + 8, :] = both[comp]
            for g in range(half // SUB):
                step = tuple(jnp.broadcast_to(dr_ref[which, comp, g:g + 1, :], shape)
                             for comp in range(2))
                yield times(fine, step)

        pairs = {}

        def put(ref, first, group, x):
            key = (id(ref), first)
            if group % 2 == 0:
                pairs[key] = x
            else:
                start = first + SUB * (group - 1)
                ref[start:start + 16, lane] = jnp.concatenate([pairs.pop(key), x], 0).astype(BF16)

        edge = (half_r - M) // SUB
        for g, (cos, sin) in enumerate(phases(0, mod_r, half_r)):
            if g >= edge:
                mine, other = taper_rows(g, half_r)
                at = slice((g - edge) * SUB, (g - edge + 1) * SUB)
                ec_ref[at, lane] = cos * other
                es_ref[at, lane] = sin * other
                cos, sin = cos * mine, sin * mine
            put(ac_ref, 0, g, cos)
            put(as_ref, 0, g, sin)
        for g, (cos, sin) in enumerate(phases(1, mod_c, half_c)):
            put(cc_ref, 0, g, cos)
            put(cs_ref, 0, g, sin)
            at = slice(g * SUB, (g + 1) * SUB)
            fc_ref[at, lane] = cos
            fs_ref[at, lane] = sin
        return carry

    lax.fori_loop(0, k_tiles, tables, 0, unroll=True)


def image_kernel(depth, s_ref, mid_ref, a_ref, b_ref, ac_ref, as_ref, ec_ref, es_ref,
                 fc_ref, fs_ref, cc_ref, cs_ref, image_ref,
                 out_ref, tc_ref, ts_ref, uc_ref, us_ref, gain_ref, w_ref,
                 m1_ref, m2_ref, g1_ref, g2_ref, sems):
    r_odd = lax.rem(lax.axis_index("frow"), 2) == 1
    c_odd = lax.rem(lax.axis_index("fcol"), 2) == 1
    k_tiles = s_ref.shape[1]
    half = depth // 2
    half_c = C // 2
    places = 2 * NT

    low_lane = lax.broadcasted_iota(jnp.int32, (places, LANES), 1) < LANES // 2
    for f in range(9):
        ref, row = (mid_ref, a_ref, b_ref)[f // 3], f % 3 * depth
        both = jnp.concatenate([ref[pl.ds(row, half, stride=2), :],
                                ref[pl.ds(row + 1, half, stride=2), :]], 0).T
        quarter = [both[i * places:(i + 1) * places] for i in range(4)]
        turned = [pltpu.roll(x, LANES // 2, 1) for x in quarter]
        for t in range(2):
            re = jnp.where(low_lane, quarter[2 * t], turned[2 * t + 1])
            im = jnp.where(low_lane, turned[2 * t], quarter[2 * t + 1])
            for comp, x in enumerate((re, im)):
                high = x.astype(BF16)
                at = (2 * (f - 1 if f else SUB) + comp) * places
                gain_ref[at:at + places, t * LANES:(t + 1) * LANES] = high
                if f == 0:
                    at += 2 * places
                    gain_ref[at:at + places, t * LANES:(t + 1) * LANES] = (
                        x - high.astype(F32)).astype(BF16)

    r_first, r_second = jnp.where(r_odd, 1, 2), jnp.where(r_odd, 2, 1)
    c_first, c_second = jnp.where(c_odd, 1, 2), jnp.where(c_odd, 2, 1)
    rows = {UP: r_first - 1, DOWN: r_second - 1, LEFT: 3 * c_first - 1, RIGHT: 3 * c_second - 1,
            UL: 3 * c_first + r_first - 1, UR: 3 * c_second + r_first - 1,
            DL: 3 * c_first + r_second - 1, DR: 3 * c_second + r_second - 1}

    step = 2 if k_tiles % 2 == 0 else 1
    wide = step * LANES
    shape = (SUB, wide)
    line_at = lax.broadcasted_iota(jnp.int32, (2 * depth, wide), 0).astype(F32)
    place_at = line_at[:places]
    row_at = lax.broadcasted_iota(jnp.int32, shape, 0)
    zero = jnp.zeros((M, wide), BF16)

    def fold(parts):
        parts = [parts[i] for i in (0, 4, 2, 6, 1, 5, 3, 7)]
        for distance in (1, 2, 4):
            low = (row_at & distance) == 0
            count = len(parts) // 2
            parts = [jnp.where(low, x, y) + pltpu.roll(jnp.where(low, y, x), distance, 0)
                     for x, y in zip(parts[:count], parts[count:])]
        return parts[0]

    def gain_product(first, second):
        (g1r, g1i), (g2r, g2i) = first, second
        return g1r * g2r + g1i * g2i, g1i * g2r - g1r * g2i

    def weight(f, lane):
        return tuple(jnp.broadcast_to(w_ref[comp, pl.ds(rows[f], 1), lane], shape)
                     for comp in range(2))

    for p in range(k_tiles // step):
        lane = slice(p * wide, (p + 1) * wide)

        def line(q):
            return jnp.concatenate([s_ref[q, p * step + i:p * step + i + 1, :]
                                    for i in range(step)], 1)

        owns, nears = [], []
        for n in range(2):
            hot = jnp.where(line_at == line(2 + n), 1.0, 0.0).astype(BF16)
            mask = jnp.where(place_at == line(4 + n), 1.0, 0.0)
            z = jnp.dot(gain_ref[...], hot, preferred_element_type=F32)

            def part(f, comp):
                at = (2 * f + comp) * places
                x = z[at:at + places]
                if f == SUB:
                    x = x + z[at + 2 * places:at + 3 * places]
                x = x * mask
                return sum((x[i * SUB:(i + 1) * SUB] for i in range(1, places // SUB)), x[:SUB])

            owns.append([jnp.sum(part(SUB, comp), axis=0, keepdims=True) for comp in range(2)])
            nears.append([fold([part(f, comp) for f in range(SUB)]) for comp in range(2)])
        value = (line(0), line(1))
        own_w = times(value, gain_product(*owns))
        near_w = times(tuple(jnp.broadcast_to(x, shape) for x in value), gain_product(*nears))
        for comp in range(2):
            w_ref[comp, :, lane] = near_w[comp]

        pairs = {}

        def put(ref, first, group, x):
            key = (id(ref), first)
            if group % 2 == 0:
                pairs[key] = x
            else:
                start = first + SUB * (group - 1)
                ref[start:start + 16, lane] = jnp.concatenate([pairs.pop(key), x], 0).astype(BF16)

        edge = (half_c - M) // SUB
        wr, wi = [jnp.broadcast_to(x, shape) for x in own_w]
        (lr, li), (rr, ri) = weight(LEFT, lane), weight(RIGHT, lane)
        for g in range(half_c // SUB):
            at = slice(g * SUB, (g + 1) * SUB)
            cos, sin = fc_ref[at, lane], fs_ref[at, lane]
            own = (cos, sin)
            if g >= edge:
                mine, other = taper_rows(g, half_c, wide)
                own = (cos * mine, sin * mine)
                cos, sin = cos * other, sin * other
                base = 2 * half_c + M
                put(tc_ref, base, g - edge, lr * cos + li * sin)
                put(ts_ref, base, g - edge, lr * sin - li * cos)
                put(tc_ref, base + 2 * M, g - edge, rr * cos - ri * sin)
                put(ts_ref, base + 2 * M, g - edge, -(rr * sin + ri * cos))
            base = g * SUB // LANES * LANES
            put(tc_ref, base, g, wr * own[0])
            put(tc_ref, base + LANES, g, -wi * own[1])
            put(ts_ref, base, g, -wi * own[0])
            put(ts_ref, base + LANES, g, -wr * own[1])
        for ref in (tc_ref, ts_ref):
            ref[2 * half_c:2 * half_c + M, lane] = zero
            ref[2 * half_c + 2 * M:2 * half_c + 3 * M, lane] = zero

    def dot(a, b):
        return lax.dot_general(a, b, (((1,), (1,)), ((), ())), preferred_element_type=F32)

    half_r = R // 2
    n_lane = half_c // LANES

    def own_products(t):
        cols = slice(2 * t * LANES, 2 * (t + 1) * LANES if t < n_lane - 1 else tc_ref.shape[0])
        m1_ref[:, cols] = dot(ac_ref[...], tc_ref[cols, :])
        m2_ref[:, cols] = dot(as_ref[...], ts_ref[cols, :])

    own_products(n_lane - 1)
    signs = (-1, 1, -1, -1, 1, 1)
    for p in range(k_tiles // step):
        lane = slice(p * wide, (p + 1) * wide)
        for n, (f, sd) in enumerate(zip((UP, DOWN, UL, UR, DL, DR), signs)):
            wr, wi = weight(f, lane)
            for g in range(0, M // SUB, 2):
                tops, lows = [], []
                for i in range(2):
                    at = slice((g + i) * SUB, (g + i + 1) * SUB)
                    cos, sin = ec_ref[at, lane], es_ref[at, lane]
                    tops.append(wr * cos - (sd * wi) * sin)
                    lows.append(-(sd * wr) * sin - wi * cos)
                at = slice(n * M + g * SUB, n * M + (g + 2) * SUB)
                uc_ref[at, lane] = jnp.concatenate(tops, 0).astype(BF16)
                us_ref[at, lane] = jnp.concatenate(lows, 0).astype(BF16)
    g1_ref[...] = dot(uc_ref[...], cc_ref[...])
    g2_ref[...] = dot(us_ref[...], cs_ref[...])

    shape = (SUB, LANES)
    iota = lax.broadcasted_iota(jnp.int32, shape, 0)
    lane_at = lax.broadcasted_iota(jnp.int32, shape, 1)
    back_lane = (LANES - 1) - lane_at
    back_row = (SUB - 1) - iota
    edge_c = half_c - M
    edge_r = half_r - M
    col_own, col_other = [], []
    for t in range(n_lane):
        index = (lane_at + t * LANES).astype(F32)
        col_own.append(jnp.minimum((half_c + M - 0.5 - index) * (1.0 / (2 * M)), 1.0))
        col_other.append(jnp.maximum((index - (half_c - M - 0.5)) * (1.0 / (2 * M)), 0.0))

    def flip(x, index, axis):
        return jnp.take_along_axis(x, index, axis=axis, mode="promise_in_bounds")

    def finish(g, t, edged):
        rows = slice(g * SUB, (g + 1) * SUB)
        def part(ref, which):
            return ref[rows, (2 * t + which) * LANES:(2 * t + which + 1) * LANES]
        p, s_, r, q = part(m1_ref, 0), part(m1_ref, 1), part(m2_ref, 0), part(m2_ref, 1)
        even, odd = p + q, p - q
        plus, minus = r + s_, r - s_
        quad = {(1, 1): even + plus, (-1, -1): even - plus,
                (1, -1): odd + minus, (-1, 1): odd - minus}
        if (t + 1) * LANES > edge_c:
            base = 2 * half_c
            off = t * LANES - (half_c - LANES)
            for se, start in ((-1, base), (1, base + LANES)):
                lc = m1_ref[rows, start + off:start + off + LANES]
                ls = m2_ref[rows, start + off:start + off + LANES]
                quad[1, se] += lc + ls
                quad[-1, se] += lc - ls
        if edged:
            def edge(n):
                at = slice(n * M + g * SUB - edge_r, n * M + (g + 1) * SUB - edge_r)
                x = g1_ref[at, t * LANES:(t + 1) * LANES]
                y = g2_ref[at, t * LANES:(t + 1) * LANES]
                return {1: x + y, -1: x - y}
            for n, sd in ((0, -1), (1, 1)):
                e = edge(n)
                for se in (-1, 1):
                    quad[sd, se] += e[se] * col_own[t]
            if (t + 1) * LANES > edge_c:
                for n, (sd, se) in ((2, (-1, -1)), (3, (-1, 1)), (4, (1, -1)), (5, (1, 1))):
                    quad[sd, se] += edge(n)[se] * col_other[t]
        for (sd, se), x in quad.items():
            if sd < 0:
                x = flip(x, back_row, 0)
                at = slice(half_r - SUB - g * SUB, half_r - g * SUB)
            else:
                at = slice(half_r + g * SUB, half_r + (g + 1) * SUB)
            if se < 0:
                x = flip(x, back_lane, 1)
                start = half_c - (t + 1) * LANES
            else:
                start = half_c + t * LANES
            out_ref[at, start:start + LANES] = x

    n_groups = half_r // M

    def sends(j, t):
        copies = []
        for row in (half_r + 2 * M * j, half_r - 2 * M * (j + 1)):
            for col in (half_c + t * LANES, half_c - (t + 1) * LANES):
                at = (slice(row, row + 2 * M), slice(col, col + LANES))
                copies.append(pltpu.make_async_copy(
                    out_ref.at[at], image_ref.at[at], sems.at[(j * n_lane + t) * 4 + len(copies)]))
        return copies

    for t in range(n_lane - 2, -1, -1):
        own_products(t)
    for t in range(n_lane - 1, -1, -1):
        for j in range(n_groups):
            for g in range(j * M // SUB, (j + 1) * M // SUB):
                finish(g, t, j == n_groups - 1)
            if j % 2:
                for copy in sends(j // 2, t):
                    copy.start()
    for t in range(n_lane):
        for j in range(n_groups // 2):
            for copy in sends(j, t):
                copy.wait()


def swaps(size):
    both = []
    for first in (0, 1):
        pairs = [(i, i + 1) for i in range(first, size - 1, 2)]
        both.append(pairs + [(j, i) for i, j in pairs])
    return both


def shards(vis, station_pairs, visibility_time_slot, station_u_cells, station_v_cells,
           facet_station_gains, holder_device_order):
    n_frow = lax.axis_size("frow")
    n_fcol = lax.axis_size("fcol")
    block = vis.shape[1]
    k_tiles = NBLK * block // LANES
    k = k_tiles * LANES
    half_r, half_c = R // 2, C // 2
    wide = 2 * half_c + 4 * M
    vmem = pl.BlockSpec(memory_space=pltpu.VMEM)
    smem = pl.BlockSpec(memory_space=pltpu.SMEM)

    def lines(x):
        return x.reshape(-1, LANES)

    def shaped(*dims, dtype=F32):
        return jax.ShapeDtypeStruct(dims, dtype)

    def params(mib):
        return pltpu.CompilerParams(vmem_limit_bytes=mib * 1024 * 1024)

    n_lines = station_u_cells.size // LANES
    packed, labels = pl.pallas_call(
        pack_kernel,
        out_shape=[shaped(n_frow * n_fcol, 1, 5 * block), shaped(SUB + 2 * n_lines, LANES)],
        in_specs=[smem] + [vmem] * 5,
        name="pack",
    )(holder_device_order, vis, station_pairs, visibility_time_slot.reshape(1, block),
      lines(station_u_cells), lines(station_v_cells))
    facet_station_gains, packed = lax.optimization_barrier((facet_station_gains, packed))
    gains = facet_station_gains[0, 0]
    depth = gains.size // LANES
    own = gains.reshape(2, -1, LANES).transpose(1, 0, 2).reshape(depth, LANES)
    row_a, row_b = [lax.ppermute(own, "frow", pairs) for pairs in swaps(n_frow)]
    blocks = lax.all_to_all(packed, ("frow", "fcol"), 0, 0)
    mid = jnp.concatenate([own, row_a, row_b, labels], 0)
    col_a, col_b = [lax.ppermute(mid, "fcol", pairs) for pairs in swaps(n_fcol)]
    s, a_cos, a_sin, e_cos, e_sin, f_cos, f_sin, c_cos, c_sin = pl.pallas_call(
        functools.partial(table_kernel, n_frow, n_fcol, 3 * depth, n_lines),
        out_shape=[
            shaped(6, k_tiles, LANES),
            shaped(half_r, k, dtype=BF16), shaped(half_r, k, dtype=BF16),
            shaped(M, k), shaped(M, k),
            shaped(half_c, k), shaped(half_c, k),
            shaped(half_c, k, dtype=BF16), shaped(half_c, k, dtype=BF16),
        ],
        in_specs=[vmem] * 2,
        out_specs=[vmem] * 9,
        scratch_shapes=[
            pltpu.VMEM((5, k_tiles, LANES), F32),
            pltpu.VMEM((2, k_tiles, LANES), jnp.int32),
            pltpu.VMEM((2, 2, half_r // SUB, LANES), F32),
        ],
        compiler_params=params(24),
        name="tables",
    )(blocks, mid)
    return pl.pallas_call(
        functools.partial(image_kernel, depth),
        out_shape=shaped(R, C),
        in_specs=[vmem] * 12,
        out_specs=pl.BlockSpec(memory_space=pl.ANY),
        scratch_shapes=[
            pltpu.VMEM((R, C), F32),
            pltpu.VMEM((wide, k), BF16),
            pltpu.VMEM((wide, k), BF16),
            pltpu.VMEM((6 * M, k), BF16),
            pltpu.VMEM((6 * M, k), BF16),
            pltpu.VMEM((40 * NT, 2 * depth), BF16),
            pltpu.VMEM((2, SUB, k), F32),
            pltpu.VMEM((half_r, wide), F32),
            pltpu.VMEM((half_r, wide), F32),
            pltpu.VMEM((6 * M, half_c), F32),
            pltpu.VMEM((6 * M, half_c), F32),
            pltpu.SemaphoreType.DMA((2 * half_r // M * (half_c // LANES),)),
        ],
        compiler_params=params(36),
        name="image",
    )(s, mid, col_a, col_b, a_cos, a_sin, e_cos, e_sin, f_cos, f_sin, c_cos, c_sin)


def solution(mesh):
    return jax.shard_map(
        shards,
        mesh=mesh,
        in_specs=(
            P(None, ("frow", "fcol")),
            P(None, ("frow", "fcol")),
            P(("frow", "fcol")),
            P(),
            P(),
            P("frow", "fcol", None, None),
            P(),
        ),
        out_specs=P("frow", "fcol"),
        check_vma=False,
    )
```

```python
import functools
import math

import jax
import jax.numpy as jnp
from jax import lax
from jax.experimental import pallas as pl
from jax.experimental.pallas import tpu as pltpu
from jax.sharding import PartitionSpec as P

R = 1024
C = 512
M = 64
NT = 16
NBLK = 4
LANES = 128
SUB = 8
OWN, LEFT, RIGHT, UP, DOWN, UL, UR, DL, DR = range(9)
F32 = jnp.float32
BF16 = jnp.bfloat16


def wrap(m, modulus):
    if modulus & (modulus - 1) == 0:
        return m & (modulus - 1)
    return jnp.remainder(m, modulus)


def turn(m, modulus):
    m = wrap(m, modulus)
    quarter = modulus // 4
    q = (m + modulus // 8) // quarter if quarter & (quarter - 1) else (
        (m + modulus // 8) >> (quarter.bit_length() - 1))
    x = (m - q * quarter).astype(F32) * (2.0 * math.pi / modulus)
    x2 = x * x
    s = x + x * x2 * (-1 / 6 + x2 * (1 / 120 + x2 * (-1 / 5040 + x2 * (1 / 362880))))
    c = 1.0 + x2 * (-0.5 + x2 * (1 / 24 + x2 * (-1 / 720 + x2 * (1 / 40320))))
    odd = (q & 1) == 1
    cos = jnp.where(odd, s, c)
    sin = jnp.where(odd, c, s)
    cos = jnp.where(((q + 1) & 2) != 0, -cos, cos)
    sin = jnp.where((q & 2) != 0, -sin, sin)
    return cos, sin


def times(a, b):
    return a[0] * b[0] - a[1] * b[1], a[0] * b[1] + a[1] * b[0]


def pack_kernel(order_ref, vis_ref, pair_ref, slot_ref, u_ref, v_ref, out_ref, label_ref):
    block = vis_ref.shape[1]
    lines = [vis_ref[0:1, :], vis_ref[1:2, :], pair_ref[0:1, :].astype(F32),
             pair_ref[1:2, :].astype(F32), slot_ref[...].astype(F32)]
    for copy in range(out_ref.shape[0]):
        for q, line in enumerate(lines):
            out_ref[copy, :, q * block:(q + 1) * block] = line
    n_lines = u_ref.shape[0]
    at = lax.broadcasted_iota(jnp.int32, (SUB, LANES), 1)
    order = jnp.zeros((SUB, LANES), jnp.int32)
    for b in range(NBLK):
        order = jnp.where(at == b, order_ref[b], order)
    label_ref[:SUB] = order.astype(F32)
    label_ref[SUB:SUB + n_lines] = u_ref[...].astype(F32)
    label_ref[SUB + n_lines:SUB + 2 * n_lines] = v_ref[...].astype(F32)


def pick(row, lane):
    return jnp.take_along_axis(
        jnp.broadcast_to(row, lane.shape), lane, axis=1, mode="promise_in_bounds")


def taper_rows(group, half, wide=LANES):
    index = (lax.broadcasted_iota(jnp.int32, (SUB, wide), 0) + SUB * group).astype(F32)
    return ((half + M - 0.5 - index) * (1.0 / (2 * M)),
            (index - (half - M - 0.5)) * (1.0 / (2 * M)))


def table_kernel(n_frow, n_fcol, first, n_lines, block_ref, cell_ref,
                 s_ref, ac_ref, as_ref, ec_ref, es_ref, fc_ref, fs_ref, cc_ref, cs_ref,
                 q_ref, uv_ref, dr_ref):
    frow_at = lax.axis_index("frow")
    fcol_at = lax.axis_index("fcol")
    half_r, half_c = R // 2, C // 2
    mod_r, mod_c = 2 * R * n_frow, 2 * C * n_fcol
    k_tiles = s_ref.shape[1]
    per_block = k_tiles // NBLK
    block = per_block * LANES
    shape = (SUB, LANES)

    order = cell_ref[first:first + 1, :]
    place = lax.broadcasted_iota(jnp.int32, (1, LANES), 1)
    owners = [jnp.sum(jnp.where(place == b, order, 0.0)).astype(jnp.int32) for b in range(NBLK)]
    for b, owner in enumerate(owners):
        for q in range(5):
            for j in range(per_block):
                q_ref[q, b * per_block + j:b * per_block + j + 1, :] = block_ref[
                    owner, :, q * block + j * LANES:q * block + (j + 1) * LANES]
    a1 = q_ref[2].astype(jnp.int32)
    a2 = q_ref[3].astype(jnp.int32)
    slot = q_ref[4].astype(jnp.int32)

    at = first + SUB

    def cells(table):
        got = [jnp.zeros(shape, F32)] * 2
        for h in range(table.shape[0]):
            row = table[h:h + 1, :]
            got = [jnp.where((a >> 7) == h, pick(row, a & 127), g)
                   for a, g in zip((a1, a2), got)]
        return (got[0] - got[1]).astype(jnp.int32)

    u = cells(cell_ref[at:at + n_lines, :])
    v = cells(cell_ref[at + n_lines:at + 2 * n_lines, :])
    uv_ref[0] = u
    uv_ref[1] = v
    centre = times(turn(u * (frow_at * (2 * R) + (R - 1)), mod_r),
                   turn(v * (fcol_at * (2 * C) + (C - 1)), mod_c))
    scale = 0.5 / math.sqrt(NBLK * per_block * LANES)
    value = times((q_ref[0] * scale, q_ref[1] * scale), centre)
    s_ref[0] = value[0]
    s_ref[1] = value[1]
    for n, a in enumerate((a1, a2)):
        s_ref[2 + n] = ((a >> 3) + (a & 6) * 32).astype(F32)
        s_ref[4 + n] = ((a & 1) * NT + slot).astype(F32)

    iota = lax.broadcasted_iota(jnp.int32, shape, 0)

    def tables(s, carry):
        lane = pl.ds(pl.multiple_of(s * LANES, LANES), LANES)

        def phases(which, modulus, half):
            freq = jnp.broadcast_to(uv_ref[which, pl.ds(s, 1), :], shape)
            fine = turn(freq * (2 * iota + 1), modulus)
            middle = turn(freq * (16 * iota), modulus)
            coarse = turn(freq * (128 * iota), modulus)
            for a in range(half // 64):
                top = tuple(jnp.broadcast_to(x[a:a + 1], shape) for x in coarse)
                both = times(middle, top)
                for comp in range(2):
                    dr_ref[which, comp, 8 * a:8 * a + 8, :] = both[comp]
            for g in range(half // SUB):
                step = tuple(jnp.broadcast_to(dr_ref[which, comp, g:g + 1, :], shape)
                             for comp in range(2))
                yield times(fine, step)

        pairs = {}

        def put(ref, first, group, x):
            key = (id(ref), first)
            if group % 2 == 0:
                pairs[key] = x
            else:
                start = first + SUB * (group - 1)
                ref[start:start + 16, lane] = jnp.concatenate([pairs.pop(key), x], 0).astype(BF16)

        edge = (half_r - M) // SUB
        for g, (cos, sin) in enumerate(phases(0, mod_r, half_r)):
            if g >= edge:
                mine, other = taper_rows(g, half_r)
                at = slice((g - edge) * SUB, (g - edge + 1) * SUB)
                ec_ref[at, lane] = cos * other
                es_ref[at, lane] = sin * other
                cos, sin = cos * mine, sin * mine
            put(ac_ref, 0, g, cos)
            put(as_ref, 0, g, sin)
        for g, (cos, sin) in enumerate(phases(1, mod_c, half_c)):
            put(cc_ref, 0, g, cos)
            put(cs_ref, 0, g, sin)
            at = slice(g * SUB, (g + 1) * SUB)
            fc_ref[at, lane] = cos
            fs_ref[at, lane] = sin
        return carry

    lax.fori_loop(0, k_tiles, tables, 0, unroll=True)


def image_kernel(n_frow, depth, s_ref, mid_ref, a_ref, b_ref, ac_ref, as_ref, ec_ref, es_ref,
                 fc_ref, fs_ref, cc_ref, cs_ref, image_ref,
                 out_ref, tc_ref, ts_ref, uc_ref, us_ref, gain_ref, w_ref,
                 m1_ref, m2_ref, g1_ref, g2_ref, sems):
    frow_at = lax.axis_index("frow")
    r_odd = lax.rem(frow_at, 2) == 1
    c_odd = lax.rem(lax.axis_index("fcol"), 2) == 1
    k_tiles = s_ref.shape[1]
    half = depth // 2
    half_c = C // 2
    places = 2 * NT

    low_lane = lax.broadcasted_iota(jnp.int32, (places, LANES), 1) < LANES // 2
    for f in range(9):
        ref, row = (mid_ref, a_ref, b_ref)[f // 3], f % 3 * depth
        both = jnp.concatenate([ref[pl.ds(row, half, stride=2), :],
                                ref[pl.ds(row + 1, half, stride=2), :]], 0).T
        quarter = [both[i * places:(i + 1) * places] for i in range(4)]
        turned = [pltpu.roll(x, LANES // 2, 1) for x in quarter]
        for t in range(2):
            re = jnp.where(low_lane, quarter[2 * t], turned[2 * t + 1])
            im = jnp.where(low_lane, turned[2 * t], quarter[2 * t + 1])
            for comp, x in enumerate((re, im)):
                high = x.astype(BF16)
                at = (2 * (f - 1 if f else SUB) + comp) * places
                gain_ref[at:at + places, t * LANES:(t + 1) * LANES] = high
                if f == 0:
                    at += 2 * places
                    gain_ref[at:at + places, t * LANES:(t + 1) * LANES] = (
                        x - high.astype(F32)).astype(BF16)

    r_first, r_second = jnp.where(r_odd, 1, 2), jnp.where(r_odd, 2, 1)
    c_first, c_second = jnp.where(c_odd, 1, 2), jnp.where(c_odd, 2, 1)
    rows = {UP: r_first - 1, DOWN: r_second - 1, LEFT: 3 * c_first - 1, RIGHT: 3 * c_second - 1,
            UL: 3 * c_first + r_first - 1, UR: 3 * c_second + r_first - 1,
            DL: 3 * c_first + r_second - 1, DR: 3 * c_second + r_second - 1}

    step = 2 if k_tiles % 2 == 0 else 1
    wide = step * LANES
    shape = (SUB, wide)
    line_at = lax.broadcasted_iota(jnp.int32, (2 * depth, wide), 0).astype(F32)
    place_at = line_at[:places]
    row_at = lax.broadcasted_iota(jnp.int32, shape, 0)
    zero = jnp.zeros((M, wide), BF16)
    at_edge = jnp.logical_or(frow_at == 0, frow_at == n_frow - 1)
    keep = jnp.where(lax.rem(row_at, 3) == 1, jnp.where(at_edge, 0.0, 1.0), 1.0)

    def fold(parts):
        parts = [parts[i] for i in (0, 4, 2, 6, 1, 5, 3, 7)]
        for distance in (1, 2, 4):
            low = (row_at & distance) == 0
            count = len(parts) // 2
            parts = [jnp.where(low, x, y) + pltpu.roll(jnp.where(low, y, x), distance, 0)
                     for x, y in zip(parts[:count], parts[count:])]
        return parts[0]

    def gain_product(first, second):
        (g1r, g1i), (g2r, g2i) = first, second
        return g1r * g2r + g1i * g2i, g1i * g2r - g1r * g2i

    def weight(f, lane):
        return tuple(jnp.broadcast_to(w_ref[comp, pl.ds(rows[f], 1), lane], shape)
                     for comp in range(2))

    for p in range(k_tiles // step):
        lane = slice(p * wide, (p + 1) * wide)

        def line(q):
            return jnp.concatenate([s_ref[q, p * step + i:p * step + i + 1, :]
                                    for i in range(step)], 1)

        owns, nears = [], []
        for n in range(2):
            hot = jnp.where(line_at == line(2 + n), 1.0, 0.0).astype(BF16)
            mask = jnp.where(place_at == line(4 + n), 1.0, 0.0)
            z = jnp.dot(gain_ref[...], hot, preferred_element_type=F32)

            def part(f, comp):
                at = (2 * f + comp) * places
                x = z[at:at + places]
                if f == SUB:
                    x = x + z[at + 2 * places:at + 3 * places]
                x = x * mask
                return sum((x[i * SUB:(i + 1) * SUB] for i in range(1, places // SUB)), x[:SUB])

            owns.append([jnp.sum(part(SUB, comp), axis=0, keepdims=True) for comp in range(2)])
            nears.append([fold([part(f, comp) for f in range(SUB)]) for comp in range(2)])
        value = (line(0), line(1))
        own_w = times(value, gain_product(*owns))
        near_w = times(tuple(x * keep for x in value), gain_product(*nears))
        for comp in range(2):
            w_ref[comp, :, lane] = near_w[comp]

        pairs = {}

        def put(ref, first, group, x):
            key = (id(ref), first)
            if group % 2 == 0:
                pairs[key] = x
            else:
                start = first + SUB * (group - 1)
                ref[start:start + 16, lane] = jnp.concatenate([pairs.pop(key), x], 0).astype(BF16)

        edge = (half_c - M) // SUB
        wr, wi = [jnp.broadcast_to(x, shape) for x in own_w]
        (lr, li), (rr, ri) = weight(LEFT, lane), weight(RIGHT, lane)
        for g in range(half_c // SUB):
            at = slice(g * SUB, (g + 1) * SUB)
            cos, sin = fc_ref[at, lane], fs_ref[at, lane]
            own = (cos, sin)
            if g >= edge:
                mine, other = taper_rows(g, half_c, wide)
                own = (cos * mine, sin * mine)
                cos, sin = cos * other, sin * other
                base = 2 * half_c + M
                put(tc_ref, base, g - edge, lr * cos + li * sin)
                put(ts_ref, base, g - edge, lr * sin - li * cos)
                put(tc_ref, base + 2 * M, g - edge, rr * cos - ri * sin)
                put(ts_ref, base + 2 * M, g - edge, -(rr * sin + ri * cos))
            base = g * SUB // LANES * LANES
            put(tc_ref, base, g, wr * own[0])
            put(tc_ref, base + LANES, g, -wi * own[1])
            put(ts_ref, base, g, -wi * own[0])
            put(ts_ref, base + LANES, g, -wr * own[1])
        for ref in (tc_ref, ts_ref):
            ref[2 * half_c:2 * half_c + M, lane] = zero
            ref[2 * half_c + 2 * M:2 * half_c + 3 * M, lane] = zero

    def dot(a, b):
        return lax.dot_general(a, b, (((1,), (1,)), ((), ())), preferred_element_type=F32)

    half_r = R // 2
    n_lane = half_c // LANES

    def own_products(t):
        cols = slice(2 * t * LANES, 2 * (t + 1) * LANES if t < n_lane - 1 else tc_ref.shape[0])
        m1_ref[:, cols] = dot(ac_ref[...], tc_ref[cols, :])
        m2_ref[:, cols] = dot(as_ref[...], ts_ref[cols, :])

    own_products(n_lane - 1)
    signs = (-1, 1, -1, -1, 1, 1)
    for p in range(k_tiles // step):
        lane = slice(p * wide, (p + 1) * wide)
        for n, (f, sd) in enumerate(zip((UP, DOWN, UL, UR, DL, DR), signs)):
            wr, wi = weight(f, lane)
            for g in range(0, M // SUB, 2):
                tops, lows = [], []
                for i in range(2):
                    at = slice((g + i) * SUB, (g + i + 1) * SUB)
                    cos, sin = ec_ref[at, lane], es_ref[at, lane]
                    tops.append(wr * cos - (sd * wi) * sin)
                    lows.append(-(sd * wr) * sin - wi * cos)
                at = slice(n * M + g * SUB, n * M + (g + 2) * SUB)
                uc_ref[at, lane] = jnp.concatenate(tops, 0).astype(BF16)
                us_ref[at, lane] = jnp.concatenate(lows, 0).astype(BF16)
    g1_ref[...] = dot(uc_ref[...], cc_ref[...])
    g2_ref[...] = dot(us_ref[...], cs_ref[...])

    shape = (SUB, LANES)
    iota = lax.broadcasted_iota(jnp.int32, shape, 0)
    lane_at = lax.broadcasted_iota(jnp.int32, shape, 1)
    back_lane = (LANES - 1) - lane_at
    back_row = (SUB - 1) - iota
    edge_c = half_c - M
    edge_r = half_r - M
    col_own, col_other = [], []
    for t in range(n_lane):
        index = (lane_at + t * LANES).astype(F32)
        col_own.append(jnp.minimum((half_c + M - 0.5 - index) * (1.0 / (2 * M)), 1.0))
        col_other.append(jnp.maximum((index - (half_c - M - 0.5)) * (1.0 / (2 * M)), 0.0))

    def flip(x, index, axis):
        return jnp.take_along_axis(x, index, axis=axis, mode="promise_in_bounds")

    def finish(g, t, edged):
        rows = slice(g * SUB, (g + 1) * SUB)
        def part(ref, which):
            return ref[rows, (2 * t + which) * LANES:(2 * t + which + 1) * LANES]
        p, s_, r, q = part(m1_ref, 0), part(m1_ref, 1), part(m2_ref, 0), part(m2_ref, 1)
        even, odd = p + q, p - q
        plus, minus = r + s_, r - s_
        quad = {(1, 1): even + plus, (-1, -1): even - plus,
                (1, -1): odd + minus, (-1, 1): odd - minus}
        if (t + 1) * LANES > edge_c:
            base = 2 * half_c
            off = t * LANES - (half_c - LANES)
            for se, start in ((-1, base), (1, base + LANES)):
                lc = m1_ref[rows, start + off:start + off + LANES]
                ls = m2_ref[rows, start + off:start + off + LANES]
                quad[1, se] += lc + ls
                quad[-1, se] += lc - ls
        if edged:
            def edge(n):
                at = slice(n * M + g * SUB - edge_r, n * M + (g + 1) * SUB - edge_r)
                x = g1_ref[at, t * LANES:(t + 1) * LANES]
                y = g2_ref[at, t * LANES:(t + 1) * LANES]
                return {1: x + y, -1: x - y}
            for n, sd in ((0, -1), (1, 1)):
                e = edge(n)
                for se in (-1, 1):
                    quad[sd, se] += e[se] * col_own[t]
            if (t + 1) * LANES > edge_c:
                for n, (sd, se) in ((2, (-1, -1)), (3, (-1, 1)), (4, (1, -1)), (5, (1, 1))):
                    quad[sd, se] += edge(n)[se] * col_other[t]
        for (sd, se), x in quad.items():
            if sd < 0:
                x = flip(x, back_row, 0)
                at = slice(half_r - SUB - g * SUB, half_r - g * SUB)
            else:
                at = slice(half_r + g * SUB, half_r + (g + 1) * SUB)
            if se < 0:
                x = flip(x, back_lane, 1)
                start = half_c - (t + 1) * LANES
            else:
                start = half_c + t * LANES
            out_ref[at, start:start + LANES] = x

    n_groups = half_r // M

    def sends(j, t):
        copies = []
        for row in (half_r + 2 * M * j, half_r - 2 * M * (j + 1)):
            for col in (half_c + t * LANES, half_c - (t + 1) * LANES):
                at = (slice(row, row + 2 * M), slice(col, col + LANES))
                copies.append(pltpu.make_async_copy(
                    out_ref.at[at], image_ref.at[at], sems.at[(j * n_lane + t) * 4 + len(copies)]))
        return copies

    for t in range(n_lane - 2, -1, -1):
        own_products(t)
    for t in range(n_lane - 1, -1, -1):
        for j in range(n_groups):
            for g in range(j * M // SUB, (j + 1) * M // SUB):
                finish(g, t, j == n_groups - 1)
            if j % 2:
                for copy in sends(j // 2, t):
                    copy.start()
    for t in range(n_lane):
        for j in range(n_groups // 2):
            for copy in sends(j, t):
                copy.wait()


def swaps(size, around=False):
    both = []
    for first in (0, 1):
        pairs = [(i, i + 1) for i in range(first, size - 1, 2)]
        if around and first and size % 2 == 0:
            pairs.append((size - 1, 0))
        both.append(pairs + [(j, i) for i, j in pairs])
    return both


def shards(vis, station_pairs, visibility_time_slot, station_u_cells, station_v_cells,
           facet_station_gains, holder_device_order):
    n_frow = lax.axis_size("frow")
    n_fcol = lax.axis_size("fcol")
    block = vis.shape[1]
    k_tiles = NBLK * block // LANES
    k = k_tiles * LANES
    half_r, half_c = R // 2, C // 2
    wide = 2 * half_c + 4 * M
    vmem = pl.BlockSpec(memory_space=pltpu.VMEM)
    smem = pl.BlockSpec(memory_space=pltpu.SMEM)

    def lines(x):
        return x.reshape(-1, LANES)

    def shaped(*dims, dtype=F32):
        return jax.ShapeDtypeStruct(dims, dtype)

    def params(mib):
        return pltpu.CompilerParams(vmem_limit_bytes=mib * 1024 * 1024)

    n_lines = station_u_cells.size // LANES
    packed, labels = pl.pallas_call(
        pack_kernel,
        out_shape=[shaped(n_frow * n_fcol, 1, 5 * block), shaped(SUB + 2 * n_lines, LANES)],
        in_specs=[smem] + [vmem] * 5,
        name="pack",
    )(holder_device_order, vis, station_pairs, visibility_time_slot.reshape(1, block),
      lines(station_u_cells), lines(station_v_cells))
    facet_station_gains, packed = lax.optimization_barrier((facet_station_gains, packed))
    gains = facet_station_gains[0, 0]
    depth = gains.size // LANES
    own = gains.reshape(2, -1, LANES).transpose(1, 0, 2).reshape(depth, LANES)
    row_a, row_b = [lax.ppermute(own, "frow", pairs) for pairs in swaps(n_frow, True)]
    blocks = lax.all_to_all(packed, ("frow", "fcol"), 0, 0)
    mid = jnp.concatenate([own, row_a, row_b, labels], 0)
    col_a, col_b = [lax.ppermute(mid, "fcol", pairs) for pairs in swaps(n_fcol)]
    s, a_cos, a_sin, e_cos, e_sin, f_cos, f_sin, c_cos, c_sin = pl.pallas_call(
        functools.partial(table_kernel, n_frow, n_fcol, 3 * depth, n_lines),
        out_shape=[
            shaped(6, k_tiles, LANES),
            shaped(half_r, k, dtype=BF16), shaped(half_r, k, dtype=BF16),
            shaped(M, k), shaped(M, k),
            shaped(half_c, k), shaped(half_c, k),
            shaped(half_c, k, dtype=BF16), shaped(half_c, k, dtype=BF16),
        ],
        in_specs=[vmem] * 2,
        out_specs=[vmem] * 9,
        scratch_shapes=[
            pltpu.VMEM((5, k_tiles, LANES), F32),
            pltpu.VMEM((2, k_tiles, LANES), jnp.int32),
            pltpu.VMEM((2, 2, half_r // SUB, LANES), F32),
        ],
        compiler_params=params(24),
        name="tables",
    )(blocks, mid)
    return pl.pallas_call(
        functools.partial(image_kernel, n_frow, depth),
        out_shape=shaped(R, C),
        in_specs=[vmem] * 12,
        out_specs=pl.BlockSpec(memory_space=pl.ANY),
        scratch_shapes=[
            pltpu.VMEM((R, C), F32),
            pltpu.VMEM((wide, k), BF16),
            pltpu.VMEM((wide, k), BF16),
            pltpu.VMEM((6 * M, k), BF16),
            pltpu.VMEM((6 * M, k), BF16),
            pltpu.VMEM((40 * NT, 2 * depth), BF16),
            pltpu.VMEM((2, SUB, k), F32),
            pltpu.VMEM((half_r, wide), F32),
            pltpu.VMEM((half_r, wide), F32),
            pltpu.VMEM((6 * M, half_c), F32),
            pltpu.VMEM((6 * M, half_c), F32),
            pltpu.SemaphoreType.DMA((2 * half_r // M * (half_c // LANES),)),
        ],
        compiler_params=params(36),
        name="image",
    )(s, mid, col_a, col_b, a_cos, a_sin, e_cos, e_sin, f_cos, f_sin, c_cos, c_sin)


def solution(mesh):
    return jax.shard_map(
        shards,
        mesh=mesh,
        in_specs=(
            P(None, ("frow", "fcol")),
            P(None, ("frow", "fcol")),
            P(("frow", "fcol")),
            P(),
            P(),
            P("frow", "fcol", None, None),
            P(),
        ),
        out_specs=P("frow", "fcol"),
        check_vma=False,
    )
```

```python
import functools
import math

import jax
import jax.numpy as jnp
from jax import lax
from jax.experimental import pallas as pl
from jax.experimental.pallas import tpu as pltpu
from jax.sharding import PartitionSpec as P

R = 1024
C = 512
M = 64
NT = 16
NBLK = 4
LANES = 128
SUB = 8
OWN, LEFT, RIGHT, UP, DOWN, UL, UR, DL, DR = range(9)
F32 = jnp.float32
BF16 = jnp.bfloat16


def wrap(m, modulus):
    if modulus & (modulus - 1) == 0:
        return m & (modulus - 1)
    return jnp.remainder(m, modulus)


def turn(m, modulus):
    m = wrap(m, modulus)
    quarter = modulus // 4
    q = (m + modulus // 8) // quarter if quarter & (quarter - 1) else (
        (m + modulus // 8) >> (quarter.bit_length() - 1))
    x = (m - q * quarter).astype(F32) * (2.0 * math.pi / modulus)
    x2 = x * x
    s = x + x * x2 * (-1 / 6 + x2 * (1 / 120 + x2 * (-1 / 5040 + x2 * (1 / 362880))))
    c = 1.0 + x2 * (-0.5 + x2 * (1 / 24 + x2 * (-1 / 720 + x2 * (1 / 40320))))
    odd = (q & 1) == 1
    cos = jnp.where(odd, s, c)
    sin = jnp.where(odd, c, s)
    cos = jnp.where(((q + 1) & 2) != 0, -cos, cos)
    sin = jnp.where((q & 2) != 0, -sin, sin)
    return cos, sin


def times(a, b):
    return a[0] * b[0] - a[1] * b[1], a[0] * b[1] + a[1] * b[0]


def pack_kernel(order_ref, vis_ref, pair_ref, slot_ref, u_ref, v_ref, out_ref, label_ref):
    block = vis_ref.shape[1]
    lines = [vis_ref[0:1, :], vis_ref[1:2, :], pair_ref[0:1, :].astype(F32),
             pair_ref[1:2, :].astype(F32), slot_ref[...].astype(F32)]
    for copy in range(out_ref.shape[0]):
        for q, line in enumerate(lines):
            out_ref[copy, :, q * block:(q + 1) * block] = line
    n_lines = u_ref.shape[0]
    at = lax.broadcasted_iota(jnp.int32, (SUB, LANES), 1)
    order = jnp.zeros((SUB, LANES), jnp.int32)
    for b in range(NBLK):
        order = jnp.where(at == b, order_ref[b], order)
    label_ref[:SUB] = order.astype(F32)
    label_ref[SUB:SUB + n_lines] = u_ref[...].astype(F32)
    label_ref[SUB + n_lines:SUB + 2 * n_lines] = v_ref[...].astype(F32)


def pick(row, lane):
    return jnp.take_along_axis(
        jnp.broadcast_to(row, lane.shape), lane, axis=1, mode="promise_in_bounds")


def taper_rows(group, half, wide=LANES):
    index = (lax.broadcasted_iota(jnp.int32, (SUB, wide), 0) + SUB * group).astype(F32)
    return ((half + M - 0.5 - index) * (1.0 / (2 * M)),
            (index - (half - M - 0.5)) * (1.0 / (2 * M)))


def table_kernel(n_frow, n_fcol, first, n_lines, block_ref, cell_ref,
                 s_ref, ac_ref, as_ref, ec_ref, es_ref, fc_ref, fs_ref, cc_ref, cs_ref,
                 q_ref, uv_ref, dr_ref):
    frow_at = lax.axis_index("frow")
    fcol_at = lax.axis_index("fcol")
    half_r, half_c = R // 2, C // 2
    mod_r, mod_c = 2 * R * n_frow, 2 * C * n_fcol
    k_tiles = s_ref.shape[1]
    per_block = k_tiles // NBLK
    block = per_block * LANES
    shape = (SUB, LANES)

    order = cell_ref[first:first + 1, :]
    place = lax.broadcasted_iota(jnp.int32, (1, LANES), 1)
    owners = [jnp.sum(jnp.where(place == b, order, 0.0)).astype(jnp.int32) for b in range(NBLK)]
    for b, owner in enumerate(owners):
        for q in range(5):
            for j in range(per_block):
                q_ref[q, b * per_block + j:b * per_block + j + 1, :] = block_ref[
                    owner, :, q * block + j * LANES:q * block + (j + 1) * LANES]
    a1 = q_ref[2].astype(jnp.int32)
    a2 = q_ref[3].astype(jnp.int32)
    slot = q_ref[4].astype(jnp.int32)

    at = first + SUB

    def cells(table):
        got = [jnp.zeros(shape, F32)] * 2
        for h in range(table.shape[0]):
            row = table[h:h + 1, :]
            got = [jnp.where((a >> 7) == h, pick(row, a & 127), g)
                   for a, g in zip((a1, a2), got)]
        return (got[0] - got[1]).astype(jnp.int32)

    u = cells(cell_ref[at:at + n_lines, :])
    v = cells(cell_ref[at + n_lines:at + 2 * n_lines, :])
    uv_ref[0] = u
    uv_ref[1] = v
    centre = times(turn(u * (frow_at * (2 * R) + (R - 1)), mod_r),
                   turn(v * (fcol_at * (2 * C) + (C - 1)), mod_c))
    scale = 0.5 / math.sqrt(NBLK * per_block * LANES)
    value = times((q_ref[0] * scale, q_ref[1] * scale), centre)
    s_ref[0] = value[0]
    s_ref[1] = value[1]
    for n, a in enumerate((a1, a2)):
        s_ref[2 + n] = ((a >> 3) + (a & 6) * 32).astype(F32)
        s_ref[4 + n] = ((a & 1) * NT + slot).astype(F32)

    iota = lax.broadcasted_iota(jnp.int32, shape, 0)

    def tables(s, carry):
        lane = pl.ds(pl.multiple_of(s * LANES, LANES), LANES)

        def phases(which, modulus, half):
            freq = jnp.broadcast_to(uv_ref[which, pl.ds(s, 1), :], shape)
            fine = turn(freq * (2 * iota + 1), modulus)
            middle = turn(freq * (16 * iota), modulus)
            coarse = turn(freq * (128 * iota), modulus)
            for a in range(half // 64):
                top = tuple(jnp.broadcast_to(x[a:a + 1], shape) for x in coarse)
                both = times(middle, top)
                for comp in range(2):
                    dr_ref[which, comp, 8 * a:8 * a + 8, :] = both[comp]
            for g in range(half // SUB):
                step = tuple(jnp.broadcast_to(dr_ref[which, comp, g:g + 1, :], shape)
                             for comp in range(2))
                yield times(fine, step)

        pairs = {}

        def put(ref, first, group, x):
            key = (id(ref), first)
            if group % 2 == 0:
                pairs[key] = x
            else:
                start = first + SUB * (group - 1)
                ref[start:start + 16, lane] = jnp.concatenate([pairs.pop(key), x], 0).astype(BF16)

        edge = (half_r - M) // SUB
        for g, (cos, sin) in enumerate(phases(0, mod_r, half_r)):
            if g >= edge:
                mine, other = taper_rows(g, half_r)
                at = slice((g - edge) * SUB, (g - edge + 1) * SUB)
                ec_ref[at, lane] = cos * other
                es_ref[at, lane] = sin * other
                cos, sin = cos * mine, sin * mine
            put(ac_ref, 0, g, cos)
            put(as_ref, 0, g, sin)
        for g, (cos, sin) in enumerate(phases(1, mod_c, half_c)):
            put(cc_ref, 0, g, cos)
            put(cs_ref, 0, g, sin)
            at = slice(g * SUB, (g + 1) * SUB)
            fc_ref[at, lane] = cos
            fs_ref[at, lane] = sin
        return carry

    lax.fori_loop(0, k_tiles, tables, 0, unroll=True)


def image_kernel(n_frow, n_fcol, depth, s_ref, mid_ref, a_ref, b_ref, ac_ref, as_ref, ec_ref, es_ref,
                 fc_ref, fs_ref, cc_ref, cs_ref, image_ref,
                 out_ref, tc_ref, ts_ref, uc_ref, us_ref, gain_ref, w_ref,
                 m1_ref, m2_ref, g1_ref, g2_ref, sems):
    frow_at = lax.axis_index("frow")
    r_odd = lax.rem(frow_at, 2) == 1
    fcol_at = lax.axis_index("fcol")
    c_odd = lax.rem(fcol_at, 2) == 1
    k_tiles = s_ref.shape[1]
    half = depth // 2
    half_c = C // 2
    places = 2 * NT

    low_lane = lax.broadcasted_iota(jnp.int32, (places, LANES), 1) < LANES // 2
    for f in range(9):
        ref, row = (mid_ref, a_ref, b_ref)[f // 3], f % 3 * depth
        both = jnp.concatenate([ref[pl.ds(row, half, stride=2), :],
                                ref[pl.ds(row + 1, half, stride=2), :]], 0).T
        quarter = [both[i * places:(i + 1) * places] for i in range(4)]
        turned = [pltpu.roll(x, LANES // 2, 1) for x in quarter]
        for t in range(2):
            re = jnp.where(low_lane, quarter[2 * t], turned[2 * t + 1])
            im = jnp.where(low_lane, turned[2 * t], quarter[2 * t + 1])
            for comp, x in enumerate((re, im)):
                high = x.astype(BF16)
                at = (2 * (f - 1 if f else SUB) + comp) * places
                gain_ref[at:at + places, t * LANES:(t + 1) * LANES] = high
                if f == 0:
                    at += 2 * places
                    gain_ref[at:at + places, t * LANES:(t + 1) * LANES] = (
                        x - high.astype(F32)).astype(BF16)

    r_first, r_second = jnp.where(r_odd, 1, 2), jnp.where(r_odd, 2, 1)
    c_first, c_second = jnp.where(c_odd, 1, 2), jnp.where(c_odd, 2, 1)
    rows = {UP: r_first - 1, DOWN: r_second - 1, LEFT: 3 * c_first - 1, RIGHT: 3 * c_second - 1,
            UL: 3 * c_first + r_first - 1, UR: 3 * c_second + r_first - 1,
            DL: 3 * c_first + r_second - 1, DR: 3 * c_second + r_second - 1}

    step = 2 if k_tiles % 2 == 0 else 1
    wide = step * LANES
    shape = (SUB, wide)
    line_at = lax.broadcasted_iota(jnp.int32, (2 * depth, wide), 0).astype(F32)
    place_at = line_at[:places]
    row_at = lax.broadcasted_iota(jnp.int32, shape, 0)
    zero = jnp.zeros((M, wide), BF16)
    r_edge = jnp.logical_or(frow_at == 0, frow_at == n_frow - 1)
    c_edge = jnp.logical_or(fcol_at == 0, fcol_at == n_fcol - 1)
    keep = (jnp.where(lax.rem(row_at, 3) == 1, jnp.where(r_edge, 0.0, 1.0), 1.0)
            * jnp.where(row_at >= 5, jnp.where(c_edge, 0.0, 1.0), 1.0))

    def fold(parts):
        parts = [parts[i] for i in (0, 4, 2, 6, 1, 5, 3, 7)]
        for distance in (1, 2, 4):
            low = (row_at & distance) == 0
            count = len(parts) // 2
            parts = [jnp.where(low, x, y) + pltpu.roll(jnp.where(low, y, x), distance, 0)
                     for x, y in zip(parts[:count], parts[count:])]
        return parts[0]

    def gain_product(first, second):
        (g1r, g1i), (g2r, g2i) = first, second
        return g1r * g2r + g1i * g2i, g1i * g2r - g1r * g2i

    def weight(f, lane):
        return tuple(jnp.broadcast_to(w_ref[comp, pl.ds(rows[f], 1), lane], shape)
                     for comp in range(2))

    for p in range(k_tiles // step):
        lane = slice(p * wide, (p + 1) * wide)

        def line(q):
            return jnp.concatenate([s_ref[q, p * step + i:p * step + i + 1, :]
                                    for i in range(step)], 1)

        owns, nears = [], []
        for n in range(2):
            hot = jnp.where(line_at == line(2 + n), 1.0, 0.0).astype(BF16)
            mask = jnp.where(place_at == line(4 + n), 1.0, 0.0)
            z = jnp.dot(gain_ref[...], hot, preferred_element_type=F32)

            def part(f, comp):
                at = (2 * f + comp) * places
                x = z[at:at + places]
                if f == SUB:
                    x = x + z[at + 2 * places:at + 3 * places]
                x = x * mask
                return sum((x[i * SUB:(i + 1) * SUB] for i in range(1, places // SUB)), x[:SUB])

            owns.append([jnp.sum(part(SUB, comp), axis=0, keepdims=True) for comp in range(2)])
            nears.append([fold([part(f, comp) for f in range(SUB)]) for comp in range(2)])
        value = (line(0), line(1))
        own_w = times(value, gain_product(*owns))
        near_w = times(tuple(x * keep for x in value), gain_product(*nears))
        for comp in range(2):
            w_ref[comp, :, lane] = near_w[comp]

        pairs = {}

        def put(ref, first, group, x):
            key = (id(ref), first)
            if group % 2 == 0:
                pairs[key] = x
            else:
                start = first + SUB * (group - 1)
                ref[start:start + 16, lane] = jnp.concatenate([pairs.pop(key), x], 0).astype(BF16)

        edge = (half_c - M) // SUB
        wr, wi = [jnp.broadcast_to(x, shape) for x in own_w]
        (lr, li), (rr, ri) = weight(LEFT, lane), weight(RIGHT, lane)
        for g in range(half_c // SUB):
            at = slice(g * SUB, (g + 1) * SUB)
            cos, sin = fc_ref[at, lane], fs_ref[at, lane]
            own = (cos, sin)
            if g >= edge:
                mine, other = taper_rows(g, half_c, wide)
                own = (cos * mine, sin * mine)
                cos, sin = cos * other, sin * other
                base = 2 * half_c + M
                put(tc_ref, base, g - edge, lr * cos + li * sin)
                put(ts_ref, base, g - edge, lr * sin - li * cos)
                put(tc_ref, base + 2 * M, g - edge, rr * cos - ri * sin)
                put(ts_ref, base + 2 * M, g - edge, -(rr * sin + ri * cos))
            base = g * SUB // LANES * LANES
            put(tc_ref, base, g, wr * own[0])
            put(tc_ref, base + LANES, g, -wi * own[1])
            put(ts_ref, base, g, -wi * own[0])
            put(ts_ref, base + LANES, g, -wr * own[1])
        for ref in (tc_ref, ts_ref):
            ref[2 * half_c:2 * half_c + M, lane] = zero
            ref[2 * half_c + 2 * M:2 * half_c + 3 * M, lane] = zero

    def dot(a, b):
        return lax.dot_general(a, b, (((1,), (1,)), ((), ())), preferred_element_type=F32)

    half_r = R // 2
    n_lane = half_c // LANES

    def own_products(t):
        cols = slice(2 * t * LANES, 2 * (t + 1) * LANES if t < n_lane - 1 else tc_ref.shape[0])
        m1_ref[:, cols] = dot(ac_ref[...], tc_ref[cols, :])
        m2_ref[:, cols] = dot(as_ref[...], ts_ref[cols, :])

    own_products(n_lane - 1)
    signs = (-1, 1, -1, -1, 1, 1)
    for p in range(k_tiles // step):
        lane = slice(p * wide, (p + 1) * wide)
        for n, (f, sd) in enumerate(zip((UP, DOWN, UL, UR, DL, DR), signs)):
            wr, wi = weight(f, lane)
            for g in range(0, M // SUB, 2):
                tops, lows = [], []
                for i in range(2):
                    at = slice((g + i) * SUB, (g + i + 1) * SUB)
                    cos, sin = ec_ref[at, lane], es_ref[at, lane]
                    tops.append(wr * cos - (sd * wi) * sin)
                    lows.append(-(sd * wr) * sin - wi * cos)
                at = slice(n * M + g * SUB, n * M + (g + 2) * SUB)
                uc_ref[at, lane] = jnp.concatenate(tops, 0).astype(BF16)
                us_ref[at, lane] = jnp.concatenate(lows, 0).astype(BF16)
    g1_ref[...] = dot(uc_ref[...], cc_ref[...])
    g2_ref[...] = dot(us_ref[...], cs_ref[...])

    shape = (SUB, LANES)
    iota = lax.broadcasted_iota(jnp.int32, shape, 0)
    lane_at = lax.broadcasted_iota(jnp.int32, shape, 1)
    back_lane = (LANES - 1) - lane_at
    back_row = (SUB - 1) - iota
    edge_c = half_c - M
    edge_r = half_r - M
    col_own, col_other = [], []
    for t in range(n_lane):
        index = (lane_at + t * LANES).astype(F32)
        col_own.append(jnp.minimum((half_c + M - 0.5 - index) * (1.0 / (2 * M)), 1.0))
        col_other.append(jnp.maximum((index - (half_c - M - 0.5)) * (1.0 / (2 * M)), 0.0))

    def flip(x, index, axis):
        return jnp.take_along_axis(x, index, axis=axis, mode="promise_in_bounds")

    def finish(g, t, edged):
        rows = slice(g * SUB, (g + 1) * SUB)
        def part(ref, which):
            return ref[rows, (2 * t + which) * LANES:(2 * t + which + 1) * LANES]
        p, s_, r, q = part(m1_ref, 0), part(m1_ref, 1), part(m2_ref, 0), part(m2_ref, 1)
        even, odd = p + q, p - q
        plus, minus = r + s_, r - s_
        quad = {(1, 1): even + plus, (-1, -1): even - plus,
                (1, -1): odd + minus, (-1, 1): odd - minus}
        if (t + 1) * LANES > edge_c:
            base = 2 * half_c
            off = t * LANES - (half_c - LANES)
            for se, start in ((-1, base), (1, base + LANES)):
                lc = m1_ref[rows, start + off:start + off + LANES]
                ls = m2_ref[rows, start + off:start + off + LANES]
                quad[1, se] += lc + ls
                quad[-1, se] += lc - ls
        if edged:
            def edge(n):
                at = slice(n * M + g * SUB - edge_r, n * M + (g + 1) * SUB - edge_r)
                x = g1_ref[at, t * LANES:(t + 1) * LANES]
                y = g2_ref[at, t * LANES:(t + 1) * LANES]
                return {1: x + y, -1: x - y}
            for n, sd in ((0, -1), (1, 1)):
                e = edge(n)
                for se in (-1, 1):
                    quad[sd, se] += e[se] * col_own[t]
            if (t + 1) * LANES > edge_c:
                for n, (sd, se) in ((2, (-1, -1)), (3, (-1, 1)), (4, (1, -1)), (5, (1, 1))):
                    quad[sd, se] += edge(n)[se] * col_other[t]
        for (sd, se), x in quad.items():
            if sd < 0:
                x = flip(x, back_row, 0)
                at = slice(half_r - SUB - g * SUB, half_r - g * SUB)
            else:
                at = slice(half_r + g * SUB, half_r + (g + 1) * SUB)
            if se < 0:
                x = flip(x, back_lane, 1)
                start = half_c - (t + 1) * LANES
            else:
                start = half_c + t * LANES
            out_ref[at, start:start + LANES] = x

    n_groups = half_r // M

    def sends(j, t):
        copies = []
        for row in (half_r + 2 * M * j, half_r - 2 * M * (j + 1)):
            for col in (half_c + t * LANES, half_c - (t + 1) * LANES):
                at = (slice(row, row + 2 * M), slice(col, col + LANES))
                copies.append(pltpu.make_async_copy(
                    out_ref.at[at], image_ref.at[at], sems.at[(j * n_lane + t) * 4 + len(copies)]))
        return copies

    for t in range(n_lane - 2, -1, -1):
        own_products(t)
    for t in range(n_lane - 1, -1, -1):
        for j in range(n_groups):
            for g in range(j * M // SUB, (j + 1) * M // SUB):
                finish(g, t, j == n_groups - 1)
            if j % 2:
                for copy in sends(j // 2, t):
                    copy.start()
    for t in range(n_lane):
        for j in range(n_groups // 2):
            for copy in sends(j, t):
                copy.wait()


def swaps(size, around):
    both = []
    for first in (0, 1):
        pairs = [(i, i + 1) for i in range(first, size - 1, 2)]
        if around and first and size % 2 == 0:
            pairs.append((size - 1, 0))
        swap = dict(pairs) | {j: i for i, j in pairs}
        both.append([(i, swap.get(i, i)) for i in range(size)])
    return both


def shards(vis, station_pairs, visibility_time_slot, station_u_cells, station_v_cells,
           facet_station_gains, holder_device_order):
    n_frow = lax.axis_size("frow")
    n_fcol = lax.axis_size("fcol")
    block = vis.shape[1]
    k_tiles = NBLK * block // LANES
    k = k_tiles * LANES
    half_r, half_c = R // 2, C // 2
    wide = 2 * half_c + 4 * M
    vmem = pl.BlockSpec(memory_space=pltpu.VMEM)
    smem = pl.BlockSpec(memory_space=pltpu.SMEM)

    def lines(x):
        return x.reshape(-1, LANES)

    def shaped(*dims, dtype=F32):
        return jax.ShapeDtypeStruct(dims, dtype)

    def params(mib):
        return pltpu.CompilerParams(vmem_limit_bytes=mib * 1024 * 1024)

    n_lines = station_u_cells.size // LANES
    packed, labels = pl.pallas_call(
        pack_kernel,
        out_shape=[shaped(n_frow * n_fcol, 1, 5 * block), shaped(SUB + 2 * n_lines, LANES)],
        in_specs=[smem] + [vmem] * 5,
        name="pack",
    )(holder_device_order, vis, station_pairs, visibility_time_slot.reshape(1, block),
      lines(station_u_cells), lines(station_v_cells))
    facet_station_gains, packed = lax.optimization_barrier((facet_station_gains, packed))
    gains = facet_station_gains[0, 0]
    depth = gains.size // LANES
    own = gains.reshape(2, -1, LANES).transpose(1, 0, 2).reshape(depth, LANES)
    row_a, row_b = [lax.ppermute(own, "frow", pairs) for pairs in swaps(n_frow, True)]
    blocks = lax.all_to_all(packed, ("frow", "fcol"), 0, 0)
    mid = jnp.concatenate([own, row_a, row_b, labels], 0)
    col_a, col_b = [lax.ppermute(mid, "fcol", pairs) for pairs in swaps(n_fcol, False)]
    s, a_cos, a_sin, e_cos, e_sin, f_cos, f_sin, c_cos, c_sin = pl.pallas_call(
        functools.partial(table_kernel, n_frow, n_fcol, 3 * depth, n_lines),
        out_shape=[
            shaped(6, k_tiles, LANES),
            shaped(half_r, k, dtype=BF16), shaped(half_r, k, dtype=BF16),
            shaped(M, k), shaped(M, k),
            shaped(half_c, k), shaped(half_c, k),
            shaped(half_c, k, dtype=BF16), shaped(half_c, k, dtype=BF16),
        ],
        in_specs=[vmem] * 2,
        out_specs=[vmem] * 9,
        scratch_shapes=[
            pltpu.VMEM((5, k_tiles, LANES), F32),
            pltpu.VMEM((2, k_tiles, LANES), jnp.int32),
            pltpu.VMEM((2, 2, half_r // SUB, LANES), F32),
        ],
        compiler_params=params(24),
        name="tables",
    )(blocks, mid)
    return pl.pallas_call(
        functools.partial(image_kernel, n_frow, n_fcol, depth),
        out_shape=shaped(R, C),
        in_specs=[vmem] * 12,
        out_specs=pl.BlockSpec(memory_space=pl.ANY),
        scratch_shapes=[
            pltpu.VMEM((R, C), F32),
            pltpu.VMEM((wide, k), BF16),
            pltpu.VMEM((wide, k), BF16),
            pltpu.VMEM((6 * M, k), BF16),
            pltpu.VMEM((6 * M, k), BF16),
            pltpu.VMEM((40 * NT, 2 * depth), BF16),
            pltpu.VMEM((2, SUB, k), F32),
            pltpu.VMEM((half_r, wide), F32),
            pltpu.VMEM((half_r, wide), F32),
            pltpu.VMEM((6 * M, half_c), F32),
            pltpu.VMEM((6 * M, half_c), F32),
            pltpu.SemaphoreType.DMA((2 * half_r // M * (half_c // LANES),)),
        ],
        compiler_params=params(36),
        name="image",
    )(s, mid, col_a, col_b, a_cos, a_sin, e_cos, e_sin, f_cos, f_sin, c_cos, c_sin)


def solution(mesh):
    return jax.shard_map(
        shards,
        mesh=mesh,
        in_specs=(
            P(None, ("frow", "fcol")),
            P(None, ("frow", "fcol")),
            P(("frow", "fcol")),
            P(),
            P(),
            P("frow", "fcol", None, None),
            P(),
        ),
        out_specs=P("frow", "fcol"),
        check_vma=False,
    )
```

```python
import functools
import math

import jax
import jax.numpy as jnp
from jax import lax
from jax.experimental import pallas as pl
from jax.experimental.pallas import tpu as pltpu
from jax.sharding import PartitionSpec as P

R = 1024
C = 512
M = 64
NT = 16
NBLK = 4
LANES = 128
SUB = 8
OWN, LEFT, RIGHT, UP, DOWN, UL, UR, DL, DR = range(9)
F32 = jnp.float32
BF16 = jnp.bfloat16


def wrap(m, modulus):
    if modulus & (modulus - 1) == 0:
        return m & (modulus - 1)
    return jnp.remainder(m, modulus)


def turn(m, modulus):
    m = wrap(m, modulus)
    quarter = modulus // 4
    q = (m + modulus // 8) // quarter if quarter & (quarter - 1) else (
        (m + modulus // 8) >> (quarter.bit_length() - 1))
    x = (m - q * quarter).astype(F32) * (2.0 * math.pi / modulus)
    x2 = x * x
    s = x + x * x2 * (-1 / 6 + x2 * (1 / 120 + x2 * (-1 / 5040 + x2 * (1 / 362880))))
    c = 1.0 + x2 * (-0.5 + x2 * (1 / 24 + x2 * (-1 / 720 + x2 * (1 / 40320))))
    odd = (q & 1) == 1
    cos = jnp.where(odd, s, c)
    sin = jnp.where(odd, c, s)
    cos = jnp.where(((q + 1) & 2) != 0, -cos, cos)
    sin = jnp.where((q & 2) != 0, -sin, sin)
    return cos, sin


def times(a, b):
    return a[0] * b[0] - a[1] * b[1], a[0] * b[1] + a[1] * b[0]


def pack_kernel(order_ref, vis_ref, pair_ref, slot_ref, u_ref, v_ref, out_ref, label_ref):
    block = vis_ref.shape[1]
    lines = [vis_ref[0:1, :], vis_ref[1:2, :], pair_ref[0:1, :].astype(F32),
             pair_ref[1:2, :].astype(F32), slot_ref[...].astype(F32)]
    for copy in range(out_ref.shape[0]):
        for q, line in enumerate(lines):
            out_ref[copy, :, q * block:(q + 1) * block] = line
    n_lines = u_ref.shape[0]
    at = lax.broadcasted_iota(jnp.int32, (SUB, LANES), 1)
    order = jnp.zeros((SUB, LANES), jnp.int32)
    for b in range(NBLK):
        order = jnp.where(at == b, order_ref[b], order)
    label_ref[:SUB] = order.astype(F32)
    label_ref[SUB:SUB + n_lines] = u_ref[...].astype(F32)
    label_ref[SUB + n_lines:SUB + 2 * n_lines] = v_ref[...].astype(F32)


def pick(row, lane):
    return jnp.take_along_axis(
        jnp.broadcast_to(row, lane.shape), lane, axis=1, mode="promise_in_bounds")


def taper_rows(group, half, wide=LANES):
    index = (lax.broadcasted_iota(jnp.int32, (SUB, wide), 0) + SUB * group).astype(F32)
    return ((half + M - 0.5 - index) * (1.0 / (2 * M)),
            (index - (half - M - 0.5)) * (1.0 / (2 * M)))


def table_kernel(n_frow, n_fcol, first, n_lines, block_ref, cell_ref,
                 s_ref, ac_ref, as_ref, ec_ref, es_ref, fc_ref, fs_ref, cc_ref, cs_ref,
                 q_ref, uv_ref, dr_ref):
    frow_at = lax.axis_index("frow")
    fcol_at = lax.axis_index("fcol")
    half_r, half_c = R // 2, C // 2
    mod_r, mod_c = 2 * R * n_frow, 2 * C * n_fcol
    k_tiles = s_ref.shape[1]
    per_block = k_tiles // NBLK
    block = per_block * LANES
    shape = (SUB, LANES)

    order = cell_ref[first:first + 1, :]
    place = lax.broadcasted_iota(jnp.int32, (1, LANES), 1)
    owners = [jnp.sum(jnp.where(place == b, order, 0.0)).astype(jnp.int32) for b in range(NBLK)]
    for b, owner in enumerate(owners):
        for q in range(5):
            for j in range(per_block):
                q_ref[q, b * per_block + j:b * per_block + j + 1, :] = block_ref[
                    owner, :, q * block + j * LANES:q * block + (j + 1) * LANES]
    a1 = q_ref[2].astype(jnp.int32)
    a2 = q_ref[3].astype(jnp.int32)
    slot = q_ref[4].astype(jnp.int32)

    at = first + SUB

    def cells(table):
        got = [jnp.zeros(shape, F32)] * 2
        for h in range(table.shape[0]):
            row = table[h:h + 1, :]
            got = [jnp.where((a >> 7) == h, pick(row, a & 127), g)
                   for a, g in zip((a1, a2), got)]
        return (got[0] - got[1]).astype(jnp.int32)

    u = cells(cell_ref[at:at + n_lines, :])
    v = cells(cell_ref[at + n_lines:at + 2 * n_lines, :])
    uv_ref[0] = u
    uv_ref[1] = v
    centre = times(turn(u * (frow_at * (2 * R) + (R - 1)), mod_r),
                   turn(v * (fcol_at * (2 * C) + (C - 1)), mod_c))
    scale = 0.5 / math.sqrt(NBLK * per_block * LANES)
    value = times((q_ref[0] * scale, q_ref[1] * scale), centre)
    s_ref[0] = value[0]
    s_ref[1] = value[1]
    for n, a in enumerate((a1, a2)):
        s_ref[2 + n] = ((a >> 3) + (a & 6) * 32).astype(F32)
        s_ref[4 + n] = ((a & 1) * NT + slot).astype(F32)

    iota = lax.broadcasted_iota(jnp.int32, shape, 0)

    def tables(s, carry):
        lane = pl.ds(pl.multiple_of(s * LANES, LANES), LANES)

        def phases(which, modulus, half):
            freq = jnp.broadcast_to(uv_ref[which, pl.ds(s, 1), :], shape)
            fine = turn(freq * (2 * iota + 1), modulus)
            middle = turn(freq * (16 * iota), modulus)
            coarse = turn(freq * (128 * iota), modulus)
            for a in range(half // 64):
                top = tuple(jnp.broadcast_to(x[a:a + 1], shape) for x in coarse)
                both = times(middle, top)
                for comp in range(2):
                    dr_ref[which, comp, 8 * a:8 * a + 8, :] = both[comp]
            for g in range(half // SUB):
                step = tuple(jnp.broadcast_to(dr_ref[which, comp, g:g + 1, :], shape)
                             for comp in range(2))
                yield times(fine, step)

        pairs = {}

        def put(ref, first, group, x):
            key = (id(ref), first)
            if group % 2 == 0:
                pairs[key] = x
            else:
                start = first + SUB * (group - 1)
                ref[start:start + 16, lane] = jnp.concatenate([pairs.pop(key), x], 0).astype(BF16)

        edge = (half_r - M) // SUB
        for g, (cos, sin) in enumerate(phases(0, mod_r, half_r)):
            if g >= edge:
                mine, other = taper_rows(g, half_r)
                at = slice((g - edge) * SUB, (g - edge + 1) * SUB)
                ec_ref[at, lane] = cos * other
                es_ref[at, lane] = sin * other
                cos, sin = cos * mine, sin * mine
            put(ac_ref, 0, g, cos)
            put(as_ref, 0, g, sin)
        for g, (cos, sin) in enumerate(phases(1, mod_c, half_c)):
            put(cc_ref, 0, g, cos)
            put(cs_ref, 0, g, sin)
            at = slice(g * SUB, (g + 1) * SUB)
            fc_ref[at, lane] = cos
            fs_ref[at, lane] = sin
        return carry

    lax.fori_loop(0, k_tiles, tables, 0, unroll=True)


def image_kernel(n_frow, n_fcol, depth, s_ref, mid_ref, a_ref, b_ref, ac_ref, as_ref, ec_ref, es_ref,
                 fc_ref, fs_ref, cc_ref, cs_ref, image_ref,
                 out_ref, tc_ref, ts_ref, uc_ref, us_ref, gain_ref, w_ref,
                 m1_ref, m2_ref, g1_ref, g2_ref, sems):
    frow_at = lax.axis_index("frow")
    r_odd = lax.rem(frow_at, 2) == 1
    fcol_at = lax.axis_index("fcol")
    c_odd = lax.rem(fcol_at, 2) == 1
    k_tiles = s_ref.shape[1]
    half = depth // 2
    half_c = C // 2
    places = 2 * NT

    low_lane = lax.broadcasted_iota(jnp.int32, (places, LANES), 1) < LANES // 2
    for f in range(9):
        ref, row = (mid_ref, a_ref, b_ref)[f // 3], f % 3 * depth
        both = jnp.concatenate([ref[pl.ds(row, half, stride=2), :],
                                ref[pl.ds(row + 1, half, stride=2), :]], 0).T
        quarter = [both[i * places:(i + 1) * places] for i in range(4)]
        turned = [pltpu.roll(x, LANES // 2, 1) for x in quarter]
        for t in range(2):
            re = jnp.where(low_lane, quarter[2 * t], turned[2 * t + 1])
            im = jnp.where(low_lane, turned[2 * t], quarter[2 * t + 1])
            for comp, x in enumerate((re, im)):
                high = x.astype(BF16)
                at = (2 * (f - 1 if f else SUB) + comp) * places
                gain_ref[at:at + places, t * LANES:(t + 1) * LANES] = high
                if f == 0:
                    at += 2 * places
                    gain_ref[at:at + places, t * LANES:(t + 1) * LANES] = (
                        x - high.astype(F32)).astype(BF16)

    r_first, r_second = jnp.where(r_odd, 1, 2), jnp.where(r_odd, 2, 1)
    c_first, c_second = jnp.where(c_odd, 1, 2), jnp.where(c_odd, 2, 1)
    rows = {UP: r_first - 1, DOWN: r_second - 1, LEFT: 3 * c_first - 1, RIGHT: 3 * c_second - 1,
            UL: 3 * c_first + r_first - 1, UR: 3 * c_second + r_first - 1,
            DL: 3 * c_first + r_second - 1, DR: 3 * c_second + r_second - 1}

    step = 2 if k_tiles % 2 == 0 else 1
    wide = step * LANES
    shape = (SUB, wide)
    line_at = lax.broadcasted_iota(jnp.int32, (2 * depth, wide), 0).astype(F32)
    place_at = line_at[:places]
    row_at = lax.broadcasted_iota(jnp.int32, shape, 0)
    zero = jnp.zeros((M, wide), BF16)
    r_edge = jnp.logical_or(frow_at == 0, frow_at == n_frow - 1)
    c_edge = jnp.logical_or(fcol_at == 0, fcol_at == n_fcol - 1)
    keep = (jnp.where(lax.rem(row_at, 3) == 1, jnp.where(r_edge, 0.0, 1.0), 1.0)
            * jnp.where(row_at >= 5, jnp.where(c_edge, 0.0, 1.0), 1.0))

    def fold(parts):
        parts = [parts[i] for i in (0, 4, 2, 6, 1, 5, 3, 7)]
        for distance in (1, 2, 4):
            low = (row_at & distance) == 0
            count = len(parts) // 2
            parts = [jnp.where(low, x, y) + pltpu.roll(jnp.where(low, y, x), distance, 0)
                     for x, y in zip(parts[:count], parts[count:])]
        return parts[0]

    def gain_product(first, second):
        (g1r, g1i), (g2r, g2i) = first, second
        return g1r * g2r + g1i * g2i, g1i * g2r - g1r * g2i

    def weight(f, lane):
        return tuple(jnp.broadcast_to(w_ref[comp, pl.ds(rows[f], 1), lane], shape)
                     for comp in range(2))

    for p in range(k_tiles // step):
        lane = slice(p * wide, (p + 1) * wide)

        def line(q):
            return jnp.concatenate([s_ref[q, p * step + i:p * step + i + 1, :]
                                    for i in range(step)], 1)

        owns, nears = [], []
        for n in range(2):
            hot = jnp.where(line_at == line(2 + n), 1.0, 0.0).astype(BF16)
            mask = jnp.where(place_at == line(4 + n), 1.0, 0.0)
            z = jnp.dot(gain_ref[...], hot, preferred_element_type=F32)

            def part(f, comp):
                at = (2 * f + comp) * places
                x = z[at:at + places]
                if f == SUB:
                    x = x + z[at + 2 * places:at + 3 * places]
                x = x * mask
                return sum((x[i * SUB:(i + 1) * SUB] for i in range(1, places // SUB)), x[:SUB])

            owns.append([jnp.sum(part(SUB, comp), axis=0, keepdims=True) for comp in range(2)])
            nears.append([fold([part(f, comp) for f in range(SUB)]) for comp in range(2)])
        value = (line(0), line(1))
        own_w = times(value, gain_product(*owns))
        near_w = times(tuple(x * keep for x in value), gain_product(*nears))
        for comp in range(2):
            w_ref[comp, :, lane] = near_w[comp]

        pairs = {}

        def put(ref, first, group, x):
            key = (id(ref), first)
            if group % 2 == 0:
                pairs[key] = x
            else:
                start = first + SUB * (group - 1)
                ref[start:start + 16, lane] = jnp.concatenate([pairs.pop(key), x], 0).astype(BF16)

        edge = (half_c - M) // SUB
        wr, wi = [jnp.broadcast_to(x, shape) for x in own_w]
        (lr, li), (rr, ri) = weight(LEFT, lane), weight(RIGHT, lane)
        for g in range(half_c // SUB):
            at = slice(g * SUB, (g + 1) * SUB)
            cos, sin = fc_ref[at, lane], fs_ref[at, lane]
            own = (cos, sin)
            if g >= edge:
                mine, other = taper_rows(g, half_c, wide)
                own = (cos * mine, sin * mine)
                cos, sin = cos * other, sin * other
                base = 2 * half_c + M
                put(tc_ref, base, g - edge, lr * cos + li * sin)
                put(ts_ref, base, g - edge, lr * sin - li * cos)
                put(tc_ref, base + 2 * M, g - edge, rr * cos - ri * sin)
                put(ts_ref, base + 2 * M, g - edge, -(rr * sin + ri * cos))
            base = g * SUB // LANES * LANES
            put(tc_ref, base, g, wr * own[0])
            put(tc_ref, base + LANES, g, -wi * own[1])
            put(ts_ref, base, g, -wi * own[0])
            put(ts_ref, base + LANES, g, -wr * own[1])
        for ref in (tc_ref, ts_ref):
            ref[2 * half_c:2 * half_c + M, lane] = zero
            ref[2 * half_c + 2 * M:2 * half_c + 3 * M, lane] = zero

    def dot(a, b):
        return lax.dot_general(a, b, (((1,), (1,)), ((), ())), preferred_element_type=F32)

    half_r = R // 2
    n_lane = half_c // LANES

    def own_products(t):
        cols = slice(2 * t * LANES, 2 * (t + 1) * LANES if t < n_lane - 1 else tc_ref.shape[0])
        m1_ref[:, cols] = dot(ac_ref[...], tc_ref[cols, :])
        m2_ref[:, cols] = dot(as_ref[...], ts_ref[cols, :])

    own_products(n_lane - 1)
    signs = (-1, 1, -1, -1, 1, 1)
    for p in range(k_tiles // step):
        lane = slice(p * wide, (p + 1) * wide)
        for n, (f, sd) in enumerate(zip((UP, DOWN, UL, UR, DL, DR), signs)):
            wr, wi = weight(f, lane)
            for g in range(0, M // SUB, 2):
                tops, lows = [], []
                for i in range(2):
                    at = slice((g + i) * SUB, (g + i + 1) * SUB)
                    cos, sin = ec_ref[at, lane], es_ref[at, lane]
                    tops.append(wr * cos - (sd * wi) * sin)
                    lows.append(-(sd * wr) * sin - wi * cos)
                at = slice(n * M + g * SUB, n * M + (g + 2) * SUB)
                uc_ref[at, lane] = jnp.concatenate(tops, 0).astype(BF16)
                us_ref[at, lane] = jnp.concatenate(lows, 0).astype(BF16)
    g1_ref[...] = dot(uc_ref[...], cc_ref[...])
    g2_ref[...] = dot(us_ref[...], cs_ref[...])

    shape = (SUB, LANES)
    iota = lax.broadcasted_iota(jnp.int32, shape, 0)
    lane_at = lax.broadcasted_iota(jnp.int32, shape, 1)
    back_lane = (LANES - 1) - lane_at
    back_row = (SUB - 1) - iota
    edge_c = half_c - M
    edge_r = half_r - M
    col_own, col_other = [], []
    for t in range(n_lane):
        index = (lane_at + t * LANES).astype(F32)
        col_own.append(jnp.minimum((half_c + M - 0.5 - index) * (1.0 / (2 * M)), 1.0))
        col_other.append(jnp.maximum((index - (half_c - M - 0.5)) * (1.0 / (2 * M)), 0.0))

    def flip(x, index, axis):
        return jnp.take_along_axis(x, index, axis=axis, mode="promise_in_bounds")

    def finish(g, t, edged):
        rows = slice(g * SUB, (g + 1) * SUB)
        def part(ref, which):
            return ref[rows, (2 * t + which) * LANES:(2 * t + which + 1) * LANES]
        p, s_, r, q = part(m1_ref, 0), part(m1_ref, 1), part(m2_ref, 0), part(m2_ref, 1)
        even, odd = p + q, p - q
        plus, minus = r + s_, r - s_
        quad = {(1, 1): even + plus, (-1, -1): even - plus,
                (1, -1): odd + minus, (-1, 1): odd - minus}
        if (t + 1) * LANES > edge_c:
            base = 2 * half_c
            off = t * LANES - (half_c - LANES)
            for se, start in ((-1, base), (1, base + LANES)):
                lc = m1_ref[rows, start + off:start + off + LANES]
                ls = m2_ref[rows, start + off:start + off + LANES]
                quad[1, se] += lc + ls
                quad[-1, se] += lc - ls
        if edged:
            def edge(n):
                at = slice(n * M + g * SUB - edge_r, n * M + (g + 1) * SUB - edge_r)
                x = g1_ref[at, t * LANES:(t + 1) * LANES]
                y = g2_ref[at, t * LANES:(t + 1) * LANES]
                return {1: x + y, -1: x - y}
            for n, sd in ((0, -1), (1, 1)):
                e = edge(n)
                for se in (-1, 1):
                    quad[sd, se] += e[se] * col_own[t]
            if (t + 1) * LANES > edge_c:
                for n, (sd, se) in ((2, (-1, -1)), (3, (-1, 1)), (4, (1, -1)), (5, (1, 1))):
                    quad[sd, se] += edge(n)[se] * col_other[t]
        for (sd, se), x in quad.items():
            if sd < 0:
                x = flip(x, back_row, 0)
                at = slice(half_r - SUB - g * SUB, half_r - g * SUB)
            else:
                at = slice(half_r + g * SUB, half_r + (g + 1) * SUB)
            if se < 0:
                x = flip(x, back_lane, 1)
                start = half_c - (t + 1) * LANES
            else:
                start = half_c + t * LANES
            out_ref[at, start:start + LANES] = x

    n_groups = half_r // M

    def sends(j, t):
        copies = []
        for row in (half_r + 2 * M * j, half_r - 2 * M * (j + 1)):
            for col in (half_c + t * LANES, half_c - (t + 1) * LANES):
                at = (slice(row, row + 2 * M), slice(col, col + LANES))
                copies.append(pltpu.make_async_copy(
                    out_ref.at[at], image_ref.at[at], sems.at[(j * n_lane + t) * 4 + len(copies)]))
        return copies

    for t in range(n_lane - 2, -1, -1):
        own_products(t)
    for t in range(n_lane - 1, -1, -1):
        for j in range(n_groups):
            for g in range(j * M // SUB, (j + 1) * M // SUB):
                finish(g, t, j == n_groups - 1)
            if j % 2:
                for copy in sends(j // 2, t):
                    copy.start()
    for t in range(n_lane):
        for j in range(n_groups // 2):
            for copy in sends(j, t):
                copy.wait()


def swaps(size):
    both = []
    for first in (0, 1):
        pairs = [(i, i + 1) for i in range(first, size - 1, 2)]
        both.append(pairs + [(j, i) for i, j in pairs])
    return both


def all_paired(pairs, count, other):
    swap = dict(pairs)
    for i in range(count):
        if i not in swap and other(i) not in swap:
            swap[i], swap[other(i)] = other(i), i
    return list(swap.items())


def shards(vis, station_pairs, visibility_time_slot, station_u_cells, station_v_cells,
           facet_station_gains, holder_device_order):
    n_frow = lax.axis_size("frow")
    n_fcol = lax.axis_size("fcol")
    block = vis.shape[1]
    k_tiles = NBLK * block // LANES
    k = k_tiles * LANES
    half_r, half_c = R // 2, C // 2
    wide = 2 * half_c + 4 * M
    vmem = pl.BlockSpec(memory_space=pltpu.VMEM)
    smem = pl.BlockSpec(memory_space=pltpu.SMEM)

    def lines(x):
        return x.reshape(-1, LANES)

    def shaped(*dims, dtype=F32):
        return jax.ShapeDtypeStruct(dims, dtype)

    def params(mib):
        return pltpu.CompilerParams(vmem_limit_bytes=mib * 1024 * 1024)

    n_lines = station_u_cells.size // LANES
    packed, labels = pl.pallas_call(
        pack_kernel,
        out_shape=[shaped(n_frow * n_fcol, 1, 5 * block), shaped(SUB + 2 * n_lines, LANES)],
        in_specs=[smem] + [vmem] * 5,
        name="pack",
    )(holder_device_order, vis, station_pairs, visibility_time_slot.reshape(1, block),
      lines(station_u_cells), lines(station_v_cells))
    facet_station_gains, packed = lax.optimization_barrier((facet_station_gains, packed))
    gains = facet_station_gains[0, 0]
    depth = gains.size // LANES
    own = gains.reshape(2, -1, LANES).transpose(1, 0, 2).reshape(depth, LANES)
    row_a, row_b = [lax.ppermute(own, "frow", all_paired(pairs, n_frow, lambda r: n_frow - 1 - r))
                    for pairs in swaps(n_frow)]
    blocks = lax.all_to_all(packed, ("frow", "fcol"), 0, 0)
    mid = jnp.concatenate([own, row_a, row_b, labels], 0)
    count = n_frow * n_fcol

    def next_row(i):
        j = i ^ n_fcol if n_fcol & (n_fcol - 1) == 0 else i
        return j if j < count else i

    col_a, col_b = [
        lax.ppermute(mid, ("frow", "fcol"), all_paired(
            [(r * n_fcol + i, r * n_fcol + j) for r in range(n_frow) for i, j in pairs],
            count, next_row))
        for pairs in swaps(n_fcol)]
    s, a_cos, a_sin, e_cos, e_sin, f_cos, f_sin, c_cos, c_sin = pl.pallas_call(
        functools.partial(table_kernel, n_frow, n_fcol, 3 * depth, n_lines),
        out_shape=[
            shaped(6, k_tiles, LANES),
            shaped(half_r, k, dtype=BF16), shaped(half_r, k, dtype=BF16),
            shaped(M, k), shaped(M, k),
            shaped(half_c, k), shaped(half_c, k),
            shaped(half_c, k, dtype=BF16), shaped(half_c, k, dtype=BF16),
        ],
        in_specs=[vmem] * 2,
        out_specs=[vmem] * 9,
        scratch_shapes=[
            pltpu.VMEM((5, k_tiles, LANES), F32),
            pltpu.VMEM((2, k_tiles, LANES), jnp.int32),
            pltpu.VMEM((2, 2, half_r // SUB, LANES), F32),
        ],
        compiler_params=params(24),
        name="tables",
    )(blocks, mid)
    return pl.pallas_call(
        functools.partial(image_kernel, n_frow, n_fcol, depth),
        out_shape=shaped(R, C),
        in_specs=[vmem] * 12,
        out_specs=pl.BlockSpec(memory_space=pl.ANY),
        scratch_shapes=[
            pltpu.VMEM((R, C), F32),
            pltpu.VMEM((wide, k), BF16),
            pltpu.VMEM((wide, k), BF16),
            pltpu.VMEM((6 * M, k), BF16),
            pltpu.VMEM((6 * M, k), BF16),
            pltpu.VMEM((40 * NT, 2 * depth), BF16),
            pltpu.VMEM((2, SUB, k), F32),
            pltpu.VMEM((half_r, wide), F32),
            pltpu.VMEM((half_r, wide), F32),
            pltpu.VMEM((6 * M, half_c), F32),
            pltpu.VMEM((6 * M, half_c), F32),
            pltpu.SemaphoreType.DMA((2 * half_r // M * (half_c // LANES),)),
        ],
        compiler_params=params(36),
        name="image",
    )(s, mid, col_a, col_b, a_cos, a_sin, e_cos, e_sin, f_cos, f_sin, c_cos, c_sin)


def solution(mesh):
    return jax.shard_map(
        shards,
        mesh=mesh,
        in_specs=(
            P(None, ("frow", "fcol")),
            P(None, ("frow", "fcol")),
            P(("frow", "fcol")),
            P(),
            P(),
            P("frow", "fcol", None, None),
            P(),
        ),
        out_specs=P("frow", "fcol"),
        check_vma=False,
    )
```

```python
import functools
import math

import jax
import jax.numpy as jnp
from jax import lax
from jax.experimental import pallas as pl
from jax.experimental.pallas import tpu as pltpu
from jax.sharding import PartitionSpec as P

R = 1024
C = 512
M = 64
NT = 16
NBLK = 4
LANES = 128
SUB = 8
OWN, LEFT, RIGHT, UP, DOWN, UL, UR, DL, DR = range(9)
F32 = jnp.float32
BF16 = jnp.bfloat16


def wrap(m, modulus):
    if modulus & (modulus - 1) == 0:
        return m & (modulus - 1)
    return jnp.remainder(m, modulus)


def turn(m, modulus):
    m = wrap(m, modulus)
    quarter = modulus // 4
    q = (m + modulus // 8) // quarter if quarter & (quarter - 1) else (
        (m + modulus // 8) >> (quarter.bit_length() - 1))
    x = (m - q * quarter).astype(F32) * (2.0 * math.pi / modulus)
    x2 = x * x
    s = x + x * x2 * (-1 / 6 + x2 * (1 / 120 + x2 * (-1 / 5040 + x2 * (1 / 362880))))
    c = 1.0 + x2 * (-0.5 + x2 * (1 / 24 + x2 * (-1 / 720 + x2 * (1 / 40320))))
    odd = (q & 1) == 1
    cos = jnp.where(odd, s, c)
    sin = jnp.where(odd, c, s)
    cos = jnp.where(((q + 1) & 2) != 0, -cos, cos)
    sin = jnp.where((q & 2) != 0, -sin, sin)
    return cos, sin


def times(a, b):
    return a[0] * b[0] - a[1] * b[1], a[0] * b[1] + a[1] * b[0]


def pack_kernel(order_ref, vis_ref, pair_ref, slot_ref, u_ref, v_ref, out_ref, label_ref):
    block = vis_ref.shape[1]
    lines = [vis_ref[0:1, :], vis_ref[1:2, :], pair_ref[0:1, :].astype(F32),
             pair_ref[1:2, :].astype(F32), slot_ref[...].astype(F32)]
    for copy in range(out_ref.shape[0]):
        for q, line in enumerate(lines):
            out_ref[copy, :, q * block:(q + 1) * block] = line
    n_lines = u_ref.shape[0]
    at = lax.broadcasted_iota(jnp.int32, (SUB, LANES), 1)
    order = jnp.zeros((SUB, LANES), jnp.int32)
    for b in range(NBLK):
        order = jnp.where(at == b, order_ref[b], order)
    label_ref[:SUB] = order.astype(F32)
    label_ref[SUB:SUB + n_lines] = u_ref[...].astype(F32)
    label_ref[SUB + n_lines:SUB + 2 * n_lines] = v_ref[...].astype(F32)


def pick(row, lane):
    return jnp.take_along_axis(
        jnp.broadcast_to(row, lane.shape), lane, axis=1, mode="promise_in_bounds")


def taper_rows(group, half, wide=LANES):
    index = (lax.broadcasted_iota(jnp.int32, (SUB, wide), 0) + SUB * group).astype(F32)
    return ((half + M - 0.5 - index) * (1.0 / (2 * M)),
            (index - (half - M - 0.5)) * (1.0 / (2 * M)))


def table_kernel(n_frow, n_fcol, first, n_lines, block_ref, cell_ref,
                 s_ref, ac_ref, as_ref, ec_ref, es_ref, fc_ref, fs_ref, cc_ref, cs_ref,
                 q_ref, uv_ref, dr_ref):
    frow_at = lax.axis_index("frow")
    fcol_at = lax.axis_index("fcol")
    half_r, half_c = R // 2, C // 2
    mod_r, mod_c = 2 * R * n_frow, 2 * C * n_fcol
    k_tiles = s_ref.shape[1]
    per_block = k_tiles // NBLK
    block = per_block * LANES
    shape = (SUB, LANES)

    order = cell_ref[first:first + 1, :]
    place = lax.broadcasted_iota(jnp.int32, (1, LANES), 1)
    owners = [jnp.sum(jnp.where(place == b, order, 0.0)).astype(jnp.int32) for b in range(NBLK)]
    for b, owner in enumerate(owners):
        for q in range(5):
            for j in range(per_block):
                q_ref[q, b * per_block + j:b * per_block + j + 1, :] = block_ref[
                    owner, :, q * block + j * LANES:q * block + (j + 1) * LANES]
    a1 = q_ref[2].astype(jnp.int32)
    a2 = q_ref[3].astype(jnp.int32)
    slot = q_ref[4].astype(jnp.int32)

    at = first + SUB

    def cells(table):
        got = [jnp.zeros(shape, F32)] * 2
        for h in range(table.shape[0]):
            row = table[h:h + 1, :]
            got = [jnp.where((a >> 7) == h, pick(row, a & 127), g)
                   for a, g in zip((a1, a2), got)]
        return (got[0] - got[1]).astype(jnp.int32)

    u = cells(cell_ref[at:at + n_lines, :])
    v = cells(cell_ref[at + n_lines:at + 2 * n_lines, :])
    uv_ref[0] = u
    uv_ref[1] = v
    centre = times(turn(u * (frow_at * (2 * R) + (R - 1)), mod_r),
                   turn(v * (fcol_at * (2 * C) + (C - 1)), mod_c))
    scale = 0.5 / math.sqrt(NBLK * per_block * LANES)
    value = times((q_ref[0] * scale, q_ref[1] * scale), centre)
    s_ref[0] = value[0]
    s_ref[1] = value[1]
    for n, a in enumerate((a1, a2)):
        s_ref[2 + n] = ((a >> 3) + (a & 6) * 32).astype(F32)
        s_ref[4 + n] = ((a & 1) * NT + slot).astype(F32)

    iota = lax.broadcasted_iota(jnp.int32, shape, 0)

    def tables(s, carry):
        lane = pl.ds(pl.multiple_of(s * LANES, LANES), LANES)

        def phases(which, modulus, half):
            freq = jnp.broadcast_to(uv_ref[which, pl.ds(s, 1), :], shape)
            fine = turn(freq * (2 * iota + 1), modulus)
            middle = turn(freq * (16 * iota), modulus)
            coarse = turn(freq * (128 * iota), modulus)
            for a in range(half // 64):
                top = tuple(jnp.broadcast_to(x[a:a + 1], shape) for x in coarse)
                both = times(middle, top)
                for comp in range(2):
                    dr_ref[which, comp, 8 * a:8 * a + 8, :] = both[comp]
            for g in range(half // SUB):
                step = tuple(jnp.broadcast_to(dr_ref[which, comp, g:g + 1, :], shape)
                             for comp in range(2))
                yield times(fine, step)

        pairs = {}

        def put(ref, first, group, x):
            key = (id(ref), first)
            if group % 2 == 0:
                pairs[key] = x
            else:
                start = first + SUB * (group - 1)
                ref[start:start + 16, lane] = jnp.concatenate([pairs.pop(key), x], 0).astype(BF16)

        edge = (half_r - M) // SUB
        for g, (cos, sin) in enumerate(phases(0, mod_r, half_r)):
            if g >= edge:
                mine, other = taper_rows(g, half_r)
                at = slice((g - edge) * SUB, (g - edge + 1) * SUB)
                ec_ref[at, lane] = cos * other
                es_ref[at, lane] = sin * other
                cos, sin = cos * mine, sin * mine
            put(ac_ref, 0, g, cos)
            put(as_ref, 0, g, sin)
        for g, (cos, sin) in enumerate(phases(1, mod_c, half_c)):
            put(cc_ref, 0, g, cos)
            put(cs_ref, 0, g, sin)
            at = slice(g * SUB, (g + 1) * SUB)
            fc_ref[at, lane] = cos
            fs_ref[at, lane] = sin
        return carry

    lax.fori_loop(0, k_tiles, tables, 0, unroll=True)


def gain_kernel(depth, mid_ref, a_ref, b_ref, gain_ref):
    half = depth // 2
    places = 2 * NT
    low_lane = lax.broadcasted_iota(jnp.int32, (places, LANES), 1) < LANES // 2
    for f in range(9):
        ref, row = (mid_ref, a_ref, b_ref)[f // 3], f % 3 * depth
        both = jnp.concatenate([ref[pl.ds(row, half, stride=2), :],
                                ref[pl.ds(row + 1, half, stride=2), :]], 0).T
        quarter = [both[i * places:(i + 1) * places] for i in range(4)]
        turned = [pltpu.roll(x, LANES // 2, 1) for x in quarter]
        for t in range(2):
            re = jnp.where(low_lane, quarter[2 * t], turned[2 * t + 1])
            im = jnp.where(low_lane, turned[2 * t], quarter[2 * t + 1])
            for comp, x in enumerate((re, im)):
                high = x.astype(BF16)
                at = (2 * (f - 1 if f else SUB) + comp) * places
                gain_ref[at:at + places, t * LANES:(t + 1) * LANES] = high
                if f == 0:
                    at += 2 * places
                    gain_ref[at:at + places, t * LANES:(t + 1) * LANES] = (
                        x - high.astype(F32)).astype(BF16)


def image_kernel(n_frow, n_fcol, depth, s_ref, gain_ref, ac_ref, as_ref, ec_ref, es_ref,
                 fc_ref, fs_ref, cc_ref, cs_ref, image_ref,
                 out_ref, tc_ref, ts_ref, uc_ref, us_ref, w_ref,
                 m1_ref, m2_ref, g1_ref, g2_ref, sems):
    frow_at = lax.axis_index("frow")
    r_odd = lax.rem(frow_at, 2) == 1
    fcol_at = lax.axis_index("fcol")
    c_odd = lax.rem(fcol_at, 2) == 1
    k_tiles = s_ref.shape[1]
    half_c = C // 2
    places = 2 * NT

    r_first, r_second = jnp.where(r_odd, 1, 2), jnp.where(r_odd, 2, 1)
    c_first, c_second = jnp.where(c_odd, 1, 2), jnp.where(c_odd, 2, 1)
    rows = {UP: r_first - 1, DOWN: r_second - 1, LEFT: 3 * c_first - 1, RIGHT: 3 * c_second - 1,
            UL: 3 * c_first + r_first - 1, UR: 3 * c_second + r_first - 1,
            DL: 3 * c_first + r_second - 1, DR: 3 * c_second + r_second - 1}

    step = 2 if k_tiles % 2 == 0 else 1
    wide = step * LANES
    shape = (SUB, wide)
    line_at = lax.broadcasted_iota(jnp.int32, (2 * depth, wide), 0).astype(F32)
    place_at = line_at[:places]
    row_at = lax.broadcasted_iota(jnp.int32, shape, 0)
    zero = jnp.zeros((M, wide), BF16)
    r_edge = jnp.logical_or(frow_at == 0, frow_at == n_frow - 1)
    c_edge = jnp.logical_or(fcol_at == 0, fcol_at == n_fcol - 1)
    keep = (jnp.where(lax.rem(row_at, 3) == 1, jnp.where(r_edge, 0.0, 1.0), 1.0)
            * jnp.where(row_at >= 5, jnp.where(c_edge, 0.0, 1.0), 1.0))

    def fold(parts):
        parts = [parts[i] for i in (0, 4, 2, 6, 1, 5, 3, 7)]
        for distance in (1, 2, 4):
            low = (row_at & distance) == 0
            count = len(parts) // 2
            parts = [jnp.where(low, x, y) + pltpu.roll(jnp.where(low, y, x), distance, 0)
                     for x, y in zip(parts[:count], parts[count:])]
        return parts[0]

    def gain_product(first, second):
        (g1r, g1i), (g2r, g2i) = first, second
        return g1r * g2r + g1i * g2i, g1i * g2r - g1r * g2i

    def weight(f, lane):
        return tuple(jnp.broadcast_to(w_ref[comp, pl.ds(rows[f], 1), lane], shape)
                     for comp in range(2))

    for p in range(k_tiles // step):
        lane = slice(p * wide, (p + 1) * wide)

        def line(q):
            return jnp.concatenate([s_ref[q, p * step + i:p * step + i + 1, :]
                                    for i in range(step)], 1)

        owns, nears = [], []
        for n in range(2):
            hot = jnp.where(line_at == line(2 + n), 1.0, 0.0).astype(BF16)
            mask = jnp.where(place_at == line(4 + n), 1.0, 0.0)
            z = jnp.dot(gain_ref[...], hot, preferred_element_type=F32)

            def part(f, comp):
                at = (2 * f + comp) * places
                x = z[at:at + places]
                if f == SUB:
                    x = x + z[at + 2 * places:at + 3 * places]
                x = x * mask
                return sum((x[i * SUB:(i + 1) * SUB] for i in range(1, places // SUB)), x[:SUB])

            owns.append([jnp.sum(part(SUB, comp), axis=0, keepdims=True) for comp in range(2)])
            nears.append([fold([part(f, comp) for f in range(SUB)]) for comp in range(2)])
        value = (line(0), line(1))
        own_w = times(value, gain_product(*owns))
        near_w = times(tuple(x * keep for x in value), gain_product(*nears))
        for comp in range(2):
            w_ref[comp, :, lane] = near_w[comp]

        pairs = {}

        def put(ref, first, group, x):
            key = (id(ref), first)
            if group % 2 == 0:
                pairs[key] = x
            else:
                start = first + SUB * (group - 1)
                ref[start:start + 16, lane] = jnp.concatenate([pairs.pop(key), x], 0).astype(BF16)

        edge = (half_c - M) // SUB
        wr, wi = [jnp.broadcast_to(x, shape) for x in own_w]
        (lr, li), (rr, ri) = weight(LEFT, lane), weight(RIGHT, lane)
        for g in range(half_c // SUB):
            at = slice(g * SUB, (g + 1) * SUB)
            cos, sin = fc_ref[at, lane], fs_ref[at, lane]
            own = (cos, sin)
            if g >= edge:
                mine, other = taper_rows(g, half_c, wide)
                own = (cos * mine, sin * mine)
                cos, sin = cos * other, sin * other
                base = 2 * half_c + M
                put(tc_ref, base, g - edge, lr * cos + li * sin)
                put(ts_ref, base, g - edge, lr * sin - li * cos)
                put(tc_ref, base + 2 * M, g - edge, rr * cos - ri * sin)
                put(ts_ref, base + 2 * M, g - edge, -(rr * sin + ri * cos))
            base = g * SUB // LANES * LANES
            put(tc_ref, base, g, wr * own[0])
            put(tc_ref, base + LANES, g, -wi * own[1])
            put(ts_ref, base, g, -wi * own[0])
            put(ts_ref, base + LANES, g, -wr * own[1])
        for ref in (tc_ref, ts_ref):
            ref[2 * half_c:2 * half_c + M, lane] = zero
            ref[2 * half_c + 2 * M:2 * half_c + 3 * M, lane] = zero

    def dot(a, b):
        return lax.dot_general(a, b, (((1,), (1,)), ((), ())), preferred_element_type=F32)

    half_r = R // 2
    n_lane = half_c // LANES

    def own_products(t):
        cols = slice(2 * t * LANES, 2 * (t + 1) * LANES if t < n_lane - 1 else tc_ref.shape[0])
        m1_ref[:, cols] = dot(ac_ref[...], tc_ref[cols, :])
        m2_ref[:, cols] = dot(as_ref[...], ts_ref[cols, :])

    own_products(n_lane - 1)
    signs = (-1, 1, -1, -1, 1, 1)
    for p in range(k_tiles // step):
        lane = slice(p * wide, (p + 1) * wide)
        for n, (f, sd) in enumerate(zip((UP, DOWN, UL, UR, DL, DR), signs)):
            wr, wi = weight(f, lane)
            for g in range(0, M // SUB, 2):
                tops, lows = [], []
                for i in range(2):
                    at = slice((g + i) * SUB, (g + i + 1) * SUB)
                    cos, sin = ec_ref[at, lane], es_ref[at, lane]
                    tops.append(wr * cos - (sd * wi) * sin)
                    lows.append(-(sd * wr) * sin - wi * cos)
                at = slice(n * M + g * SUB, n * M + (g + 2) * SUB)
                uc_ref[at, lane] = jnp.concatenate(tops, 0).astype(BF16)
                us_ref[at, lane] = jnp.concatenate(lows, 0).astype(BF16)
    g1_ref[...] = dot(uc_ref[...], cc_ref[...])
    g2_ref[...] = dot(us_ref[...], cs_ref[...])

    shape = (SUB, LANES)
    iota = lax.broadcasted_iota(jnp.int32, shape, 0)
    lane_at = lax.broadcasted_iota(jnp.int32, shape, 1)
    back_lane = (LANES - 1) - lane_at
    back_row = (SUB - 1) - iota
    edge_c = half_c - M
    edge_r = half_r - M
    col_own, col_other = [], []
    for t in range(n_lane):
        index = (lane_at + t * LANES).astype(F32)
        col_own.append(jnp.minimum((half_c + M - 0.5 - index) * (1.0 / (2 * M)), 1.0))
        col_other.append(jnp.maximum((index - (half_c - M - 0.5)) * (1.0 / (2 * M)), 0.0))

    def flip(x, index, axis):
        return jnp.take_along_axis(x, index, axis=axis, mode="promise_in_bounds")

    def finish(g, t, edged):
        rows = slice(g * SUB, (g + 1) * SUB)
        def part(ref, which):
            return ref[rows, (2 * t + which) * LANES:(2 * t + which + 1) * LANES]
        p, s_, r, q = part(m1_ref, 0), part(m1_ref, 1), part(m2_ref, 0), part(m2_ref, 1)
        even, odd = p + q, p - q
        plus, minus = r + s_, r - s_
        quad = {(1, 1): even + plus, (-1, -1): even - plus,
                (1, -1): odd + minus, (-1, 1): odd - minus}
        if (t + 1) * LANES > edge_c:
            base = 2 * half_c
            off = t * LANES - (half_c - LANES)
            for se, start in ((-1, base), (1, base + LANES)):
                lc = m1_ref[rows, start + off:start + off + LANES]
                ls = m2_ref[rows, start + off:start + off + LANES]
                quad[1, se] += lc + ls
                quad[-1, se] += lc - ls
        if edged:
            def edge(n):
                at = slice(n * M + g * SUB - edge_r, n * M + (g + 1) * SUB - edge_r)
                x = g1_ref[at, t * LANES:(t + 1) * LANES]
                y = g2_ref[at, t * LANES:(t + 1) * LANES]
                return {1: x + y, -1: x - y}
            for n, sd in ((0, -1), (1, 1)):
                e = edge(n)
                for se in (-1, 1):
                    quad[sd, se] += e[se] * col_own[t]
            if (t + 1) * LANES > edge_c:
                for n, (sd, se) in ((2, (-1, -1)), (3, (-1, 1)), (4, (1, -1)), (5, (1, 1))):
                    quad[sd, se] += edge(n)[se] * col_other[t]
        for (sd, se), x in quad.items():
            if sd < 0:
                x = flip(x, back_row, 0)
                at = slice(half_r - SUB - g * SUB, half_r - g * SUB)
            else:
                at = slice(half_r + g * SUB, half_r + (g + 1) * SUB)
            if se < 0:
                x = flip(x, back_lane, 1)
                start = half_c - (t + 1) * LANES
            else:
                start = half_c + t * LANES
            out_ref[at, start:start + LANES] = x

    n_groups = half_r // M

    def sends(j, t):
        copies = []
        for row in (half_r + 2 * M * j, half_r - 2 * M * (j + 1)):
            for col in (half_c + t * LANES, half_c - (t + 1) * LANES):
                at = (slice(row, row + 2 * M), slice(col, col + LANES))
                copies.append(pltpu.make_async_copy(
                    out_ref.at[at], image_ref.at[at], sems.at[(j * n_lane + t) * 4 + len(copies)]))
        return copies

    for t in range(n_lane - 2, -1, -1):
        own_products(t)
    for t in range(n_lane - 1, -1, -1):
        for j in range(n_groups):
            for g in range(j * M // SUB, (j + 1) * M // SUB):
                finish(g, t, j == n_groups - 1)
            if j % 2:
                for copy in sends(j // 2, t):
                    copy.start()
    for t in range(n_lane):
        for j in range(n_groups // 2):
            for copy in sends(j, t):
                copy.wait()


def swaps(size):
    both = []
    for first in (0, 1):
        pairs = [(i, i + 1) for i in range(first, size - 1, 2)]
        both.append(pairs + [(j, i) for i, j in pairs])
    return both


def all_paired(pairs, count, other):
    swap = dict(pairs)
    for i in range(count):
        if i not in swap and other(i) not in swap:
            swap[i], swap[other(i)] = other(i), i
    return list(swap.items())


def shards(vis, station_pairs, visibility_time_slot, station_u_cells, station_v_cells,
           facet_station_gains, holder_device_order):
    n_frow = lax.axis_size("frow")
    n_fcol = lax.axis_size("fcol")
    block = vis.shape[1]
    k_tiles = NBLK * block // LANES
    k = k_tiles * LANES
    half_r, half_c = R // 2, C // 2
    wide = 2 * half_c + 4 * M
    vmem = pl.BlockSpec(memory_space=pltpu.VMEM)
    smem = pl.BlockSpec(memory_space=pltpu.SMEM)

    def lines(x):
        return x.reshape(-1, LANES)

    def shaped(*dims, dtype=F32):
        return jax.ShapeDtypeStruct(dims, dtype)

    def params(mib):
        return pltpu.CompilerParams(vmem_limit_bytes=mib * 1024 * 1024)

    n_lines = station_u_cells.size // LANES
    packed, labels = pl.pallas_call(
        pack_kernel,
        out_shape=[shaped(n_frow * n_fcol, 1, 5 * block), shaped(SUB + 2 * n_lines, LANES)],
        in_specs=[smem] + [vmem] * 5,
        name="pack",
    )(holder_device_order, vis, station_pairs, visibility_time_slot.reshape(1, block),
      lines(station_u_cells), lines(station_v_cells))
    facet_station_gains, packed = lax.optimization_barrier((facet_station_gains, packed))
    gains = facet_station_gains[0, 0]
    depth = gains.size // LANES
    own = gains.reshape(2, -1, LANES).transpose(1, 0, 2).reshape(depth, LANES)
    row_a, row_b = [lax.ppermute(own, "frow", all_paired(pairs, n_frow, lambda r: n_frow - 1 - r))
                    for pairs in swaps(n_frow)]
    blocks = lax.all_to_all(packed, ("frow", "fcol"), 0, 0)
    mid = jnp.concatenate([own, row_a, row_b, labels], 0)
    count = n_frow * n_fcol

    def next_row(i):
        j = i ^ n_fcol if n_fcol & (n_fcol - 1) == 0 else i
        return j if j < count else i

    col_a, col_b = [
        lax.ppermute(mid, ("frow", "fcol"), all_paired(
            [(r * n_fcol + i, r * n_fcol + j) for r in range(n_frow) for i, j in pairs],
            count, next_row))
        for pairs in swaps(n_fcol)]
    s, a_cos, a_sin, e_cos, e_sin, f_cos, f_sin, c_cos, c_sin = pl.pallas_call(
        functools.partial(table_kernel, n_frow, n_fcol, 3 * depth, n_lines),
        out_shape=[
            shaped(6, k_tiles, LANES),
            shaped(half_r, k, dtype=BF16), shaped(half_r, k, dtype=BF16),
            shaped(M, k), shaped(M, k),
            shaped(half_c, k), shaped(half_c, k),
            shaped(half_c, k, dtype=BF16), shaped(half_c, k, dtype=BF16),
        ],
        in_specs=[vmem] * 2,
        out_specs=[vmem] * 9,
        scratch_shapes=[
            pltpu.VMEM((5, k_tiles, LANES), F32),
            pltpu.VMEM((2, k_tiles, LANES), jnp.int32),
            pltpu.VMEM((2, 2, half_r // SUB, LANES), F32),
        ],
        compiler_params=params(24),
        name="tables",
    )(blocks, mid)
    looked = pl.pallas_call(
        functools.partial(gain_kernel, depth),
        out_shape=shaped(40 * NT, 2 * depth, dtype=BF16),
        in_specs=[vmem] * 3,
        out_specs=vmem,
        compiler_params=params(8),
        name="gains",
    )(mid, col_a, col_b)
    return pl.pallas_call(
        functools.partial(image_kernel, n_frow, n_fcol, depth),
        out_shape=shaped(R, C),
        in_specs=[vmem] * 10,
        out_specs=pl.BlockSpec(memory_space=pl.ANY),
        scratch_shapes=[
            pltpu.VMEM((R, C), F32),
            pltpu.VMEM((wide, k), BF16),
            pltpu.VMEM((wide, k), BF16),
            pltpu.VMEM((6 * M, k), BF16),
            pltpu.VMEM((6 * M, k), BF16),
            pltpu.VMEM((2, SUB, k), F32),
            pltpu.VMEM((half_r, wide), F32),
            pltpu.VMEM((half_r, wide), F32),
            pltpu.VMEM((6 * M, half_c), F32),
            pltpu.VMEM((6 * M, half_c), F32),
            pltpu.SemaphoreType.DMA((2 * half_r // M * (half_c // LANES),)),
        ],
        compiler_params=params(36),
        name="image",
    )(s, looked, a_cos, a_sin, e_cos, e_sin, f_cos, f_sin, c_cos, c_sin)


def solution(mesh):
    return jax.shard_map(
        shards,
        mesh=mesh,
        in_specs=(
            P(None, ("frow", "fcol")),
            P(None, ("frow", "fcol")),
            P(("frow", "fcol")),
            P(),
            P(),
            P("frow", "fcol", None, None),
            P(),
        ),
        out_specs=P("frow", "fcol"),
        check_vma=False,
    )
```

```python
import functools
import math

import jax
import jax.numpy as jnp
from jax import lax
from jax.experimental import pallas as pl
from jax.experimental.pallas import tpu as pltpu
from jax.sharding import PartitionSpec as P

R = 1024
C = 512
M = 64
NT = 16
NBLK = 4
LANES = 128
SUB = 8
OWN, LEFT, RIGHT, UP, DOWN, UL, UR, DL, DR = range(9)
F32 = jnp.float32
BF16 = jnp.bfloat16


def wrap(m, modulus):
    if modulus & (modulus - 1) == 0:
        return m & (modulus - 1)
    return jnp.remainder(m, modulus)


def turn(m, modulus):
    m = wrap(m, modulus)
    quarter = modulus // 4
    q = (m + modulus // 8) // quarter if quarter & (quarter - 1) else (
        (m + modulus // 8) >> (quarter.bit_length() - 1))
    x = (m - q * quarter).astype(F32) * (2.0 * math.pi / modulus)
    x2 = x * x
    s = x + x * x2 * (-1 / 6 + x2 * (1 / 120 + x2 * (-1 / 5040 + x2 * (1 / 362880))))
    c = 1.0 + x2 * (-0.5 + x2 * (1 / 24 + x2 * (-1 / 720 + x2 * (1 / 40320))))
    odd = (q & 1) == 1
    cos = jnp.where(odd, s, c)
    sin = jnp.where(odd, c, s)
    cos = jnp.where(((q + 1) & 2) != 0, -cos, cos)
    sin = jnp.where((q & 2) != 0, -sin, sin)
    return cos, sin


def times(a, b):
    return a[0] * b[0] - a[1] * b[1], a[0] * b[1] + a[1] * b[0]


def pack_kernel(order_ref, vis_ref, pair_ref, slot_ref, u_ref, v_ref, out_ref, label_ref):
    block = vis_ref.shape[1]
    lines = [vis_ref[0:1, :], vis_ref[1:2, :], pair_ref[0:1, :].astype(F32),
             pair_ref[1:2, :].astype(F32), slot_ref[...].astype(F32)]
    for copy in range(out_ref.shape[0]):
        for q, line in enumerate(lines):
            out_ref[copy, :, q * block:(q + 1) * block] = line
    n_lines = u_ref.shape[0]
    at = lax.broadcasted_iota(jnp.int32, (SUB, LANES), 1)
    order = jnp.zeros((SUB, LANES), jnp.int32)
    for b in range(NBLK):
        order = jnp.where(at == b, order_ref[b], order)
    label_ref[:SUB] = order.astype(F32)
    label_ref[SUB:SUB + n_lines] = u_ref[...].astype(F32)
    label_ref[SUB + n_lines:SUB + 2 * n_lines] = v_ref[...].astype(F32)


def pick(row, lane):
    return jnp.take_along_axis(
        jnp.broadcast_to(row, lane.shape), lane, axis=1, mode="promise_in_bounds")


def taper_rows(group, half, wide=LANES):
    index = (lax.broadcasted_iota(jnp.int32, (SUB, wide), 0) + SUB * group).astype(F32)
    return ((half + M - 0.5 - index) * (1.0 / (2 * M)),
            (index - (half - M - 0.5)) * (1.0 / (2 * M)))


def phase_tables(n_frow, n_fcol, first, n_lines, block_ref, cell_ref,
                 s_ref, ac_ref, as_ref, ec_ref, es_ref, fc_ref, fs_ref, cc_ref, cs_ref,
                 q_ref, uv_ref, dr_ref):
    frow_at = lax.axis_index("frow")
    fcol_at = lax.axis_index("fcol")
    half_r, half_c = R // 2, C // 2
    mod_r, mod_c = 2 * R * n_frow, 2 * C * n_fcol
    k_tiles = s_ref.shape[1]
    per_block = k_tiles // NBLK
    block = per_block * LANES
    shape = (SUB, LANES)

    order = cell_ref[first:first + 1, :]
    place = lax.broadcasted_iota(jnp.int32, (1, LANES), 1)
    owners = [jnp.sum(jnp.where(place == b, order, 0.0)).astype(jnp.int32) for b in range(NBLK)]
    for b, owner in enumerate(owners):
        for q in range(5):
            for j in range(per_block):
                q_ref[q, b * per_block + j:b * per_block + j + 1, :] = block_ref[
                    owner, :, q * block + j * LANES:q * block + (j + 1) * LANES]
    a1 = q_ref[2].astype(jnp.int32)
    a2 = q_ref[3].astype(jnp.int32)
    slot = q_ref[4].astype(jnp.int32)

    at = first + SUB

    def cells(table):
        got = [jnp.zeros(shape, F32)] * 2
        for h in range(table.shape[0]):
            row = table[h:h + 1, :]
            got = [jnp.where((a >> 7) == h, pick(row, a & 127), g)
                   for a, g in zip((a1, a2), got)]
        return (got[0] - got[1]).astype(jnp.int32)

    u = cells(cell_ref[at:at + n_lines, :])
    v = cells(cell_ref[at + n_lines:at + 2 * n_lines, :])
    uv_ref[0] = u
    uv_ref[1] = v
    centre = times(turn(u * (frow_at * (2 * R) + (R - 1)), mod_r),
                   turn(v * (fcol_at * (2 * C) + (C - 1)), mod_c))
    scale = 0.5 / math.sqrt(NBLK * per_block * LANES)
    value = times((q_ref[0] * scale, q_ref[1] * scale), centre)
    s_ref[0] = value[0]
    s_ref[1] = value[1]
    for n, a in enumerate((a1, a2)):
        s_ref[2 + n] = ((a >> 3) + (a & 6) * 32).astype(F32)
        s_ref[4 + n] = ((a & 1) * NT + slot).astype(F32)

    iota = lax.broadcasted_iota(jnp.int32, shape, 0)

    def tables(s):
        lane = slice(s * LANES, (s + 1) * LANES)

        def phases(which, modulus, half):
            freq = jnp.broadcast_to(uv_ref[which, s:s + 1, :], shape)
            fine = turn(freq * (2 * iota + 1), modulus)
            middle = turn(freq * (16 * iota), modulus)
            coarse = turn(freq * (128 * iota), modulus)
            for a in range(half // 64):
                top = tuple(jnp.broadcast_to(x[a:a + 1], shape) for x in coarse)
                both = times(middle, top)
                for comp in range(2):
                    dr_ref[s, which, comp, 8 * a:8 * a + 8, :] = both[comp]
            for g in range(half // SUB):
                step = tuple(jnp.broadcast_to(dr_ref[s, which, comp, g:g + 1, :], shape)
                             for comp in range(2))
                yield times(fine, step)

        pairs = {}

        def put(ref, first, group, x):
            key = (id(ref), first)
            if group % 2 == 0:
                pairs[key] = x
            else:
                start = first + SUB * (group - 1)
                ref[start:start + 16, lane] = jnp.concatenate([pairs.pop(key), x], 0).astype(BF16)

        edge = (half_r - M) // SUB
        for g, (cos, sin) in enumerate(phases(0, mod_r, half_r)):
            if g >= edge:
                mine, other = taper_rows(g, half_r)
                at = slice((g - edge) * SUB, (g - edge + 1) * SUB)
                ec_ref[at, lane] = cos * other
                es_ref[at, lane] = sin * other
                cos, sin = cos * mine, sin * mine
            put(ac_ref, 0, g, cos)
            put(as_ref, 0, g, sin)
        for g, (cos, sin) in enumerate(phases(1, mod_c, half_c)):
            put(cc_ref, 0, g, cos)
            put(cs_ref, 0, g, sin)
            at = slice(g * SUB, (g + 1) * SUB)
            fc_ref[at, lane] = cos
            fs_ref[at, lane] = sin

    return tables


def gain_kernel(depth, mid_ref, a_ref, b_ref, gain_ref):
    half = depth // 2
    places = 2 * NT
    low_lane = lax.broadcasted_iota(jnp.int32, (places, LANES), 1) < LANES // 2
    for f in range(9):
        ref, row = (mid_ref, a_ref, b_ref)[f // 3], f % 3 * depth
        both = jnp.concatenate([ref[pl.ds(row, half, stride=2), :],
                                ref[pl.ds(row + 1, half, stride=2), :]], 0).T
        quarter = [both[i * places:(i + 1) * places] for i in range(4)]
        turned = [pltpu.roll(x, LANES // 2, 1) for x in quarter]
        for t in range(2):
            re = jnp.where(low_lane, quarter[2 * t], turned[2 * t + 1])
            im = jnp.where(low_lane, turned[2 * t], quarter[2 * t + 1])
            for comp, x in enumerate((re, im)):
                high = x.astype(BF16)
                at = (2 * (f - 1 if f else SUB) + comp) * places
                gain_ref[at:at + places, t * LANES:(t + 1) * LANES] = high
                if f == 0:
                    at += 2 * places
                    gain_ref[at:at + places, t * LANES:(t + 1) * LANES] = (
                        x - high.astype(F32)).astype(BF16)


def image_kernel(n_frow, n_fcol, first, n_lines, depth, block_ref, cell_ref, gain_ref, image_ref,
                 s_ref, ac_ref, as_ref, ec_ref, es_ref, fc_ref, fs_ref, cc_ref, cs_ref,
                 q_ref, uv_ref, dr_ref, out_ref, tc_ref, ts_ref, uc_ref, us_ref, w_ref,
                 m1_ref, m2_ref, g1_ref, g2_ref, sems):
    tables = phase_tables(n_frow, n_fcol, first, n_lines, block_ref, cell_ref, s_ref, ac_ref,
                          as_ref, ec_ref, es_ref, fc_ref, fs_ref, cc_ref, cs_ref,
                          q_ref, uv_ref, dr_ref)
    frow_at = lax.axis_index("frow")
    r_odd = lax.rem(frow_at, 2) == 1
    fcol_at = lax.axis_index("fcol")
    c_odd = lax.rem(fcol_at, 2) == 1
    k_tiles = s_ref.shape[1]
    half_c = C // 2
    places = 2 * NT

    r_first, r_second = jnp.where(r_odd, 1, 2), jnp.where(r_odd, 2, 1)
    c_first, c_second = jnp.where(c_odd, 1, 2), jnp.where(c_odd, 2, 1)
    rows = {UP: r_first - 1, DOWN: r_second - 1, LEFT: 3 * c_first - 1, RIGHT: 3 * c_second - 1,
            UL: 3 * c_first + r_first - 1, UR: 3 * c_second + r_first - 1,
            DL: 3 * c_first + r_second - 1, DR: 3 * c_second + r_second - 1}

    step = 2 if k_tiles % 2 == 0 else 1
    wide = step * LANES
    shape = (SUB, wide)
    line_at = lax.broadcasted_iota(jnp.int32, (2 * depth, wide), 0).astype(F32)
    place_at = line_at[:places]
    row_at = lax.broadcasted_iota(jnp.int32, shape, 0)
    zero = jnp.zeros((M, wide), BF16)
    r_edge = jnp.logical_or(frow_at == 0, frow_at == n_frow - 1)
    c_edge = jnp.logical_or(fcol_at == 0, fcol_at == n_fcol - 1)
    keep = (jnp.where(lax.rem(row_at, 3) == 1, jnp.where(r_edge, 0.0, 1.0), 1.0)
            * jnp.where(row_at >= 5, jnp.where(c_edge, 0.0, 1.0), 1.0))

    def fold(parts):
        parts = [parts[i] for i in (0, 4, 2, 6, 1, 5, 3, 7)]
        for distance in (1, 2, 4):
            low = (row_at & distance) == 0
            count = len(parts) // 2
            parts = [jnp.where(low, x, y) + pltpu.roll(jnp.where(low, y, x), distance, 0)
                     for x, y in zip(parts[:count], parts[count:])]
        return parts[0]

    def gain_product(first, second):
        (g1r, g1i), (g2r, g2i) = first, second
        return g1r * g2r + g1i * g2i, g1i * g2r - g1r * g2i

    def weight(f, lane):
        return tuple(jnp.broadcast_to(w_ref[comp, pl.ds(rows[f], 1), lane], shape)
                     for comp in range(2))

    for p in range(k_tiles // step):
        lane = slice(p * wide, (p + 1) * wide)

        def line(q):
            return jnp.concatenate([s_ref[q, p * step + i:p * step + i + 1, :]
                                    for i in range(step)], 1)

        for i in range(step):
            tables(p * step + i)
        owns, nears = [], []
        for n in range(2):
            hot = jnp.where(line_at == line(2 + n), 1.0, 0.0).astype(BF16)
            mask = jnp.where(place_at == line(4 + n), 1.0, 0.0)
            z = jnp.dot(gain_ref[...], hot, preferred_element_type=F32)

            def part(f, comp):
                at = (2 * f + comp) * places
                x = z[at:at + places]
                if f == SUB:
                    x = x + z[at + 2 * places:at + 3 * places]
                x = x * mask
                return sum((x[i * SUB:(i + 1) * SUB] for i in range(1, places // SUB)), x[:SUB])

            owns.append([jnp.sum(part(SUB, comp), axis=0, keepdims=True) for comp in range(2)])
            nears.append([fold([part(f, comp) for f in range(SUB)]) for comp in range(2)])
        value = (line(0), line(1))
        own_w = times(value, gain_product(*owns))
        near_w = times(tuple(x * keep for x in value), gain_product(*nears))
        for comp in range(2):
            w_ref[comp, :, lane] = near_w[comp]

        pairs = {}

        def put(ref, first, group, x):
            key = (id(ref), first)
            if group % 2 == 0:
                pairs[key] = x
            else:
                start = first + SUB * (group - 1)
                ref[start:start + 16, lane] = jnp.concatenate([pairs.pop(key), x], 0).astype(BF16)

        edge = (half_c - M) // SUB
        wr, wi = [jnp.broadcast_to(x, shape) for x in own_w]
        (lr, li), (rr, ri) = weight(LEFT, lane), weight(RIGHT, lane)
        for g in range(half_c // SUB):
            at = slice(g * SUB, (g + 1) * SUB)
            cos, sin = fc_ref[at, lane], fs_ref[at, lane]
            own = (cos, sin)
            if g >= edge:
                mine, other = taper_rows(g, half_c, wide)
                own = (cos * mine, sin * mine)
                cos, sin = cos * other, sin * other
                base = 2 * half_c + M
                put(tc_ref, base, g - edge, lr * cos + li * sin)
                put(ts_ref, base, g - edge, lr * sin - li * cos)
                put(tc_ref, base + 2 * M, g - edge, rr * cos - ri * sin)
                put(ts_ref, base + 2 * M, g - edge, -(rr * sin + ri * cos))
            base = g * SUB // LANES * LANES
            put(tc_ref, base, g, wr * own[0])
            put(tc_ref, base + LANES, g, -wi * own[1])
            put(ts_ref, base, g, -wi * own[0])
            put(ts_ref, base + LANES, g, -wr * own[1])
        for ref in (tc_ref, ts_ref):
            ref[2 * half_c:2 * half_c + M, lane] = zero
            ref[2 * half_c + 2 * M:2 * half_c + 3 * M, lane] = zero

    def dot(a, b):
        return lax.dot_general(a, b, (((1,), (1,)), ((), ())), preferred_element_type=F32)

    half_r = R // 2
    n_lane = half_c // LANES

    def own_products(t):
        cols = slice(2 * t * LANES, 2 * (t + 1) * LANES if t < n_lane - 1 else tc_ref.shape[0])
        m1_ref[:, cols] = dot(ac_ref[...], tc_ref[cols, :])
        m2_ref[:, cols] = dot(as_ref[...], ts_ref[cols, :])

    own_products(n_lane - 1)
    signs = (-1, 1, -1, -1, 1, 1)
    for p in range(k_tiles // step):
        lane = slice(p * wide, (p + 1) * wide)
        for n, (f, sd) in enumerate(zip((UP, DOWN, UL, UR, DL, DR), signs)):
            wr, wi = weight(f, lane)
            for g in range(0, M // SUB, 2):
                tops, lows = [], []
                for i in range(2):
                    at = slice((g + i) * SUB, (g + i + 1) * SUB)
                    cos, sin = ec_ref[at, lane], es_ref[at, lane]
                    tops.append(wr * cos - (sd * wi) * sin)
                    lows.append(-(sd * wr) * sin - wi * cos)
                at = slice(n * M + g * SUB, n * M + (g + 2) * SUB)
                uc_ref[at, lane] = jnp.concatenate(tops, 0).astype(BF16)
                us_ref[at, lane] = jnp.concatenate(lows, 0).astype(BF16)
    g1_ref[...] = dot(uc_ref[...], cc_ref[...])
    g2_ref[...] = dot(us_ref[...], cs_ref[...])

    shape = (SUB, LANES)
    iota = lax.broadcasted_iota(jnp.int32, shape, 0)
    lane_at = lax.broadcasted_iota(jnp.int32, shape, 1)
    back_lane = (LANES - 1) - lane_at
    back_row = (SUB - 1) - iota
    edge_c = half_c - M
    edge_r = half_r - M
    col_own, col_other = [], []
    for t in range(n_lane):
        index = (lane_at + t * LANES).astype(F32)
        col_own.append(jnp.minimum((half_c + M - 0.5 - index) * (1.0 / (2 * M)), 1.0))
        col_other.append(jnp.maximum((index - (half_c - M - 0.5)) * (1.0 / (2 * M)), 0.0))

    def flip(x, index, axis):
        return jnp.take_along_axis(x, index, axis=axis, mode="promise_in_bounds")

    def finish(g, t, edged):
        rows = slice(g * SUB, (g + 1) * SUB)
        def part(ref, which):
            return ref[rows, (2 * t + which) * LANES:(2 * t + which + 1) * LANES]
        p, s_, r, q = part(m1_ref, 0), part(m1_ref, 1), part(m2_ref, 0), part(m2_ref, 1)
        even, odd = p + q, p - q
        plus, minus = r + s_, r - s_
        quad = {(1, 1): even + plus, (-1, -1): even - plus,
                (1, -1): odd + minus, (-1, 1): odd - minus}
        if (t + 1) * LANES > edge_c:
            base = 2 * half_c
            off = t * LANES - (half_c - LANES)
            for se, start in ((-1, base), (1, base + LANES)):
                lc = m1_ref[rows, start + off:start + off + LANES]
                ls = m2_ref[rows, start + off:start + off + LANES]
                quad[1, se] += lc + ls
                quad[-1, se] += lc - ls
        if edged:
            def edge(n):
                at = slice(n * M + g * SUB - edge_r, n * M + (g + 1) * SUB - edge_r)
                x = g1_ref[at, t * LANES:(t + 1) * LANES]
                y = g2_ref[at, t * LANES:(t + 1) * LANES]
                return {1: x + y, -1: x - y}
            for n, sd in ((0, -1), (1, 1)):
                e = edge(n)
                for se in (-1, 1):
                    quad[sd, se] += e[se] * col_own[t]
            if (t + 1) * LANES > edge_c:
                for n, (sd, se) in ((2, (-1, -1)), (3, (-1, 1)), (4, (1, -1)), (5, (1, 1))):
                    quad[sd, se] += edge(n)[se] * col_other[t]
        for (sd, se), x in quad.items():
            if sd < 0:
                x = flip(x, back_row, 0)
                at = slice(half_r - SUB - g * SUB, half_r - g * SUB)
            else:
                at = slice(half_r + g * SUB, half_r + (g + 1) * SUB)
            if se < 0:
                x = flip(x, back_lane, 1)
                start = half_c - (t + 1) * LANES
            else:
                start = half_c + t * LANES
            out_ref[at, start:start + LANES] = x

    n_groups = half_r // M

    def sends(j, t):
        copies = []
        for row in (half_r + 2 * M * j, half_r - 2 * M * (j + 1)):
            for col in (half_c + t * LANES, half_c - (t + 1) * LANES):
                at = (slice(row, row + 2 * M), slice(col, col + LANES))
                copies.append(pltpu.make_async_copy(
                    out_ref.at[at], image_ref.at[at], sems.at[(j * n_lane + t) * 4 + len(copies)]))
        return copies

    for t in range(n_lane - 2, -1, -1):
        own_products(t)
    for t in range(n_lane - 1, -1, -1):
        for j in range(n_groups):
            for g in range(j * M // SUB, (j + 1) * M // SUB):
                finish(g, t, j == n_groups - 1)
            if j % 2:
                for copy in sends(j // 2, t):
                    copy.start()
    for t in range(n_lane):
        for j in range(n_groups // 2):
            for copy in sends(j, t):
                copy.wait()


def swaps(size):
    both = []
    for first in (0, 1):
        pairs = [(i, i + 1) for i in range(first, size - 1, 2)]
        both.append(pairs + [(j, i) for i, j in pairs])
    return both


def all_paired(pairs, count, other):
    swap = dict(pairs)
    for i in range(count):
        if i not in swap and other(i) not in swap:
            swap[i], swap[other(i)] = other(i), i
    return list(swap.items())


def shards(vis, station_pairs, visibility_time_slot, station_u_cells, station_v_cells,
           facet_station_gains, holder_device_order):
    n_frow = lax.axis_size("frow")
    n_fcol = lax.axis_size("fcol")
    block = vis.shape[1]
    k_tiles = NBLK * block // LANES
    k = k_tiles * LANES
    half_r, half_c = R // 2, C // 2
    wide = 2 * half_c + 4 * M
    vmem = pl.BlockSpec(memory_space=pltpu.VMEM)
    smem = pl.BlockSpec(memory_space=pltpu.SMEM)

    def lines(x):
        return x.reshape(-1, LANES)

    def shaped(*dims, dtype=F32):
        return jax.ShapeDtypeStruct(dims, dtype)

    def params(mib):
        return pltpu.CompilerParams(vmem_limit_bytes=mib * 1024 * 1024)

    n_lines = station_u_cells.size // LANES
    packed, labels = pl.pallas_call(
        pack_kernel,
        out_shape=[shaped(n_frow * n_fcol, 1, 5 * block), shaped(SUB + 2 * n_lines, LANES)],
        in_specs=[smem] + [vmem] * 5,
        name="pack",
    )(holder_device_order, vis, station_pairs, visibility_time_slot.reshape(1, block),
      lines(station_u_cells), lines(station_v_cells))
    facet_station_gains, packed = lax.optimization_barrier((facet_station_gains, packed))
    gains = facet_station_gains[0, 0]
    depth = gains.size // LANES
    own = gains.reshape(2, -1, LANES).transpose(1, 0, 2).reshape(depth, LANES)
    row_a, row_b = [lax.ppermute(own, "frow", all_paired(pairs, n_frow, lambda r: n_frow - 1 - r))
                    for pairs in swaps(n_frow)]
    blocks = lax.all_to_all(packed, ("frow", "fcol"), 0, 0)
    mid = jnp.concatenate([own, row_a, row_b, labels], 0)
    count = n_frow * n_fcol

    def next_row(i):
        j = i ^ n_fcol if n_fcol & (n_fcol - 1) == 0 else i
        return j if j < count else i

    col_a, col_b = [
        lax.ppermute(mid, ("frow", "fcol"), all_paired(
            [(r * n_fcol + i, r * n_fcol + j) for r in range(n_frow) for i, j in pairs],
            count, next_row))
        for pairs in swaps(n_fcol)]
    looked = pl.pallas_call(
        functools.partial(gain_kernel, depth),
        out_shape=shaped(40 * NT, 2 * depth, dtype=BF16),
        in_specs=[vmem] * 3,
        out_specs=vmem,
        compiler_params=params(8),
        name="gains",
    )(mid, col_a, col_b)
    return pl.pallas_call(
        functools.partial(image_kernel, n_frow, n_fcol, 3 * depth, n_lines, depth),
        out_shape=shaped(R, C),
        in_specs=[vmem] * 3,
        out_specs=pl.BlockSpec(memory_space=pl.ANY),
        scratch_shapes=[
            pltpu.VMEM((6, k_tiles, LANES), F32),
            pltpu.VMEM((half_r, k), BF16),
            pltpu.VMEM((half_r, k), BF16),
            pltpu.VMEM((M, k), F32),
            pltpu.VMEM((M, k), F32),
            pltpu.VMEM((half_c, k), F32),
            pltpu.VMEM((half_c, k), F32),
            pltpu.VMEM((half_c, k), BF16),
            pltpu.VMEM((half_c, k), BF16),
            pltpu.VMEM((5, k_tiles, LANES), F32),
            pltpu.VMEM((2, k_tiles, LANES), jnp.int32),
            pltpu.VMEM((k_tiles, 2, 2, half_r // SUB, LANES), F32),
            pltpu.VMEM((R, C), F32),
            pltpu.VMEM((wide, k), BF16),
            pltpu.VMEM((wide, k), BF16),
            pltpu.VMEM((6 * M, k), BF16),
            pltpu.VMEM((6 * M, k), BF16),
            pltpu.VMEM((2, SUB, k), F32),
            pltpu.VMEM((half_r, wide), F32),
            pltpu.VMEM((half_r, wide), F32),
            pltpu.VMEM((6 * M, half_c), F32),
            pltpu.VMEM((6 * M, half_c), F32),
            pltpu.SemaphoreType.DMA((2 * half_r // M * (half_c // LANES),)),
        ],
        compiler_params=params(36),
        name="image",
    )(blocks, mid, looked)


def solution(mesh):
    return jax.shard_map(
        shards,
        mesh=mesh,
        in_specs=(
            P(None, ("frow", "fcol")),
            P(None, ("frow", "fcol")),
            P(("frow", "fcol")),
            P(),
            P(),
            P("frow", "fcol", None, None),
            P(),
        ),
        out_specs=P("frow", "fcol"),
        check_vma=False,
    )
```

```python
import functools
import math

import jax
import jax.numpy as jnp
from jax import lax
from jax.experimental import pallas as pl
from jax.experimental.pallas import tpu as pltpu
from jax.sharding import PartitionSpec as P

R = 1024
C = 512
M = 64
NT = 16
NBLK = 4
LANES = 128
SUB = 8
OWN, LEFT, RIGHT, UP, DOWN, UL, UR, DL, DR = range(9)
F32 = jnp.float32
BF16 = jnp.bfloat16


def wrap(m, modulus):
    if modulus & (modulus - 1) == 0:
        return m & (modulus - 1)
    return jnp.remainder(m, modulus)


def turn(m, modulus):
    m = wrap(m, modulus)
    quarter = modulus // 4
    q = (m + modulus // 8) // quarter if quarter & (quarter - 1) else (
        (m + modulus // 8) >> (quarter.bit_length() - 1))
    x = (m - q * quarter).astype(F32) * (2.0 * math.pi / modulus)
    x2 = x * x
    s = x + x * x2 * (-1 / 6 + x2 * (1 / 120 + x2 * (-1 / 5040 + x2 * (1 / 362880))))
    c = 1.0 + x2 * (-0.5 + x2 * (1 / 24 + x2 * (-1 / 720 + x2 * (1 / 40320))))
    odd = (q & 1) == 1
    cos = jnp.where(odd, s, c)
    sin = jnp.where(odd, c, s)
    cos = jnp.where(((q + 1) & 2) != 0, -cos, cos)
    sin = jnp.where((q & 2) != 0, -sin, sin)
    return cos, sin


def times(a, b):
    return a[0] * b[0] - a[1] * b[1], a[0] * b[1] + a[1] * b[0]


def pack_kernel(order_ref, vis_ref, pair_ref, slot_ref, u_ref, v_ref, out_ref, label_ref):
    block = vis_ref.shape[1]
    lines = [vis_ref[0:1, :], vis_ref[1:2, :], pair_ref[0:1, :].astype(F32),
             pair_ref[1:2, :].astype(F32), slot_ref[...].astype(F32)]
    for copy in range(out_ref.shape[0]):
        for q, line in enumerate(lines):
            out_ref[copy, :, q * block:(q + 1) * block] = line
    n_lines = u_ref.shape[0]
    at = lax.broadcasted_iota(jnp.int32, (SUB, LANES), 1)
    order = jnp.zeros((SUB, LANES), jnp.int32)
    for b in range(NBLK):
        order = jnp.where(at == b, order_ref[b], order)
    label_ref[:SUB] = order.astype(F32)
    label_ref[SUB:SUB + n_lines] = u_ref[...].astype(F32)
    label_ref[SUB + n_lines:SUB + 2 * n_lines] = v_ref[...].astype(F32)


def pick(row, lane):
    return jnp.take_along_axis(
        jnp.broadcast_to(row, lane.shape), lane, axis=1, mode="promise_in_bounds")


def taper_rows(group, half, wide=LANES):
    index = (lax.broadcasted_iota(jnp.int32, (SUB, wide), 0) + SUB * group).astype(F32)
    return ((half + M - 0.5 - index) * (1.0 / (2 * M)),
            (index - (half - M - 0.5)) * (1.0 / (2 * M)))


def phase_tables(n_frow, n_fcol, first, n_lines, block_ref, cell_ref,
                 s_ref, ac_ref, as_ref, ec_ref, es_ref, fc_ref, fs_ref, cc_ref, cs_ref,
                 q_ref, uv_ref, dr_ref):
    frow_at = lax.axis_index("frow")
    fcol_at = lax.axis_index("fcol")
    half_r, half_c = R // 2, C // 2
    mod_r, mod_c = 2 * R * n_frow, 2 * C * n_fcol
    k_tiles = s_ref.shape[1]
    per_block = k_tiles // NBLK
    block = per_block * LANES
    shape = (SUB, LANES)

    order = cell_ref[first:first + 1, :]
    place = lax.broadcasted_iota(jnp.int32, (1, LANES), 1)
    owners = [jnp.sum(jnp.where(place == b, order, 0.0)).astype(jnp.int32) for b in range(NBLK)]
    for b, owner in enumerate(owners):
        for q in range(5):
            for j in range(per_block):
                q_ref[q, b * per_block + j:b * per_block + j + 1, :] = block_ref[
                    owner, :, q * block + j * LANES:q * block + (j + 1) * LANES]
    a1 = q_ref[2].astype(jnp.int32)
    a2 = q_ref[3].astype(jnp.int32)
    slot = q_ref[4].astype(jnp.int32)

    at = first + SUB

    def cells(table):
        got = [jnp.zeros(shape, F32)] * 2
        for h in range(table.shape[0]):
            row = table[h:h + 1, :]
            got = [jnp.where((a >> 7) == h, pick(row, a & 127), g)
                   for a, g in zip((a1, a2), got)]
        return (got[0] - got[1]).astype(jnp.int32)

    u = cells(cell_ref[at:at + n_lines, :])
    v = cells(cell_ref[at + n_lines:at + 2 * n_lines, :])
    uv_ref[0] = u
    uv_ref[1] = v
    centre = times(turn(u * (frow_at * (2 * R) + (R - 1)), mod_r),
                   turn(v * (fcol_at * (2 * C) + (C - 1)), mod_c))
    scale = 0.5 / math.sqrt(NBLK * per_block * LANES)
    value = times((q_ref[0] * scale, q_ref[1] * scale), centre)
    s_ref[0] = value[0]
    s_ref[1] = value[1]
    for n, a in enumerate((a1, a2)):
        s_ref[2 + n] = ((a >> 3) + (a & 6) * 32).astype(F32)
        s_ref[4 + n] = ((a & 1) * NT + slot).astype(F32)

    iota = lax.broadcasted_iota(jnp.int32, shape, 0)

    def tables(s):
        lane = slice(s * LANES, (s + 1) * LANES)

        def phases(which, modulus, half):
            freq = jnp.broadcast_to(uv_ref[which, s:s + 1, :], shape)
            fine = turn(freq * (2 * iota + 1), modulus)
            middle = turn(freq * (16 * iota), modulus)
            coarse = turn(freq * (128 * iota), modulus)
            for a in range(half // 64):
                top = tuple(jnp.broadcast_to(x[a:a + 1], shape) for x in coarse)
                both = times(middle, top)
                for comp in range(2):
                    dr_ref[s, which, comp, 8 * a:8 * a + 8, :] = both[comp]
            for g in range(half // SUB):
                step = tuple(jnp.broadcast_to(dr_ref[s, which, comp, g:g + 1, :], shape)
                             for comp in range(2))
                yield times(fine, step)

        pairs = {}

        def put(ref, first, group, x):
            key = (id(ref), first)
            if group % 2 == 0:
                pairs[key] = x
            else:
                start = first + SUB * (group - 1)
                ref[start:start + 16, lane] = jnp.concatenate([pairs.pop(key), x], 0).astype(BF16)

        edge = (half_r - M) // SUB
        for g, (cos, sin) in enumerate(phases(0, mod_r, half_r)):
            if g >= edge:
                mine, other = taper_rows(g, half_r)
                at = slice((g - edge) * SUB, (g - edge + 1) * SUB)
                ec_ref[at, lane] = cos * other
                es_ref[at, lane] = sin * other
                cos, sin = cos * mine, sin * mine
            put(ac_ref, 0, g, cos)
            put(as_ref, 0, g, sin)
        for g, (cos, sin) in enumerate(phases(1, mod_c, half_c)):
            put(cc_ref, 0, g, cos)
            put(cs_ref, 0, g, sin)
            at = slice(g * SUB, (g + 1) * SUB)
            fc_ref[at, lane] = cos
            fs_ref[at, lane] = sin

    return tables


def gain_kernel(depth, mid_ref, a_ref, b_ref, gain_ref):
    half = depth // 2
    places = 2 * NT
    low_lane = lax.broadcasted_iota(jnp.int32, (places, LANES), 1) < LANES // 2
    for f in range(9):
        ref, row = (mid_ref, a_ref, b_ref)[f // 3], f % 3 * depth
        both = jnp.concatenate([ref[pl.ds(row, half, stride=2), :],
                                ref[pl.ds(row + 1, half, stride=2), :]], 0).T
        quarter = [both[i * places:(i + 1) * places] for i in range(4)]
        turned = [pltpu.roll(x, LANES // 2, 1) for x in quarter]
        for t in range(2):
            re = jnp.where(low_lane, quarter[2 * t], turned[2 * t + 1])
            im = jnp.where(low_lane, turned[2 * t], quarter[2 * t + 1])
            for comp, x in enumerate((re, im)):
                high = x.astype(BF16)
                at = (2 * (f - 1 if f else SUB) + comp) * places
                gain_ref[at:at + places, t * LANES:(t + 1) * LANES] = high
                if f == 0:
                    at += 2 * places
                    gain_ref[at:at + places, t * LANES:(t + 1) * LANES] = (
                        x - high.astype(F32)).astype(BF16)


def image_kernel(n_frow, n_fcol, first, n_lines, depth, block_ref, cell_ref, gain_ref, image_ref,
                 s_ref, ac_ref, as_ref, ec_ref, es_ref, fc_ref, fs_ref, cc_ref, cs_ref,
                 q_ref, uv_ref, dr_ref, out_ref, tc_ref, ts_ref, uc_ref, us_ref, w_ref,
                 m1_ref, m2_ref, g1_ref, g2_ref, sems):
    tables = phase_tables(n_frow, n_fcol, first, n_lines, block_ref, cell_ref, s_ref, ac_ref,
                          as_ref, ec_ref, es_ref, fc_ref, fs_ref, cc_ref, cs_ref,
                          q_ref, uv_ref, dr_ref)
    frow_at = lax.axis_index("frow")
    r_odd = lax.rem(frow_at, 2) == 1
    fcol_at = lax.axis_index("fcol")
    c_odd = lax.rem(fcol_at, 2) == 1
    k_tiles = s_ref.shape[1]
    half_c = C // 2
    places = 2 * NT

    r_first, r_second = jnp.where(r_odd, 1, 2), jnp.where(r_odd, 2, 1)
    c_first, c_second = jnp.where(c_odd, 1, 2), jnp.where(c_odd, 2, 1)
    rows = {UP: r_first - 1, DOWN: r_second - 1, LEFT: 3 * c_first - 1, RIGHT: 3 * c_second - 1,
            UL: 3 * c_first + r_first - 1, UR: 3 * c_second + r_first - 1,
            DL: 3 * c_first + r_second - 1, DR: 3 * c_second + r_second - 1}

    step = 2 if k_tiles % 2 == 0 else 1
    wide = step * LANES
    shape = (SUB, wide)
    line_at = lax.broadcasted_iota(jnp.int32, (2 * depth, wide), 0).astype(F32)
    place_at = line_at[:places]
    row_at = lax.broadcasted_iota(jnp.int32, shape, 0)
    zero = jnp.zeros((M, wide), BF16)
    r_edge = jnp.logical_or(frow_at == 0, frow_at == n_frow - 1)
    c_edge = jnp.logical_or(fcol_at == 0, fcol_at == n_fcol - 1)
    keep = (jnp.where(lax.rem(row_at, 3) == 1, jnp.where(r_edge, 0.0, 1.0), 1.0)
            * jnp.where(row_at >= 5, jnp.where(c_edge, 0.0, 1.0), 1.0))

    def fold(parts):
        parts = [parts[i] for i in (0, 4, 2, 6, 1, 5, 3, 7)]
        for distance in (1, 2, 4):
            low = (row_at & distance) == 0
            count = len(parts) // 2
            parts = [jnp.where(low, x, y) + pltpu.roll(jnp.where(low, y, x), distance, 0)
                     for x, y in zip(parts[:count], parts[count:])]
        return parts[0]

    def gain_product(first, second):
        (g1r, g1i), (g2r, g2i) = first, second
        return g1r * g2r + g1i * g2i, g1i * g2r - g1r * g2i

    def weight(f, lane):
        return tuple(jnp.broadcast_to(w_ref[comp, pl.ds(rows[f], 1), lane], shape)
                     for comp in range(2))

    for p in range(k_tiles // step):
        lane = slice(p * wide, (p + 1) * wide)

        def line(q):
            return jnp.concatenate([s_ref[q, p * step + i:p * step + i + 1, :]
                                    for i in range(step)], 1)

        for i in range(step):
            tables(p * step + i)
        owns, nears = [], []
        for n in range(2):
            hot = jnp.where(line_at == line(2 + n), 1.0, 0.0).astype(BF16)
            mask = jnp.where(place_at == line(4 + n), 1.0, 0.0)
            z = jnp.dot(gain_ref[...], hot, preferred_element_type=F32)

            def part(f, comp):
                at = (2 * f + comp) * places
                x = z[at:at + places]
                if f == SUB:
                    x = x + z[at + 2 * places:at + 3 * places]
                x = x * mask
                return sum((x[i * SUB:(i + 1) * SUB] for i in range(1, places // SUB)), x[:SUB])

            owns.append([jnp.sum(part(SUB, comp), axis=0, keepdims=True) for comp in range(2)])
            nears.append([fold([part(f, comp) for f in range(SUB)]) for comp in range(2)])
        value = (line(0), line(1))
        own_w = times(value, gain_product(*owns))
        near_w = times(tuple(x * keep for x in value), gain_product(*nears))
        for comp in range(2):
            w_ref[comp, :, lane] = near_w[comp]

        pairs = {}

        def put(ref, first, group, x):
            key = (id(ref), first)
            if group % 2 == 0:
                pairs[key] = x
            else:
                start = first + SUB * (group - 1)
                ref[start:start + 16, lane] = jnp.concatenate([pairs.pop(key), x], 0).astype(BF16)

        edge = (half_c - M) // SUB
        wr, wi = [jnp.broadcast_to(x, shape) for x in own_w]
        (lr, li), (rr, ri) = weight(LEFT, lane), weight(RIGHT, lane)
        for g in range(half_c // SUB):
            at = slice(g * SUB, (g + 1) * SUB)
            cos, sin = fc_ref[at, lane], fs_ref[at, lane]
            own = (cos, sin)
            if g >= edge:
                mine, other = taper_rows(g, half_c, wide)
                own = (cos * mine, sin * mine)
                cos, sin = cos * other, sin * other
                base = 2 * half_c + M
                put(tc_ref, base, g - edge, lr * cos + li * sin)
                put(ts_ref, base, g - edge, lr * sin - li * cos)
                put(tc_ref, base + 2 * M, g - edge, rr * cos - ri * sin)
                put(ts_ref, base + 2 * M, g - edge, -(rr * sin + ri * cos))
            base = g * SUB // LANES * LANES
            put(tc_ref, base, g, wr * own[0])
            put(tc_ref, base + LANES, g, -wi * own[1])
            put(ts_ref, base, g, -wi * own[0])
            put(ts_ref, base + LANES, g, -wr * own[1])
        for ref in (tc_ref, ts_ref):
            ref[2 * half_c:2 * half_c + M, lane] = zero
            ref[2 * half_c + 2 * M:2 * half_c + 3 * M, lane] = zero

    def dot(a, b):
        return lax.dot_general(a, b, (((1,), (1,)), ((), ())), preferred_element_type=F32)

    half_r = R // 2
    n_lane = half_c // LANES

    def own_products(t):
        cols = slice(2 * t * LANES, 2 * (t + 1) * LANES if t < n_lane - 1 else tc_ref.shape[0])
        m1_ref[:, cols] = dot(ac_ref[...], tc_ref[cols, :])
        m2_ref[:, cols] = dot(as_ref[...], ts_ref[cols, :])

    own_products(n_lane - 1)
    signs = (-1, 1, -1, -1, 1, 1)
    for p in range(k_tiles // step):
        lane = slice(p * wide, (p + 1) * wide)
        for n, (f, sd) in enumerate(zip((UP, DOWN, UL, UR, DL, DR), signs)):
            wr, wi = weight(f, lane)
            for g in range(0, M // SUB, 2):
                tops, lows = [], []
                for i in range(2):
                    at = slice((g + i) * SUB, (g + i + 1) * SUB)
                    cos, sin = ec_ref[at, lane], es_ref[at, lane]
                    tops.append(wr * cos - (sd * wi) * sin)
                    lows.append(-(sd * wr) * sin - wi * cos)
                at = slice(n * M + g * SUB, n * M + (g + 2) * SUB)
                uc_ref[at, lane] = jnp.concatenate(tops, 0).astype(BF16)
                us_ref[at, lane] = jnp.concatenate(lows, 0).astype(BF16)
    g1_ref[...] = dot(uc_ref[...], cc_ref[...])
    g2_ref[...] = dot(us_ref[...], cs_ref[...])

    shape = (SUB, LANES)
    iota = lax.broadcasted_iota(jnp.int32, shape, 0)
    lane_at = lax.broadcasted_iota(jnp.int32, shape, 1)
    back_lane = (LANES - 1) - lane_at
    back_row = (SUB - 1) - iota
    edge_c = half_c - M
    edge_r = half_r - M
    col_own, col_other = [], []
    for t in range(n_lane):
        index = (lane_at + t * LANES).astype(F32)
        col_own.append(jnp.minimum((half_c + M - 0.5 - index) * (1.0 / (2 * M)), 1.0))
        col_other.append(jnp.maximum((index - (half_c - M - 0.5)) * (1.0 / (2 * M)), 0.0))

    def flip(x, index, axis):
        return jnp.take_along_axis(x, index, axis=axis, mode="promise_in_bounds")

    def finish(g, t, edged):
        rows = slice(g * SUB, (g + 1) * SUB)
        def part(ref, which):
            return ref[rows, (2 * t + which) * LANES:(2 * t + which + 1) * LANES]
        p, s_, r, q = part(m1_ref, 0), part(m1_ref, 1), part(m2_ref, 0), part(m2_ref, 1)
        even, odd = p + q, p - q
        plus, minus = r + s_, r - s_
        quad = {(1, 1): even + plus, (-1, -1): even - plus,
                (1, -1): odd + minus, (-1, 1): odd - minus}
        if (t + 1) * LANES > edge_c:
            base = 2 * half_c
            off = t * LANES - (half_c - LANES)
            for se, start in ((-1, base), (1, base + LANES)):
                lc = m1_ref[rows, start + off:start + off + LANES]
                ls = m2_ref[rows, start + off:start + off + LANES]
                quad[1, se] += lc + ls
                quad[-1, se] += lc - ls
        if edged:
            def edge(n):
                at = slice(n * M + g * SUB - edge_r, n * M + (g + 1) * SUB - edge_r)
                x = g1_ref[at, t * LANES:(t + 1) * LANES]
                y = g2_ref[at, t * LANES:(t + 1) * LANES]
                return {1: x + y, -1: x - y}
            for n, sd in ((0, -1), (1, 1)):
                e = edge(n)
                for se in (-1, 1):
                    quad[sd, se] += e[se] * col_own[t]
            if (t + 1) * LANES > edge_c:
                for n, (sd, se) in ((2, (-1, -1)), (3, (-1, 1)), (4, (1, -1)), (5, (1, 1))):
                    quad[sd, se] += edge(n)[se] * col_other[t]
        for (sd, se), x in quad.items():
            if sd < 0:
                x = flip(x, back_row, 0)
                at = slice(half_r - SUB - g * SUB, half_r - g * SUB)
            else:
                at = slice(half_r + g * SUB, half_r + (g + 1) * SUB)
            if se < 0:
                x = flip(x, back_lane, 1)
                start = half_c - (t + 1) * LANES
            else:
                start = half_c + t * LANES
            out_ref[at, start:start + LANES] = x

    n_groups = half_r // M

    def sends(j, t):
        copies = []
        for row in (half_r + 2 * M * j, half_r - 2 * M * (j + 1)):
            for col in (half_c + t * LANES, half_c - (t + 1) * LANES):
                at = (slice(row, row + 2 * M), slice(col, col + LANES))
                copies.append(pltpu.make_async_copy(
                    out_ref.at[at], image_ref.at[at], sems.at[(j * n_lane + t) * 4 + len(copies)]))
        return copies

    for t in range(n_lane - 2, -1, -1):
        own_products(t)
    for t in range(n_lane - 1, -1, -1):
        for j in range(n_groups):
            for g in range(j * M // SUB, (j + 1) * M // SUB):
                finish(g, t, j == n_groups - 1)
            if j % 2:
                for copy in sends(j // 2, t):
                    copy.start()
    for t in range(n_lane):
        for j in range(n_groups // 2):
            for copy in sends(j, t):
                copy.wait()


def swaps(size):
    both = []
    for first in (0, 1):
        pairs = [(i, i + 1) for i in range(first, size - 1, 2)]
        both.append(pairs + [(j, i) for i, j in pairs])
    return both


def all_paired(pairs, count, other):
    swap = dict(pairs)
    for i in range(count):
        if i not in swap and other(i) not in swap:
            swap[i], swap[other(i)] = other(i), i
    return list(swap.items())


def shards(vis, station_pairs, visibility_time_slot, station_u_cells, station_v_cells,
           facet_station_gains, holder_device_order):
    n_frow = lax.axis_size("frow")
    n_fcol = lax.axis_size("fcol")
    block = vis.shape[1]
    k_tiles = NBLK * block // LANES
    k = k_tiles * LANES
    half_r, half_c = R // 2, C // 2
    wide = 2 * half_c + 4 * M
    vmem = pl.BlockSpec(memory_space=pltpu.VMEM)
    smem = pl.BlockSpec(memory_space=pltpu.SMEM)

    def lines(x):
        return x.reshape(-1, LANES)

    def shaped(*dims, dtype=F32):
        return jax.ShapeDtypeStruct(dims, dtype)

    def params(mib):
        return pltpu.CompilerParams(vmem_limit_bytes=mib * 1024 * 1024)

    n_lines = station_u_cells.size // LANES
    packed, labels = pl.pallas_call(
        pack_kernel,
        out_shape=[shaped(n_frow * n_fcol, 1, 5 * block), shaped(SUB + 2 * n_lines, LANES)],
        in_specs=[smem] + [vmem] * 5,
        name="pack",
    )(holder_device_order, vis, station_pairs, visibility_time_slot.reshape(1, block),
      lines(station_u_cells), lines(station_v_cells))
    facet_station_gains, packed = lax.optimization_barrier((facet_station_gains, packed))
    gains = facet_station_gains[0, 0]
    depth = gains.size // LANES
    own = gains.reshape(2, -1, LANES).transpose(1, 0, 2).reshape(depth, LANES)
    count = n_frow * n_fcol

    def beside(i):
        return i ^ 1 if n_fcol % 2 == 0 else i

    row_a, row_b = [
        lax.ppermute(own, ("frow", "fcol"), all_paired(
            [(i * n_fcol + c, j * n_fcol + c) for i, j in pairs for c in range(n_fcol)],
            count, beside))
        for pairs in swaps(n_frow)]
    blocks = lax.all_to_all(packed, ("frow", "fcol"), 0, 0)
    mid = jnp.concatenate([own, row_a, row_b, labels], 0)
    def next_row(i):
        j = i ^ n_fcol if n_fcol & (n_fcol - 1) == 0 else i
        return j if j < count else i

    col_a, col_b = [
        lax.ppermute(mid, ("frow", "fcol"), all_paired(
            [(r * n_fcol + i, r * n_fcol + j) for r in range(n_frow) for i, j in pairs],
            count, next_row))
        for pairs in swaps(n_fcol)]
    looked = pl.pallas_call(
        functools.partial(gain_kernel, depth),
        out_shape=shaped(40 * NT, 2 * depth, dtype=BF16),
        in_specs=[vmem] * 3,
        out_specs=vmem,
        compiler_params=params(8),
        name="gains",
    )(mid, col_a, col_b)
    return pl.pallas_call(
        functools.partial(image_kernel, n_frow, n_fcol, 3 * depth, n_lines, depth),
        out_shape=shaped(R, C),
        in_specs=[vmem] * 3,
        out_specs=pl.BlockSpec(memory_space=pl.ANY),
        scratch_shapes=[
            pltpu.VMEM((6, k_tiles, LANES), F32),
            pltpu.VMEM((half_r, k), BF16),
            pltpu.VMEM((half_r, k), BF16),
            pltpu.VMEM((M, k), F32),
            pltpu.VMEM((M, k), F32),
            pltpu.VMEM((half_c, k), F32),
            pltpu.VMEM((half_c, k), F32),
            pltpu.VMEM((half_c, k), BF16),
            pltpu.VMEM((half_c, k), BF16),
            pltpu.VMEM((5, k_tiles, LANES), F32),
            pltpu.VMEM((2, k_tiles, LANES), jnp.int32),
            pltpu.VMEM((k_tiles, 2, 2, half_r // SUB, LANES), F32),
            pltpu.VMEM((R, C), F32),
            pltpu.VMEM((wide, k), BF16),
            pltpu.VMEM((wide, k), BF16),
            pltpu.VMEM((6 * M, k), BF16),
            pltpu.VMEM((6 * M, k), BF16),
            pltpu.VMEM((2, SUB, k), F32),
            pltpu.VMEM((half_r, wide), F32),
            pltpu.VMEM((half_r, wide), F32),
            pltpu.VMEM((6 * M, half_c), F32),
            pltpu.VMEM((6 * M, half_c), F32),
            pltpu.SemaphoreType.DMA((2 * half_r // M * (half_c // LANES),)),
        ],
        compiler_params=params(36),
        name="image",
    )(blocks, mid, looked)


def solution(mesh):
    return jax.shard_map(
        shards,
        mesh=mesh,
        in_specs=(
            P(None, ("frow", "fcol")),
            P(None, ("frow", "fcol")),
            P(("frow", "fcol")),
            P(),
            P(),
            P("frow", "fcol", None, None),
            P(),
        ),
        out_specs=P("frow", "fcol"),
        check_vma=False,
    )
```

```python
import functools
import math

import jax
import jax.numpy as jnp
from jax import lax
from jax.experimental import pallas as pl
from jax.experimental.pallas import tpu as pltpu
from jax.sharding import PartitionSpec as P

R = 1024
C = 512
M = 64
NT = 16
NBLK = 4
LANES = 128
SUB = 8
OWN, LEFT, RIGHT, UP, DOWN, UL, UR, DL, DR = range(9)
F32 = jnp.float32
BF16 = jnp.bfloat16


def wrap(m, modulus):
    if modulus & (modulus - 1) == 0:
        return m & (modulus - 1)
    return jnp.remainder(m, modulus)


def turn(m, modulus):
    m = wrap(m, modulus)
    quarter = modulus // 4
    q = (m + modulus // 8) // quarter if quarter & (quarter - 1) else (
        (m + modulus // 8) >> (quarter.bit_length() - 1))
    x = (m - q * quarter).astype(F32) * (2.0 * math.pi / modulus)
    x2 = x * x
    s = x + x * x2 * (-1 / 6 + x2 * (1 / 120 + x2 * (-1 / 5040 + x2 * (1 / 362880))))
    c = 1.0 + x2 * (-0.5 + x2 * (1 / 24 + x2 * (-1 / 720 + x2 * (1 / 40320))))
    odd = (q & 1) == 1
    cos = jnp.where(odd, s, c)
    sin = jnp.where(odd, c, s)
    cos = jnp.where(((q + 1) & 2) != 0, -cos, cos)
    sin = jnp.where((q & 2) != 0, -sin, sin)
    return cos, sin


def times(a, b):
    return a[0] * b[0] - a[1] * b[1], a[0] * b[1] + a[1] * b[0]


def pack_kernel(order_ref, vis_ref, pair_ref, slot_ref, u_ref, v_ref, out_ref, label_ref):
    block = vis_ref.shape[1]
    lines = [vis_ref[0:1, :], vis_ref[1:2, :], pair_ref[0:1, :].astype(F32),
             pair_ref[1:2, :].astype(F32), slot_ref[...].astype(F32)]
    for copy in range(out_ref.shape[0]):
        for q, line in enumerate(lines):
            out_ref[copy, :, q * block:(q + 1) * block] = line
    n_lines = u_ref.shape[0]
    at = lax.broadcasted_iota(jnp.int32, (SUB, LANES), 1)
    order = jnp.zeros((SUB, LANES), jnp.int32)
    for b in range(NBLK):
        order = jnp.where(at == b, order_ref[b], order)
    label_ref[:SUB] = order.astype(F32)
    label_ref[SUB:SUB + n_lines] = u_ref[...].astype(F32)
    label_ref[SUB + n_lines:SUB + 2 * n_lines] = v_ref[...].astype(F32)


def pick(row, lane):
    return jnp.take_along_axis(
        jnp.broadcast_to(row, lane.shape), lane, axis=1, mode="promise_in_bounds")


def taper_rows(group, half, wide=LANES):
    index = (lax.broadcasted_iota(jnp.int32, (SUB, wide), 0) + SUB * group).astype(F32)
    return ((half + M - 0.5 - index) * (1.0 / (2 * M)),
            (index - (half - M - 0.5)) * (1.0 / (2 * M)))


def phase_tables(n_frow, n_fcol, first, n_lines, block_ref, cell_ref,
                 s_ref, ac_ref, as_ref, ec_ref, es_ref, q_ref, uv_ref, dr_ref):
    frow_at = lax.axis_index("frow")
    fcol_at = lax.axis_index("fcol")
    half_r, half_c = R // 2, C // 2
    mod_r, mod_c = 2 * R * n_frow, 2 * C * n_fcol
    k_tiles = s_ref.shape[1]
    per_block = k_tiles // NBLK
    block = per_block * LANES
    shape = (SUB, LANES)

    order = cell_ref[first:first + 1, :]
    place = lax.broadcasted_iota(jnp.int32, (1, LANES), 1)
    owners = [jnp.sum(jnp.where(place == b, order, 0.0)).astype(jnp.int32) for b in range(NBLK)]
    for b, owner in enumerate(owners):
        for q in range(5):
            for j in range(per_block):
                q_ref[q, b * per_block + j:b * per_block + j + 1, :] = block_ref[
                    owner, :, q * block + j * LANES:q * block + (j + 1) * LANES]
    a1 = q_ref[2].astype(jnp.int32)
    a2 = q_ref[3].astype(jnp.int32)
    slot = q_ref[4].astype(jnp.int32)

    at = first + SUB

    def cells(table):
        got = [jnp.zeros(shape, F32)] * 2
        for h in range(table.shape[0]):
            row = table[h:h + 1, :]
            got = [jnp.where((a >> 7) == h, pick(row, a & 127), g)
                   for a, g in zip((a1, a2), got)]
        return (got[0] - got[1]).astype(jnp.int32)

    u = cells(cell_ref[at:at + n_lines, :])
    v = cells(cell_ref[at + n_lines:at + 2 * n_lines, :])
    uv_ref[0] = u
    uv_ref[1] = v
    centre = times(turn(u * (frow_at * (2 * R) + (R - 1)), mod_r),
                   turn(v * (fcol_at * (2 * C) + (C - 1)), mod_c))
    scale = 0.5 / math.sqrt(NBLK * per_block * LANES)
    value = times((q_ref[0] * scale, q_ref[1] * scale), centre)
    s_ref[0] = value[0]
    s_ref[1] = value[1]
    for n, a in enumerate((a1, a2)):
        s_ref[2 + n] = ((a >> 3) + (a & 6) * 32).astype(F32)
        s_ref[4 + n] = ((a & 1) * NT + slot).astype(F32)

    iota = lax.broadcasted_iota(jnp.int32, shape, 0)

    def phases(s, which, modulus, half):
        freq = jnp.broadcast_to(uv_ref[which, s:s + 1, :], shape)
        fine = turn(freq * (2 * iota + 1), modulus)
        middle = turn(freq * (16 * iota), modulus)
        coarse = turn(freq * (128 * iota), modulus)
        for a in range(half // 64):
            top = tuple(jnp.broadcast_to(x[a:a + 1], shape) for x in coarse)
            both = times(middle, top)
            for comp in range(2):
                dr_ref[s, which, comp, 8 * a:8 * a + 8, :] = both[comp]
        for g in range(half // SUB):
            step = tuple(jnp.broadcast_to(dr_ref[s, which, comp, g:g + 1, :], shape)
                         for comp in range(2))
            yield times(fine, step)

    def rows(s):
        lane = slice(s * LANES, (s + 1) * LANES)
        put = putter(lane)
        edge = (half_r - M) // SUB
        for g, (cos, sin) in enumerate(phases(s, 0, mod_r, half_r)):
            if g >= edge:
                mine, other = taper_rows(g, half_r)
                at = slice((g - edge) * SUB, (g - edge + 1) * SUB)
                ec_ref[at, lane] = cos * other
                es_ref[at, lane] = sin * other
                cos, sin = cos * mine, sin * mine
            put(ac_ref, 0, g, cos)
            put(as_ref, 0, g, sin)

    return rows, lambda s: phases(s, 1, mod_c, half_c)


def putter(lane):
    pairs = {}

    def put(ref, first, group, x):
        key = (id(ref), first)
        if group % 2 == 0:
            pairs[key] = x
        else:
            start = first + SUB * (group - 1)
            ref[start:start + 16, lane] = jnp.concatenate([pairs.pop(key), x], 0).astype(BF16)

    return put


def gain_kernel(depth, mid_ref, a_ref, b_ref, gain_ref):
    half = depth // 2
    places = 2 * NT
    low_lane = lax.broadcasted_iota(jnp.int32, (places, LANES), 1) < LANES // 2
    for f in range(9):
        ref, row = (mid_ref, a_ref, b_ref)[f // 3], f % 3 * depth
        both = jnp.concatenate([ref[pl.ds(row, half, stride=2), :],
                                ref[pl.ds(row + 1, half, stride=2), :]], 0).T
        quarter = [both[i * places:(i + 1) * places] for i in range(4)]
        turned = [pltpu.roll(x, LANES // 2, 1) for x in quarter]
        for t in range(2):
            re = jnp.where(low_lane, quarter[2 * t], turned[2 * t + 1])
            im = jnp.where(low_lane, turned[2 * t], quarter[2 * t + 1])
            for comp, x in enumerate((re, im)):
                high = x.astype(BF16)
                at = (2 * (f - 1 if f else SUB) + comp) * places
                gain_ref[at:at + places, t * LANES:(t + 1) * LANES] = high
                if f == 0:
                    at += 2 * places
                    gain_ref[at:at + places, t * LANES:(t + 1) * LANES] = (
                        x - high.astype(F32)).astype(BF16)


def image_kernel(n_frow, n_fcol, first, n_lines, depth, block_ref, cell_ref, gain_ref, image_ref,
                 s_ref, ac_ref, as_ref, ec_ref, es_ref, cc_ref, cs_ref,
                 q_ref, uv_ref, dr_ref, out_ref, tc_ref, ts_ref, uc_ref, us_ref, w_ref,
                 m1_ref, m2_ref, g1_ref, g2_ref, sems):
    row_tables, column_phases = phase_tables(
        n_frow, n_fcol, first, n_lines, block_ref, cell_ref, s_ref, ac_ref, as_ref, ec_ref, es_ref,
        q_ref, uv_ref, dr_ref)
    frow_at = lax.axis_index("frow")
    r_odd = lax.rem(frow_at, 2) == 1
    fcol_at = lax.axis_index("fcol")
    c_odd = lax.rem(fcol_at, 2) == 1
    k_tiles = s_ref.shape[1]
    half_c = C // 2
    places = 2 * NT

    r_first, r_second = jnp.where(r_odd, 1, 2), jnp.where(r_odd, 2, 1)
    c_first, c_second = jnp.where(c_odd, 1, 2), jnp.where(c_odd, 2, 1)
    rows = {UP: r_first - 1, DOWN: r_second - 1, LEFT: 3 * c_first - 1, RIGHT: 3 * c_second - 1,
            UL: 3 * c_first + r_first - 1, UR: 3 * c_second + r_first - 1,
            DL: 3 * c_first + r_second - 1, DR: 3 * c_second + r_second - 1}

    step = 2 if k_tiles % 2 == 0 else 1
    wide = step * LANES
    shape = (SUB, wide)
    line_at = lax.broadcasted_iota(jnp.int32, (2 * depth, wide), 0).astype(F32)
    place_at = line_at[:places]
    row_at = lax.broadcasted_iota(jnp.int32, shape, 0)
    zero = jnp.zeros((M, wide), BF16)
    r_edge = jnp.logical_or(frow_at == 0, frow_at == n_frow - 1)
    c_edge = jnp.logical_or(fcol_at == 0, fcol_at == n_fcol - 1)
    keep = (jnp.where(lax.rem(row_at, 3) == 1, jnp.where(r_edge, 0.0, 1.0), 1.0)
            * jnp.where(row_at >= 5, jnp.where(c_edge, 0.0, 1.0), 1.0))

    def fold(parts):
        parts = [parts[i] for i in (0, 4, 2, 6, 1, 5, 3, 7)]
        for distance in (1, 2, 4):
            low = (row_at & distance) == 0
            count = len(parts) // 2
            parts = [jnp.where(low, x, y) + pltpu.roll(jnp.where(low, y, x), distance, 0)
                     for x, y in zip(parts[:count], parts[count:])]
        return parts[0]

    def gain_product(first, second):
        (g1r, g1i), (g2r, g2i) = first, second
        return g1r * g2r + g1i * g2i, g1i * g2r - g1r * g2i

    def weight(f, lane):
        return tuple(jnp.broadcast_to(w_ref[comp, pl.ds(rows[f], 1), lane], shape)
                     for comp in range(2))

    for p in range(k_tiles // step):
        lane = slice(p * wide, (p + 1) * wide)

        def line(q):
            return jnp.concatenate([s_ref[q, p * step + i:p * step + i + 1, :]
                                    for i in range(step)], 1)

        for i in range(step):
            row_tables(p * step + i)
        owns, nears = [], []
        for n in range(2):
            hot = jnp.where(line_at == line(2 + n), 1.0, 0.0).astype(BF16)
            mask = jnp.where(place_at == line(4 + n), 1.0, 0.0)
            z = jnp.dot(gain_ref[...], hot, preferred_element_type=F32)

            def part(f, comp):
                at = (2 * f + comp) * places
                x = z[at:at + places]
                if f == SUB:
                    x = x + z[at + 2 * places:at + 3 * places]
                x = x * mask
                return sum((x[i * SUB:(i + 1) * SUB] for i in range(1, places // SUB)), x[:SUB])

            owns.append([jnp.sum(part(SUB, comp), axis=0, keepdims=True) for comp in range(2)])
            nears.append([fold([part(f, comp) for f in range(SUB)]) for comp in range(2)])
        value = (line(0), line(1))
        own_w = times(value, gain_product(*owns))
        near_w = times(tuple(x * keep for x in value), gain_product(*nears))
        for comp in range(2):
            w_ref[comp, :, lane] = near_w[comp]

        edge = (half_c - M) // SUB
        step_w = [weight(LEFT, lane), weight(RIGHT, lane),
                  [jnp.broadcast_to(x, shape) for x in own_w]]
        for i in range(step):
            tile = p * step + i
            lane = slice(tile * LANES, (tile + 1) * LANES)
            put = putter(lane)
            (lr, li), (rr, ri), (wr, wi) = [
                [x[:, i * LANES:(i + 1) * LANES] for x in w] for w in step_w]
            for g, (cos, sin) in enumerate(column_phases(tile)):
                put(cc_ref, 0, g, cos)
                put(cs_ref, 0, g, sin)
                own = (cos, sin)
                if g >= edge:
                    mine, other = taper_rows(g, half_c)
                    own = (cos * mine, sin * mine)
                    cos, sin = cos * other, sin * other
                    base = 2 * half_c + M
                    put(tc_ref, base, g - edge, lr * cos + li * sin)
                    put(ts_ref, base, g - edge, lr * sin - li * cos)
                    put(tc_ref, base + 2 * M, g - edge, rr * cos - ri * sin)
                    put(ts_ref, base + 2 * M, g - edge, -(rr * sin + ri * cos))
                base = g * SUB // LANES * LANES
                put(tc_ref, base, g, wr * own[0])
                put(tc_ref, base + LANES, g, -wi * own[1])
                put(ts_ref, base, g, -wi * own[0])
                put(ts_ref, base + LANES, g, -wr * own[1])
        lane = slice(p * wide, (p + 1) * wide)
        for ref in (tc_ref, ts_ref):
            ref[2 * half_c:2 * half_c + M, lane] = zero
            ref[2 * half_c + 2 * M:2 * half_c + 3 * M, lane] = zero

    def dot(a, b):
        return lax.dot_general(a, b, (((1,), (1,)), ((), ())), preferred_element_type=F32)

    half_r = R // 2
    n_lane = half_c // LANES

    def own_products(t):
        cols = slice(2 * t * LANES, 2 * (t + 1) * LANES if t < n_lane - 1 else tc_ref.shape[0])
        m1_ref[:, cols] = dot(ac_ref[...], tc_ref[cols, :])
        m2_ref[:, cols] = dot(as_ref[...], ts_ref[cols, :])

    own_products(n_lane - 1)
    signs = (-1, 1, -1, -1, 1, 1)
    for p in range(k_tiles // step):
        lane = slice(p * wide, (p + 1) * wide)
        for n, (f, sd) in enumerate(zip((UP, DOWN, UL, UR, DL, DR), signs)):
            wr, wi = weight(f, lane)
            for g in range(0, M // SUB, 2):
                tops, lows = [], []
                for i in range(2):
                    at = slice((g + i) * SUB, (g + i + 1) * SUB)
                    cos, sin = ec_ref[at, lane], es_ref[at, lane]
                    tops.append(wr * cos - (sd * wi) * sin)
                    lows.append(-(sd * wr) * sin - wi * cos)
                at = slice(n * M + g * SUB, n * M + (g + 2) * SUB)
                uc_ref[at, lane] = jnp.concatenate(tops, 0).astype(BF16)
                us_ref[at, lane] = jnp.concatenate(lows, 0).astype(BF16)
    g1_ref[...] = dot(uc_ref[...], cc_ref[...])
    g2_ref[...] = dot(us_ref[...], cs_ref[...])

    shape = (SUB, LANES)
    iota = lax.broadcasted_iota(jnp.int32, shape, 0)
    lane_at = lax.broadcasted_iota(jnp.int32, shape, 1)
    back_lane = (LANES - 1) - lane_at
    back_row = (SUB - 1) - iota
    edge_c = half_c - M
    edge_r = half_r - M
    col_own, col_other = [], []
    for t in range(n_lane):
        index = (lane_at + t * LANES).astype(F32)
        col_own.append(jnp.minimum((half_c + M - 0.5 - index) * (1.0 / (2 * M)), 1.0))
        col_other.append(jnp.maximum((index - (half_c - M - 0.5)) * (1.0 / (2 * M)), 0.0))

    def flip(x, index, axis):
        return jnp.take_along_axis(x, index, axis=axis, mode="promise_in_bounds")

    def finish(g, t, edged):
        rows = slice(g * SUB, (g + 1) * SUB)
        def part(ref, which):
            return ref[rows, (2 * t + which) * LANES:(2 * t + which + 1) * LANES]
        p, s_, r, q = part(m1_ref, 0), part(m1_ref, 1), part(m2_ref, 0), part(m2_ref, 1)
        even, odd = p + q, p - q
        plus, minus = r + s_, r - s_
        quad = {(1, 1): even + plus, (-1, -1): even - plus,
                (1, -1): odd + minus, (-1, 1): odd - minus}
        if (t + 1) * LANES > edge_c:
            base = 2 * half_c
            off = t * LANES - (half_c - LANES)
            for se, start in ((-1, base), (1, base + LANES)):
                lc = m1_ref[rows, start + off:start + off + LANES]
                ls = m2_ref[rows, start + off:start + off + LANES]
                quad[1, se] += lc + ls
                quad[-1, se] += lc - ls
        if edged:
            def edge(n):
                at = slice(n * M + g * SUB - edge_r, n * M + (g + 1) * SUB - edge_r)
                x = g1_ref[at, t * LANES:(t + 1) * LANES]
                y = g2_ref[at, t * LANES:(t + 1) * LANES]
                return {1: x + y, -1: x - y}
            for n, sd in ((0, -1), (1, 1)):
                e = edge(n)
                for se in (-1, 1):
                    quad[sd, se] += e[se] * col_own[t]
            if (t + 1) * LANES > edge_c:
                for n, (sd, se) in ((2, (-1, -1)), (3, (-1, 1)), (4, (1, -1)), (5, (1, 1))):
                    quad[sd, se] += edge(n)[se] * col_other[t]
        for (sd, se), x in quad.items():
            if sd < 0:
                x = flip(x, back_row, 0)
                at = slice(half_r - SUB - g * SUB, half_r - g * SUB)
            else:
                at = slice(half_r + g * SUB, half_r + (g + 1) * SUB)
            if se < 0:
                x = flip(x, back_lane, 1)
                start = half_c - (t + 1) * LANES
            else:
                start = half_c + t * LANES
            out_ref[at, start:start + LANES] = x

    n_groups = half_r // M

    def sends(j, t):
        copies = []
        for row in (half_r + 2 * M * j, half_r - 2 * M * (j + 1)):
            for col in (half_c + t * LANES, half_c - (t + 1) * LANES):
                at = (slice(row, row + 2 * M), slice(col, col + LANES))
                copies.append(pltpu.make_async_copy(
                    out_ref.at[at], image_ref.at[at], sems.at[(j * n_lane + t) * 4 + len(copies)]))
        return copies

    for t in range(n_lane - 2, -1, -1):
        own_products(t)
    for t in range(n_lane - 1, -1, -1):
        for j in range(n_groups):
            for g in range(j * M // SUB, (j + 1) * M // SUB):
                finish(g, t, j == n_groups - 1)
            if j % 2:
                for copy in sends(j // 2, t):
                    copy.start()
    for t in range(n_lane):
        for j in range(n_groups // 2):
            for copy in sends(j, t):
                copy.wait()


def swaps(size):
    both = []
    for first in (0, 1):
        pairs = [(i, i + 1) for i in range(first, size - 1, 2)]
        both.append(pairs + [(j, i) for i, j in pairs])
    return both


def all_paired(pairs, count, other):
    swap = dict(pairs)
    for i in range(count):
        if i not in swap and other(i) not in swap:
            swap[i], swap[other(i)] = other(i), i
    return list(swap.items())


def shards(vis, station_pairs, visibility_time_slot, station_u_cells, station_v_cells,
           facet_station_gains, holder_device_order):
    n_frow = lax.axis_size("frow")
    n_fcol = lax.axis_size("fcol")
    block = vis.shape[1]
    k_tiles = NBLK * block // LANES
    k = k_tiles * LANES
    half_r, half_c = R // 2, C // 2
    wide = 2 * half_c + 4 * M
    vmem = pl.BlockSpec(memory_space=pltpu.VMEM)
    smem = pl.BlockSpec(memory_space=pltpu.SMEM)

    def lines(x):
        return x.reshape(-1, LANES)

    def shaped(*dims, dtype=F32):
        return jax.ShapeDtypeStruct(dims, dtype)

    def params(mib):
        return pltpu.CompilerParams(vmem_limit_bytes=mib * 1024 * 1024)

    n_lines = station_u_cells.size // LANES
    packed, labels = pl.pallas_call(
        pack_kernel,
        out_shape=[shaped(n_frow * n_fcol, 1, 5 * block), shaped(SUB + 2 * n_lines, LANES)],
        in_specs=[smem] + [vmem] * 5,
        name="pack",
    )(holder_device_order, vis, station_pairs, visibility_time_slot.reshape(1, block),
      lines(station_u_cells), lines(station_v_cells))
    facet_station_gains, packed = lax.optimization_barrier((facet_station_gains, packed))
    gains = facet_station_gains[0, 0]
    depth = gains.size // LANES
    own = gains.reshape(2, -1, LANES).transpose(1, 0, 2).reshape(depth, LANES)
    row_a, row_b = [lax.ppermute(own, "frow", all_paired(pairs, n_frow, lambda r: n_frow - 1 - r))
                    for pairs in swaps(n_frow)]
    blocks = lax.all_to_all(packed, ("frow", "fcol"), 0, 0)
    mid = jnp.concatenate([own, row_a, row_b, labels], 0)
    count = n_frow * n_fcol

    def next_row(i):
        j = i ^ n_fcol if n_fcol & (n_fcol - 1) == 0 else i
        return j if j < count else i

    col_a, col_b = [
        lax.ppermute(mid, ("frow", "fcol"), all_paired(
            [(r * n_fcol + i, r * n_fcol + j) for r in range(n_frow) for i, j in pairs],
            count, next_row))
        for pairs in swaps(n_fcol)]
    looked = pl.pallas_call(
        functools.partial(gain_kernel, depth),
        out_shape=shaped(40 * NT, 2 * depth, dtype=BF16),
        in_specs=[vmem] * 3,
        out_specs=vmem,
        compiler_params=params(8),
        name="gains",
    )(mid, col_a, col_b)
    return pl.pallas_call(
        functools.partial(image_kernel, n_frow, n_fcol, 3 * depth, n_lines, depth),
        out_shape=shaped(R, C),
        in_specs=[vmem] * 3,
        out_specs=pl.BlockSpec(memory_space=pl.ANY),
        scratch_shapes=[
            pltpu.VMEM((6, k_tiles, LANES), F32),
            pltpu.VMEM((half_r, k), BF16),
            pltpu.VMEM((half_r, k), BF16),
            pltpu.VMEM((M, k), F32),
            pltpu.VMEM((M, k), F32),
            pltpu.VMEM((half_c, k), BF16),
            pltpu.VMEM((half_c, k), BF16),
            pltpu.VMEM((5, k_tiles, LANES), F32),
            pltpu.VMEM((2, k_tiles, LANES), jnp.int32),
            pltpu.VMEM((k_tiles, 2, 2, half_r // SUB, LANES), F32),
            pltpu.VMEM((R, C), F32),
            pltpu.VMEM((wide, k), BF16),
            pltpu.VMEM((wide, k), BF16),
            pltpu.VMEM((6 * M, k), BF16),
            pltpu.VMEM((6 * M, k), BF16),
            pltpu.VMEM((2, SUB, k), F32),
            pltpu.VMEM((half_r, wide), F32),
            pltpu.VMEM((half_r, wide), F32),
            pltpu.VMEM((6 * M, half_c), F32),
            pltpu.VMEM((6 * M, half_c), F32),
            pltpu.SemaphoreType.DMA((2 * half_r // M * (half_c // LANES),)),
        ],
        compiler_params=params(36),
        name="image",
    )(blocks, mid, looked)


def solution(mesh):
    return jax.shard_map(
        shards,
        mesh=mesh,
        in_specs=(
            P(None, ("frow", "fcol")),
            P(None, ("frow", "fcol")),
            P(("frow", "fcol")),
            P(),
            P(),
            P("frow", "fcol", None, None),
            P(),
        ),
        out_specs=P("frow", "fcol"),
        check_vma=False,
    )
```

```python
import functools
import math

import jax
import jax.numpy as jnp
from jax import lax
from jax.experimental import pallas as pl
from jax.experimental.pallas import tpu as pltpu
from jax.sharding import PartitionSpec as P

R = 1024
C = 512
M = 64
NT = 16
NBLK = 4
LANES = 128
SUB = 8
OWN, LEFT, RIGHT, UP, DOWN, UL, UR, DL, DR = range(9)
F32 = jnp.float32
BF16 = jnp.bfloat16


def wrap(m, modulus):
    if modulus & (modulus - 1) == 0:
        return m & (modulus - 1)
    return jnp.remainder(m, modulus)


def turn(m, modulus):
    m = wrap(m, modulus)
    quarter = modulus // 4
    q = (m + modulus // 8) // quarter if quarter & (quarter - 1) else (
        (m + modulus // 8) >> (quarter.bit_length() - 1))
    x = (m - q * quarter).astype(F32) * (2.0 * math.pi / modulus)
    x2 = x * x
    s = x + x * x2 * (-1 / 6 + x2 * (1 / 120 + x2 * (-1 / 5040 + x2 * (1 / 362880))))
    c = 1.0 + x2 * (-0.5 + x2 * (1 / 24 + x2 * (-1 / 720 + x2 * (1 / 40320))))
    odd = (q & 1) == 1
    cos = jnp.where(odd, s, c)
    sin = jnp.where(odd, c, s)
    cos = jnp.where(((q + 1) & 2) != 0, -cos, cos)
    sin = jnp.where((q & 2) != 0, -sin, sin)
    return cos, sin


def times(a, b):
    return a[0] * b[0] - a[1] * b[1], a[0] * b[1] + a[1] * b[0]


def pack_kernel(order_ref, vis_ref, pair_ref, slot_ref, u_ref, v_ref, out_ref, label_ref):
    block = vis_ref.shape[1]
    lines = [vis_ref[0:1, :], vis_ref[1:2, :], pair_ref[0:1, :].astype(F32),
             pair_ref[1:2, :].astype(F32), slot_ref[...].astype(F32)]
    for copy in range(out_ref.shape[0]):
        for q, line in enumerate(lines):
            out_ref[copy, :, q * block:(q + 1) * block] = line
    n_lines = u_ref.shape[0]
    at = lax.broadcasted_iota(jnp.int32, (SUB, LANES), 1)
    order = jnp.zeros((SUB, LANES), jnp.int32)
    for b in range(NBLK):
        order = jnp.where(at == b, order_ref[b], order)
    label_ref[:SUB] = order.astype(F32)
    label_ref[SUB:SUB + n_lines] = u_ref[...].astype(F32)
    label_ref[SUB + n_lines:SUB + 2 * n_lines] = v_ref[...].astype(F32)


def pick(row, lane):
    return jnp.take_along_axis(
        jnp.broadcast_to(row, lane.shape), lane, axis=1, mode="promise_in_bounds")


def taper_rows(group, half, wide=LANES):
    index = (lax.broadcasted_iota(jnp.int32, (SUB, wide), 0) + SUB * group).astype(F32)
    return ((half + M - 0.5 - index) * (1.0 / (2 * M)),
            (index - (half - M - 0.5)) * (1.0 / (2 * M)))


def phase_tables(n_frow, n_fcol, first, n_lines, block_ref, cell_ref,
                 s_ref, ac_ref, as_ref, ec_ref, es_ref, fc_ref, fs_ref, cc_ref, cs_ref,
                 q_ref, uv_ref, dr_ref):
    frow_at = lax.axis_index("frow")
    fcol_at = lax.axis_index("fcol")
    half_r, half_c = R // 2, C // 2
    mod_r, mod_c = 2 * R * n_frow, 2 * C * n_fcol
    k_tiles = s_ref.shape[1]
    per_block = k_tiles // NBLK
    block = per_block * LANES
    shape = (SUB, LANES)

    order = cell_ref[first:first + 1, :]
    place = lax.broadcasted_iota(jnp.int32, (1, LANES), 1)
    owners = [jnp.sum(jnp.where(place == b, order, 0.0)).astype(jnp.int32) for b in range(NBLK)]
    for b, owner in enumerate(owners):
        for q in range(5):
            for j in range(per_block):
                q_ref[q, b * per_block + j:b * per_block + j + 1, :] = block_ref[
                    owner, :, q * block + j * LANES:q * block + (j + 1) * LANES]
    a1 = q_ref[2].astype(jnp.int32)
    a2 = q_ref[3].astype(jnp.int32)
    slot = q_ref[4].astype(jnp.int32)

    at = first + SUB

    def cells(table):
        got = [jnp.zeros(shape, F32)] * 2
        for h in range(table.shape[0]):
            row = table[h:h + 1, :]
            got = [jnp.where((a >> 7) == h, pick(row, a & 127), g)
                   for a, g in zip((a1, a2), got)]
        return (got[0] - got[1]).astype(jnp.int32)

    u = cells(cell_ref[at:at + n_lines, :])
    v = cells(cell_ref[at + n_lines:at + 2 * n_lines, :])
    uv_ref[0] = u
    uv_ref[1] = v
    centre = times(turn(u * (frow_at * (2 * R) + (R - 1)), mod_r),
                   turn(v * (fcol_at * (2 * C) + (C - 1)), mod_c))
    scale = 0.5 / math.sqrt(NBLK * per_block * LANES)
    value = times((q_ref[0] * scale, q_ref[1] * scale), centre)
    s_ref[0] = value[0]
    s_ref[1] = value[1]
    for n, a in enumerate((a1, a2)):
        s_ref[2 + n] = ((a >> 3) + (a & 6) * 32).astype(F32)
        s_ref[4 + n] = ((a & 1) * NT + slot).astype(F32)

    iota = lax.broadcasted_iota(jnp.int32, shape, 0)

    def tables(s):
        lane = slice(s * LANES, (s + 1) * LANES)

        def phases(which, modulus, half):
            freq = jnp.broadcast_to(uv_ref[which, s:s + 1, :], shape)
            fine = turn(freq * (2 * iota + 1), modulus)
            middle = turn(freq * (16 * iota), modulus)
            coarse = turn(freq * (128 * iota), modulus)
            for a in range(half // 64):
                top = tuple(jnp.broadcast_to(x[a:a + 1], shape) for x in coarse)
                both = times(middle, top)
                for comp in range(2):
                    dr_ref[s, which, comp, 8 * a:8 * a + 8, :] = both[comp]
            for g in range(half // SUB):
                step = tuple(jnp.broadcast_to(dr_ref[s, which, comp, g:g + 1, :], shape)
                             for comp in range(2))
                yield times(fine, step)

        pairs = {}

        def put(ref, first, group, x):
            key = (id(ref), first)
            if group % 2 == 0:
                pairs[key] = x
            else:
                start = first + SUB * (group - 1)
                ref[start:start + 16, lane] = jnp.concatenate([pairs.pop(key), x], 0).astype(BF16)

        edge = (half_r - M) // SUB
        for g, (cos, sin) in enumerate(phases(0, mod_r, half_r)):
            if g >= edge:
                mine, other = taper_rows(g, half_r)
                at = slice((g - edge) * SUB, (g - edge + 1) * SUB)
                ec_ref[at, lane] = cos * other
                es_ref[at, lane] = sin * other
                cos, sin = cos * mine, sin * mine
            put(ac_ref, 0, g, cos)
            put(as_ref, 0, g, sin)
        for g, (cos, sin) in enumerate(phases(1, mod_c, half_c)):
            put(cc_ref, 0, g, cos)
            put(cs_ref, 0, g, sin)
            at = slice(g * SUB, (g + 1) * SUB)
            fc_ref[at, lane] = cos
            fs_ref[at, lane] = sin

    return tables


def gain_kernel(depth, mid_ref, a_ref, b_ref, gain_ref):
    half = depth // 2
    places = 2 * NT
    low_lane = lax.broadcasted_iota(jnp.int32, (places, LANES), 1) < LANES // 2
    for f in range(9):
        ref, row = (mid_ref, a_ref, b_ref)[f // 3], f % 3 * depth
        both = jnp.concatenate([ref[pl.ds(row, half, stride=2), :],
                                ref[pl.ds(row + 1, half, stride=2), :]], 0).T
        quarter = [both[i * places:(i + 1) * places] for i in range(4)]
        turned = [pltpu.roll(x, LANES // 2, 1) for x in quarter]
        for t in range(2):
            re = jnp.where(low_lane, quarter[2 * t], turned[2 * t + 1])
            im = jnp.where(low_lane, turned[2 * t], quarter[2 * t + 1])
            for comp, x in enumerate((re, im)):
                high = x.astype(BF16)
                at = (2 * (f - 1 if f else SUB) + comp) * places
                gain_ref[at:at + places, t * LANES:(t + 1) * LANES] = high
                if f == 0:
                    at += 2 * places
                    gain_ref[at:at + places, t * LANES:(t + 1) * LANES] = (
                        x - high.astype(F32)).astype(BF16)


def image_kernel(n_frow, n_fcol, first, n_lines, depth, block_ref, cell_ref, gain_ref, image_ref,
                 s_ref, ac_ref, as_ref, ec_ref, es_ref, fc_ref, fs_ref, cc_ref, cs_ref,
                 q_ref, uv_ref, dr_ref, out_ref, tc_ref, ts_ref, uc_ref, us_ref, w_ref,
                 m1_ref, m2_ref, g1_ref, g2_ref, sems):
    tables = phase_tables(n_frow, n_fcol, first, n_lines, block_ref, cell_ref, s_ref, ac_ref,
                          as_ref, ec_ref, es_ref, fc_ref, fs_ref, cc_ref, cs_ref,
                          q_ref, uv_ref, dr_ref)
    frow_at = lax.axis_index("frow")
    r_odd = lax.rem(frow_at, 2) == 1
    fcol_at = lax.axis_index("fcol")
    c_odd = lax.rem(fcol_at, 2) == 1
    k_tiles = s_ref.shape[1]
    half_c = C // 2
    places = 2 * NT

    r_first, r_second = jnp.where(r_odd, 1, 2), jnp.where(r_odd, 2, 1)
    c_first, c_second = jnp.where(c_odd, 1, 2), jnp.where(c_odd, 2, 1)
    rows = {UP: r_first - 1, DOWN: r_second - 1, LEFT: 3 * c_first - 1, RIGHT: 3 * c_second - 1,
            UL: 3 * c_first + r_first - 1, UR: 3 * c_second + r_first - 1,
            DL: 3 * c_first + r_second - 1, DR: 3 * c_second + r_second - 1}

    step = 2 if k_tiles % 2 == 0 else 1
    wide = step * LANES
    shape = (SUB, wide)
    line_at = lax.broadcasted_iota(jnp.int32, (2 * depth, wide), 0).astype(F32)
    place_at = line_at[:places]
    row_at = lax.broadcasted_iota(jnp.int32, shape, 0)
    zero = jnp.zeros((M, wide), BF16)
    r_edge = jnp.logical_or(frow_at == 0, frow_at == n_frow - 1)
    c_edge = jnp.logical_or(fcol_at == 0, fcol_at == n_fcol - 1)
    keep = (jnp.where(lax.rem(row_at, 3) == 1, jnp.where(r_edge, 0.0, 1.0), 1.0)
            * jnp.where(row_at >= 5, jnp.where(c_edge, 0.0, 1.0), 1.0))

    def fold(parts):
        parts = [parts[i] for i in (0, 4, 2, 6, 1, 5, 3, 7)]
        for distance in (1, 2, 4):
            low = (row_at & distance) == 0
            count = len(parts) // 2
            parts = [jnp.where(low, x, y) + pltpu.roll(jnp.where(low, y, x), distance, 0)
                     for x, y in zip(parts[:count], parts[count:])]
        return parts[0]

    def gain_product(first, second):
        (g1r, g1i), (g2r, g2i) = first, second
        return g1r * g2r + g1i * g2i, g1i * g2r - g1r * g2i

    def weight(f, lane):
        return tuple(jnp.broadcast_to(w_ref[comp, pl.ds(rows[f], 1), lane], shape)
                     for comp in range(2))

    def line(p, q):
        return jnp.concatenate([s_ref[q, p * step + i:p * step + i + 1, :]
                                for i in range(step)], 1)

    def look_up(p):
        for i in range(step):
            tables(p * step + i)
        found = []
        for n in range(2):
            hot = jnp.where(line_at == line(p, 2 + n), 1.0, 0.0).astype(BF16)
            found.append(jnp.dot(gain_ref[...], hot, preferred_element_type=F32))
        return found

    def weigh(p, found):
        lane = slice(p * wide, (p + 1) * wide)
        owns, nears = [], []
        for n, z in enumerate(found):
            mask = jnp.where(place_at == line(p, 4 + n), 1.0, 0.0)

            def part(f, comp):
                at = (2 * f + comp) * places
                x = z[at:at + places]
                if f == SUB:
                    x = x + z[at + 2 * places:at + 3 * places]
                x = x * mask
                return sum((x[i * SUB:(i + 1) * SUB] for i in range(1, places // SUB)), x[:SUB])

            owns.append([jnp.sum(part(SUB, comp), axis=0, keepdims=True) for comp in range(2)])
            nears.append([fold([part(f, comp) for f in range(SUB)]) for comp in range(2)])
        value = (line(p, 0), line(p, 1))
        own_w = times(value, gain_product(*owns))
        near_w = times(tuple(x * keep for x in value), gain_product(*nears))
        for comp in range(2):
            w_ref[comp, :, lane] = near_w[comp]

        pairs = {}

        def put(ref, first, group, x):
            key = (id(ref), first)
            if group % 2 == 0:
                pairs[key] = x
            else:
                start = first + SUB * (group - 1)
                ref[start:start + 16, lane] = jnp.concatenate([pairs.pop(key), x], 0).astype(BF16)

        edge = (half_c - M) // SUB
        wr, wi = [jnp.broadcast_to(x, shape) for x in own_w]
        (lr, li), (rr, ri) = weight(LEFT, lane), weight(RIGHT, lane)
        for g in range(half_c // SUB):
            at = slice(g * SUB, (g + 1) * SUB)
            cos, sin = fc_ref[at, lane], fs_ref[at, lane]
            own = (cos, sin)
            if g >= edge:
                mine, other = taper_rows(g, half_c, wide)
                own = (cos * mine, sin * mine)
                cos, sin = cos * other, sin * other
                base = 2 * half_c + M
                put(tc_ref, base, g - edge, lr * cos + li * sin)
                put(ts_ref, base, g - edge, lr * sin - li * cos)
                put(tc_ref, base + 2 * M, g - edge, rr * cos - ri * sin)
                put(ts_ref, base + 2 * M, g - edge, -(rr * sin + ri * cos))
            base = g * SUB // LANES * LANES
            put(tc_ref, base, g, wr * own[0])
            put(tc_ref, base + LANES, g, -wi * own[1])
            put(ts_ref, base, g, -wi * own[0])
            put(ts_ref, base + LANES, g, -wr * own[1])
        for ref in (tc_ref, ts_ref):
            ref[2 * half_c:2 * half_c + M, lane] = zero
            ref[2 * half_c + 2 * M:2 * half_c + 3 * M, lane] = zero

    steps = k_tiles // step
    ahead = look_up(0)
    for p in range(steps):
        found = ahead
        if p + 1 < steps:
            ahead = look_up(p + 1)
        weigh(p, found)

    def dot(a, b):
        return lax.dot_general(a, b, (((1,), (1,)), ((), ())), preferred_element_type=F32)

    half_r = R // 2
    n_lane = half_c // LANES

    def own_products(t):
        cols = slice(2 * t * LANES, 2 * (t + 1) * LANES if t < n_lane - 1 else tc_ref.shape[0])
        m1_ref[:, cols] = dot(ac_ref[...], tc_ref[cols, :])
        m2_ref[:, cols] = dot(as_ref[...], ts_ref[cols, :])

    own_products(n_lane - 1)
    signs = (-1, 1, -1, -1, 1, 1)
    for p in range(k_tiles // step):
        lane = slice(p * wide, (p + 1) * wide)
        for n, (f, sd) in enumerate(zip((UP, DOWN, UL, UR, DL, DR), signs)):
            wr, wi = weight(f, lane)
            for g in range(0, M // SUB, 2):
                tops, lows = [], []
                for i in range(2):
                    at = slice((g + i) * SUB, (g + i + 1) * SUB)
                    cos, sin = ec_ref[at, lane], es_ref[at, lane]
                    tops.append(wr * cos - (sd * wi) * sin)
                    lows.append(-(sd * wr) * sin - wi * cos)
                at = slice(n * M + g * SUB, n * M + (g + 2) * SUB)
                uc_ref[at, lane] = jnp.concatenate(tops, 0).astype(BF16)
                us_ref[at, lane] = jnp.concatenate(lows, 0).astype(BF16)
    g1_ref[...] = dot(uc_ref[...], cc_ref[...])
    g2_ref[...] = dot(us_ref[...], cs_ref[...])

    shape = (SUB, LANES)
    iota = lax.broadcasted_iota(jnp.int32, shape, 0)
    lane_at = lax.broadcasted_iota(jnp.int32, shape, 1)
    back_lane = (LANES - 1) - lane_at
    back_row = (SUB - 1) - iota
    edge_c = half_c - M
    edge_r = half_r - M
    col_own, col_other = [], []
    for t in range(n_lane):
        index = (lane_at + t * LANES).astype(F32)
        col_own.append(jnp.minimum((half_c + M - 0.5 - index) * (1.0 / (2 * M)), 1.0))
        col_other.append(jnp.maximum((index - (half_c - M - 0.5)) * (1.0 / (2 * M)), 0.0))

    def flip(x, index, axis):
        return jnp.take_along_axis(x, index, axis=axis, mode="promise_in_bounds")

    def finish(g, t, edged):
        rows = slice(g * SUB, (g + 1) * SUB)
        def part(ref, which):
            return ref[rows, (2 * t + which) * LANES:(2 * t + which + 1) * LANES]
        p, s_, r, q = part(m1_ref, 0), part(m1_ref, 1), part(m2_ref, 0), part(m2_ref, 1)
        even, odd = p + q, p - q
        plus, minus = r + s_, r - s_
        quad = {(1, 1): even + plus, (-1, -1): even - plus,
                (1, -1): odd + minus, (-1, 1): odd - minus}
        if (t + 1) * LANES > edge_c:
            base = 2 * half_c
            off = t * LANES - (half_c - LANES)
            for se, start in ((-1, base), (1, base + LANES)):
                lc = m1_ref[rows, start + off:start + off + LANES]
                ls = m2_ref[rows, start + off:start + off + LANES]
                quad[1, se] += lc + ls
                quad[-1, se] += lc - ls
        if edged:
            def edge(n):
                at = slice(n * M + g * SUB - edge_r, n * M + (g + 1) * SUB - edge_r)
                x = g1_ref[at, t * LANES:(t + 1) * LANES]
                y = g2_ref[at, t * LANES:(t + 1) * LANES]
                return {1: x + y, -1: x - y}
            for n, sd in ((0, -1), (1, 1)):
                e = edge(n)
                for se in (-1, 1):
                    quad[sd, se] += e[se] * col_own[t]
            if (t + 1) * LANES > edge_c:
                for n, (sd, se) in ((2, (-1, -1)), (3, (-1, 1)), (4, (1, -1)), (5, (1, 1))):
                    quad[sd, se] += edge(n)[se] * col_other[t]
        for (sd, se), x in quad.items():
            if sd < 0:
                x = flip(x, back_row, 0)
                at = slice(half_r - SUB - g * SUB, half_r - g * SUB)
            else:
                at = slice(half_r + g * SUB, half_r + (g + 1) * SUB)
            if se < 0:
                x = flip(x, back_lane, 1)
                start = half_c - (t + 1) * LANES
            else:
                start = half_c + t * LANES
            out_ref[at, start:start + LANES] = x

    n_groups = half_r // M

    def sends(j, t):
        copies = []
        for row in (half_r + 2 * M * j, half_r - 2 * M * (j + 1)):
            for col in (half_c + t * LANES, half_c - (t + 1) * LANES):
                at = (slice(row, row + 2 * M), slice(col, col + LANES))
                copies.append(pltpu.make_async_copy(
                    out_ref.at[at], image_ref.at[at], sems.at[(j * n_lane + t) * 4 + len(copies)]))
        return copies

    for t in range(n_lane - 2, -1, -1):
        own_products(t)
    for t in range(n_lane - 1, -1, -1):
        for j in range(n_groups):
            for g in range(j * M // SUB, (j + 1) * M // SUB):
                finish(g, t, j == n_groups - 1)
            if j % 2:
                for copy in sends(j // 2, t):
                    copy.start()
    for t in range(n_lane):
        for j in range(n_groups // 2):
            for copy in sends(j, t):
                copy.wait()


def swaps(size):
    both = []
    for first in (0, 1):
        pairs = [(i, i + 1) for i in range(first, size - 1, 2)]
        both.append(pairs + [(j, i) for i, j in pairs])
    return both


def all_paired(pairs, count, other):
    swap = dict(pairs)
    for i in range(count):
        if i not in swap and other(i) not in swap:
            swap[i], swap[other(i)] = other(i), i
    return list(swap.items())


def shards(vis, station_pairs, visibility_time_slot, station_u_cells, station_v_cells,
           facet_station_gains, holder_device_order):
    n_frow = lax.axis_size("frow")
    n_fcol = lax.axis_size("fcol")
    block = vis.shape[1]
    k_tiles = NBLK * block // LANES
    k = k_tiles * LANES
    half_r, half_c = R // 2, C // 2
    wide = 2 * half_c + 4 * M
    vmem = pl.BlockSpec(memory_space=pltpu.VMEM)
    smem = pl.BlockSpec(memory_space=pltpu.SMEM)

    def lines(x):
        return x.reshape(-1, LANES)

    def shaped(*dims, dtype=F32):
        return jax.ShapeDtypeStruct(dims, dtype)

    def params(mib):
        return pltpu.CompilerParams(vmem_limit_bytes=mib * 1024 * 1024)

    n_lines = station_u_cells.size // LANES
    packed, labels = pl.pallas_call(
        pack_kernel,
        out_shape=[shaped(n_frow * n_fcol, 1, 5 * block), shaped(SUB + 2 * n_lines, LANES)],
        in_specs=[smem] + [vmem] * 5,
        name="pack",
    )(holder_device_order, vis, station_pairs, visibility_time_slot.reshape(1, block),
      lines(station_u_cells), lines(station_v_cells))
    facet_station_gains, packed = lax.optimization_barrier((facet_station_gains, packed))
    gains = facet_station_gains[0, 0]
    depth = gains.size // LANES
    own = gains.reshape(2, -1, LANES).transpose(1, 0, 2).reshape(depth, LANES)
    row_a, row_b = [lax.ppermute(own, "frow", all_paired(pairs, n_frow, lambda r: n_frow - 1 - r))
                    for pairs in swaps(n_frow)]
    blocks = lax.all_to_all(packed, ("frow", "fcol"), 0, 0)
    mid = jnp.concatenate([own, row_a, row_b, labels], 0)
    count = n_frow * n_fcol

    def next_row(i):
        j = i ^ n_fcol if n_fcol & (n_fcol - 1) == 0 else i
        return j if j < count else i

    col_a, col_b = [
        lax.ppermute(mid, ("frow", "fcol"), all_paired(
            [(r * n_fcol + i, r * n_fcol + j) for r in range(n_frow) for i, j in pairs],
            count, next_row))
        for pairs in swaps(n_fcol)]
    looked = pl.pallas_call(
        functools.partial(gain_kernel, depth),
        out_shape=shaped(40 * NT, 2 * depth, dtype=BF16),
        in_specs=[vmem] * 3,
        out_specs=vmem,
        compiler_params=params(8),
        name="gains",
    )(mid, col_a, col_b)
    return pl.pallas_call(
        functools.partial(image_kernel, n_frow, n_fcol, 3 * depth, n_lines, depth),
        out_shape=shaped(R, C),
        in_specs=[vmem] * 3,
        out_specs=pl.BlockSpec(memory_space=pl.ANY),
        scratch_shapes=[
            pltpu.VMEM((6, k_tiles, LANES), F32),
            pltpu.VMEM((half_r, k), BF16),
            pltpu.VMEM((half_r, k), BF16),
            pltpu.VMEM((M, k), F32),
            pltpu.VMEM((M, k), F32),
            pltpu.VMEM((half_c, k), F32),
            pltpu.VMEM((half_c, k), F32),
            pltpu.VMEM((half_c, k), BF16),
            pltpu.VMEM((half_c, k), BF16),
            pltpu.VMEM((5, k_tiles, LANES), F32),
            pltpu.VMEM((2, k_tiles, LANES), jnp.int32),
            pltpu.VMEM((k_tiles, 2, 2, half_r // SUB, LANES), F32),
            pltpu.VMEM((R, C), F32),
            pltpu.VMEM((wide, k), BF16),
            pltpu.VMEM((wide, k), BF16),
            pltpu.VMEM((6 * M, k), BF16),
            pltpu.VMEM((6 * M, k), BF16),
            pltpu.VMEM((2, SUB, k), F32),
            pltpu.VMEM((half_r, wide), F32),
            pltpu.VMEM((half_r, wide), F32),
            pltpu.VMEM((6 * M, half_c), F32),
            pltpu.VMEM((6 * M, half_c), F32),
            pltpu.SemaphoreType.DMA((2 * half_r // M * (half_c // LANES),)),
        ],
        compiler_params=params(36),
        name="image",
    )(blocks, mid, looked)


def solution(mesh):
    return jax.shard_map(
        shards,
        mesh=mesh,
        in_specs=(
            P(None, ("frow", "fcol")),
            P(None, ("frow", "fcol")),
            P(("frow", "fcol")),
            P(),
            P(),
            P("frow", "fcol", None, None),
            P(),
        ),
        out_specs=P("frow", "fcol"),
        check_vma=False,
    )
```

```python
import functools
import math

import jax
import jax.numpy as jnp
from jax import lax
from jax.experimental import pallas as pl
from jax.experimental.pallas import tpu as pltpu
from jax.sharding import PartitionSpec as P

R = 1024
C = 512
M = 64
NT = 16
NBLK = 4
LANES = 128
SUB = 8
OWN, LEFT, RIGHT, UP, DOWN, UL, UR, DL, DR = range(9)
F32 = jnp.float32
BF16 = jnp.bfloat16


def wrap(m, modulus):
    if modulus & (modulus - 1) == 0:
        return m & (modulus - 1)
    return jnp.remainder(m, modulus)


def turn(m, modulus):
    m = wrap(m, modulus)
    quarter = modulus // 4
    q = (m + modulus // 8) // quarter if quarter & (quarter - 1) else (
        (m + modulus // 8) >> (quarter.bit_length() - 1))
    x = (m - q * quarter).astype(F32) * (2.0 * math.pi / modulus)
    x2 = x * x
    s = x + x * x2 * (-1 / 6 + x2 * (1 / 120 + x2 * (-1 / 5040 + x2 * (1 / 362880))))
    c = 1.0 + x2 * (-0.5 + x2 * (1 / 24 + x2 * (-1 / 720 + x2 * (1 / 40320))))
    odd = (q & 1) == 1
    cos = jnp.where(odd, s, c)
    sin = jnp.where(odd, c, s)
    cos = jnp.where(((q + 1) & 2) != 0, -cos, cos)
    sin = jnp.where((q & 2) != 0, -sin, sin)
    return cos, sin


def times(a, b):
    return a[0] * b[0] - a[1] * b[1], a[0] * b[1] + a[1] * b[0]


def pack_kernel(order_ref, vis_ref, pair_ref, slot_ref, u_ref, v_ref, out_ref, label_ref):
    block = vis_ref.shape[1]
    lines = [vis_ref[0:1, :], vis_ref[1:2, :], pair_ref[0:1, :].astype(F32),
             pair_ref[1:2, :].astype(F32), slot_ref[...].astype(F32)]
    for copy in range(out_ref.shape[0]):
        for q, line in enumerate(lines):
            out_ref[copy, :, q * block:(q + 1) * block] = line
    n_lines = u_ref.shape[0]
    at = lax.broadcasted_iota(jnp.int32, (SUB, LANES), 1)
    order = jnp.zeros((SUB, LANES), jnp.int32)
    for b in range(NBLK):
        order = jnp.where(at == b, order_ref[b], order)
    label_ref[:SUB] = order.astype(F32)
    label_ref[SUB:SUB + n_lines] = u_ref[...].astype(F32)
    label_ref[SUB + n_lines:SUB + 2 * n_lines] = v_ref[...].astype(F32)


def pick(row, lane):
    return jnp.take_along_axis(
        jnp.broadcast_to(row, lane.shape), lane, axis=1, mode="promise_in_bounds")


def taper_rows(group, half, wide=LANES):
    index = (lax.broadcasted_iota(jnp.int32, (SUB, wide), 0) + SUB * group).astype(F32)
    return ((half + M - 0.5 - index) * (1.0 / (2 * M)),
            (index - (half - M - 0.5)) * (1.0 / (2 * M)))


def phase_tables(n_frow, n_fcol, first, n_lines, block_ref, cell_ref,
                 s_ref, ac_ref, as_ref, ec_ref, es_ref, fc_ref, fs_ref, cc_ref, cs_ref,
                 q_ref, uv_ref, dr_ref):
    frow_at = lax.axis_index("frow")
    fcol_at = lax.axis_index("fcol")
    half_r, half_c = R // 2, C // 2
    mod_r, mod_c = 2 * R * n_frow, 2 * C * n_fcol
    k_tiles = s_ref.shape[1]
    per_block = k_tiles // NBLK
    block = per_block * LANES
    shape = (SUB, LANES)

    order = cell_ref[first:first + 1, :]
    place = lax.broadcasted_iota(jnp.int32, (1, LANES), 1)
    owners = [jnp.sum(jnp.where(place == b, order, 0.0)).astype(jnp.int32) for b in range(NBLK)]
    for b, owner in enumerate(owners):
        for q in range(5):
            for j in range(per_block):
                q_ref[q, b * per_block + j:b * per_block + j + 1, :] = block_ref[
                    owner, :, q * block + j * LANES:q * block + (j + 1) * LANES]
    a1 = q_ref[2].astype(jnp.int32)
    a2 = q_ref[3].astype(jnp.int32)
    slot = q_ref[4].astype(jnp.int32)

    at = first + SUB

    def cells(table):
        got = [jnp.zeros(shape, F32)] * 2
        for h in range(table.shape[0]):
            row = table[h:h + 1, :]
            got = [jnp.where((a >> 7) == h, pick(row, a & 127), g)
                   for a, g in zip((a1, a2), got)]
        return (got[0] - got[1]).astype(jnp.int32)

    u = cells(cell_ref[at:at + n_lines, :])
    v = cells(cell_ref[at + n_lines:at + 2 * n_lines, :])
    uv_ref[0] = u
    uv_ref[1] = v
    centre = times(turn(u * (frow_at * (2 * R) + (R - 1)), mod_r),
                   turn(v * (fcol_at * (2 * C) + (C - 1)), mod_c))
    scale = 0.5 / math.sqrt(NBLK * per_block * LANES)
    value = times((q_ref[0] * scale, q_ref[1] * scale), centre)
    s_ref[0] = value[0]
    s_ref[1] = value[1]
    for n, a in enumerate((a1, a2)):
        s_ref[2 + n] = ((a >> 3) + (a & 6) * 32).astype(F32)
        s_ref[4 + n] = ((a & 1) * NT + slot).astype(F32)

    iota = lax.broadcasted_iota(jnp.int32, shape, 0)

    def tables(s):
        lane = slice(s * LANES, (s + 1) * LANES)

        def phases(which, modulus, half):
            freq = jnp.broadcast_to(uv_ref[which, s:s + 1, :], shape)
            fine = turn(freq * (2 * iota + 1), modulus)
            middle = turn(freq * (16 * iota), modulus)
            coarse = turn(freq * (128 * iota), modulus)
            for a in range(half // 64):
                top = tuple(jnp.broadcast_to(x[a:a + 1], shape) for x in coarse)
                both = times(middle, top)
                for comp in range(2):
                    dr_ref[s, which, comp, 8 * a:8 * a + 8, :] = both[comp]
            for g in range(half // SUB):
                step = tuple(jnp.broadcast_to(dr_ref[s, which, comp, g:g + 1, :], shape)
                             for comp in range(2))
                yield times(fine, step)

        pairs = {}

        def put(ref, first, group, x):
            key = (id(ref), first)
            if group % 2 == 0:
                pairs[key] = x
            else:
                start = first + SUB * (group - 1)
                ref[start:start + 16, lane] = jnp.concatenate([pairs.pop(key), x], 0).astype(BF16)

        edge = (half_r - M) // SUB
        for g, (cos, sin) in enumerate(phases(0, mod_r, half_r)):
            if g >= edge:
                mine, other = taper_rows(g, half_r)
                at = slice((g - edge) * SUB, (g - edge + 1) * SUB)
                ec_ref[at, lane] = cos * other
                es_ref[at, lane] = sin * other
                cos, sin = cos * mine, sin * mine
            put(ac_ref, 0, g, cos)
            put(as_ref, 0, g, sin)
        for g, (cos, sin) in enumerate(phases(1, mod_c, half_c)):
            put(cc_ref, 0, g, cos)
            put(cs_ref, 0, g, sin)
            at = slice(g * SUB, (g + 1) * SUB)
            fc_ref[at, lane] = cos
            fs_ref[at, lane] = sin

    return tables


def gain_kernel(depth, mid_ref, a_ref, b_ref, gain_ref):
    half = depth // 2
    places = 2 * NT
    low_lane = lax.broadcasted_iota(jnp.int32, (places, LANES), 1) < LANES // 2
    for f in range(9):
        ref, row = (mid_ref, a_ref, b_ref)[f // 3], f % 3 * depth
        both = jnp.concatenate([ref[pl.ds(row, half, stride=2), :],
                                ref[pl.ds(row + 1, half, stride=2), :]], 0).T
        quarter = [both[i * places:(i + 1) * places] for i in range(4)]
        turned = [pltpu.roll(x, LANES // 2, 1) for x in quarter]
        for t in range(2):
            re = jnp.where(low_lane, quarter[2 * t], turned[2 * t + 1])
            im = jnp.where(low_lane, turned[2 * t], quarter[2 * t + 1])
            for comp, x in enumerate((re, im)):
                high = x.astype(BF16)
                at = (2 * (f - 1 if f else SUB) + comp) * places
                gain_ref[at:at + places, t * LANES:(t + 1) * LANES] = high
                if f == 0:
                    at += 2 * places
                    gain_ref[at:at + places, t * LANES:(t + 1) * LANES] = (
                        x - high.astype(F32)).astype(BF16)


def image_kernel(n_frow, n_fcol, first, n_lines, depth, block_ref, cell_ref, gain_ref, image_ref,
                 s_ref, ac_ref, as_ref, ec_ref, es_ref, fc_ref, fs_ref, cc_ref, cs_ref,
                 q_ref, uv_ref, dr_ref, out_ref, tc_ref, ts_ref, uc_ref, us_ref, w_ref,
                 m1_ref, m2_ref, g1_ref, g2_ref, sems):
    tables = phase_tables(n_frow, n_fcol, first, n_lines, block_ref, cell_ref, s_ref, ac_ref,
                          as_ref, ec_ref, es_ref, fc_ref, fs_ref, cc_ref, cs_ref,
                          q_ref, uv_ref, dr_ref)
    frow_at = lax.axis_index("frow")
    r_odd = lax.rem(frow_at, 2) == 1
    fcol_at = lax.axis_index("fcol")
    c_odd = lax.rem(fcol_at, 2) == 1
    k_tiles = s_ref.shape[1]
    half_c = C // 2
    places = 2 * NT

    r_first, r_second = jnp.where(r_odd, 1, 2), jnp.where(r_odd, 2, 1)
    c_first, c_second = jnp.where(c_odd, 1, 2), jnp.where(c_odd, 2, 1)
    rows = {UP: r_first - 1, DOWN: r_second - 1, LEFT: 3 * c_first - 1, RIGHT: 3 * c_second - 1,
            UL: 3 * c_first + r_first - 1, UR: 3 * c_second + r_first - 1,
            DL: 3 * c_first + r_second - 1, DR: 3 * c_second + r_second - 1}

    step = 2 if k_tiles % 2 == 0 else 1
    wide = step * LANES
    shape = (SUB, wide)
    line_at = lax.broadcasted_iota(jnp.int32, (2 * depth, wide), 0).astype(F32)
    place_at = line_at[:places]
    row_at = lax.broadcasted_iota(jnp.int32, shape, 0)
    zero = jnp.zeros((M, wide), BF16)
    r_edge = jnp.logical_or(frow_at == 0, frow_at == n_frow - 1)
    c_edge = jnp.logical_or(fcol_at == 0, fcol_at == n_fcol - 1)
    keep = (jnp.where(lax.rem(row_at, 3) == 1, jnp.where(r_edge, 0.0, 1.0), 1.0)
            * jnp.where(row_at >= 5, jnp.where(c_edge, 0.0, 1.0), 1.0))

    def fold(parts):
        parts = [parts[i] for i in (0, 4, 2, 6, 1, 5, 3, 7)]
        for distance in (1, 2, 4):
            low = (row_at & distance) == 0
            count = len(parts) // 2
            parts = [jnp.where(low, x, y) + pltpu.roll(jnp.where(low, y, x), distance, 0)
                     for x, y in zip(parts[:count], parts[count:])]
        return parts[0]

    def gain_product(first, second):
        (g1r, g1i), (g2r, g2i) = first, second
        return g1r * g2r + g1i * g2i, g1i * g2r - g1r * g2i

    def weight(f, lane):
        return tuple(jnp.broadcast_to(w_ref[comp, pl.ds(rows[f], 1), lane], shape)
                     for comp in range(2))

    for p in range(k_tiles // step):
        lane = slice(p * wide, (p + 1) * wide)

        def line(q):
            return jnp.concatenate([s_ref[q, p * step + i:p * step + i + 1, :]
                                    for i in range(step)], 1)

        for i in range(step):
            tables(p * step + i)
        owns, nears = [], []
        for n in range(2):
            hot = jnp.where(line_at == line(2 + n), 1.0, 0.0).astype(BF16)
            mask = jnp.where(place_at == line(4 + n), 1.0, 0.0)
            z = jnp.dot(gain_ref[...], hot, preferred_element_type=F32)

            def part(f, comp):
                at = (2 * f + comp) * places
                x = z[at:at + places]
                if f == SUB:
                    x = x + z[at + 2 * places:at + 3 * places]
                x = x * mask
                return sum((x[i * SUB:(i + 1) * SUB] for i in range(1, places // SUB)), x[:SUB])

            owns.append([jnp.sum(part(SUB, comp), axis=0, keepdims=True) for comp in range(2)])
            nears.append([fold([part(f, comp) for f in range(SUB)]) for comp in range(2)])
        value = (line(0), line(1))
        own_w = times(value, gain_product(*owns))
        near_w = times(tuple(x * keep for x in value), gain_product(*nears))
        for comp in range(2):
            w_ref[comp, :, lane] = near_w[comp]

        pairs = {}

        def put(ref, first, group, x):
            key = (id(ref), first)
            if group % 2 == 0:
                pairs[key] = x
            else:
                start = first + SUB * (group - 1)
                ref[start:start + 16, lane] = jnp.concatenate([pairs.pop(key), x], 0).astype(BF16)

        edge = (half_c - M) // SUB
        wr, wi = [jnp.broadcast_to(x, shape) for x in own_w]
        (lr, li), (rr, ri) = weight(LEFT, lane), weight(RIGHT, lane)
        for g in range(half_c // SUB):
            at = slice(g * SUB, (g + 1) * SUB)
            cos, sin = fc_ref[at, lane], fs_ref[at, lane]
            own = (cos, sin)
            if g >= edge:
                mine, other = taper_rows(g, half_c, wide)
                own = (cos * mine, sin * mine)
                cos, sin = cos * other, sin * other
                base = 2 * half_c + M
                put(tc_ref, base, g - edge, lr * cos + li * sin)
                put(ts_ref, base, g - edge, lr * sin - li * cos)
                put(tc_ref, base + 2 * M, g - edge, rr * cos - ri * sin)
                put(ts_ref, base + 2 * M, g - edge, -(rr * sin + ri * cos))
            base = g * SUB // LANES * LANES
            put(tc_ref, base, g, wr * own[0])
            put(tc_ref, base + LANES, g, -wi * own[1])
            put(ts_ref, base, g, -wi * own[0])
            put(ts_ref, base + LANES, g, -wr * own[1])
        for ref in (tc_ref, ts_ref):
            ref[2 * half_c:2 * half_c + M, lane] = zero
            ref[2 * half_c + 2 * M:2 * half_c + 3 * M, lane] = zero

    def dot(a, b):
        return lax.dot_general(a, b, (((1,), (1,)), ((), ())), preferred_element_type=F32)

    half_r = R // 2
    n_lane = half_c // LANES

    def own_products(t, first=0, last=half_r):
        cols = slice(2 * t * LANES, 2 * (t + 1) * LANES if t < n_lane - 1 else tc_ref.shape[0])
        m1_ref[first:last, cols] = dot(ac_ref[first:last, :], tc_ref[cols, :])
        m2_ref[first:last, cols] = dot(as_ref[first:last, :], ts_ref[cols, :])

    own_products(n_lane - 1)
    signs = (-1, 1, -1, -1, 1, 1)
    for p in range(k_tiles // step):
        lane = slice(p * wide, (p + 1) * wide)
        for n, (f, sd) in enumerate(zip((UP, DOWN, UL, UR, DL, DR), signs)):
            wr, wi = weight(f, lane)
            for g in range(0, M // SUB, 2):
                tops, lows = [], []
                for i in range(2):
                    at = slice((g + i) * SUB, (g + i + 1) * SUB)
                    cos, sin = ec_ref[at, lane], es_ref[at, lane]
                    tops.append(wr * cos - (sd * wi) * sin)
                    lows.append(-(sd * wr) * sin - wi * cos)
                at = slice(n * M + g * SUB, n * M + (g + 2) * SUB)
                uc_ref[at, lane] = jnp.concatenate(tops, 0).astype(BF16)
                us_ref[at, lane] = jnp.concatenate(lows, 0).astype(BF16)
    g1_ref[...] = dot(uc_ref[...], cc_ref[...])
    g2_ref[...] = dot(us_ref[...], cs_ref[...])

    shape = (SUB, LANES)
    iota = lax.broadcasted_iota(jnp.int32, shape, 0)
    lane_at = lax.broadcasted_iota(jnp.int32, shape, 1)
    back_lane = (LANES - 1) - lane_at
    back_row = (SUB - 1) - iota
    edge_c = half_c - M
    edge_r = half_r - M
    col_own, col_other = [], []
    for t in range(n_lane):
        index = (lane_at + t * LANES).astype(F32)
        col_own.append(jnp.minimum((half_c + M - 0.5 - index) * (1.0 / (2 * M)), 1.0))
        col_other.append(jnp.maximum((index - (half_c - M - 0.5)) * (1.0 / (2 * M)), 0.0))

    def flip(x, index, axis):
        return jnp.take_along_axis(x, index, axis=axis, mode="promise_in_bounds")

    def finish(g, t, edged):
        rows = slice(g * SUB, (g + 1) * SUB)
        def part(ref, which):
            return ref[rows, (2 * t + which) * LANES:(2 * t + which + 1) * LANES]
        p, s_, r, q = part(m1_ref, 0), part(m1_ref, 1), part(m2_ref, 0), part(m2_ref, 1)
        even, odd = p + q, p - q
        plus, minus = r + s_, r - s_
        quad = {(1, 1): even + plus, (-1, -1): even - plus,
                (1, -1): odd + minus, (-1, 1): odd - minus}
        if (t + 1) * LANES > edge_c:
            base = 2 * half_c
            off = t * LANES - (half_c - LANES)
            for se, start in ((-1, base), (1, base + LANES)):
                lc = m1_ref[rows, start + off:start + off + LANES]
                ls = m2_ref[rows, start + off:start + off + LANES]
                quad[1, se] += lc + ls
                quad[-1, se] += lc - ls
        if edged:
            def edge(n):
                at = slice(n * M + g * SUB - edge_r, n * M + (g + 1) * SUB - edge_r)
                x = g1_ref[at, t * LANES:(t + 1) * LANES]
                y = g2_ref[at, t * LANES:(t + 1) * LANES]
                return {1: x + y, -1: x - y}
            for n, sd in ((0, -1), (1, 1)):
                e = edge(n)
                for se in (-1, 1):
                    quad[sd, se] += e[se] * col_own[t]
            if (t + 1) * LANES > edge_c:
                for n, (sd, se) in ((2, (-1, -1)), (3, (-1, 1)), (4, (1, -1)), (5, (1, 1))):
                    quad[sd, se] += edge(n)[se] * col_other[t]
        for (sd, se), x in quad.items():
            if sd < 0:
                x = flip(x, back_row, 0)
                at = slice(half_r - SUB - g * SUB, half_r - g * SUB)
            else:
                at = slice(half_r + g * SUB, half_r + (g + 1) * SUB)
            if se < 0:
                x = flip(x, back_lane, 1)
                start = half_c - (t + 1) * LANES
            else:
                start = half_c + t * LANES
            out_ref[at, start:start + LANES] = x

    n_groups = half_r // M

    def sends(j, t):
        copies = []
        for row in (half_r + 2 * M * j, half_r - 2 * M * (j + 1)):
            for col in (half_c + t * LANES, half_c - (t + 1) * LANES):
                at = (slice(row, row + 2 * M), slice(col, col + LANES))
                copies.append(pltpu.make_async_copy(
                    out_ref.at[at], image_ref.at[at], sems.at[(j * n_lane + t) * 4 + len(copies)]))
        return copies

    def finish_groups(t, first, last):
        for j in range(first, last):
            for g in range(j * M // SUB, (j + 1) * M // SUB):
                finish(g, t, j == n_groups - 1)
            if j % 2:
                for copy in sends(j // 2, t):
                    copy.start()

    middle = n_groups // 2
    for t in range(n_lane - 1, -1, -1):
        if t:
            own_products(t - 1, 0, half_r // 2)
        finish_groups(t, 0, middle)
        if t:
            own_products(t - 1, half_r // 2, half_r)
        finish_groups(t, middle, n_groups)
    for t in range(n_lane):
        for j in range(n_groups // 2):
            for copy in sends(j, t):
                copy.wait()


def swaps(size):
    both = []
    for first in (0, 1):
        pairs = [(i, i + 1) for i in range(first, size - 1, 2)]
        both.append(pairs + [(j, i) for i, j in pairs])
    return both


def all_paired(pairs, count, other):
    swap = dict(pairs)
    for i in range(count):
        if i not in swap and other(i) not in swap:
            swap[i], swap[other(i)] = other(i), i
    return list(swap.items())


def shards(vis, station_pairs, visibility_time_slot, station_u_cells, station_v_cells,
           facet_station_gains, holder_device_order):
    n_frow = lax.axis_size("frow")
    n_fcol = lax.axis_size("fcol")
    block = vis.shape[1]
    k_tiles = NBLK * block // LANES
    k = k_tiles * LANES
    half_r, half_c = R // 2, C // 2
    wide = 2 * half_c + 4 * M
    vmem = pl.BlockSpec(memory_space=pltpu.VMEM)
    smem = pl.BlockSpec(memory_space=pltpu.SMEM)

    def lines(x):
        return x.reshape(-1, LANES)

    def shaped(*dims, dtype=F32):
        return jax.ShapeDtypeStruct(dims, dtype)

    def params(mib):
        return pltpu.CompilerParams(vmem_limit_bytes=mib * 1024 * 1024)

    n_lines = station_u_cells.size // LANES
    packed, labels = pl.pallas_call(
        pack_kernel,
        out_shape=[shaped(n_frow * n_fcol, 1, 5 * block), shaped(SUB + 2 * n_lines, LANES)],
        in_specs=[smem] + [vmem] * 5,
        name="pack",
    )(holder_device_order, vis, station_pairs, visibility_time_slot.reshape(1, block),
      lines(station_u_cells), lines(station_v_cells))
    facet_station_gains, packed = lax.optimization_barrier((facet_station_gains, packed))
    gains = facet_station_gains[0, 0]
    depth = gains.size // LANES
    own = gains.reshape(2, -1, LANES).transpose(1, 0, 2).reshape(depth, LANES)
    row_a, row_b = [lax.ppermute(own, "frow", all_paired(pairs, n_frow, lambda r: n_frow - 1 - r))
                    for pairs in swaps(n_frow)]
    blocks = lax.all_to_all(packed, ("frow", "fcol"), 0, 0)
    mid = jnp.concatenate([own, row_a, row_b, labels], 0)
    count = n_frow * n_fcol

    def next_row(i):
        j = i ^ n_fcol if n_fcol & (n_fcol - 1) == 0 else i
        return j if j < count else i

    col_a, col_b = [
        lax.ppermute(mid, ("frow", "fcol"), all_paired(
            [(r * n_fcol + i, r * n_fcol + j) for r in range(n_frow) for i, j in pairs],
            count, next_row))
        for pairs in swaps(n_fcol)]
    looked = pl.pallas_call(
        functools.partial(gain_kernel, depth),
        out_shape=shaped(40 * NT, 2 * depth, dtype=BF16),
        in_specs=[vmem] * 3,
        out_specs=vmem,
        compiler_params=params(8),
        name="gains",
    )(mid, col_a, col_b)
    return pl.pallas_call(
        functools.partial(image_kernel, n_frow, n_fcol, 3 * depth, n_lines, depth),
        out_shape=shaped(R, C),
        in_specs=[vmem] * 3,
        out_specs=pl.BlockSpec(memory_space=pl.ANY),
        scratch_shapes=[
            pltpu.VMEM((6, k_tiles, LANES), F32),
            pltpu.VMEM((half_r, k), BF16),
            pltpu.VMEM((half_r, k), BF16),
            pltpu.VMEM((M, k), F32),
            pltpu.VMEM((M, k), F32),
            pltpu.VMEM((half_c, k), F32),
            pltpu.VMEM((half_c, k), F32),
            pltpu.VMEM((half_c, k), BF16),
            pltpu.VMEM((half_c, k), BF16),
            pltpu.VMEM((5, k_tiles, LANES), F32),
            pltpu.VMEM((2, k_tiles, LANES), jnp.int32),
            pltpu.VMEM((k_tiles, 2, 2, half_r // SUB, LANES), F32),
            pltpu.VMEM((R, C), F32),
            pltpu.VMEM((wide, k), BF16),
            pltpu.VMEM((wide, k), BF16),
            pltpu.VMEM((6 * M, k), BF16),
            pltpu.VMEM((6 * M, k), BF16),
            pltpu.VMEM((2, SUB, k), F32),
            pltpu.VMEM((half_r, wide), F32),
            pltpu.VMEM((half_r, wide), F32),
            pltpu.VMEM((6 * M, half_c), F32),
            pltpu.VMEM((6 * M, half_c), F32),
            pltpu.SemaphoreType.DMA((2 * half_r // M * (half_c // LANES),)),
        ],
        compiler_params=params(36),
        name="image",
    )(blocks, mid, looked)


def solution(mesh):
    return jax.shard_map(
        shards,
        mesh=mesh,
        in_specs=(
            P(None, ("frow", "fcol")),
            P(None, ("frow", "fcol")),
            P(("frow", "fcol")),
            P(),
            P(),
            P("frow", "fcol", None, None),
            P(),
        ),
        out_specs=P("frow", "fcol"),
        check_vma=False,
    )
```
